32 devices in a mesh: grp: 2 (over x), dev: 8 (over z, y), sub: 2 (over core).
Axes of the slice: x: 2, y: 2, z: 4, core: 2. Of those that a mesh axis runs over, the one named last changes fastest.
Arguments:
- tiles: bfloat16 [64, 256, 1536], P(('grp', 'dev')), parts along dimension 0, may hold values from -6 to 6
- counts: int32 [16], P('grp'), parts along dimension 0, may hold values from 1 to 4, as said below
- slide_of: int32 [16], P('grp'), parts along dimension 0, may hold values from 0 to 1, as said below
- rates: int32 [12], replicated, may hold values from 1 to 4
- tile_gain: float32 [1536], replicated, may hold values from 0.1 to 1.9
- gate_weight: bfloat16 [1536, 2048], P('dev', 'sub'), may hold values from -0.15625 to 0.15625
- up_weight: bfloat16 [1536, 2048], P('dev', 'sub'), may hold values from -0.15625 to 0.15625
- embed_proj: bfloat16 [2048, 768], P('sub'), may hold values from -0.5 to 0.5
- slide_gain: float32 [768], replicated, may hold values from 0.1 to 1.9
- slide_wq: bfloat16 [768, 768], P(None, 'sub'), may hold values from -2 to 2
- slide_wk: bfloat16 [768, 768], P(None, 'sub'), may hold values from -2 to 2
- slide_wv: bfloat16 [768, 768], P(None, 'sub'), may hold values from -0.21875 to 0.21875
- slide_wo: bfloat16 [768, 768], P('sub'), may hold values from -0.875 to 0.875
Outputs:
- tile_embed: bfloat16 [64, 2048], P(('grp', 'dev'), 'sub'), parts along dimension 0
- slide_out: bfloat16 [64, 768], P(('grp', 'dev'), 'sub'), parts along dimension 0
The draws below stay inside these ranges and needn't reach their ends.
There are 2 independent parts, one for each index of `grp`. The reference program is written for one: setup_inputs(seed, part) draws one part's arguments, and reference() takes and returns one part's arrays. A program takes and returns all parts, laid end to end along the dimension named above; an argument that names none is the same for every part. Nothing has to cross between parts.
Inputs may be any that keep to these rules, and one draw needn't show every extreme that they name: `counts`: exactly 4 devices of a group hold 4 tiles; every other device holds at most 2. slide_of never falls from one device to the next and names every slide; each slide covers 1 to 6 devices, and exactly one slide of each group covers 8 // 2 + 2.
All inputs are finite; a program needn't handle non-finite values.
Results may differ from the reference program's by a relative error of at most 0.02.
Values may be sent and summed in bfloat16 or wider, within the bound.
No kernel may reach another device: no remote copies, remote signals or barrier semaphores. Data moves between devices by JAX's collectives and lax.ppermute only.
A program may use at most 64 MiB of HBM per device.

```python
import math
import jax
import jax.numpy as jnp
from jax import lax

D = 1536
FF = 2048
TT = 256
E = 768
SH = 12
HD = 64
LOAD = 3
SLOTS = 4
TILES = 32
SLIDES = 2
N_DEV = 8


def draw_counts(key, part):
    key = jax.random.fold_in(key, 1)
    perm_key, count_key = jax.random.split(key)
    is_busy = jax.random.permutation(perm_key, N_DEV) < N_DEV // 2
    light_load = jax.random.randint(count_key, (N_DEV,), 1, LOAD)
    return jnp.where(is_busy, SLOTS, light_load).astype(jnp.int32)


def draw_slide_of(key, part):
    key = jax.random.fold_in(key, 11)
    cut_key, place_key = jax.random.split(key)
    remaining = N_DEV // 2 - 2
    order = jax.random.permutation(cut_key, remaining - 1).astype(jnp.int32) + 1
    cuts = jnp.sort(order[:SLIDES - 2])
    bounds = jnp.concatenate([jnp.zeros((1,), jnp.int32), cuts, jnp.full((1,), remaining, jnp.int32)])
    smaller = bounds[1:] - bounds[:-1]
    big_at = jax.random.randint(place_key, (), 0, SLIDES)
    slide_ids = jnp.arange(SLIDES, dtype=jnp.int32)
    source = jnp.clip(slide_ids - (slide_ids > big_at).astype(jnp.int32), 0, SLIDES - 2)
    widths = jnp.where(slide_ids == big_at, N_DEV // 2 + 2, smaller[source])
    ends = jnp.cumsum(widths)
    devices = jnp.arange(N_DEV, dtype=jnp.int32)
    return jnp.sum((ends[None, :] <= devices[:, None]).astype(jnp.int32), axis=1).astype(jnp.int32)


def draw_tiles(key, part):
    key = jax.random.fold_in(key, 3)
    common_key, token_key = jax.random.split(key, 2)
    common = jax.random.normal(common_key, (TILES, 1, D), jnp.float32)
    own_part = jax.random.normal(token_key, (TILES, TT, D), jnp.float32)
    values = 0.7 * common + 0.7 * own_part
    return jnp.clip(values, -6.0, 6.0).astype(jnp.bfloat16)


def draw_slide_wq(key, part):
    key = jax.random.fold_in(key, 6)
    private = jax.random.normal(key, (E, SH * HD), jnp.float32) * (1.4 / math.sqrt(E))
    return jnp.clip(private, -2.0, 2.0).astype(jnp.bfloat16)


def draw_slide_wk(key, part):
    key = jax.random.fold_in(key, 7)
    private = jax.random.normal(key, (E, SH * HD), jnp.float32) * (1.4 / math.sqrt(E))
    return jnp.clip(private, -2.0, 2.0).astype(jnp.bfloat16)


def set_ends(array, rng, least, largest):
    dims = array.shape
    spot = [jax.random.randint(jax.random.fold_in(rng, axis), (), 0, dims[axis]) for axis in range(len(dims))]
    array = array.at[tuple(spot)].set(least)
    longest = dims.index(max(dims))
    spot[longest] = (spot[longest] + 1) % dims[longest]
    return array.at[tuple(spot)].set(largest)


def block_scale(key, shape, pieces, low, high):
    gain, own = 1.0, jax.random.fold_in(key, 6)
    for dim, blocks in pieces:
        steps = jnp.exp(jax.random.uniform(jax.random.fold_in(own, dim), (blocks,), jnp.float32, low / len(pieces), high / len(pieces)))
        gain = gain * jnp.repeat(steps, shape[dim] // blocks).reshape([-1 if axis == dim else 1 for axis in range(len(shape))])
    return gain


def bell_draw(rng, shape, deviation, reach, shards=(), kind=jnp.bfloat16):
    values = jax.random.normal(rng, shape, jnp.float32) * deviation
    if len(shards) > 0:
        values = block_scale(rng, shape, shards, -0.22, 0.18) * values
    return jnp.clip(values, min=-reach, max=reach).astype(kind)


def setup_inputs(seed: int = 0, part: int = 0) -> dict:
    splits = jax.random.split(jax.random.key(seed), 14)
    own_keys = jax.random.split(jax.random.fold_in(splits[13], part), 14)
    return {
        "tiles": draw_tiles(jax.random.fold_in(jax.random.fold_in(splits[13], part), 71), part),
        "counts": draw_counts(jax.random.fold_in(jax.random.fold_in(splits[13], part), 71), part),
        "slide_of": draw_slide_of(jax.random.fold_in(jax.random.fold_in(splits[13], part), 71), part),
        "rates": set_ends(jax.random.randint(splits[3], (SH,), 1, 5), jax.random.fold_in(splits[3], 1), 1, 4).astype(jnp.int32),
        "tile_gain": jnp.clip(1.0 + 0.18 * jax.random.normal(splits[4], (D,), jnp.float32), 0.1, 1.9),
        "gate_weight": bell_draw(splits[5], (D, FF), D ** -0.5, 0.15625, ((0, 8), (1, 2))),
        "up_weight": bell_draw(splits[6], (D, FF), D ** -0.5, 0.15625, ((0, 8), (1, 2))),
        "embed_proj": bell_draw(splits[7], (FF, E), (FF // 16) ** -0.5, 0.5, ((0, 2),)),
        "slide_gain": jnp.clip(1.0 + 0.18 * jax.random.normal(splits[8], (E,), jnp.float32), 0.1, 1.9),
        "slide_wq": draw_slide_wq(jax.random.fold_in(splits[13], 71), part),
        "slide_wk": draw_slide_wk(jax.random.fold_in(splits[13], 71), part),
        "slide_wv": bell_draw(splits[11], (E, SH * HD), E ** -0.5, 0.21875, ((1, 2),)),
        "slide_wo": bell_draw(splits[12], (SH * HD, E), (SH * HD // 16) ** -0.5, 0.875, ((0, 2),)),
    }


epsilon = 1e-06
floor_value = -1e+30

def normed(rows_in, gains):
    average = lax.optimization_barrier(jnp.mean(rows_in, axis=-1, keepdims=True))
    centred = rows_in - average
    variance = lax.optimization_barrier(jnp.mean(centred * centred, axis=-1, keepdims=True))
    return (centred * lax.rsqrt(variance + epsilon) * gains).astype(jnp.bfloat16)

def pool_tile(tile_rows, tile_gain, gate_weight, up_weight):
    hidden = normed(tile_rows.astype(jnp.float32), tile_gain)
    gate = jnp.dot(hidden, gate_weight, preferred_element_type=jnp.float32)
    up_part = jnp.dot(hidden, up_weight, preferred_element_type=jnp.float32)
    gated = (jax.nn.silu(gate) * up_part).astype(jnp.bfloat16)
    return lax.optimization_barrier(jnp.sum(gated.astype(jnp.float32), axis=0))

def reference(tiles, counts, slide_of, rates, tile_gain, gate_weight, up_weight, embed_proj, slide_gain, slide_wq, slide_wk, slide_wv, slide_wo):
    pooled = lax.map(lambda tile_rows: pool_tile(tile_rows, tile_gain, gate_weight, up_weight), tiles)
    device = jnp.arange(TILES, dtype=jnp.int32) // SLOTS
    slot_pos = jnp.arange(TILES, dtype=jnp.int32) % SLOTS
    is_valid = slot_pos < counts[device]
    tile_embed = jnp.where(is_valid[:, None], pooled / TT, 0.0).astype(jnp.bfloat16)
    mixed_rows = jnp.dot(tile_embed, embed_proj, preferred_element_type=jnp.float32)
    hidden = normed(mixed_rows, slide_gain)
    heads = SH
    slide_query = jnp.dot(hidden, slide_wq, preferred_element_type=jnp.float32).astype(jnp.bfloat16)
    slide_keys = jnp.dot(hidden, slide_wk, preferred_element_type=jnp.float32).astype(jnp.bfloat16)
    slide_values = jnp.dot(hidden, slide_wv, preferred_element_type=jnp.float32).astype(jnp.bfloat16)
    slide_query = slide_query.astype(jnp.float32).reshape(TILES, heads, HD)
    slide_keys = slide_keys.astype(jnp.float32).reshape(TILES, heads, HD)
    slide_values = slide_values.astype(jnp.float32).reshape(TILES, heads, HD)
    same_slide = slide_of[:, None] == slide_of[None, :]
    first_dev = jnp.argmax(same_slide, axis=1).astype(jnp.int32)
    slide_ids = slide_of[device]
    position = (device - first_dev[device]) * SLOTS + slot_pos
    head_ids = jnp.arange(heads, dtype=jnp.int32)
    offset = head_ids % rates
    chosen = position[:, None] % rates[None, :] == offset[None, :]
    near_keys = (device[:, None] == device[None, :]) & is_valid[None, :]
    far_keys = (slide_ids[:, None] == slide_ids[None, :]) & is_valid[None, :]
    far_heads = far_keys[:, :, None] & chosen[:, None, :] & chosen[None, :, :]
    multiplicity = near_keys[:, :, None].astype(jnp.float32) + far_heads.astype(jnp.float32)
    scores = jnp.einsum('ihd,jhd->ijh', slide_query, slide_keys) * (1.0 / math.sqrt(HD))
    masked = jnp.where(multiplicity > 0.0, scores, floor_value)
    highest = lax.optimization_barrier(jnp.max(masked, axis=1, keepdims=True))
    weights = multiplicity * jnp.exp(masked - highest)
    weights = weights / lax.optimization_barrier(jnp.sum(weights, axis=1, keepdims=True))
    context = jnp.einsum('ijh,jhd->ihd', weights, slide_values)
    context = context.reshape(TILES, heads * HD).astype(jnp.bfloat16)
    attended = jnp.dot(context, slide_wo, preferred_element_type=jnp.float32)
    slide_out = jnp.where(is_valid[:, None], mixed_rows + attended, 0.0).astype(jnp.bfloat16)
    return (tile_embed, slide_out)
```

```python
import functools
import math

import jax
import jax.numpy as jnp
from jax import lax
from jax.experimental import pallas as pl
from jax.experimental.pallas import tpu as pltpu
from jax.sharding import PartitionSpec as P

HD = 64
EPSILON = 1e-06
FLOOR = -1e30
CHUNKS = 2
QROWS = 8
VMEM_LIMIT = 48 * 1024 * 1024


def normed(rows_in, gains):
    average = jnp.mean(rows_in, axis=-1, keepdims=True)
    centred = rows_in - average
    variance = jnp.mean(centred * centred, axis=-1, keepdims=True)
    return (centred * lax.rsqrt(variance + EPSILON) * gains).astype(jnp.bfloat16)


def norm_kernel(ids_ref, tiles_ref, gain_ref, out_ref):
    out_ref[...] = normed(tiles_ref[0].astype(jnp.float32), gain_ref[...])


def norm_tiles(ids, tiles, gain, flip):
    slot_count, length, width = tiles.shape
    half = slot_count // 2

    def tile_map(i, ids_ref):
        core = ids_ref[2]
        first = (1 - core if flip else core) * half
        return (first + i, 0, 0)

    return pl.pallas_call(
        norm_kernel,
        grid_spec=pltpu.PrefetchScalarGridSpec(
            num_scalar_prefetch=1,
            grid=(half,),
            in_specs=[
                pl.BlockSpec((1, length, width), tile_map),
                pl.BlockSpec((1, width), lambda i, ids_ref: (0, 0)),
            ],
            out_specs=pl.BlockSpec((length, width), lambda i, ids_ref: (i, 0)),
        ),
        out_shape=jax.ShapeDtypeStruct((half * length, width), jnp.bfloat16),
        compiler_params=pltpu.CompilerParams(vmem_limit_bytes=VMEM_LIMIT),
        cost_estimate=pl.CostEstimate(
            flops=8 * half * length * width,
            bytes_accessed=4 * half * length * width,
            transcendentals=half * length,
        ),
    )(ids, tiles, gain)


def mlp_kernel(n_chunks, n_dev, ny, length, ids_ref, *refs):
    n_blocks = n_dev * n_chunks
    blocks = refs[:n_blocks]
    first_ref, second_ref, out_ref, weights, rows, sums, weight_sems, row_sems = refs[n_blocks:]
    me = ids_ref[1]
    core = ids_ref[2]
    nz = n_dev // ny
    my_z = me // ny
    my_y = me - my_z * ny
    depth = blocks[0].shape[0]
    cols = blocks[0].shape[1] // 2
    row_copies = [
        pltpu.make_async_copy(ref, rows.at[i], row_sems.at[i])
        for i, ref in enumerate((first_ref, second_ref))
    ]
    weight_copies = []
    for c in range(n_chunks):
        copies = []
        for k in range(n_dev):
            step, flip = k // ny, k % ny
            z = my_z - step
            z = jnp.where(z < 0, z + nz, z)
            y = 1 - my_y if flip else my_y
            start = pl.multiple_of((z * ny + y) * depth, depth)
            copies.append(
                pltpu.make_async_copy(
                    blocks[c * n_dev + k], weights.at[c, pl.ds(start, depth)], weight_sems.at[c, k]
                )
            )
        weight_copies.append(copies)
    row_copies[0].start()
    for copy in weight_copies[0]:
        copy.start()
    row_copies[1].start()
    for copies in weight_copies[1:]:
        for copy in copies:
            copy.start()
    half = rows.shape[1] // length
    for c in range(n_chunks):
        for copy in weight_copies[c]:
            copy.wait()
        for i in range(2):
            if c == 0:
                row_copies[i].wait()
            first = (1 - core if i else core) * half

            def one_tile(j, carry):
                start = pl.multiple_of(j * length, length)
                both = jnp.dot(
                    rows[i, pl.ds(start, length), :],
                    weights[c],
                    preferred_element_type=jnp.float32,
                )
                gate, up_part = both[:, :cols], both[:, cols:]
                silu = gate * (0.5 * jnp.tanh(0.5 * gate) + 0.5)
                gated = (silu * up_part).astype(jnp.bfloat16).astype(jnp.float32)
                sums[pl.ds(first + j, 1), c * cols : (c + 1) * cols] = jnp.sum(
                    gated, axis=0, keepdims=True
                )
                return carry

            lax.fori_loop(0, half, one_tile, 0)
    out_ref[...] = (sums[: 2 * half] * (1.0 / length)).astype(jnp.bfloat16)


def mlp(ids, chunks, first, second, length, ny):
    n_chunks, n_dev = len(chunks), len(chunks[0])
    depth, both_cols = chunks[0][0].shape
    width = depth * n_dev
    cols = both_cols // 2
    total_rows = 2 * first.shape[0]
    slot_count = total_rows // length
    any_spec = pl.BlockSpec(memory_space=pl.ANY)
    flat = [block for chunk in chunks for block in chunk]
    return pl.pallas_call(
        functools.partial(mlp_kernel, n_chunks, n_dev, ny, length),
        in_specs=[pl.BlockSpec(memory_space=pltpu.SMEM)] + [any_spec] * (len(flat) + 2),
        out_specs=pl.BlockSpec(memory_space=pltpu.VMEM),
        out_shape=jax.ShapeDtypeStruct((slot_count, n_chunks * cols), jnp.bfloat16),
        scratch_shapes=[
            pltpu.VMEM((n_chunks, width, both_cols), jnp.bfloat16),
            pltpu.VMEM((2, first.shape[0], width), jnp.bfloat16),
            pltpu.VMEM((8, n_chunks * cols), jnp.float32),
            pltpu.SemaphoreType.DMA((n_chunks, n_dev)),
            pltpu.SemaphoreType.DMA((2,)),
        ],
        compiler_params=pltpu.CompilerParams(vmem_limit_bytes=VMEM_LIMIT),
        cost_estimate=pl.CostEstimate(
            flops=2 * total_rows * width * n_chunks * both_cols,
            bytes_accessed=2 * (total_rows * width + n_chunks * width * both_cols),
            transcendentals=total_rows * n_chunks * cols,
        ),
    )(ids, *flat, first, second)


def small_mod(value, rate):
    return jnp.where(
        rate == 1,
        0,
        jnp.where(rate == 2, value & 1, jnp.where(rate == 3, lax.rem(value, 3), value & 3)),
    )


def multiplicity_kernel(n_dev, slot_count, heads, ids_ref, counts_ref, slide_ref, rates_ref, out_ref):
    me, core = ids_ref[1], ids_ref[2]
    shape = out_ref.shape
    row = lax.broadcasted_iota(jnp.int32, shape, 0)
    col = lax.broadcasted_iota(jnp.int32, shape, 1)
    head = row // QROWS + core * (heads // 2)
    head = jnp.where(head >= heads, head - heads, head)
    query = row % QROWS
    step, slot = col // slot_count, col % slot_count
    device = me - step
    device = jnp.where(device < 0, device + n_dev, device)
    rate = jnp.full(shape, 1, jnp.int32)
    for h in range(heads):
        rate = jnp.where(head == h, rates_ref[h], rate)
    my_slide = slide_ref[me]
    first = me
    count = jnp.zeros(shape, jnp.int32)
    slide = jnp.zeros(shape, jnp.int32)
    for k in reversed(range(n_dev)):
        first = jnp.where(slide_ref[k] == my_slide, k, first)
        count = jnp.where(device == k, counts_ref[k], count)
        slide = jnp.where(device == k, slide_ref[k], slide)
    offset = small_mod(head, rate)
    query_position = (me - first) * slot_count + query
    key_position = (device - first) * slot_count + slot
    valid = slot < count
    near = jnp.where((step == 0) & valid, 1.0, 0.0)
    far = jnp.where(
        (slide == my_slide)
        & valid
        & (small_mod(query_position, rate) == offset)
        & (small_mod(key_position, rate) == offset),
        1.0,
        0.0,
    )
    out_ref[...] = near + far


def embed_kernel(ids_ref, counts_ref, mine_ref, theirs_ref, proj_ref, embed_ref, mixed_ref):
    mine, theirs = mine_ref[...], theirs_ref[...]
    low = lax.rem(ids_ref[0], 2) == 0
    rows = jnp.concatenate(
        [jnp.where(low, mine, theirs), jnp.where(low, theirs, mine)], axis=1
    )
    slot = lax.broadcasted_iota(jnp.int32, rows.shape, 0)
    rows = jnp.where(slot < counts_ref[ids_ref[1]], rows.astype(jnp.float32), 0.0)
    rows = rows.astype(jnp.bfloat16)
    embed_ref[...] = rows
    mixed_ref[...] = jnp.dot(rows, proj_ref[...], preferred_element_type=jnp.float32)


def slide_kernel(n_dev, slot_count, heads, ids_ref, counts_ref, *refs):
    terms = refs[: 2 * n_dev]
    (
        many_ref,
        gain_ref,
        wq_ref,
        wq_far_ref,
        wk_ref,
        wk_far_ref,
        wv_ref,
        wv_far_ref,
        wo_ref,
        wo_far_ref,
        out_ref,
        mixed,
    ) = refs[2 * n_dev :]
    core = ids_ref[2]
    for k in range(n_dev):
        mixed[k * slot_count : (k + 1) * slot_count, :] = (
            terms[2 * k][...] + terms[2 * k + 1][...]
        )
    hidden = normed(mixed[...], gain_ref[...])

    def project(rows, near_ref, far_ref):
        return jnp.concatenate(
            [
                jnp.dot(rows, near_ref[...], preferred_element_type=jnp.float32),
                jnp.dot(rows, far_ref[...], preferred_element_type=jnp.float32),
            ],
            axis=1,
        )

    query = project(hidden[:QROWS], wq_ref, wq_far_ref)
    keys = project(hidden, wk_ref, wk_far_ref).astype(jnp.bfloat16)
    values = project(hidden, wv_ref, wv_far_ref).astype(jnp.bfloat16)
    wide = (heads * QROWS, query.shape[1])
    own_head = (
        lax.broadcasted_iota(jnp.int32, wide, 0) // QROWS
        == lax.broadcasted_iota(jnp.int32, wide, 1) // HD
    )
    spread = jnp.where(own_head, jnp.concatenate([query] * heads, axis=0), 0.0)
    scores = lax.dot_general(
        spread.astype(jnp.bfloat16), keys, (((1,), (1,)), ((), ())), preferred_element_type=jnp.float32
    ) * (1.0 / math.sqrt(HD))
    many = many_ref[...]
    masked = jnp.where(many > 0.0, scores, FLOOR)
    weights = many * jnp.exp(masked - jnp.max(masked, axis=1, keepdims=True))
    weights = weights / jnp.sum(weights, axis=1, keepdims=True)
    context = jnp.dot(weights.astype(jnp.bfloat16), values, preferred_element_type=jnp.float32)
    context = jnp.where(own_head, context, 0.0).reshape(heads, QROWS, wide[1])
    context = jnp.sum(context, axis=0).astype(jnp.bfloat16)
    half = wide[1] // 2
    columns = pl.ds(pl.multiple_of(core * half, 128), half)
    attended = jnp.dot(
        context[:, :half], wo_ref[:, columns], preferred_element_type=jnp.float32
    ) + jnp.dot(context[:, half:], wo_far_ref[...], preferred_element_type=jnp.float32)
    total = mixed[:QROWS, columns] + attended
    slot = lax.broadcasted_iota(jnp.int32, total.shape, 0)
    total = jnp.where(slot < counts_ref[ids_ref[1]], total, 0.0)
    out_ref[...] = total[:slot_count].astype(jnp.bfloat16)


def on_device(
    tiles,
    counts,
    slide_of,
    rates,
    tile_gain,
    gate_weight,
    up_weight,
    embed_proj,
    slide_gain,
    slide_wq,
    slide_wk,
    slide_wv,
    slide_wo,
):
    slot_count, length, width = tiles.shape
    hidden_cols = gate_weight.shape[1]
    n_grp, n_dev, n_sub = (lax.axis_size(a) for a in ("grp", "dev", "sub"))
    ny = 2
    nz = n_dev // ny
    heads = slide_wq.shape[1] * n_sub // HD
    group, me, core = (lax.axis_index(a) for a in ("grp", "dev", "sub"))
    ids = jnp.stack([group, me, core]).astype(jnp.int32)

    to_pair = [(g, g ^ 1) for g in range(n_grp)]
    to_sibling = [(s, s ^ 1) for s in range(n_sub)]
    along_z = [(d, (d + ny) % n_dev) for d in range(n_dev)]
    along_y = [(d, d ^ 1) for d in range(n_dev)]

    half_cols = hidden_cols // 2
    cols = half_cols // CHUNKS
    base = (group % 2) * half_cols
    own_blocks = [
        jnp.concatenate(
            [
                lax.dynamic_slice_in_dim(w, base + c * cols, cols, 1)
                for w in (gate_weight, up_weight)
            ],
            axis=1,
        )
        for c in range(CHUNKS)
    ]
    gain_row = tile_gain[None, :]
    first = norm_tiles(ids, tiles, gain_row, False)
    chunks = []
    for block in own_blocks:
        blocks = []
        for step in range(nz):
            if step:
                block = lax.ppermute(block, "dev", along_z)
            blocks += [block, lax.ppermute(block, "dev", along_y)]
        chunks.append(blocks)
    pair_first = lax.ppermute(first, "grp", to_pair)
    pair_second = lax.ppermute(pair_first, "sub", to_sibling)
    second = norm_tiles(ids, tiles, gain_row, True)

    wq_far = lax.ppermute(slide_wq, "sub", to_sibling)
    wk_far = lax.ppermute(slide_wk, "sub", to_sibling)
    wv_far = lax.ppermute(slide_wv, "sub", to_sibling)
    out_cols = slide_wo.shape[1] // n_sub
    wo_far = lax.ppermute(
        lax.dynamic_slice_in_dim(slide_wo, (1 - core) * out_cols, out_cols, 1), "sub", to_sibling
    )

    smem = pl.BlockSpec(memory_space=pltpu.SMEM)
    vmem = pl.BlockSpec(memory_space=pltpu.VMEM)
    many = pl.pallas_call(
        functools.partial(multiplicity_kernel, n_dev, slot_count, heads),
        in_specs=[smem] * 4,
        out_specs=vmem,
        out_shape=jax.ShapeDtypeStruct((heads * QROWS, n_dev * slot_count), jnp.float32),
    )(ids, counts, slide_of, rates)

    own = [mlp(ids, [chunk], first, second, length, ny) for chunk in chunks]
    pair = mlp(ids, chunks, pair_first, pair_second, length, ny)
    theirs = lax.ppermute(pair, "grp", to_pair)
    mine = jnp.concatenate(own, axis=1)

    tile_embed, term = pl.pallas_call(
        embed_kernel,
        in_specs=[smem, smem, vmem, vmem, vmem],
        out_specs=(vmem, vmem),
        out_shape=(
            jax.ShapeDtypeStruct((slot_count, hidden_cols), jnp.bfloat16),
            jax.ShapeDtypeStruct((slot_count, embed_proj.shape[1]), jnp.float32),
        ),
        compiler_params=pltpu.CompilerParams(vmem_limit_bytes=VMEM_LIMIT),
    )(ids, counts, mine, theirs, embed_proj)

    terms = []
    for step in range(n_dev):
        for flip in range(2):
            if step == 0 and flip == 0:
                terms.append(term)
                continue
            perm = [
                (d * n_sub + s, ((d + step) % n_dev) * n_sub + (s ^ flip))
                for d in range(n_dev)
                for s in range(n_sub)
            ]
            terms.append(lax.ppermute(term, ("dev", "sub"), perm))

    slide_out = pl.pallas_call(
        functools.partial(slide_kernel, n_dev, slot_count, heads),
        in_specs=[smem, smem] + [vmem] * (2 * n_dev + 10),
        out_specs=vmem,
        out_shape=jax.ShapeDtypeStruct((slot_count, out_cols), jnp.bfloat16),
        scratch_shapes=[pltpu.VMEM((n_dev * slot_count, embed_proj.shape[1]), jnp.float32)],
        compiler_params=pltpu.CompilerParams(vmem_limit_bytes=VMEM_LIMIT),
    )(
        ids,
        counts,
        *terms,
        many,
        slide_gain[None, :],
        slide_wq,
        wq_far,
        slide_wk,
        wk_far,
        slide_wv,
        wv_far,
        slide_wo,
        wo_far,
    )
    return (tile_embed, slide_out)


def solution(mesh):
    placed = (
        P(("grp", "dev"), None, None),
        P("grp"),
        P("grp"),
        P(),
        P(),
        P("dev", "sub"),
        P("dev", "sub"),
        P("sub", None),
        P(),
        P(None, "sub"),
        P(None, "sub"),
        P(None, "sub"),
        P("sub", None),
    )
    return jax.shard_map(
        on_device,
        mesh=mesh,
        in_specs=placed,
        out_specs=(P(("grp", "dev"), "sub"), P(("grp", "dev"), "sub")),
        check_vma=False,
    )
```

```python
import functools
import math

import jax
import jax.numpy as jnp
from jax import lax
from jax.experimental import pallas as pl
from jax.experimental.pallas import tpu as pltpu
from jax.sharding import PartitionSpec as P

HD = 64
EPSILON = 1e-06
FLOOR = -1e30
CHUNKS = (384, 128)
QROWS = 8
VMEM_LIMIT = 60 * 1024 * 1024
SMALL_VMEM = 24 * 1024 * 1024


def normed(rows_in, gains):
    average = jnp.mean(rows_in, axis=-1, keepdims=True)
    centred = rows_in - average
    variance = jnp.mean(centred * centred, axis=-1, keepdims=True)
    return (centred * lax.rsqrt(variance + EPSILON) * gains).astype(jnp.bfloat16)


def norm_kernel(ids_ref, tiles_ref, gain_ref, *out_refs):
    hidden = normed(tiles_ref[0].astype(jnp.float32), gain_ref[...])
    for i, out_ref in enumerate(out_refs):

        @pl.when(pl.program_id(0) == i)
        def _():
            out_ref[...] = hidden


def norm_tiles(ids, tiles, gain, flip):
    slot_count, length, width = tiles.shape
    half = slot_count // 2

    def tile_map(i, ids_ref):
        core = ids_ref[2]
        first = (1 - core if flip else core) * half
        return (first + i, 0, 0)

    return pl.pallas_call(
        norm_kernel,
        grid_spec=pltpu.PrefetchScalarGridSpec(
            num_scalar_prefetch=1,
            grid=(half,),
            in_specs=[
                pl.BlockSpec((1, length, width), tile_map),
                pl.BlockSpec((1, width), lambda i, ids_ref: (0, 0)),
            ],
            out_specs=[pl.BlockSpec((length, width), lambda i, ids_ref: (0, 0))] * half,
        ),
        out_shape=[jax.ShapeDtypeStruct((length, width), jnp.bfloat16)] * half,
        compiler_params=pltpu.CompilerParams(vmem_limit_bytes=VMEM_LIMIT),
        cost_estimate=pl.CostEstimate(
            flops=8 * half * length * width,
            bytes_accessed=4 * half * length * width,
            transcendentals=half * length,
        ),
    )(ids, tiles, gain)


def gate_kernel(value_ref, after_ref, out_ref):
    del value_ref, after_ref, out_ref


def after(value, *others):
    any_spec = pl.BlockSpec(memory_space=pl.ANY)
    for other in others:
        value = pl.pallas_call(
            gate_kernel,
            in_specs=[any_spec, any_spec],
            out_specs=any_spec,
            out_shape=jax.ShapeDtypeStruct(value.shape, value.dtype),
            input_output_aliases={0: 0},
            compiler_params=pltpu.CompilerParams(vmem_limit_bytes=VMEM_LIMIT),
        )(value, other)
    return value


def mlp_kernel(n_dev, ny, n_tiles, length, ids_ref, *refs):
    blocks = refs[:n_dev]
    tile_refs = refs[n_dev : n_dev + n_tiles]
    out_ref, weights, rows, weight_sems, row_sems = refs[n_dev + n_tiles :]
    me = ids_ref[1]
    nz = n_dev // ny
    my_z = me // ny
    my_y = me - my_z * ny
    depth, both_cols = blocks[0].shape
    cols = both_cols // 2
    row_copies = [
        pltpu.make_async_copy(ref, rows.at[pl.ds(i * length, length)], row_sems.at[i])
        for i, ref in enumerate(tile_refs)
    ]
    weight_copies = []
    for k in range(n_dev):
        step, flip = k // ny, k % ny
        z = my_z - step
        z = jnp.where(z < 0, z + nz, z)
        y = 1 - my_y if flip else my_y
        start = pl.multiple_of((z * ny + y) * depth, depth)
        weight_copies.append(
            pltpu.make_async_copy(blocks[k], weights.at[pl.ds(start, depth)], weight_sems.at[k])
        )
    for copy in row_copies[:2] + weight_copies + row_copies[2:]:
        copy.start()
    for copy in weight_copies:
        copy.wait()
    for i in range(0, n_tiles, 2):
        row_copies[i].wait()
        row_copies[i + 1].wait()
        both = jnp.dot(
            rows[i * length : (i + 2) * length, :],
            weights[...],
            preferred_element_type=jnp.float32,
        )
        gate, up_part = both[:, :cols], both[:, cols:]
        silu = gate * (0.5 * jnp.tanh(0.5 * gate) + 0.5)
        gated = (silu * up_part).astype(jnp.bfloat16).astype(jnp.float32)
        for j in range(2):
            out_ref[i + j : i + j + 1, :] = jnp.sum(
                gated[j * length : (j + 1) * length], axis=0, keepdims=True
            ) * (1.0 / length)


def mlp(ids, blocks, tiles, ny):
    n_dev, n_tiles = len(blocks), len(tiles)
    depth, both_cols = blocks[0].shape
    length, width = tiles[0].shape
    cols = both_cols // 2
    any_spec = pl.BlockSpec(memory_space=pl.ANY)
    return pl.pallas_call(
        functools.partial(mlp_kernel, n_dev, ny, n_tiles, length),
        in_specs=[pl.BlockSpec(memory_space=pltpu.SMEM)] + [any_spec] * (n_dev + n_tiles),
        out_specs=pl.BlockSpec(memory_space=pltpu.VMEM),
        out_shape=jax.ShapeDtypeStruct((n_tiles, cols), jnp.float32),
        scratch_shapes=[
            pltpu.VMEM((width, both_cols), jnp.bfloat16),
            pltpu.VMEM((n_tiles * length, width), jnp.bfloat16),
            pltpu.SemaphoreType.DMA((n_dev,)),
            pltpu.SemaphoreType.DMA((n_tiles,)),
        ],
        compiler_params=pltpu.CompilerParams(vmem_limit_bytes=VMEM_LIMIT),
        cost_estimate=pl.CostEstimate(
            flops=2 * n_tiles * length * width * both_cols,
            bytes_accessed=2 * (n_tiles * length * width + width * both_cols),
            transcendentals=n_tiles * length * cols,
        ),
    )(ids, *blocks, *tiles)


def small_mod(value, rate):
    return jnp.where(
        rate == 1,
        0,
        jnp.where(rate == 2, value & 1, jnp.where(rate == 3, lax.rem(value, 3), value & 3)),
    )


def multiplicity_kernel(n_dev, slot_count, heads, ids_ref, counts_ref, slide_ref, rates_ref, out_ref):
    me, core = ids_ref[1], ids_ref[2]
    shape = out_ref.shape
    row = lax.broadcasted_iota(jnp.int32, shape, 0)
    col = lax.broadcasted_iota(jnp.int32, shape, 1)
    head = row // QROWS + core * (heads // 2)
    head = jnp.where(head >= heads, head - heads, head)
    query = row % QROWS
    device, slot = col // slot_count, col % slot_count
    rate = jnp.full(shape, 1, jnp.int32)
    for h in range(heads):
        rate = jnp.where(head == h, rates_ref[h], rate)
    my_slide = slide_ref[me]
    first = me
    count = jnp.zeros(shape, jnp.int32)
    slide = jnp.zeros(shape, jnp.int32)
    for k in reversed(range(n_dev)):
        first = jnp.where(slide_ref[k] == my_slide, k, first)
        count = jnp.where(device == k, counts_ref[k], count)
        slide = jnp.where(device == k, slide_ref[k], slide)
    offset = small_mod(head, rate)
    query_position = (me - first) * slot_count + query
    key_position = (device - first) * slot_count + slot
    valid = slot < count
    near = jnp.where((device == me) & valid, 1.0, 0.0)
    far = jnp.where(
        (slide == my_slide)
        & valid
        & (small_mod(query_position, rate) == offset)
        & (small_mod(key_position, rate) == offset),
        1.0,
        0.0,
    )
    out_ref[...] = near + far


def order_kernel(slot_count, ids_ref, own_ref, even_ref, odd_ref, rest_ref, own_out, pair_out):
    half = slot_count // 2
    low = ids_ref[2] == 0

    def ordered(mine, others):
        return jnp.concatenate(
            [jnp.where(low, mine, others), jnp.where(low, others, mine)], axis=0
        ).astype(jnp.bfloat16)

    own = jnp.concatenate([own_ref[...], rest_ref[:slot_count, :]], axis=1)
    own_out[...] = ordered(own[:half], own[half:])
    sides = []
    for side in range(2):
        large = jnp.concatenate([ref[side : side + 1, :] for ref in (even_ref, odd_ref)], axis=0)
        start = slot_count + side * half
        sides.append(jnp.concatenate([large, rest_ref[start : start + half, :]], axis=1))
    pair_out[...] = ordered(*sides)


def embed_kernel(ids_ref, counts_ref, mine_ref, pair_ref, proj_ref, embed_ref, terms_ref):
    mine, theirs = mine_ref[...], pair_ref[...]
    low = lax.rem(ids_ref[0], 2) == 0
    rows = jnp.concatenate(
        [jnp.where(low, mine, theirs), jnp.where(low, theirs, mine)], axis=1
    )
    slot = lax.broadcasted_iota(jnp.int32, rows.shape, 0)
    rows = jnp.where(slot < counts_ref[ids_ref[1]], rows.astype(jnp.float32), 0.0)
    rows = rows.astype(jnp.bfloat16)
    embed_ref[...] = rows
    mixed = jnp.dot(rows, proj_ref[...], preferred_element_type=jnp.float32)
    half = mixed.shape[1] // 2
    packed = jnp.concatenate([mixed[:, :half], mixed[:, half:]], axis=0)
    for k in range(terms_ref.shape[0]):
        terms_ref[k] = packed


def slide_kernel(n_dev, slot_count, heads, ids_ref, counts_ref, *refs):
    (
        terms_ref,
        many_ref,
        gain_ref,
        wq_ref,
        wq_far_ref,
        wk_ref,
        wk_far_ref,
        wv_ref,
        wv_far_ref,
        wo_ref,
        wo_far_ref,
        out_ref,
        mixed,
    ) = refs
    me, core = ids_ref[1], ids_ref[2]
    for k in range(n_dev):
        packed = terms_ref[2 * k] + terms_ref[2 * k + 1]
        mixed[k * slot_count : (k + 1) * slot_count, :] = jnp.concatenate(
            [packed[:slot_count], packed[slot_count:]], axis=1
        )
    hidden = normed(mixed[...], gain_ref[...])
    per_tile = QROWS // slot_count
    around = mixed[pl.ds(pl.multiple_of(me // per_tile * QROWS, QROWS), QROWS), :]
    mine = around
    for k in range(1, per_tile):
        turned = jnp.concatenate([around[k * slot_count :], around[: k * slot_count]], axis=0)
        mine = jnp.where(lax.rem(me, per_tile) == k, turned, mine)
    my_hidden = normed(mine, gain_ref[...])

    def project(rows, near_ref, far_ref):
        return jnp.concatenate(
            [
                jnp.dot(rows, near_ref[...], preferred_element_type=jnp.float32),
                jnp.dot(rows, far_ref[...], preferred_element_type=jnp.float32),
            ],
            axis=1,
        )

    query = project(my_hidden, wq_ref, wq_far_ref)
    keys = project(hidden, wk_ref, wk_far_ref).astype(jnp.bfloat16)
    values = project(hidden, wv_ref, wv_far_ref).astype(jnp.bfloat16)
    wide = (heads * QROWS, query.shape[1])
    own_head = (
        lax.broadcasted_iota(jnp.int32, wide, 0) // QROWS
        == lax.broadcasted_iota(jnp.int32, wide, 1) // HD
    )
    spread = jnp.where(own_head, jnp.concatenate([query] * heads, axis=0), 0.0)
    scores = lax.dot_general(
        spread.astype(jnp.bfloat16), keys, (((1,), (1,)), ((), ())), preferred_element_type=jnp.float32
    ) * (1.0 / math.sqrt(HD))
    many = many_ref[...]
    masked = jnp.where(many > 0.0, scores, FLOOR)
    weights = many * jnp.exp(masked - jnp.max(masked, axis=1, keepdims=True))
    weights = weights / jnp.sum(weights, axis=1, keepdims=True)
    context = jnp.dot(weights.astype(jnp.bfloat16), values, preferred_element_type=jnp.float32)
    context = jnp.where(own_head, context, 0.0).reshape(heads, QROWS, wide[1])
    context = jnp.sum(context, axis=0).astype(jnp.bfloat16)
    half = wide[1] // 2
    columns = pl.ds(pl.multiple_of(core * half, 128), half)
    attended = jnp.dot(
        context[:, :half], wo_ref[:, columns], preferred_element_type=jnp.float32
    ) + jnp.dot(context[:, half:], wo_far_ref[...], preferred_element_type=jnp.float32)
    total = jnp.where(core == 0, mine[:, :half], mine[:, half:]) + attended
    slot = lax.broadcasted_iota(jnp.int32, total.shape, 0)
    total = jnp.where(slot < counts_ref[ids_ref[1]], total, 0.0)
    out_ref[...] = total[:slot_count].astype(jnp.bfloat16)


def on_device(
    tiles,
    counts,
    slide_of,
    rates,
    tile_gain,
    gate_weight,
    up_weight,
    embed_proj,
    slide_gain,
    slide_wq,
    slide_wk,
    slide_wv,
    slide_wo,
):
    slot_count, length, width = tiles.shape
    hidden_cols = gate_weight.shape[1]
    n_grp, n_dev, n_sub = (lax.axis_size(a) for a in ("grp", "dev", "sub"))
    ny = 2
    nz = n_dev // ny
    heads = slide_wq.shape[1] * n_sub // HD
    group, me, core = (lax.axis_index(a) for a in ("grp", "dev", "sub"))
    ids = jnp.stack([group, me, core]).astype(jnp.int32)

    to_pair = [(g, g ^ 1) for g in range(n_grp)]
    to_sibling = [(s, s ^ 1) for s in range(n_sub)]
    along_z = [(d, (d + ny) % n_dev) for d in range(n_dev)]
    along_y = [(d, d ^ 1) for d in range(n_dev)]

    half_cols = hidden_cols // 2
    base = (group % 2) * half_cols
    own_blocks = []
    for cols in CHUNKS:
        own_blocks.append(
            jnp.concatenate(
                [
                    lax.dynamic_slice_in_dim(w, base, cols, 1)
                    for w in (gate_weight, up_weight)
                ],
                axis=1,
            )
        )
        base = base + cols
    gain_row = tile_gain[None, :]
    first = norm_tiles(ids, tiles, gain_row, False)
    pair_first = [lax.ppermute(rows, "grp", to_pair) for rows in first]
    chunks = []
    for block in own_blocks:
        blocks = []
        for step in range(nz):
            if step:
                block = lax.ppermute(block, "dev", along_z)
            blocks += [block, lax.ppermute(block, "dev", along_y)]
        chunks.append(blocks)
    second = norm_tiles(ids, tiles, gain_row, True)
    pair_first = [after(pair_first[0], chunks[0][n_dev // 2]), after(pair_first[1], chunks[1][-1])]
    pair_second = [lax.ppermute(rows, "sub", to_sibling) for rows in pair_first]

    wq_far = lax.ppermute(slide_wq, "sub", to_sibling)
    wk_far = lax.ppermute(slide_wk, "sub", to_sibling)
    wv_far = lax.ppermute(slide_wv, "sub", to_sibling)
    out_cols = slide_wo.shape[1] // n_sub
    wo_far = lax.ppermute(
        lax.dynamic_slice_in_dim(slide_wo, (1 - core) * out_cols, out_cols, 1), "sub", to_sibling
    )

    smem = pl.BlockSpec(memory_space=pltpu.SMEM)
    vmem = pl.BlockSpec(memory_space=pltpu.VMEM)
    many = pl.pallas_call(
        functools.partial(multiplicity_kernel, n_dev, slot_count, heads),
        in_specs=[smem] * 4,
        out_specs=vmem,
        out_shape=jax.ShapeDtypeStruct((heads * QROWS, n_dev * slot_count), jnp.float32),
    )(ids, counts, slide_of, rates)

    large, small = chunks
    own_large = mlp(ids, large, [*first, *second], ny)
    pair_large = [mlp(ids, large, [p, q], ny) for p, q in zip(pair_first, pair_second)]
    rest = mlp(ids, small, [*first, *second, *pair_first, *pair_second], ny)
    own, pair = pl.pallas_call(
        functools.partial(order_kernel, slot_count),
        in_specs=[smem] + [vmem] * 4,
        out_specs=(vmem, vmem),
        out_shape=(
            jax.ShapeDtypeStruct((slot_count, half_cols), jnp.bfloat16),
            jax.ShapeDtypeStruct((slot_count, half_cols), jnp.bfloat16),
        ),
    )(ids, own_large, *pair_large, rest)
    theirs = lax.ppermute(pair, "grp", to_pair)

    n_rows, out_width = slot_count, embed_proj.shape[1]
    packed = (n_dev * n_sub, 2 * n_rows, out_width // 2)
    tile_embed, terms = pl.pallas_call(
        embed_kernel,
        in_specs=[smem, smem, vmem, vmem, vmem],
        out_specs=(vmem, vmem),
        out_shape=(
            jax.ShapeDtypeStruct((slot_count, hidden_cols), jnp.bfloat16),
            jax.ShapeDtypeStruct(packed, jnp.float32),
        ),
        compiler_params=pltpu.CompilerParams(vmem_limit_bytes=SMALL_VMEM),
    )(ids, counts, own, theirs, embed_proj)
    terms = lax.all_to_all(terms, ("dev", "sub"), split_axis=0, concat_axis=0, tiled=True)

    slide_out = pl.pallas_call(
        functools.partial(slide_kernel, n_dev, slot_count, heads),
        in_specs=[smem, smem] + [vmem] * 11,
        out_specs=vmem,
        out_shape=jax.ShapeDtypeStruct((slot_count, out_cols), jnp.bfloat16),
        scratch_shapes=[pltpu.VMEM((n_dev * slot_count, out_width), jnp.float32)],
        compiler_params=pltpu.CompilerParams(vmem_limit_bytes=SMALL_VMEM),
    )(
        ids,
        counts,
        terms,
        many,
        slide_gain[None, :],
        slide_wq,
        wq_far,
        slide_wk,
        wk_far,
        slide_wv,
        wv_far,
        slide_wo,
        wo_far,
    )
    return (tile_embed, slide_out)


def solution(mesh):
    placed = (
        P(("grp", "dev"), None, None),
        P("grp"),
        P("grp"),
        P(),
        P(),
        P("dev", "sub"),
        P("dev", "sub"),
        P("sub", None),
        P(),
        P(None, "sub"),
        P(None, "sub"),
        P(None, "sub"),
        P("sub", None),
    )
    return jax.shard_map(
        on_device,
        mesh=mesh,
        in_specs=placed,
        out_specs=(P(("grp", "dev"), "sub"), P(("grp", "dev"), "sub")),
        check_vma=False,
    )
```

```python
import functools
import math

import jax
import jax.numpy as jnp
from jax import lax
from jax.experimental import pallas as pl
from jax.experimental.pallas import tpu as pltpu
from jax.sharding import PartitionSpec as P

HD = 64
EPSILON = 1e-06
FLOOR = -1e30
CHUNKS = (256, 256)
QROWS = 8
NORM_ROWS = 16
LANES = 128
BLOCK_TILES = 4
VMEM_LIMIT = 28 * 1024 * 1024
SMALL_VMEM = 16 * 1024 * 1024
GATE_VMEM = 1024 * 1024


def normed(rows_in, gains):
    average = jnp.mean(rows_in, axis=-1, keepdims=True)
    centred = rows_in - average
    variance = jnp.mean(centred * centred, axis=-1, keepdims=True)
    return (centred * lax.rsqrt(variance + EPSILON) * gains).astype(jnp.bfloat16)


def norm_kernel(flip, tiles_ref, gain_ref, *refs):
    out_refs, (rows, sems) = refs[:-2], refs[-2:]
    core = lax.axis_index("sub")
    half = len(out_refs)
    first = (1 - core if flip else core) * half
    copies = [
        pltpu.make_async_copy(tiles_ref.at[first + i], rows.at[i], sems.at[i]) for i in range(half)
    ]
    for copy in copies:
        copy.start()
    gain = gain_ref[...].reshape(1, -1)
    for i, out_ref in enumerate(out_refs):
        copies[i].wait()

        def some_rows(j, carry):
            here = pl.ds(pl.multiple_of(j * NORM_ROWS, NORM_ROWS), NORM_ROWS)
            out_ref[here, :] = normed(rows[i, here, :].astype(jnp.float32), gain)
            return carry

        lax.fori_loop(0, out_ref.shape[0] // NORM_ROWS, some_rows, 0, unroll=2)


def norm_tiles(tiles, gain, flip):
    slot_count, length, width = tiles.shape
    half = slot_count // 2
    vmem = pl.BlockSpec(memory_space=pltpu.VMEM)
    return pl.pallas_call(
        functools.partial(norm_kernel, flip),
        in_specs=[pl.BlockSpec(memory_space=pl.ANY), vmem],
        out_specs=[vmem] * half,
        out_shape=[jax.ShapeDtypeStruct((length, width), jnp.bfloat16)] * half,
        scratch_shapes=[
            pltpu.VMEM((half, length, width), jnp.bfloat16),
            pltpu.SemaphoreType.DMA((half,)),
        ],
        compiler_params=pltpu.CompilerParams(vmem_limit_bytes=SMALL_VMEM),
        cost_estimate=pl.CostEstimate(
            flops=8 * half * length * width,
            bytes_accessed=4 * half * length * width,
            transcendentals=half * length,
        ),
    )(tiles, gain)


def gate_kernel(*refs):
    del refs


def after(value, *others):
    any_spec = pl.BlockSpec(memory_space=pl.ANY)
    return pl.pallas_call(
        gate_kernel,
        in_specs=[any_spec] * (1 + len(others)),
        out_specs=any_spec,
        out_shape=jax.ShapeDtypeStruct(value.shape, value.dtype),
        input_output_aliases={0: 0},
        compiler_params=pltpu.CompilerParams(vmem_limit_bytes=GATE_VMEM),
    )(value, *others)


class Mlp:
    def __init__(self, blocks, tile_refs, weights, rows, weight_sems, row_sems, ny):
        n_dev = len(blocks)
        self.length = tile_refs[0].shape[0]
        self.n_tiles = len(tile_refs)
        self.weights, self.rows = weights, rows
        me = lax.axis_index("dev")
        nz = n_dev // ny
        my_z = me // ny
        my_y = me - my_z * ny
        depth = blocks[0].shape[0]
        self.row_copies = [
            pltpu.make_async_copy(
                ref, rows.at[pl.ds(i * self.length, self.length)], row_sems.at[i]
            )
            for i, ref in enumerate(tile_refs)
        ]
        self.weight_copies = []
        for k in range(n_dev):
            step, flip = k // ny, k % ny
            z = my_z - step
            z = jnp.where(z < 0, z + nz, z)
            y = 1 - my_y if flip else my_y
            start = pl.multiple_of((z * ny + y) * depth, depth)
            self.weight_copies.append(
                pltpu.make_async_copy(blocks[k], weights.at[pl.ds(start, depth)], weight_sems.at[k])
            )

    def start(self):
        for copy in self.weight_copies + self.row_copies:
            copy.start()

    def run(self, out_ref):
        cols = self.weights.shape[1] // 2
        length = self.length
        for copy in self.weight_copies:
            copy.wait()
        for first in range(0, self.n_tiles, BLOCK_TILES):
            last = min(first + BLOCK_TILES, self.n_tiles)
            for i in range(first, last):
                self.row_copies[i].wait()
            both = jnp.dot(
                self.rows[first * length : last * length, :],
                self.weights[...],
                preferred_element_type=jnp.float32,
            )
            gate, up_part = both[:, :cols], both[:, cols:]
            silu = gate * (0.5 * jnp.tanh(0.5 * gate) + 0.5)
            gated = (silu * up_part).astype(jnp.bfloat16).astype(jnp.float32)
            for i in range(first, last):
                here = slice((i - first) * length, (i - first + 1) * length)
                out_ref[i : i + 1, :] = jnp.sum(gated[here], axis=0, keepdims=True) * (1.0 / length)


def mlp_scratch(n_dev, blocks, tiles):
    depth, both_cols = blocks[0].shape
    length, width = tiles[0].shape
    return [
        pltpu.VMEM((width, both_cols), jnp.bfloat16),
        pltpu.VMEM((len(tiles) * length, width), jnp.bfloat16),
        pltpu.SemaphoreType.DMA((n_dev,)),
        pltpu.SemaphoreType.DMA((len(tiles),)),
    ]


def mlp_cost(blocks, n_tiles, tiles):
    both_cols = blocks[0].shape[1]
    length, width = tiles[0].shape
    return pl.CostEstimate(
        flops=2 * n_tiles * length * width * both_cols,
        bytes_accessed=2 * (n_tiles * length * width + width * both_cols),
        transcendentals=n_tiles * length * both_cols // 2,
    )


def mlp_kernel(n_dev, ny, n_tiles, after_ref, *refs):
    del after_ref
    out_ref, *scratch = refs[n_dev + n_tiles :]
    part = Mlp(refs[:n_dev], refs[n_dev : n_dev + n_tiles], *scratch, ny)
    part.start()
    part.run(out_ref)


def mlp(after_this, blocks, tiles, ny):
    n_dev, n_tiles = len(blocks), len(tiles)
    any_spec = pl.BlockSpec(memory_space=pl.ANY)
    return pl.pallas_call(
        functools.partial(mlp_kernel, n_dev, ny, n_tiles),
        in_specs=[any_spec] * (1 + n_dev + n_tiles),
        out_specs=pl.BlockSpec(memory_space=pltpu.VMEM),
        out_shape=jax.ShapeDtypeStruct((n_tiles, blocks[0].shape[1] // 2), jnp.float32),
        scratch_shapes=mlp_scratch(n_dev, blocks, tiles),
        compiler_params=pltpu.CompilerParams(vmem_limit_bytes=VMEM_LIMIT),
        cost_estimate=mlp_cost(blocks, n_tiles, tiles),
    )(after_this, *blocks, *tiles)


def last_mlp_kernel(n_dev, n_grp, n_sub, ny, slot_count, own_ref, even_ref, *refs):
    n_tiles = 2 * slot_count
    half = slot_count // 2
    blocks, tile_refs = refs[: 2 * n_dev], refs[2 * n_dev : 2 * n_dev + n_tiles]
    out_ref, weights0, rows0, wsem0, rsem0, weights1, rows1, wsem1, rsem1, odd, rest = refs[
        2 * n_dev + n_tiles :
    ]
    late = [tile_refs[slot_count + 1], tile_refs[slot_count + half + 1]]
    part1 = Mlp(blocks[n_dev:], tile_refs, weights1, rows1, wsem1, rsem1, ny)
    part0 = Mlp(blocks[:n_dev], late, weights0, rows0, wsem0, rsem0, ny)
    part1.start()
    part0.start()
    part1.run(rest)
    part0.run(odd)

    group, core = lax.axis_index("grp"), lax.axis_index("sub")
    low = core == 0

    def packed(mine, others):
        rows = jnp.concatenate(
            [jnp.where(low, mine, others), jnp.where(low, others, mine)], axis=0
        )
        return jnp.concatenate(
            [rows[:, k : k + LANES] for k in range(0, rows.shape[1], LANES)], axis=0
        ).astype(jnp.bfloat16)

    own = jnp.concatenate([own_ref[...], rest[:slot_count, :]], axis=1)
    own = packed(own[:half], own[half:])
    sides = []
    for side in range(2):
        first = jnp.concatenate([ref[side : side + 1, :] for ref in (even_ref, odd)], axis=0)
        start = slot_count + side * half
        sides.append(jnp.concatenate([first, rest[start : start + half, :]], axis=1))
    pair = packed(*sides)
    for g in range(n_grp):
        rows = jnp.where(group == g, own.astype(jnp.float32), pair.astype(jnp.float32))
        for s in range(n_sub):
            out_ref[g * n_sub + s] = rows.astype(jnp.bfloat16)


def last_mlp(own, even, chunks, tiles, slot_count, n_grp, n_sub, ny):
    n_dev = len(chunks[0])
    half = slot_count // 2
    cols = sum(blocks[0].shape[1] // 2 for blocks in chunks)
    late = [tiles[slot_count + 1], tiles[slot_count + half + 1]]
    any_spec = pl.BlockSpec(memory_space=pl.ANY)
    vmem = pl.BlockSpec(memory_space=pltpu.VMEM)
    return pl.pallas_call(
        functools.partial(last_mlp_kernel, n_dev, n_grp, n_sub, ny, slot_count),
        in_specs=[vmem, vmem] + [any_spec] * (2 * n_dev + len(tiles)),
        out_specs=vmem,
        out_shape=jax.ShapeDtypeStruct(
            (n_grp * n_sub, slot_count * cols // LANES, LANES), jnp.bfloat16
        ),
        scratch_shapes=[
            *mlp_scratch(n_dev, chunks[0], late),
            *mlp_scratch(n_dev, chunks[1], tiles),
            pltpu.VMEM((len(late), chunks[0][0].shape[1] // 2), jnp.float32),
            pltpu.VMEM((len(tiles), chunks[1][0].shape[1] // 2), jnp.float32),
        ],
        compiler_params=pltpu.CompilerParams(vmem_limit_bytes=VMEM_LIMIT),
        cost_estimate=mlp_cost(chunks[1], len(tiles) + 2, tiles),
    )(own, even, *chunks[0], *chunks[1], *tiles)


def small_mod(value, rate):
    return jnp.where(
        rate == 1,
        0,
        jnp.where(rate == 2, value & 1, jnp.where(rate == 3, lax.rem(value, 3), value & 3)),
    )


def multiplicity_kernel(n_dev, slot_count, heads, counts_ref, slide_ref, rates_ref, out_ref):
    me, core = lax.axis_index("dev"), lax.axis_index("sub")
    shape = out_ref.shape
    row = lax.broadcasted_iota(jnp.int32, shape, 0)
    col = lax.broadcasted_iota(jnp.int32, shape, 1)
    head = row // QROWS + core * (heads // 2)
    head = jnp.where(head >= heads, head - heads, head)
    query = row % QROWS
    device, slot = col // slot_count, col % slot_count
    rate = jnp.full(shape, 1, jnp.int32)
    for h in range(heads):
        rate = jnp.where(head == h, rates_ref[h], rate)
    my_slide = slide_ref[me]
    first = me
    count = jnp.zeros(shape, jnp.int32)
    slide = jnp.zeros(shape, jnp.int32)
    for k in reversed(range(n_dev)):
        first = jnp.where(slide_ref[k] == my_slide, k, first)
        count = jnp.where(device == k, counts_ref[k], count)
        slide = jnp.where(device == k, slide_ref[k], slide)
    offset = small_mod(head, rate)
    query_position = (me - first) * slot_count + query
    key_position = (device - first) * slot_count + slot
    valid = slot < count
    near = jnp.where((device == me) & valid, 1.0, 0.0)
    far = jnp.where(
        (slide == my_slide)
        & valid
        & (small_mod(query_position, rate) == offset)
        & (small_mod(key_position, rate) == offset),
        1.0,
        0.0,
    )
    out_ref[...] = near + far


def embed_kernel(
    n_sub, counts_ref, parts_ref, gain_ref, near_ref, far_ref, embed_ref, mixed_ref, sent_ref
):
    slot_count, half = embed_ref.shape
    n_blocks = half // 2 // LANES
    group, core = lax.axis_index("grp"), lax.axis_index("sub")
    count = counts_ref[lax.axis_index("dev")]
    base = group // 2 * 2
    halves = []
    for s in range(n_sub):
        pieces = []
        for x in range(2):
            part = parts_ref[(base + x) * n_sub + s].astype(jnp.float32)
            pieces += [part[k * slot_count : (k + 1) * slot_count] for k in range(n_blocks)]
        rows = jnp.concatenate(pieces, axis=1)
        slot = lax.broadcasted_iota(jnp.int32, rows.shape, 0)
        halves.append(jnp.where(slot < count, rows, 0.0))
    low = core == 0
    near = jnp.where(low, halves[0], halves[1]).astype(jnp.bfloat16)
    far = jnp.where(low, halves[1], halves[0]).astype(jnp.bfloat16)
    embed_ref[...] = near
    mixed = jnp.dot(near, near_ref[...], preferred_element_type=jnp.float32) + jnp.dot(
        far, far_ref[...], preferred_element_type=jnp.float32
    )
    mixed_ref[...] = jnp.concatenate([mixed, mixed], axis=0)
    hidden = normed(mixed, gain_ref[...].reshape(1, -1)).astype(jnp.float32)
    width = sent_ref.shape[2]
    pieces = [hidden[:, k : k + width] for k in range(0, hidden.shape[1], width)]
    pieces += [jnp.zeros_like(pieces[0])] * (sent_ref.shape[1] // slot_count - len(pieces))
    sent = jnp.concatenate(pieces, axis=0).astype(jnp.bfloat16)
    for k in range(sent_ref.shape[0]):
        sent_ref[k] = sent


def project(rows, near_ref, far_ref):
    return jnp.concatenate(
        [
            jnp.dot(rows, near_ref[...], preferred_element_type=jnp.float32),
            jnp.dot(rows, far_ref[...], preferred_element_type=jnp.float32),
        ],
        axis=1,
    )


def heads_of(shape):
    return (
        lax.broadcasted_iota(jnp.int32, shape, 0) // QROWS
        == lax.broadcasted_iota(jnp.int32, shape, 1) // HD
    )


def query_kernel(heads, mixed_ref, gain_ref, wq_ref, wq_far_ref, out_ref):
    hidden = normed(mixed_ref[...], gain_ref[...].reshape(1, -1))
    query = project(hidden, wq_ref, wq_far_ref)
    spread = jnp.concatenate([query] * heads, axis=0)
    out_ref[...] = jnp.where(heads_of(spread.shape), spread, 0.0).astype(jnp.bfloat16)


def slide_kernel(
    heads,
    counts_ref,
    sent_ref,
    mixed_ref,
    query_ref,
    many_ref,
    wk_ref,
    wk_far_ref,
    wv_ref,
    wv_far_ref,
    wo_ref,
    wo_far_ref,
    out_ref,
    rows,
):
    slot_count, half = out_ref.shape
    core = lax.axis_index("sub")
    count = counts_ref[lax.axis_index("dev")]
    width = sent_ref.shape[2]
    for k in range(sent_ref.shape[0]):
        sent = sent_ref[k].astype(jnp.float32)
        rows[k * slot_count : (k + 1) * slot_count, :] = jnp.concatenate(
            [
                sent[j * slot_count : (j + 1) * slot_count]
                for j in range(rows.shape[1] // width)
            ],
            axis=1,
        )
    hidden = rows[...].astype(jnp.bfloat16)
    keys = project(hidden, wk_ref, wk_far_ref).astype(jnp.bfloat16)
    scores = lax.dot_general(
        query_ref[...], keys, (((1,), (1,)), ((), ())), preferred_element_type=jnp.float32
    ) * (1.0 / math.sqrt(HD))
    values = project(hidden, wv_ref, wv_far_ref).astype(jnp.bfloat16)
    many = many_ref[...]
    masked = jnp.where(many > 0.0, scores, FLOOR)
    weights = many * jnp.exp(masked - jnp.max(masked, axis=1, keepdims=True))
    weights = weights / jnp.sum(weights, axis=1, keepdims=True)
    context = jnp.dot(weights.astype(jnp.bfloat16), values, preferred_element_type=jnp.float32)
    context = jnp.where(heads_of(context.shape), context, 0.0)
    context = context.reshape(heads, QROWS, context.shape[1])
    context = jnp.sum(context, axis=0).astype(jnp.bfloat16)
    columns = pl.ds(pl.multiple_of(core * half, LANES), half)
    attended = jnp.dot(
        context[:, :half], wo_ref[:, columns], preferred_element_type=jnp.float32
    ) + jnp.dot(context[:, half:], wo_far_ref[...], preferred_element_type=jnp.float32)
    total = mixed_ref[:, columns] + attended
    slot = lax.broadcasted_iota(jnp.int32, total.shape, 0)
    total = jnp.where(slot < count, total, 0.0)
    out_ref[...] = total[:slot_count].astype(jnp.bfloat16)


def on_device(
    tiles,
    counts,
    slide_of,
    rates,
    tile_gain,
    gate_weight,
    up_weight,
    embed_proj,
    slide_gain,
    slide_wq,
    slide_wk,
    slide_wv,
    slide_wo,
):
    slot_count, length, width = tiles.shape
    hidden_cols = gate_weight.shape[1]
    n_grp, n_dev, n_sub = (lax.axis_size(a) for a in ("grp", "dev", "sub"))
    ny = 2
    nz = n_dev // ny
    heads = slide_wq.shape[1] * n_sub // HD
    group, core = lax.axis_index("grp"), lax.axis_index("sub")

    to_pair = [(g, g ^ 1) for g in range(n_grp)]
    to_sibling = [(s, s ^ 1) for s in range(n_sub)]
    along_z = [(d, (d + ny) % n_dev) for d in range(n_dev)]
    along_y = [(d, d ^ 1) for d in range(n_dev)]

    half_cols = hidden_cols // 2
    base = (group % 2) * half_cols
    own_blocks = []
    for cols in CHUNKS:
        own_blocks.append(
            jnp.concatenate(
                [
                    lax.dynamic_slice_in_dim(w, base, cols, 1)
                    for w in (gate_weight, up_weight)
                ],
                axis=1,
            )
        )
        base = base + cols
    first = norm_tiles(tiles, tile_gain, False)
    second = norm_tiles(tiles, tile_gain, True)
    pair_first = [lax.ppermute(rows, "grp", to_pair) for rows in first]

    proj_far = lax.ppermute(embed_proj, "sub", to_sibling)
    wq_far = lax.ppermute(slide_wq, "sub", to_sibling)
    wk_far = lax.ppermute(slide_wk, "sub", to_sibling)
    wv_far = lax.ppermute(slide_wv, "sub", to_sibling)
    out_cols = slide_wo.shape[1] // n_sub
    wo_far = lax.ppermute(
        lax.dynamic_slice_in_dim(slide_wo, (1 - core) * out_cols, out_cols, 1), "sub", to_sibling
    )
    smem = pl.BlockSpec(memory_space=pltpu.SMEM)
    vmem = pl.BlockSpec(memory_space=pltpu.VMEM)
    many = pl.pallas_call(
        functools.partial(multiplicity_kernel, n_dev, slot_count, heads),
        in_specs=[smem] * 3,
        out_specs=vmem,
        out_shape=jax.ShapeDtypeStruct((heads * QROWS, n_dev * slot_count), jnp.float32),
    )(counts, slide_of, rates)

    beside = {
        (1, 0): [many, first[0]],
        (1, 1): [second[0]],
        (2, 0): [proj_far],
        (2, 1): [wq_far, wk_far, pair_first[0]],
        (3, 0): [wv_far, wo_far],
    }
    chunks = [[] for _ in own_blocks]
    held = list(own_blocks)
    last = None
    for step in range(nz):
        for c, blocks in enumerate(chunks):
            if step:
                arrived = lax.ppermute(held[c], "dev", along_z)
                others = beside.get((step, c), [])
                if last is not None:
                    others = [last, *others]
                held[c] = after(arrived, blocks[-1], *others)
                last = held[c]
            blocks += [held[c], lax.ppermute(held[c], "dev", along_y)]
    pair_first[1] = after(pair_first[1], last)
    pair_second = [lax.ppermute(rows, "sub", to_sibling) for rows in pair_first]

    own = mlp(last, chunks[0], [*first, *second], ny)
    even = mlp(last, chunks[0], [pair_first[0], pair_second[0]], ny)
    every = [*first, *second, *pair_first, *pair_second]
    parts = last_mlp(own, even, chunks, every, slot_count, n_grp, n_sub, ny)
    parts = lax.all_to_all(parts, ("grp", "sub"), split_axis=0, concat_axis=0, tiled=True)

    out_width = embed_proj.shape[1]
    sent_rows = 16
    sent_cols = 2 * LANES
    small = pltpu.CompilerParams(vmem_limit_bytes=SMALL_VMEM)
    tile_embed, mixed, sent = pl.pallas_call(
        functools.partial(embed_kernel, n_sub),
        in_specs=[smem] + [vmem] * 4,
        out_specs=(vmem, vmem, vmem),
        out_shape=(
            jax.ShapeDtypeStruct((slot_count, hidden_cols), jnp.bfloat16),
            jax.ShapeDtypeStruct((QROWS, out_width), jnp.float32),
            jax.ShapeDtypeStruct((n_dev, sent_rows, sent_cols), jnp.bfloat16),
        ),
        compiler_params=small,
    )(counts, parts, slide_gain, embed_proj, proj_far)
    sent = lax.all_to_all(sent, "dev", split_axis=0, concat_axis=0, tiled=True)
    query = pl.pallas_call(
        functools.partial(query_kernel, heads),
        in_specs=[vmem] * 4,
        out_specs=vmem,
        out_shape=jax.ShapeDtypeStruct((heads * QROWS, out_width), jnp.bfloat16),
        compiler_params=small,
    )(mixed, slide_gain, slide_wq, wq_far)
    slide_out = pl.pallas_call(
        functools.partial(slide_kernel, heads),
        in_specs=[smem] + [vmem] * 10,
        out_specs=vmem,
        out_shape=jax.ShapeDtypeStruct((slot_count, out_cols), jnp.bfloat16),
        scratch_shapes=[pltpu.VMEM((n_dev * slot_count, out_width), jnp.float32)],
        compiler_params=small,
    )(counts, sent, mixed, query, many, slide_wk, wk_far, slide_wv, wv_far, slide_wo, wo_far)
    return (tile_embed, slide_out)


def solution(mesh):
    placed = (
        P(("grp", "dev"), None, None),
        P("grp"),
        P("grp"),
        P(),
        P(),
        P("dev", "sub"),
        P("dev", "sub"),
        P("sub", None),
        P(),
        P(None, "sub"),
        P(None, "sub"),
        P(None, "sub"),
        P("sub", None),
    )
    return jax.shard_map(
        on_device,
        mesh=mesh,
        in_specs=placed,
        out_specs=(P(("grp", "dev"), "sub"), P(("grp", "dev"), "sub")),
        check_vma=False,
    )
```

```python
import functools
import math

import jax
import jax.numpy as jnp
from jax import lax
from jax.experimental import pallas as pl
from jax.experimental.pallas import tpu as pltpu
from jax.sharding import PartitionSpec as P

HD = 64
EPSILON = 1e-06
FLOOR = -1e30
CHUNKS = (256, 256)
QROWS = 8
NORM_ROWS = 16
LANES = 128
UNIT_TILES = 2
UNIT_ROWS = 16
MLP_VMEM = 24 * 1024 * 1024
NORM_VMEM = 8 * 1024 * 1024
SMALL_VMEM = 4 * 1024 * 1024


def normed(rows_in, gains):
    average = jnp.mean(rows_in, axis=-1, keepdims=True)
    centred = rows_in - average
    variance = jnp.mean(centred * centred, axis=-1, keepdims=True)
    return (centred * lax.rsqrt(variance + EPSILON) * gains).astype(jnp.bfloat16)


def norm_kernel(flip, tiles_ref, gain_ref, *refs):
    out_refs, (rows, hidden, in_sems, out_sems) = refs[:-4], refs[-4:]
    core = lax.axis_index("sub")
    half = len(out_refs)
    first = (1 - core if flip else core) * half
    copies = [
        pltpu.make_async_copy(tiles_ref.at[first + i], rows.at[i], in_sems.at[i])
        for i in range(half)
    ]
    stores = [
        pltpu.make_async_copy(hidden.at[i], out_refs[i], out_sems.at[i]) for i in range(half)
    ]
    for copy in copies:
        copy.start()
    gain = gain_ref[...].reshape(1, -1)
    for i in range(half):
        copies[i].wait()

        def some_rows(j, carry):
            here = pl.ds(pl.multiple_of(j * NORM_ROWS, NORM_ROWS), NORM_ROWS)
            hidden[i, here, :] = normed(rows[i, here, :].astype(jnp.float32), gain)
            return carry

        lax.fori_loop(0, rows.shape[1] // NORM_ROWS, some_rows, 0, unroll=4)
        stores[i].start()
    for store in stores:
        store.wait()


def norm_tiles(tiles, gain, flip):
    slot_count, length, width = tiles.shape
    half = slot_count // 2
    hbm = pl.BlockSpec(memory_space=pltpu.HBM)
    return pl.pallas_call(
        functools.partial(norm_kernel, flip),
        in_specs=[hbm, pl.BlockSpec(memory_space=pltpu.VMEM)],
        out_specs=[hbm] * half,
        out_shape=[jax.ShapeDtypeStruct((length, width), jnp.bfloat16)] * half,
        scratch_shapes=[
            pltpu.VMEM((half, length, width), jnp.bfloat16),
            pltpu.VMEM((half, length, width), jnp.bfloat16),
            pltpu.SemaphoreType.DMA((half,)),
            pltpu.SemaphoreType.DMA((half,)),
        ],
        compiler_params=pltpu.CompilerParams(vmem_limit_bytes=NORM_VMEM),
        cost_estimate=pl.CostEstimate(
            flops=8 * half * length * width,
            bytes_accessed=4 * half * length * width,
            transcendentals=half * length,
        ),
    )(tiles, gain)


def after(value, *others):
    return lax.optimization_barrier((value, *others))[0]


def block_copies(blocks, weights, sems, ny):
    n_dev = len(blocks)
    me = lax.axis_index("dev")
    nz = n_dev // ny
    my_z = me // ny
    my_y = me - my_z * ny
    depth = blocks[0].shape[0]
    copies = []
    for k in range(n_dev):
        step, flip = k // ny, k % ny
        z = my_z - step
        z = jnp.where(z < 0, z + nz, z)
        y = 1 - my_y if flip else my_y
        start = pl.multiple_of((z * ny + y) * depth, depth)
        copies.append(
            pltpu.make_async_copy(blocks[k], weights.at[pl.ds(start, depth)], sems.at[k])
        )
    return copies


def tile_copies(tile_refs, rows, sems):
    length = tile_refs[0].shape[0]
    return [
        pltpu.make_async_copy(ref, rows.at[pl.ds(i * length, length)], sems.at[i])
        for i, ref in enumerate(tile_refs)
    ]


def gated_means(both, out_ref, at, length):
    cols = both.shape[1] // 2
    for tile in range(both.shape[0] // length):
        total = jnp.zeros((8, cols), jnp.float32)
        for first in range(tile * length, (tile + 1) * length, UNIT_ROWS):
            gate = both[first : first + UNIT_ROWS, :cols]
            up_part = both[first : first + UNIT_ROWS, cols:]
            silu = gate * (0.5 * jnp.tanh(0.5 * gate) + 0.5)
            gated = (silu * up_part).astype(jnp.bfloat16).astype(jnp.float32)
            total = total + jnp.sum(gated.reshape(UNIT_ROWS // 8, 8, cols), axis=0)
        out_ref[at + tile : at + tile + 1, :] = jnp.sum(total, axis=0, keepdims=True) * (
            1.0 / length
        )


def run_units(units, products, length):
    pending = None
    for i, (waits, rows, weights, out_ref, at) in enumerate(units):
        for copy in waits:
            copy.wait()
        both = products[i % 2]
        both[...] = jnp.dot(rows[...], weights[...], preferred_element_type=jnp.float32)
        if pending is not None:
            gated_means(*pending, length)
        pending = (both, out_ref, at)
    gated_means(*pending, length)


def mlp_scratch(n_dev, chunks, n_tiles, length):
    depth, both_cols = chunks[0][0].shape
    width = n_dev * depth
    unit = (UNIT_TILES * length, both_cols)
    return [
        pltpu.VMEM((len(chunks), width, both_cols), jnp.bfloat16),
        pltpu.VMEM((n_tiles * length, width), jnp.bfloat16),
        pltpu.VMEM(unit, jnp.float32),
        pltpu.VMEM(unit, jnp.float32),
        pltpu.SemaphoreType.DMA((len(chunks), n_dev)),
        pltpu.SemaphoreType.DMA((n_tiles,)),
    ]


def mlp_cost(blocks, n_tiles, tiles):
    both_cols = blocks[0].shape[1]
    length, width = tiles[0].shape
    return pl.CostEstimate(
        flops=2 * n_tiles * length * width * both_cols,
        bytes_accessed=2 * (n_tiles * length * width + width * both_cols),
        transcendentals=n_tiles * length * both_cols // 2,
    )


def first_mlp_kernel(n_dev, ny, n_tiles, after_ref, *refs):
    del after_ref
    blocks, tile_refs = refs[:n_dev], refs[n_dev : n_dev + n_tiles]
    out_ref, weights, rows, even, odd, weight_sems, row_sems = refs[n_dev + n_tiles :]
    length = tile_refs[0].shape[0]
    loads = block_copies(blocks, weights.at[0], weight_sems.at[0], ny)
    row_loads = tile_copies(tile_refs, rows, row_sems)
    for copy in loads + row_loads:
        copy.start()
    units = []
    for i in range(0, n_tiles, UNIT_TILES):
        here = slice(i * length, (i + UNIT_TILES) * length)
        waits = row_loads[i : i + UNIT_TILES] + (loads if i == 0 else [])
        units.append((waits, rows.at[here], weights.at[0], out_ref, i))
    run_units(units, (even, odd), length)


def first_mlp(after_this, blocks, tiles, ny):
    n_dev, n_tiles = len(blocks), len(tiles)
    hbm = pl.BlockSpec(memory_space=pltpu.HBM)
    return pl.pallas_call(
        functools.partial(first_mlp_kernel, n_dev, ny, n_tiles),
        in_specs=[hbm] * (1 + n_dev + n_tiles),
        out_specs=pl.BlockSpec(memory_space=pltpu.VMEM),
        out_shape=jax.ShapeDtypeStruct((n_tiles, blocks[0].shape[1] // 2), jnp.float32),
        scratch_shapes=mlp_scratch(n_dev, [blocks], n_tiles, tiles[0].shape[0]),
        compiler_params=pltpu.CompilerParams(vmem_limit_bytes=MLP_VMEM),
        cost_estimate=mlp_cost(blocks, n_tiles, tiles),
    )(after_this, *blocks, *tiles)


def last_mlp_kernel(n_dev, n_grp, n_sub, ny, slot_count, first_ref, *refs):
    n_tiles = 2 * slot_count
    half = slot_count // 2
    blocks, tile_refs = refs[: 2 * n_dev], refs[2 * n_dev : 2 * n_dev + n_tiles]
    out_ref, weights, rows, even, odd, weight_sems, row_sems, late, rest = refs[
        2 * n_dev + n_tiles :
    ]
    length = tile_refs[0].shape[0]
    loads = [
        block_copies(blocks[c * n_dev : (c + 1) * n_dev], weights.at[c], weight_sems.at[c], ny)
        for c in range(2)
    ]
    row_loads = tile_copies(tile_refs, rows, row_sems)
    for copy in loads[1] + row_loads + loads[0]:
        copy.start()
    units = []
    for i in range(0, n_tiles, UNIT_TILES):
        here = slice(i * length, (i + UNIT_TILES) * length)
        waits = row_loads[i : i + UNIT_TILES] + (loads[1] if i == 0 else [])
        units.append((waits, rows.at[here], weights.at[1], rest, i))
    units.append((loads[0], units[-1][1], weights.at[0], late, 0))
    run_units(units, (even, odd), length)

    group, core = lax.axis_index("grp"), lax.axis_index("sub")
    low = core == 0

    def packed(mine, others):
        rows = jnp.concatenate(
            [jnp.where(low, mine, others), jnp.where(low, others, mine)], axis=0
        )
        return jnp.concatenate(
            [rows[:, k : k + LANES] for k in range(0, rows.shape[1], LANES)], axis=0
        )

    def features(ref, at):
        return jnp.concatenate([ref[at : at + 1, :], rest[at : at + 1, :]], axis=1)

    own = [features(first_ref, i) for i in range(slot_count)]
    own = packed(jnp.concatenate(own[:half], axis=0), jnp.concatenate(own[half:], axis=0))
    at = slot_count
    early = [features(first_ref, at), features(first_ref, at + 1)]
    at += 2
    last = [
        jnp.concatenate([late[i : i + 1, :], rest[at + i : at + i + 1, :]], axis=1)
        for i in range(2)
    ]
    pair = packed(
        jnp.concatenate([early[0], last[0]], axis=0), jnp.concatenate([early[1], last[1]], axis=0)
    )
    for g in range(n_grp):
        chosen = jnp.where(group == g, own, pair).astype(jnp.bfloat16)
        for s in range(n_sub):
            out_ref[g * n_sub + s] = chosen


def last_mlp(first_means, chunks, tiles, slot_count, n_grp, n_sub, ny):
    n_dev = len(chunks[0])
    cols = sum(blocks[0].shape[1] // 2 for blocks in chunks)
    hbm = pl.BlockSpec(memory_space=pltpu.HBM)
    vmem = pl.BlockSpec(memory_space=pltpu.VMEM)
    return pl.pallas_call(
        functools.partial(last_mlp_kernel, n_dev, n_grp, n_sub, ny, slot_count),
        in_specs=[vmem] + [hbm] * (2 * n_dev + len(tiles)),
        out_specs=vmem,
        out_shape=jax.ShapeDtypeStruct(
            (n_grp * n_sub, slot_count * cols // LANES, LANES), jnp.bfloat16
        ),
        scratch_shapes=[
            *mlp_scratch(n_dev, chunks, len(tiles), tiles[0].shape[0]),
            pltpu.VMEM((UNIT_TILES, chunks[0][0].shape[1] // 2), jnp.float32),
            pltpu.VMEM((len(tiles), chunks[1][0].shape[1] // 2), jnp.float32),
        ],
        compiler_params=pltpu.CompilerParams(vmem_limit_bytes=MLP_VMEM),
        cost_estimate=mlp_cost(chunks[1], len(tiles) + UNIT_TILES, tiles),
    )(first_means, *chunks[0], *chunks[1], *tiles)


def small_mod(value, rate):
    return jnp.where(
        rate == 1,
        0,
        jnp.where(rate == 2, value & 1, jnp.where(rate == 3, lax.rem(value, 3), value & 3)),
    )


def multiplicity_kernel(n_dev, slot_count, heads, counts_ref, slide_ref, rates_ref, out_ref):
    me, core = lax.axis_index("dev"), lax.axis_index("sub")
    shape = out_ref.shape
    row = lax.broadcasted_iota(jnp.int32, shape, 0)
    col = lax.broadcasted_iota(jnp.int32, shape, 1)
    head = row // QROWS + core * (heads // 2)
    head = jnp.where(head >= heads, head - heads, head)
    query = row % QROWS
    device, slot = col // slot_count, col % slot_count
    rate = jnp.full(shape, 1, jnp.int32)
    for h in range(heads):
        rate = jnp.where(head == h, rates_ref[h], rate)
    my_slide = slide_ref[me]
    first = me
    count = jnp.zeros(shape, jnp.int32)
    slide = jnp.zeros(shape, jnp.int32)
    for k in reversed(range(n_dev)):
        first = jnp.where(slide_ref[k] == my_slide, k, first)
        count = jnp.where(device == k, counts_ref[k], count)
        slide = jnp.where(device == k, slide_ref[k], slide)
    offset = small_mod(head, rate)
    query_position = (me - first) * slot_count + query
    key_position = (device - first) * slot_count + slot
    valid = slot < count
    near = jnp.where((device == me) & valid, 1.0, 0.0)
    far = jnp.where(
        (slide == my_slide)
        & valid
        & (small_mod(query_position, rate) == offset)
        & (small_mod(key_position, rate) == offset),
        1.0,
        0.0,
    )
    out_ref[...] = near + far


def embed_kernel(
    n_sub, counts_ref, parts_ref, gain_ref, near_ref, far_ref, embed_ref, mixed_ref, sent_ref
):
    slot_count, half = embed_ref.shape
    n_blocks = half // 2 // LANES
    group, core = lax.axis_index("grp"), lax.axis_index("sub")
    count = counts_ref[lax.axis_index("dev")]
    base = group // 2 * 2
    halves = []
    for s in range(n_sub):
        pieces = []
        for x in range(2):
            part = parts_ref[(base + x) * n_sub + s].astype(jnp.float32)
            pieces += [part[k * slot_count : (k + 1) * slot_count] for k in range(n_blocks)]
        rows = jnp.concatenate(pieces, axis=1)
        slot = lax.broadcasted_iota(jnp.int32, rows.shape, 0)
        halves.append(jnp.where(slot < count, rows, 0.0))
    low = core == 0
    near = jnp.where(low, halves[0], halves[1]).astype(jnp.bfloat16)
    far = jnp.where(low, halves[1], halves[0]).astype(jnp.bfloat16)
    embed_ref[...] = near
    mixed = jnp.dot(near, near_ref[...], preferred_element_type=jnp.float32) + jnp.dot(
        far, far_ref[...], preferred_element_type=jnp.float32
    )
    mixed_ref[...] = jnp.concatenate([mixed, mixed], axis=0)
    hidden = normed(mixed, gain_ref[...].reshape(1, -1)).astype(jnp.float32)
    width = sent_ref.shape[2]
    pieces = [hidden[:, k : k + width] for k in range(0, hidden.shape[1], width)]
    pieces += [jnp.zeros_like(pieces[0])] * (sent_ref.shape[1] // slot_count - len(pieces))
    sent = jnp.concatenate(pieces, axis=0).astype(jnp.bfloat16)
    for k in range(sent_ref.shape[0]):
        sent_ref[k] = sent


def project(rows, near_ref, far_ref):
    return jnp.concatenate(
        [
            jnp.dot(rows, near_ref[...], preferred_element_type=jnp.float32),
            jnp.dot(rows, far_ref[...], preferred_element_type=jnp.float32),
        ],
        axis=1,
    )


def heads_of(shape):
    return (
        lax.broadcasted_iota(jnp.int32, shape, 0) // QROWS
        == lax.broadcasted_iota(jnp.int32, shape, 1) // HD
    )


def query_kernel(heads, mixed_ref, gain_ref, wq_ref, wq_far_ref, out_ref):
    hidden = normed(mixed_ref[...], gain_ref[...].reshape(1, -1))
    query = project(hidden, wq_ref, wq_far_ref)
    spread = jnp.concatenate([query] * heads, axis=0)
    out_ref[...] = jnp.where(heads_of(spread.shape), spread, 0.0).astype(jnp.bfloat16)


def slide_kernel(
    heads,
    counts_ref,
    sent_ref,
    mixed_ref,
    query_ref,
    many_ref,
    wk_ref,
    wk_far_ref,
    wv_ref,
    wv_far_ref,
    wo_ref,
    wo_far_ref,
    out_ref,
    rows,
):
    slot_count, half = out_ref.shape
    core = lax.axis_index("sub")
    count = counts_ref[lax.axis_index("dev")]
    width = sent_ref.shape[2]
    for k in range(sent_ref.shape[0]):
        sent = sent_ref[k].astype(jnp.float32)
        rows[k * slot_count : (k + 1) * slot_count, :] = jnp.concatenate(
            [
                sent[j * slot_count : (j + 1) * slot_count]
                for j in range(rows.shape[1] // width)
            ],
            axis=1,
        )
    hidden = rows[...].astype(jnp.bfloat16)
    keys = project(hidden, wk_ref, wk_far_ref).astype(jnp.bfloat16)
    scores = lax.dot_general(
        query_ref[...], keys, (((1,), (1,)), ((), ())), preferred_element_type=jnp.float32
    ) * (1.0 / math.sqrt(HD))
    values = project(hidden, wv_ref, wv_far_ref).astype(jnp.bfloat16)
    many = many_ref[...]
    masked = jnp.where(many > 0.0, scores, FLOOR)
    weights = many * jnp.exp(masked - jnp.max(masked, axis=1, keepdims=True))
    weights = weights / jnp.sum(weights, axis=1, keepdims=True)
    context = jnp.dot(weights.astype(jnp.bfloat16), values, preferred_element_type=jnp.float32)
    context = jnp.where(heads_of(context.shape), context, 0.0)
    context = context.reshape(heads, QROWS, context.shape[1])
    context = jnp.sum(context, axis=0).astype(jnp.bfloat16)
    columns = pl.ds(pl.multiple_of(core * half, LANES), half)
    attended = jnp.dot(
        context[:, :half], wo_ref[:, columns], preferred_element_type=jnp.float32
    ) + jnp.dot(context[:, half:], wo_far_ref[...], preferred_element_type=jnp.float32)
    total = mixed_ref[:, columns] + attended
    slot = lax.broadcasted_iota(jnp.int32, total.shape, 0)
    total = jnp.where(slot < count, total, 0.0)
    out_ref[...] = total[:slot_count].astype(jnp.bfloat16)


def on_device(
    tiles,
    counts,
    slide_of,
    rates,
    tile_gain,
    gate_weight,
    up_weight,
    embed_proj,
    slide_gain,
    slide_wq,
    slide_wk,
    slide_wv,
    slide_wo,
):
    slot_count, length, width = tiles.shape
    hidden_cols = gate_weight.shape[1]
    n_grp, n_dev, n_sub = (lax.axis_size(a) for a in ("grp", "dev", "sub"))
    ny = 2
    nz = n_dev // ny
    heads = slide_wq.shape[1] * n_sub // HD
    group, core = lax.axis_index("grp"), lax.axis_index("sub")

    to_pair = [(g, g ^ 1) for g in range(n_grp)]
    to_sibling = [(s, s ^ 1) for s in range(n_sub)]
    along_z = [(d, (d + ny) % n_dev) for d in range(n_dev)]
    along_y = [(d, d ^ 1) for d in range(n_dev)]

    half_cols = hidden_cols // 2
    base = (group % 2) * half_cols
    own_blocks = []
    for cols in CHUNKS:
        own_blocks.append(
            jnp.concatenate(
                [
                    lax.dynamic_slice_in_dim(w, base, cols, 1)
                    for w in (gate_weight, up_weight)
                ],
                axis=1,
            )
        )
        base = base + cols
    first = norm_tiles(tiles, tile_gain, False)
    second = norm_tiles(tiles, tile_gain, True)
    pair_first = [lax.ppermute(rows, "grp", to_pair) for rows in first]

    proj_far = lax.ppermute(embed_proj, "sub", to_sibling)
    wq_far = lax.ppermute(slide_wq, "sub", to_sibling)
    wk_far = lax.ppermute(slide_wk, "sub", to_sibling)
    wv_far = lax.ppermute(slide_wv, "sub", to_sibling)
    out_cols = slide_wo.shape[1] // n_sub
    wo_far = lax.ppermute(
        lax.dynamic_slice_in_dim(slide_wo, (1 - core) * out_cols, out_cols, 1), "sub", to_sibling
    )
    smem = pl.BlockSpec(memory_space=pltpu.SMEM)
    vmem = pl.BlockSpec(memory_space=pltpu.VMEM)
    many = pl.pallas_call(
        functools.partial(multiplicity_kernel, n_dev, slot_count, heads),
        in_specs=[smem] * 3,
        out_specs=vmem,
        out_shape=jax.ShapeDtypeStruct((heads * QROWS, n_dev * slot_count), jnp.float32),
        compiler_params=pltpu.CompilerParams(vmem_limit_bytes=SMALL_VMEM),
    )(counts, slide_of, rates)

    own_blocks[1] = after(own_blocks[1], first[0])
    beside = {
        (1, 1): [second[0]],
        (2, 0): [proj_far],
        (2, 1): [wq_far, pair_first[0]],
        (3, 0): [wk_far, wv_far],
        (3, 1): [wo_far, many],
    }
    chunks = [[] for _ in own_blocks]
    held = list(own_blocks)
    last = None
    for step in range(nz):
        for c, blocks in enumerate(chunks):
            if step:
                arrived = lax.ppermute(held[c], "dev", along_z)
                others = beside.get((step, c), [])
                if last is not None:
                    others = [last, *others]
                held[c] = after(arrived, blocks[-1], *others)
                last = held[c]
            blocks += [held[c], lax.ppermute(held[c], "dev", along_y)]
    pair_first[1] = after(pair_first[1], last)
    pair_second = [lax.ppermute(rows, "sub", to_sibling) for rows in pair_first]

    pieces = [rows for piece in zip(pair_first, pair_second) for rows in piece]
    own_tiles = [*first, *second]
    first_means = first_mlp(last, chunks[0], own_tiles + pieces[:2], ny)
    parts = last_mlp(first_means, chunks, own_tiles + pieces, slot_count, n_grp, n_sub, ny)
    parts = lax.all_to_all(parts, ("grp", "sub"), split_axis=0, concat_axis=0, tiled=True)

    out_width = embed_proj.shape[1]
    sent_rows = 16
    sent_cols = 2 * LANES
    small = pltpu.CompilerParams(vmem_limit_bytes=SMALL_VMEM)
    tile_embed, mixed, sent = pl.pallas_call(
        functools.partial(embed_kernel, n_sub),
        in_specs=[smem] + [vmem] * 4,
        out_specs=(vmem, vmem, vmem),
        out_shape=(
            jax.ShapeDtypeStruct((slot_count, hidden_cols), jnp.bfloat16),
            jax.ShapeDtypeStruct((QROWS, out_width), jnp.float32),
            jax.ShapeDtypeStruct((n_dev, sent_rows, sent_cols), jnp.bfloat16),
        ),
        compiler_params=small,
    )(counts, parts, slide_gain, embed_proj, proj_far)
    sent = lax.all_to_all(sent, "dev", split_axis=0, concat_axis=0, tiled=True)
    query = pl.pallas_call(
        functools.partial(query_kernel, heads),
        in_specs=[vmem] * 4,
        out_specs=vmem,
        out_shape=jax.ShapeDtypeStruct((heads * QROWS, out_width), jnp.bfloat16),
        compiler_params=small,
    )(mixed, slide_gain, slide_wq, wq_far)
    slide_out = pl.pallas_call(
        functools.partial(slide_kernel, heads),
        in_specs=[smem] + [vmem] * 10,
        out_specs=vmem,
        out_shape=jax.ShapeDtypeStruct((slot_count, out_cols), jnp.bfloat16),
        scratch_shapes=[pltpu.VMEM((n_dev * slot_count, out_width), jnp.float32)],
        compiler_params=small,
    )(counts, sent, mixed, query, many, slide_wk, wk_far, slide_wv, wv_far, slide_wo, wo_far)
    return (tile_embed, slide_out)


def solution(mesh):
    placed = (
        P(("grp", "dev"), None, None),
        P("grp"),
        P("grp"),
        P(),
        P(),
        P("dev", "sub"),
        P("dev", "sub"),
        P("sub", None),
        P(),
        P(None, "sub"),
        P(None, "sub"),
        P(None, "sub"),
        P("sub", None),
    )
    return jax.shard_map(
        on_device,
        mesh=mesh,
        in_specs=placed,
        out_specs=(P(("grp", "dev"), "sub"), P(("grp", "dev"), "sub")),
        check_vma=False,
    )
```

```python
import functools
import math

import jax
import jax.numpy as jnp
from jax import lax
from jax.experimental import pallas as pl
from jax.experimental.pallas import tpu as pltpu
from jax.sharding import PartitionSpec as P

HD = 64
EPSILON = 1e-06
FLOOR = -1e30
QROWS = 8
NORM_ROWS = 16
LANES = 128
UNIT_ROWS = 16
MLP_VMEM = 32 * 1024 * 1024
NORM_VMEM = 8 * 1024 * 1024
SMALL_VMEM = 4 * 1024 * 1024


def normed(rows_in, gains):
    average = jnp.mean(rows_in, axis=-1, keepdims=True)
    centred = rows_in - average
    variance = jnp.mean(centred * centred, axis=-1, keepdims=True)
    return (centred * lax.rsqrt(variance + EPSILON) * gains).astype(jnp.bfloat16)


def in_hbm(*arrays):
    return [pltpu.with_memory_space_constraint(x, pltpu.HBM) for x in arrays]


def norm_kernel(flip, tiles_ref, gain_ref, out_ref, rows, hidden, in_sems, out_sems):
    core = lax.axis_index("sub")
    half, length = rows.shape[:2]
    first = (1 - core if flip else core) * half
    copies = [
        pltpu.make_async_copy(tiles_ref.at[first + i], rows.at[i], in_sems.at[i])
        for i in range(half)
    ]
    stores = [
        pltpu.make_async_copy(
            hidden.at[i], out_ref.at[pl.ds(i * length, length)], out_sems.at[i]
        )
        for i in range(half)
    ]
    for copy in copies:
        copy.start()
    gain = gain_ref[...].reshape(1, -1)
    for i in range(half):
        copies[i].wait()

        def some_rows(j, carry):
            here = pl.ds(pl.multiple_of(j * NORM_ROWS, NORM_ROWS), NORM_ROWS)
            hidden[i, here, :] = normed(rows[i, here, :].astype(jnp.float32), gain)
            return carry

        lax.fori_loop(0, length // NORM_ROWS, some_rows, 0, unroll=4)
        stores[i].start()
    for store in stores:
        store.wait()


def norm_tiles(tiles, gain, flip):
    slot_count, length, width = tiles.shape
    half = slot_count // 2
    hbm = pl.BlockSpec(memory_space=pltpu.HBM)
    return pl.pallas_call(
        functools.partial(norm_kernel, flip),
        in_specs=[hbm, pl.BlockSpec(memory_space=pltpu.VMEM)],
        out_specs=hbm,
        out_shape=pltpu.HBM((half * length, width), jnp.bfloat16),
        scratch_shapes=[
            pltpu.VMEM((half, length, width), jnp.bfloat16),
            pltpu.VMEM((half, length, width), jnp.bfloat16),
            pltpu.SemaphoreType.DMA((half,)),
            pltpu.SemaphoreType.DMA((half,)),
        ],
        compiler_params=pltpu.CompilerParams(vmem_limit_bytes=NORM_VMEM),
        cost_estimate=pl.CostEstimate(flops=0, bytes_accessed=0, transcendentals=0),
    )(*in_hbm(tiles), gain)


def after(value, *others):
    return lax.optimization_barrier((value, *others))[0]


class Layout:
    def __init__(self, n_dev, ny, depth):
        self.ny, self.nz, self.depth = ny, n_dev // ny, depth
        self.pair = ny * depth
        self.relative = self.pair % LANES == 0
        self.early = self.nz // 2 * self.pair if self.relative else 0
        self.width = n_dev * depth

    def place(self):
        me = lax.axis_index("dev")
        my_z = me // self.ny
        return my_z, me - my_z * self.ny

    def source(self, step):
        my_z, _ = self.place()
        z = my_z - step
        return jnp.where(z < 0, z + self.nz, z)

    def block_copies(self, blocks, weights, sems):
        _, my_y = self.place()
        copies = []
        for k, block in enumerate(blocks):
            step, flip = k // self.ny, k % self.ny
            y = 1 - my_y if flip else my_y
            at = step if self.relative else self.source(step)
            start = pl.multiple_of(at * self.pair + y * self.depth, self.depth)
            copies.append(
                pltpu.make_async_copy(block, weights.at[pl.ds(start, self.depth)], sems.at[k])
            )
        return copies

    def row_copies(self, tiles_ref, rows, sems, steps):
        if not self.relative:
            return [pltpu.make_async_copy(tiles_ref, rows, sems.at[0])]
        copies = []
        for step in steps:
            start = pl.multiple_of(self.source(step) * self.pair, LANES)
            copies.append(
                pltpu.make_async_copy(
                    tiles_ref.at[:, pl.ds(start, self.pair)],
                    rows.at[:, step * self.pair : (step + 1) * self.pair],
                    sems.at[step],
                )
            )
        return copies


def gated_means(both, out_ref, at, length):
    cols = both.shape[1] // 2
    for tile in range(both.shape[0] // length):
        total = jnp.zeros((8, cols), jnp.float32)
        for first in range(tile * length, (tile + 1) * length, UNIT_ROWS):
            gate = both[first : first + UNIT_ROWS, :cols]
            up_part = both[first : first + UNIT_ROWS, cols:]
            silu = gate * (0.5 * jnp.tanh(0.5 * gate) + 0.5)
            gated = (silu * up_part).astype(jnp.bfloat16).astype(jnp.float32)
            total = total + jnp.sum(gated.reshape(UNIT_ROWS // 8, 8, cols), axis=0)
        out_ref[at + tile : at + tile + 1, :] = jnp.sum(total, axis=0, keepdims=True) * (
            1.0 / length
        )


def product(rows, weights, first, last):
    return jnp.dot(
        rows[:, first:last], weights[first:last, :], preferred_element_type=jnp.float32
    )


def early_kernel(layout, *refs):
    steps = range(layout.nz // 2)
    n_blocks = len(steps) * layout.ny
    blocks, tile_refs = refs[:n_blocks], refs[n_blocks : n_blocks + 2]
    out_ref, weights, rows, sums, weight_sems, row_sems, out_sems = refs[n_blocks + 2 :]
    loads = layout.block_copies(blocks, weights, weight_sems)
    row_loads = [
        layout.row_copies(ref, rows.at[i], row_sems.at[i], steps)
        for i, ref in enumerate(tile_refs)
    ]
    for copy in row_loads[0] + loads + row_loads[1]:
        copy.start()
    for copy in loads:
        copy.wait()
    stores = []
    for i in range(2):
        for copy in row_loads[i]:
            copy.wait()
        sums[i] = product(rows.at[i], weights, 0, layout.early)
        stores.append(pltpu.make_async_copy(sums.at[i], out_ref.at[i], out_sems.at[i]))
        stores[i].start()
    for store in stores:
        store.wait()


def early_mlp(layout, blocks, tiles):
    n_rows = tiles[0].shape[0]
    cols = blocks[0].shape[1]
    hbm = pl.BlockSpec(memory_space=pltpu.HBM)
    return pl.pallas_call(
        functools.partial(early_kernel, layout),
        in_specs=[hbm] * (len(blocks) + 2),
        out_specs=hbm,
        out_shape=pltpu.HBM((2, n_rows, cols), jnp.float32),
        scratch_shapes=[
            pltpu.VMEM((layout.early, cols), jnp.bfloat16),
            pltpu.VMEM((2, n_rows, layout.early), jnp.bfloat16),
            pltpu.VMEM((2, n_rows, cols), jnp.float32),
            pltpu.SemaphoreType.DMA((len(blocks),)),
            pltpu.SemaphoreType.DMA((2, layout.nz)),
            pltpu.SemaphoreType.DMA((2,)),
        ],
        compiler_params=pltpu.CompilerParams(vmem_limit_bytes=MLP_VMEM),
        cost_estimate=pl.CostEstimate(flops=0, bytes_accessed=0, transcendentals=0),
    )(*in_hbm(*blocks, *tiles))


def middle_kernel(layout, length, *refs):
    n_blocks = layout.nz * layout.ny
    n_sums = 1 if layout.relative else 0
    blocks, tile_refs = refs[:n_blocks], refs[n_blocks : n_blocks + 3]
    sum_refs = refs[n_blocks + 3 : n_blocks + 3 + n_sums]
    out_ref, weights, rows, sums, even, odd, weight_sems, row_sems, sum_sems = refs[
        n_blocks + 3 + n_sums :
    ]
    early = layout.early
    loads = layout.block_copies(blocks, weights, weight_sems)
    late_blocks = early // layout.depth
    steps = [range(early // layout.pair, layout.nz)] * 2 + [range(layout.nz)]
    row_loads = [
        layout.row_copies(ref, rows.at[i], row_sems.at[i], steps[i])
        for i, ref in enumerate(tile_refs)
    ]
    sum_loads = [
        pltpu.make_async_copy(ref.at[i], sums.at[i], sum_sems.at[i])
        for ref in sum_refs
        for i in range(2)
    ]
    for copy in loads[late_blocks:] + row_loads[0] + sum_loads[:1]:
        copy.start()
    for copy in row_loads[1] + sum_loads[1:] + row_loads[2] + loads[:late_blocks]:
        copy.start()
    waits = [
        loads[late_blocks:] + row_loads[0] + sum_loads[:1],
        row_loads[1] + sum_loads[1:],
        row_loads[2] + loads[:late_blocks],
    ]
    pending = None
    for i in range(3):
        for copy in waits[i]:
            copy.wait()
        both = (even, odd)[i % 2]
        if i < 2 and n_sums:
            both[...] = product(rows.at[i], weights, early, layout.width) + sums[i]
        else:
            both[...] = product(rows.at[i], weights, 0, layout.width)
        if pending is not None:
            gated_means(*pending, length)
        pending = (both, out_ref, 2 * i)
    gated_means(*pending, length)


def middle_mlp(layout, blocks, tiles, sums, length):
    n_rows, width = tiles[0].shape
    cols = blocks[0].shape[1]
    hbm = pl.BlockSpec(memory_space=pltpu.HBM)
    return pl.pallas_call(
        functools.partial(middle_kernel, layout, length),
        in_specs=[hbm] * (len(blocks) + 3 + len(sums)),
        out_specs=pl.BlockSpec(memory_space=pltpu.VMEM),
        out_shape=jax.ShapeDtypeStruct((3 * n_rows // length, cols // 2), jnp.float32),
        scratch_shapes=[
            pltpu.VMEM((width, cols), jnp.bfloat16),
            pltpu.VMEM((3, n_rows, width), jnp.bfloat16),
            pltpu.VMEM((2, n_rows, cols), jnp.float32),
            pltpu.VMEM((n_rows, cols), jnp.float32),
            pltpu.VMEM((n_rows, cols), jnp.float32),
            pltpu.SemaphoreType.DMA((len(blocks),)),
            pltpu.SemaphoreType.DMA((3, layout.nz)),
            pltpu.SemaphoreType.DMA((2,)),
        ],
        compiler_params=pltpu.CompilerParams(vmem_limit_bytes=MLP_VMEM),
        cost_estimate=pl.CostEstimate(
            flops=4 * n_rows * width * cols,
            bytes_accessed=2 * (3 * n_rows * width + width * cols) + 8 * n_rows * cols,
            transcendentals=0,
        ),
    )(*in_hbm(*blocks[:-1]), blocks[-1], *in_hbm(*tiles, *sums))


def last_kernel(layout, length, n_grp, n_sub, means_ref, *refs):
    n_blocks = layout.nz * layout.ny
    blocks, tiles_ref = refs[:n_blocks], refs[n_blocks]
    out_ref, weights, rows, both, means, weight_sems, row_sems = refs[n_blocks + 1 :]
    loads = layout.block_copies(blocks, weights, weight_sems)
    row_loads = layout.row_copies(tiles_ref, rows, row_sems, range(layout.nz))
    for copy in row_loads + loads:
        copy.start()
    for copy in row_loads + loads:
        copy.wait()
    n_rows = rows.shape[0]
    for i in range(0, n_rows, length):
        here = slice(i, i + length)
        both[here, :] = product(rows.at[here], weights, 0, layout.width)
    gated_means(both, means, 0, length)

    group, core = lax.axis_index("grp"), lax.axis_index("sub")
    low = core == 0
    half = n_rows // length

    def packed(mine, others):
        rows = jnp.concatenate(
            [jnp.where(low, mine, others), jnp.where(low, others, mine)], axis=0
        )
        return jnp.concatenate(
            [rows[:, k : k + LANES] for k in range(0, rows.shape[1], LANES)], axis=0
        )

    before = means_ref[...]
    own = packed(before[:half], before[half : 2 * half])
    pair = packed(before[2 * half :], means[...])
    for g in range(n_grp):
        chosen = jnp.where(group == g, own, pair).astype(jnp.bfloat16)
        for s in range(n_sub):
            out_ref[g * n_sub + s] = chosen


def last_mlp(layout, means, blocks, tiles, length, n_grp, n_sub):
    n_rows, width = tiles.shape
    cols = blocks[0].shape[1]
    half = n_rows // length
    hbm = pl.BlockSpec(memory_space=pltpu.HBM)
    vmem = pl.BlockSpec(memory_space=pltpu.VMEM)
    return pl.pallas_call(
        functools.partial(last_kernel, layout, length, n_grp, n_sub),
        in_specs=[vmem] + [hbm] * (len(blocks) + 1),
        out_specs=vmem,
        out_shape=jax.ShapeDtypeStruct(
            (n_grp * n_sub, half * cols // LANES, LANES), jnp.bfloat16
        ),
        scratch_shapes=[
            pltpu.VMEM((width, cols), jnp.bfloat16),
            pltpu.VMEM((n_rows, width), jnp.bfloat16),
            pltpu.VMEM((n_rows, cols), jnp.float32),
            pltpu.VMEM((half, cols // 2), jnp.float32),
            pltpu.SemaphoreType.DMA((len(blocks),)),
            pltpu.SemaphoreType.DMA((layout.nz,)),
        ],
        compiler_params=pltpu.CompilerParams(vmem_limit_bytes=MLP_VMEM),
        cost_estimate=pl.CostEstimate(
            flops=2 * n_rows * width * cols,
            bytes_accessed=2 * (n_rows * width + width * cols),
            transcendentals=0,
        ),
    )(means, *in_hbm(*blocks[:-1]), blocks[-1], tiles)


def small_mod(value, rate):
    return jnp.where(
        rate == 1,
        0,
        jnp.where(rate == 2, value & 1, jnp.where(rate == 3, lax.rem(value, 3), value & 3)),
    )


def multiplicity_kernel(n_dev, slot_count, heads, counts_ref, slide_ref, rates_ref, out_ref):
    me, core = lax.axis_index("dev"), lax.axis_index("sub")
    shape = out_ref.shape
    row = lax.broadcasted_iota(jnp.int32, shape, 0)
    col = lax.broadcasted_iota(jnp.int32, shape, 1)
    head = row // QROWS + core * (heads // 2)
    head = jnp.where(head >= heads, head - heads, head)
    query = row % QROWS
    device, slot = col // slot_count, col % slot_count
    rate = jnp.full(shape, 1, jnp.int32)
    for h in range(heads):
        rate = jnp.where(head == h, rates_ref[h], rate)
    my_slide = slide_ref[me]
    first = me
    count = jnp.zeros(shape, jnp.int32)
    slide = jnp.zeros(shape, jnp.int32)
    for k in reversed(range(n_dev)):
        first = jnp.where(slide_ref[k] == my_slide, k, first)
        count = jnp.where(device == k, counts_ref[k], count)
        slide = jnp.where(device == k, slide_ref[k], slide)
    offset = small_mod(head, rate)
    query_position = (me - first) * slot_count + query
    key_position = (device - first) * slot_count + slot
    valid = slot < count
    near = jnp.where((device == me) & valid, 1.0, 0.0)
    far = jnp.where(
        (slide == my_slide)
        & valid
        & (small_mod(query_position, rate) == offset)
        & (small_mod(key_position, rate) == offset),
        1.0,
        0.0,
    )
    out_ref[...] = near + far


def embed_kernel(
    n_sub, counts_ref, parts_ref, gain_ref, near_ref, far_ref, embed_ref, mixed_ref, sent_ref
):
    slot_count, half = embed_ref.shape
    n_blocks = half // 2 // LANES
    group, core = lax.axis_index("grp"), lax.axis_index("sub")
    count = counts_ref[lax.axis_index("dev")]
    base = group // 2 * 2
    halves = []
    for s in range(n_sub):
        pieces = []
        for x in range(2):
            part = parts_ref[(base + x) * n_sub + s].astype(jnp.float32)
            pieces += [part[k * slot_count : (k + 1) * slot_count] for k in range(n_blocks)]
        rows = jnp.concatenate(pieces, axis=1)
        slot = lax.broadcasted_iota(jnp.int32, rows.shape, 0)
        halves.append(jnp.where(slot < count, rows, 0.0))
    low = core == 0
    near = jnp.where(low, halves[0], halves[1]).astype(jnp.bfloat16)
    far = jnp.where(low, halves[1], halves[0]).astype(jnp.bfloat16)
    embed_ref[...] = near
    mixed = jnp.dot(near, near_ref[...], preferred_element_type=jnp.float32) + jnp.dot(
        far, far_ref[...], preferred_element_type=jnp.float32
    )
    mixed_ref[...] = jnp.concatenate([mixed, mixed], axis=0)
    hidden = normed(mixed, gain_ref[...].reshape(1, -1)).astype(jnp.float32)
    width = sent_ref.shape[2]
    pieces = [hidden[:, k : k + width] for k in range(0, hidden.shape[1], width)]
    pieces += [jnp.zeros_like(pieces[0])] * (sent_ref.shape[1] // slot_count - len(pieces))
    sent = jnp.concatenate(pieces, axis=0).astype(jnp.bfloat16)
    for k in range(sent_ref.shape[0]):
        sent_ref[k] = sent


def project(rows, near_ref, far_ref):
    return jnp.concatenate(
        [
            jnp.dot(rows, near_ref[...], preferred_element_type=jnp.float32),
            jnp.dot(rows, far_ref[...], preferred_element_type=jnp.float32),
        ],
        axis=1,
    )


def heads_of(shape):
    return (
        lax.broadcasted_iota(jnp.int32, shape, 0) // QROWS
        == lax.broadcasted_iota(jnp.int32, shape, 1) // HD
    )


def query_kernel(heads, mixed_ref, gain_ref, wq_ref, wq_far_ref, out_ref):
    hidden = normed(mixed_ref[...], gain_ref[...].reshape(1, -1))
    query = project(hidden, wq_ref, wq_far_ref)
    spread = jnp.concatenate([query] * heads, axis=0)
    out_ref[...] = jnp.where(heads_of(spread.shape), spread, 0.0).astype(jnp.bfloat16)


def slide_kernel(
    heads,
    counts_ref,
    sent_ref,
    mixed_ref,
    query_ref,
    many_ref,
    wk_ref,
    wk_far_ref,
    wv_ref,
    wv_far_ref,
    wo_ref,
    wo_far_ref,
    out_ref,
    rows,
):
    slot_count, half = out_ref.shape
    core = lax.axis_index("sub")
    count = counts_ref[lax.axis_index("dev")]
    width = sent_ref.shape[2]
    for k in range(sent_ref.shape[0]):
        sent = sent_ref[k].astype(jnp.float32)
        rows[k * slot_count : (k + 1) * slot_count, :] = jnp.concatenate(
            [
                sent[j * slot_count : (j + 1) * slot_count]
                for j in range(rows.shape[1] // width)
            ],
            axis=1,
        )
    hidden = rows[...].astype(jnp.bfloat16)
    keys = project(hidden, wk_ref, wk_far_ref).astype(jnp.bfloat16)
    scores = lax.dot_general(
        query_ref[...], keys, (((1,), (1,)), ((), ())), preferred_element_type=jnp.float32
    ) * (1.0 / math.sqrt(HD))
    values = project(hidden, wv_ref, wv_far_ref).astype(jnp.bfloat16)
    many = many_ref[...]
    masked = jnp.where(many > 0.0, scores, FLOOR)
    weights = many * jnp.exp(masked - jnp.max(masked, axis=1, keepdims=True))
    weights = weights / jnp.sum(weights, axis=1, keepdims=True)
    context = jnp.dot(weights.astype(jnp.bfloat16), values, preferred_element_type=jnp.float32)
    context = jnp.where(heads_of(context.shape), context, 0.0)
    context = context.reshape(heads, QROWS, context.shape[1])
    context = jnp.sum(context, axis=0).astype(jnp.bfloat16)
    columns = pl.ds(pl.multiple_of(core * half, LANES), half)
    attended = jnp.dot(
        context[:, :half], wo_ref[:, columns], preferred_element_type=jnp.float32
    ) + jnp.dot(context[:, half:], wo_far_ref[...], preferred_element_type=jnp.float32)
    total = mixed_ref[:, columns] + attended
    slot = lax.broadcasted_iota(jnp.int32, total.shape, 0)
    total = jnp.where(slot < count, total, 0.0)
    out_ref[...] = total[:slot_count].astype(jnp.bfloat16)


def on_device(
    tiles,
    counts,
    slide_of,
    rates,
    tile_gain,
    gate_weight,
    up_weight,
    embed_proj,
    slide_gain,
    slide_wq,
    slide_wk,
    slide_wv,
    slide_wo,
):
    slot_count, length, width = tiles.shape
    hidden_cols = gate_weight.shape[1]
    n_grp, n_dev, n_sub = (lax.axis_size(a) for a in ("grp", "dev", "sub"))
    ny = 2
    nz = n_dev // ny
    heads = slide_wq.shape[1] * n_sub // HD
    group, core = lax.axis_index("grp"), lax.axis_index("sub")

    to_pair = [(g, g ^ 1) for g in range(n_grp)]
    to_sibling = [(s, s ^ 1) for s in range(n_sub)]
    along_z = [(d, (d + ny) % n_dev) for d in range(n_dev)]
    along_y = [(d, d ^ 1) for d in range(n_dev)]

    half_cols = hidden_cols // 2
    block = jnp.concatenate(
        [
            lax.dynamic_slice_in_dim(w, (group % 2) * half_cols, half_cols, 1)
            for w in (gate_weight, up_weight)
        ],
        axis=1,
    )
    layout = Layout(n_dev, ny, gate_weight.shape[0])
    first = norm_tiles(tiles, after(tile_gain, block), False)
    second = norm_tiles(tiles, tile_gain, True)
    pair_first = lax.ppermute(first, "grp", to_pair)

    proj_far = lax.ppermute(embed_proj, "sub", to_sibling)
    wq_far = lax.ppermute(slide_wq, "sub", to_sibling)
    wk_far = lax.ppermute(slide_wk, "sub", to_sibling)
    wv_far = lax.ppermute(slide_wv, "sub", to_sibling)
    out_cols = slide_wo.shape[1] // n_sub
    wo_far = lax.ppermute(
        lax.dynamic_slice_in_dim(slide_wo, (1 - core) * out_cols, out_cols, 1), "sub", to_sibling
    )
    smem = pl.BlockSpec(memory_space=pltpu.SMEM)
    vmem = pl.BlockSpec(memory_space=pltpu.VMEM)
    many = pl.pallas_call(
        functools.partial(multiplicity_kernel, n_dev, slot_count, heads),
        in_specs=[smem] * 3,
        out_specs=vmem,
        out_shape=jax.ShapeDtypeStruct((heads * QROWS, n_dev * slot_count), jnp.float32),
        compiler_params=pltpu.CompilerParams(vmem_limit_bytes=SMALL_VMEM),
    )(counts, slide_of, rates)

    beside = {1: [first, second], 2: [proj_far, wq_far], 3: [wk_far, wv_far, wo_far, many]}
    blocks = []
    sums = []
    for step in range(nz):
        if step:
            block = lax.ppermute(block, "dev", along_z)
            others = beside.get(step, [])
            if layout.relative and step == nz - 1:
                sums = [early_mlp(layout, blocks[: nz // 2 * ny], [first, second])]
            block = after(block, blocks[-1], *others, *sums)
        blocks += [block, lax.ppermute(block, "dev", along_y)]
    pair_first = after(pair_first, block)
    pair_second = lax.ppermute(pair_first, "sub", to_sibling)

    means = middle_mlp(layout, blocks, [first, second, pair_first], sums, length)
    parts = last_mlp(layout, means, blocks, pair_second, length, n_grp, n_sub)
    parts = lax.all_to_all(parts, ("grp", "sub"), split_axis=0, concat_axis=0, tiled=True)

    out_width = embed_proj.shape[1]
    sent_rows = 16
    sent_cols = 2 * LANES
    small = pltpu.CompilerParams(vmem_limit_bytes=SMALL_VMEM)
    tile_embed, mixed, sent = pl.pallas_call(
        functools.partial(embed_kernel, n_sub),
        in_specs=[smem] + [vmem] * 4,
        out_specs=(vmem, vmem, vmem),
        out_shape=(
            jax.ShapeDtypeStruct((slot_count, hidden_cols), jnp.bfloat16),
            jax.ShapeDtypeStruct((QROWS, out_width), jnp.float32),
            jax.ShapeDtypeStruct((n_dev, sent_rows, sent_cols), jnp.bfloat16),
        ),
        compiler_params=small,
    )(counts, parts, slide_gain, embed_proj, proj_far)
    sent = lax.all_to_all(sent, "dev", split_axis=0, concat_axis=0, tiled=True)
    query = pl.pallas_call(
        functools.partial(query_kernel, heads),
        in_specs=[vmem] * 4,
        out_specs=vmem,
        out_shape=jax.ShapeDtypeStruct((heads * QROWS, out_width), jnp.bfloat16),
        compiler_params=small,
    )(mixed, slide_gain, slide_wq, wq_far)
    slide_out = pl.pallas_call(
        functools.partial(slide_kernel, heads),
        in_specs=[smem] + [vmem] * 10,
        out_specs=vmem,
        out_shape=jax.ShapeDtypeStruct((slot_count, out_cols), jnp.bfloat16),
        scratch_shapes=[pltpu.VMEM((n_dev * slot_count, out_width), jnp.float32)],
        compiler_params=small,
    )(counts, sent, mixed, query, many, slide_wk, wk_far, slide_wv, wv_far, slide_wo, wo_far)
    return (tile_embed, slide_out)


def solution(mesh):
    placed = (
        P(("grp", "dev"), None, None),
        P("grp"),
        P("grp"),
        P(),
        P(),
        P("dev", "sub"),
        P("dev", "sub"),
        P("sub", None),
        P(),
        P(None, "sub"),
        P(None, "sub"),
        P(None, "sub"),
        P("sub", None),
    )
    return jax.shard_map(
        on_device,
        mesh=mesh,
        in_specs=placed,
        out_specs=(P(("grp", "dev"), "sub"), P(("grp", "dev"), "sub")),
        check_vma=False,
    )
```

```python
import functools
import math

import jax
import jax.numpy as jnp
from jax import lax
from jax.experimental import pallas as pl
from jax.experimental.pallas import tpu as pltpu
from jax.sharding import PartitionSpec as P

HD = 64
EPSILON = 1e-06
FLOOR = -1e30
QROWS = 8
NORM_ROWS = 16
LANES = 128
UNIT_ROWS = 16
ROW_TILE = 16
MLP_VMEM = 32 * 1024 * 1024
NORM_VMEM = 8 * 1024 * 1024
SMALL_VMEM = 4 * 1024 * 1024


def normed(rows_in, gains):
    average = jnp.mean(rows_in, axis=-1, keepdims=True)
    centred = rows_in - average
    variance = jnp.mean(centred * centred, axis=-1, keepdims=True)
    return (centred * lax.rsqrt(variance + EPSILON) * gains).astype(jnp.bfloat16)


def in_hbm(*arrays):
    return [pltpu.with_memory_space_constraint(x, pltpu.HBM) for x in arrays]


def in_vmem(*arrays):
    return [pltpu.with_memory_space_constraint(x, pltpu.VMEM) for x in arrays]


def norm_kernel(flip, tiles_ref, gain_ref, out_ref, rows, hidden, in_sems, out_sems):
    core = lax.axis_index("sub")
    half, length = rows.shape[:2]
    first = (1 - core if flip else core) * half
    copies = [
        pltpu.make_async_copy(tiles_ref.at[first + i], rows.at[i], in_sems.at[i])
        for i in range(half)
    ]
    stores = [
        pltpu.make_async_copy(
            hidden.at[i], out_ref.at[pl.ds(i * length, length)], out_sems.at[i]
        )
        for i in range(half)
    ]
    for copy in copies:
        copy.start()
    gain = gain_ref[...].reshape(1, -1)
    for i in range(half):
        copies[i].wait()

        def some_rows(j, carry):
            here = pl.ds(pl.multiple_of(j * NORM_ROWS, NORM_ROWS), NORM_ROWS)
            hidden[i, here, :] = normed(rows[i, here, :].astype(jnp.float32), gain)
            return carry

        lax.fori_loop(0, length // NORM_ROWS, some_rows, 0, unroll=4)
        stores[i].start()
    for store in stores:
        store.wait()


def norm_tiles(tiles, gain, flip):
    slot_count, length, width = tiles.shape
    half = slot_count // 2
    hbm = pl.BlockSpec(memory_space=pltpu.HBM)
    return pl.pallas_call(
        functools.partial(norm_kernel, flip),
        in_specs=[hbm, pl.BlockSpec(memory_space=pltpu.VMEM)],
        out_specs=hbm,
        out_shape=pltpu.HBM((half * length, width), jnp.bfloat16),
        scratch_shapes=[
            pltpu.VMEM((half, length, width), jnp.bfloat16),
            pltpu.VMEM((half, length, width), jnp.bfloat16),
            pltpu.SemaphoreType.DMA((half,)),
            pltpu.SemaphoreType.DMA((half,)),
        ],
        compiler_params=pltpu.CompilerParams(vmem_limit_bytes=NORM_VMEM),
        cost_estimate=pl.CostEstimate(flops=0, bytes_accessed=0, transcendentals=0),
    )(*in_hbm(tiles), gain)


def after(value, *others):
    return lax.optimization_barrier((value, *others))[0]


class Layout:
    def __init__(self, n_dev, ny, depth):
        self.ny, self.nz, self.depth = ny, n_dev // ny, depth
        self.pair = ny * depth
        self.relative = self.pair % LANES == 0
        self.early_steps = self.nz - 1
        self.early = self.early_steps * self.pair if self.relative else 0
        cut = max(ROW_TILE, depth // 2 // ROW_TILE * ROW_TILE)
        self.parts = [slice(0, cut), slice(cut, depth)]
        self.width = n_dev * depth

    def place(self):
        me = lax.axis_index("dev")
        my_z = me // self.ny
        return my_z, me - my_z * self.ny

    def source(self, step):
        my_z, _ = self.place()
        z = my_z - step
        return jnp.where(z < 0, z + self.nz, z)

    def block_copies(self, blocks, weights, sems):
        _, my_y = self.place()
        copies = []
        n_parts = len(self.parts)
        for k, block in enumerate(blocks):
            step, flip, part = k // n_parts // self.ny, k // n_parts % self.ny, k % n_parts
            y = 1 - my_y if flip else my_y
            at = step if self.relative else self.source(step)
            here = self.parts[part]
            start = pl.multiple_of(at * self.pair + y * self.depth + here.start, ROW_TILE)
            place = weights.at[pl.ds(start, here.stop - here.start)]
            copies.append(pltpu.make_async_copy(block, place, sems.at[k]))
        return copies

    def row_copies(self, tiles_ref, rows, sems, steps):
        if not self.relative:
            return [pltpu.make_async_copy(tiles_ref, rows, sems.at[0])]
        copies = []
        for step in steps:
            start = pl.multiple_of(self.source(step) * self.pair, LANES)
            copies.append(
                pltpu.make_async_copy(
                    tiles_ref.at[:, pl.ds(start, self.pair)],
                    rows.at[:, step * self.pair : (step + 1) * self.pair],
                    sems.at[step],
                )
            )
        return copies


def gated_means(both, out_ref, at, length):
    cols = both.shape[1] // 2
    for tile in range(both.shape[0] // length):
        total = jnp.zeros((8, cols), jnp.float32)
        for first in range(tile * length, (tile + 1) * length, UNIT_ROWS):
            gate = both[first : first + UNIT_ROWS, :cols]
            up_part = both[first : first + UNIT_ROWS, cols:]
            silu = gate * (0.5 * jnp.tanh(0.5 * gate) + 0.5)
            gated = (silu * up_part).astype(jnp.bfloat16).astype(jnp.float32)
            total = total + jnp.sum(gated.reshape(UNIT_ROWS // 8, 8, cols), axis=0)
        out_ref[at + tile : at + tile + 1, :] = jnp.sum(total, axis=0, keepdims=True) * (
            1.0 / length
        )


def product(rows, weights, first, last):
    return jnp.dot(
        rows[:, first:last], weights[first:last, :], preferred_element_type=jnp.float32
    )


def early_kernel(layout, *refs):
    steps = range(layout.early_steps)
    n_blocks = len(steps) * layout.ny * len(layout.parts)
    blocks, tile_refs = refs[:n_blocks], refs[n_blocks : n_blocks + 2]
    out_ref, weights, rows, sums, weight_sems, row_sems, out_sems = refs[n_blocks + 2 :]
    loads = layout.block_copies(blocks, weights, weight_sems)
    row_loads = [
        layout.row_copies(ref, rows.at[i], row_sems.at[i], steps)
        for i, ref in enumerate(tile_refs)
    ]
    for copy in row_loads[0] + loads + row_loads[1]:
        copy.start()
    for copy in loads:
        copy.wait()
    stores = []
    for i in range(2):
        for copy in row_loads[i]:
            copy.wait()
        sums[i] = product(rows.at[i], weights, 0, layout.early)
        stores.append(pltpu.make_async_copy(sums.at[i], out_ref.at[i], out_sems.at[i]))
        stores[i].start()
    for store in stores:
        store.wait()


def early_mlp(layout, blocks, tiles):
    n_rows = tiles[0].shape[0]
    cols = blocks[0].shape[1]
    hbm = pl.BlockSpec(memory_space=pltpu.HBM)
    return pl.pallas_call(
        functools.partial(early_kernel, layout),
        in_specs=[hbm] * (len(blocks) + 2),
        out_specs=hbm,
        out_shape=pltpu.HBM((2, n_rows, cols), jnp.float32),
        scratch_shapes=[
            pltpu.VMEM((layout.early, cols), jnp.bfloat16),
            pltpu.VMEM((2, n_rows, layout.early), jnp.bfloat16),
            pltpu.VMEM((2, n_rows, cols), jnp.float32),
            pltpu.SemaphoreType.DMA((len(blocks),)),
            pltpu.SemaphoreType.DMA((2, layout.nz)),
            pltpu.SemaphoreType.DMA((2,)),
        ],
        compiler_params=pltpu.CompilerParams(vmem_limit_bytes=MLP_VMEM),
        cost_estimate=pl.CostEstimate(
            flops=4 * n_rows * layout.early * cols,
            bytes_accessed=2 * layout.early * (cols + 2 * n_rows) + 8 * n_rows * cols,
            transcendentals=0,
        ),
    )(*in_hbm(*blocks, *tiles))


def middle_kernel(layout, length, *refs):
    n_blocks = layout.nz * layout.ny * len(layout.parts)
    n_sums = 1 if layout.relative else 0
    blocks, tile_refs = refs[:n_blocks], refs[n_blocks : n_blocks + 3]
    sum_refs = refs[n_blocks + 3 : n_blocks + 3 + n_sums]
    out_ref, weights, rows, sums, even, odd, weight_sems, row_sems, sum_sems = refs[
        n_blocks + 3 + n_sums :
    ]
    early = layout.early
    loads = layout.block_copies(blocks, weights, weight_sems)
    late_blocks = early // layout.depth * len(layout.parts)
    steps = [range(early // layout.pair, layout.nz)] * 2 + [range(layout.nz)]
    row_loads = [
        layout.row_copies(ref, rows.at[i], row_sems.at[i], steps[i])
        for i, ref in enumerate(tile_refs)
    ]
    sum_loads = [
        pltpu.make_async_copy(ref.at[i], sums.at[i], sum_sems.at[i])
        for ref in sum_refs
        for i in range(2)
    ]
    for copy in loads[late_blocks:] + row_loads[0] + sum_loads[:1]:
        copy.start()
    for copy in row_loads[1] + sum_loads[1:] + row_loads[2] + loads[:late_blocks]:
        copy.start()
    waits = [
        loads[late_blocks:] + row_loads[0] + sum_loads[:1],
        row_loads[1] + sum_loads[1:],
        row_loads[2] + loads[:late_blocks],
    ]
    pending = None
    for i in range(3):
        for copy in waits[i]:
            copy.wait()
        both = (even, odd)[i % 2]
        if i < 2 and n_sums:
            both[...] = product(rows.at[i], weights, early, layout.width) + sums[i]
        else:
            both[...] = product(rows.at[i], weights, 0, layout.width)
        if pending is not None:
            gated_means(*pending, length)
        pending = (both, out_ref, 2 * i)
    gated_means(*pending, length)


def middle_mlp(layout, blocks, tiles, sums, length):
    n_rows, width = tiles[0].shape
    cols = blocks[0].shape[1]
    hbm = pl.BlockSpec(memory_space=pltpu.HBM)
    return pl.pallas_call(
        functools.partial(middle_kernel, layout, length),
        in_specs=[hbm] * (len(blocks) + 3 + len(sums)),
        out_specs=pl.BlockSpec(memory_space=pltpu.VMEM),
        out_shape=jax.ShapeDtypeStruct((3 * n_rows // length, cols // 2), jnp.float32),
        scratch_shapes=[
            pltpu.VMEM((width, cols), jnp.bfloat16),
            pltpu.VMEM((3, n_rows, width), jnp.bfloat16),
            pltpu.VMEM((2, n_rows, cols), jnp.float32),
            pltpu.VMEM((n_rows, cols), jnp.float32),
            pltpu.VMEM((n_rows, cols), jnp.float32),
            pltpu.SemaphoreType.DMA((len(blocks),)),
            pltpu.SemaphoreType.DMA((3, layout.nz)),
            pltpu.SemaphoreType.DMA((2,)),
        ],
        compiler_params=pltpu.CompilerParams(vmem_limit_bytes=MLP_VMEM),
        cost_estimate=pl.CostEstimate(
            flops=4 * n_rows * width * cols,
            bytes_accessed=2 * (3 * n_rows * width + width * cols) + 8 * n_rows * cols,
            transcendentals=0,
        ),
    )(*in_hbm(*blocks[:-2]), *blocks[-2:], *in_hbm(*tiles, *sums))


def last_kernel(layout, length, n_grp, n_sub, means_ref, *refs):
    n_blocks = layout.nz * layout.ny * len(layout.parts)
    blocks, tiles_ref = refs[:n_blocks], refs[n_blocks]
    out_ref, weights, rows, both, means, weight_sems, row_sems = refs[n_blocks + 1 :]
    loads = layout.block_copies(blocks, weights, weight_sems)
    row_loads = layout.row_copies(tiles_ref, rows, row_sems, range(layout.nz))
    for copy in row_loads + loads:
        copy.start()
    for copy in row_loads + loads:
        copy.wait()
    n_rows = rows.shape[0]
    for i in range(0, n_rows, length):
        here = slice(i, i + length)
        both[here, :] = product(rows.at[here], weights, 0, layout.width)
    gated_means(both, means, 0, length)

    group, core = lax.axis_index("grp"), lax.axis_index("sub")
    low = core == 0
    half = n_rows // length

    def packed(mine, others):
        rows = jnp.concatenate(
            [jnp.where(low, mine, others), jnp.where(low, others, mine)], axis=0
        )
        return jnp.concatenate(
            [rows[:, k : k + LANES] for k in range(0, rows.shape[1], LANES)], axis=0
        )

    before = means_ref[...]
    own = packed(before[:half], before[half : 2 * half])
    pair = packed(before[2 * half :], means[...])
    for g in range(n_grp):
        chosen = jnp.where(group == g, own, pair).astype(jnp.bfloat16)
        for s in range(n_sub):
            out_ref[g * n_sub + s] = chosen


def last_mlp(layout, means, blocks, tiles, length, n_grp, n_sub):
    n_rows, width = tiles.shape
    cols = blocks[0].shape[1]
    half = n_rows // length
    hbm = pl.BlockSpec(memory_space=pltpu.HBM)
    vmem = pl.BlockSpec(memory_space=pltpu.VMEM)
    return pl.pallas_call(
        functools.partial(last_kernel, layout, length, n_grp, n_sub),
        in_specs=[vmem] + [hbm] * (len(blocks) + 1),
        out_specs=vmem,
        out_shape=jax.ShapeDtypeStruct(
            (n_grp * n_sub, half * cols // LANES, LANES), jnp.bfloat16
        ),
        scratch_shapes=[
            pltpu.VMEM((width, cols), jnp.bfloat16),
            pltpu.VMEM((n_rows, width), jnp.bfloat16),
            pltpu.VMEM((n_rows, cols), jnp.float32),
            pltpu.VMEM((half, cols // 2), jnp.float32),
            pltpu.SemaphoreType.DMA((len(blocks),)),
            pltpu.SemaphoreType.DMA((layout.nz,)),
        ],
        compiler_params=pltpu.CompilerParams(vmem_limit_bytes=MLP_VMEM),
        cost_estimate=pl.CostEstimate(
            flops=2 * n_rows * width * cols,
            bytes_accessed=2 * (n_rows * width + width * cols),
            transcendentals=0,
        ),
    )(means, *in_hbm(*blocks[:-2]), *blocks[-2:], tiles)


def small_mod(value, rate):
    return jnp.where(
        rate == 1,
        0,
        jnp.where(rate == 2, value & 1, jnp.where(rate == 3, lax.rem(value, 3), value & 3)),
    )


def multiplicity_kernel(n_dev, slot_count, heads, counts_ref, slide_ref, rates_ref, out_ref):
    me, core = lax.axis_index("dev"), lax.axis_index("sub")
    shape = out_ref.shape
    row = lax.broadcasted_iota(jnp.int32, shape, 0)
    col = lax.broadcasted_iota(jnp.int32, shape, 1)
    head = row // QROWS + core * (heads // 2)
    head = jnp.where(head >= heads, head - heads, head)
    query = row % QROWS
    device, slot = col // slot_count, col % slot_count
    rate = jnp.full(shape, 1, jnp.int32)
    for h in range(heads):
        rate = jnp.where(head == h, rates_ref[h], rate)
    my_slide = slide_ref[me]
    first = me
    count = jnp.zeros(shape, jnp.int32)
    slide = jnp.zeros(shape, jnp.int32)
    for k in reversed(range(n_dev)):
        first = jnp.where(slide_ref[k] == my_slide, k, first)
        count = jnp.where(device == k, counts_ref[k], count)
        slide = jnp.where(device == k, slide_ref[k], slide)
    offset = small_mod(head, rate)
    query_position = (me - first) * slot_count + query
    key_position = (device - first) * slot_count + slot
    valid = slot < count
    near = jnp.where((device == me) & valid, 1.0, 0.0)
    far = jnp.where(
        (slide == my_slide)
        & valid
        & (small_mod(query_position, rate) == offset)
        & (small_mod(key_position, rate) == offset),
        1.0,
        0.0,
    )
    out_ref[...] = near + far


def embed_kernel(
    n_sub, counts_ref, parts_ref, gain_ref, near_ref, far_ref, embed_ref, mixed_ref, sent_ref
):
    slot_count, half = embed_ref.shape
    n_blocks = half // 2 // LANES
    group, core = lax.axis_index("grp"), lax.axis_index("sub")
    count = counts_ref[lax.axis_index("dev")]
    base = group // 2 * 2
    halves = []
    for s in range(n_sub):
        pieces = []
        for x in range(2):
            part = parts_ref[(base + x) * n_sub + s].astype(jnp.float32)
            pieces += [part[k * slot_count : (k + 1) * slot_count] for k in range(n_blocks)]
        rows = jnp.concatenate(pieces, axis=1)
        slot = lax.broadcasted_iota(jnp.int32, rows.shape, 0)
        halves.append(jnp.where(slot < count, rows, 0.0))
    low = core == 0
    near = jnp.where(low, halves[0], halves[1]).astype(jnp.bfloat16)
    far = jnp.where(low, halves[1], halves[0]).astype(jnp.bfloat16)
    embed_ref[...] = near
    mixed = jnp.dot(near, near_ref[...], preferred_element_type=jnp.float32) + jnp.dot(
        far, far_ref[...], preferred_element_type=jnp.float32
    )
    mixed_ref[...] = jnp.concatenate([mixed, mixed], axis=0)
    hidden = normed(mixed, gain_ref[...].reshape(1, -1)).astype(jnp.float32)
    width = sent_ref.shape[2]
    pieces = [hidden[:, k : k + width] for k in range(0, hidden.shape[1], width)]
    pieces += [jnp.zeros_like(pieces[0])] * (sent_ref.shape[1] // slot_count - len(pieces))
    sent = jnp.concatenate(pieces, axis=0).astype(jnp.bfloat16)
    for k in range(sent_ref.shape[0]):
        sent_ref[k] = sent


def project(rows, near_ref, far_ref):
    return jnp.concatenate(
        [
            jnp.dot(rows, near_ref[...], preferred_element_type=jnp.float32),
            jnp.dot(rows, far_ref[...], preferred_element_type=jnp.float32),
        ],
        axis=1,
    )


def heads_of(shape):
    return (
        lax.broadcasted_iota(jnp.int32, shape, 0) // QROWS
        == lax.broadcasted_iota(jnp.int32, shape, 1) // HD
    )


def query_kernel(heads, mixed_ref, gain_ref, *refs):
    n_in = (len(refs) - 1) // 2
    weights, (out_ref, *kept), (wq, sems) = refs[:n_in], refs[n_in:-2], refs[-2:]
    copies = [
        pltpu.make_async_copy(weight, place, sems.at[k])
        for k, (weight, place) in enumerate(zip(weights, [wq.at[0], wq.at[1], *kept]))
    ]
    for copy in copies:
        copy.start()
    hidden = normed(mixed_ref[...], gain_ref[...].reshape(1, -1))
    for copy in copies[:2]:
        copy.wait()
    query = project(hidden, wq.at[0], wq.at[1])
    spread = jnp.concatenate([query] * heads, axis=0)
    out_ref[...] = jnp.where(heads_of(spread.shape), spread, 0.0).astype(jnp.bfloat16)
    for copy in copies[2:]:
        copy.wait()


def slide_kernel(
    heads,
    counts_ref,
    sent_ref,
    mixed_ref,
    query_ref,
    wk_ref,
    wk_far_ref,
    wv_ref,
    wv_far_ref,
    wo_ref,
    wo_far_ref,
    many_ref,
    out_ref,
    rows,
):
    slot_count, half = out_ref.shape
    core = lax.axis_index("sub")
    count = counts_ref[lax.axis_index("dev")]
    width = sent_ref.shape[2]
    for k in range(sent_ref.shape[0]):
        sent = sent_ref[k].astype(jnp.float32)
        rows[k * slot_count : (k + 1) * slot_count, :] = jnp.concatenate(
            [
                sent[j * slot_count : (j + 1) * slot_count]
                for j in range(rows.shape[1] // width)
            ],
            axis=1,
        )
    hidden = rows[...].astype(jnp.bfloat16)
    keys = project(hidden, wk_ref, wk_far_ref).astype(jnp.bfloat16)
    scores = lax.dot_general(
        query_ref[...], keys, (((1,), (1,)), ((), ())), preferred_element_type=jnp.float32
    ) * (1.0 / math.sqrt(HD))
    values = project(hidden, wv_ref, wv_far_ref).astype(jnp.bfloat16)
    many = many_ref[...]
    masked = jnp.where(many > 0.0, scores, FLOOR)
    weights = many * jnp.exp(masked - jnp.max(masked, axis=1, keepdims=True))
    weights = weights / jnp.sum(weights, axis=1, keepdims=True)
    context = jnp.dot(weights.astype(jnp.bfloat16), values, preferred_element_type=jnp.float32)
    context = jnp.where(heads_of(context.shape), context, 0.0)
    context = context.reshape(heads, QROWS, context.shape[1])
    context = jnp.sum(context, axis=0).astype(jnp.bfloat16)
    columns = pl.ds(pl.multiple_of(core * half, LANES), half)
    attended = jnp.dot(
        context[:, :half], wo_ref[:, columns], preferred_element_type=jnp.float32
    ) + jnp.dot(context[:, half:], wo_far_ref[...], preferred_element_type=jnp.float32)
    total = mixed_ref[:, columns] + attended
    slot = lax.broadcasted_iota(jnp.int32, total.shape, 0)
    total = jnp.where(slot < count, total, 0.0)
    out_ref[...] = total[:slot_count].astype(jnp.bfloat16)


def on_device(
    tiles,
    counts,
    slide_of,
    rates,
    tile_gain,
    gate_weight,
    up_weight,
    embed_proj,
    slide_gain,
    slide_wq,
    slide_wk,
    slide_wv,
    slide_wo,
):
    slot_count, length, width = tiles.shape
    hidden_cols = gate_weight.shape[1]
    n_grp, n_dev, n_sub = (lax.axis_size(a) for a in ("grp", "dev", "sub"))
    ny = 2
    nz = n_dev // ny
    heads = slide_wq.shape[1] * n_sub // HD
    group, core = lax.axis_index("grp"), lax.axis_index("sub")

    to_pair = [(g, g ^ 1) for g in range(n_grp)]
    to_sibling = [(s, s ^ 1) for s in range(n_sub)]
    along_z = [(d, (d + ny) % n_dev) for d in range(n_dev)]
    along_y = [(d, d ^ 1) for d in range(n_dev)]

    half_cols = hidden_cols // 2
    layout = Layout(n_dev, ny, gate_weight.shape[0])
    held = [
        jnp.concatenate(
            [
                lax.dynamic_slice_in_dim(w[part], (group % 2) * half_cols, half_cols, 1)
                for w in (gate_weight, up_weight)
            ],
            axis=1,
        )
        for part in layout.parts
    ]
    first = norm_tiles(tiles, tile_gain, False)
    second = norm_tiles(tiles, tile_gain, True)
    pair_first = lax.ppermute(first, "grp", to_pair)

    proj_far = lax.ppermute(embed_proj, "sub", to_sibling)
    wq_far = lax.ppermute(slide_wq, "sub", to_sibling)
    wk_far = lax.ppermute(slide_wk, "sub", to_sibling)
    wv_far = lax.ppermute(slide_wv, "sub", to_sibling)
    out_cols = slide_wo.shape[1] // n_sub
    wo_far = lax.ppermute(
        lax.dynamic_slice_in_dim(slide_wo, (1 - core) * out_cols, out_cols, 1), "sub", to_sibling
    )
    smem = pl.BlockSpec(memory_space=pltpu.SMEM)
    vmem = pl.BlockSpec(memory_space=pltpu.VMEM)
    many = pl.pallas_call(
        functools.partial(multiplicity_kernel, n_dev, slot_count, heads),
        in_specs=[smem] * 3,
        out_specs=vmem,
        out_shape=jax.ShapeDtypeStruct((heads * QROWS, n_dev * slot_count), jnp.float32),
        compiler_params=pltpu.CompilerParams(vmem_limit_bytes=SMALL_VMEM),
    )(counts, slide_of, rates)

    held[1] = after(held[1], first, proj_far, wq_far, many)
    steps = []
    last = None
    for step in range(nz):
        sent = []
        for part in range(len(held)):
            if step:
                arrived = lax.ppermute(held[part], "dev", along_z)
                others = [steps[-1][len(held) + part]]
                if last is not None:
                    others.append(last)
                held[part] = last = after(arrived, *others)
            sent.append(lax.ppermute(held[part], "dev", along_y))
        steps.append([*held, *sent])
    blocks = [block for step in steps for block in step]
    sums = []
    if layout.relative:
        early_blocks = blocks[: layout.early_steps * len(steps[0])]
        sums = [early_mlp(layout, early_blocks, [after(first, last, wk_far, wv_far, wo_far), second])]
    pair_first = after(pair_first, *steps[-1][-2:], *sums)
    pair_second = lax.ppermute(pair_first, "sub", to_sibling)

    means = middle_mlp(layout, blocks, [first, second, pair_first], sums, length)
    parts = last_mlp(layout, means, blocks, pair_second, length, n_grp, n_sub)
    parts = lax.all_to_all(parts, ("grp", "sub"), split_axis=0, concat_axis=0, tiled=True)

    out_width = embed_proj.shape[1]
    sent_rows = 16
    sent_cols = 2 * LANES
    small = pltpu.CompilerParams(vmem_limit_bytes=SMALL_VMEM)
    tile_embed, mixed, sent = pl.pallas_call(
        functools.partial(embed_kernel, n_sub),
        in_specs=[smem] + [vmem] * 4,
        out_specs=(vmem, vmem, vmem),
        out_shape=(
            jax.ShapeDtypeStruct((slot_count, hidden_cols), jnp.bfloat16),
            pltpu.VMEM((QROWS, out_width), jnp.float32),
            pltpu.VMEM((n_dev, sent_rows, sent_cols), jnp.bfloat16),
        ),
        compiler_params=small,
    )(counts, *in_vmem(parts), slide_gain, embed_proj, proj_far)
    sent = lax.all_to_all(sent, "dev", split_axis=0, concat_axis=0, tiled=True)
    hbm = pl.BlockSpec(memory_space=pltpu.HBM)
    weights = [slide_wk, wk_far, slide_wv, wv_far, slide_wo, wo_far, many]
    query, *weights = pl.pallas_call(
        functools.partial(query_kernel, heads),
        in_specs=[vmem] * 2 + [hbm] * (2 + len(weights)),
        out_specs=[vmem] * (1 + len(weights)),
        out_shape=[
            pltpu.VMEM((heads * QROWS, out_width), jnp.bfloat16),
            *[pltpu.VMEM(x.shape, x.dtype) for x in weights],
        ],
        scratch_shapes=[
            pltpu.VMEM((2, *slide_wq.shape), jnp.bfloat16),
            pltpu.SemaphoreType.DMA((2 + len(weights),)),
        ],
        compiler_params=small,
    )(*in_vmem(mixed), slide_gain, *in_hbm(slide_wq, wq_far, *weights))
    slide_out = pl.pallas_call(
        functools.partial(slide_kernel, heads),
        in_specs=[smem] + [vmem] * 10,
        out_specs=vmem,
        out_shape=jax.ShapeDtypeStruct((slot_count, out_cols), jnp.bfloat16),
        scratch_shapes=[pltpu.VMEM((n_dev * slot_count, out_width), jnp.float32)],
        compiler_params=small,
    )(counts, *in_vmem(sent, mixed, query, *weights))
    return (tile_embed, slide_out)


def solution(mesh):
    placed = (
        P(("grp", "dev"), None, None),
        P("grp"),
        P("grp"),
        P(),
        P(),
        P("dev", "sub"),
        P("dev", "sub"),
        P("sub", None),
        P(),
        P(None, "sub"),
        P(None, "sub"),
        P(None, "sub"),
        P("sub", None),
    )
    return jax.shard_map(
        on_device,
        mesh=mesh,
        in_specs=placed,
        out_specs=(P(("grp", "dev"), "sub"), P(("grp", "dev"), "sub")),
        check_vma=False,
    )
```

```python
import functools
import math

import jax
import jax.numpy as jnp
from jax import lax
from jax.experimental import pallas as pl
from jax.experimental.pallas import tpu as pltpu
from jax.sharding import PartitionSpec as P

HD = 64
EPSILON = 1e-06
FLOOR = -1e30
QROWS = 8
NORM_ROWS = 16
LANES = 128
UNIT_ROWS = 16
ROW_TILE = 16
MLP_VMEM = 32 * 1024 * 1024
NORM_VMEM = 8 * 1024 * 1024
SMALL_VMEM = 4 * 1024 * 1024


def normed(rows_in, gains):
    average = jnp.mean(rows_in, axis=-1, keepdims=True)
    centred = rows_in - average
    variance = jnp.mean(centred * centred, axis=-1, keepdims=True)
    return (centred * lax.rsqrt(variance + EPSILON) * gains).astype(jnp.bfloat16)


def in_hbm(*arrays):
    return [pltpu.with_memory_space_constraint(x, pltpu.HBM) for x in arrays]


def in_vmem(*arrays):
    return [pltpu.with_memory_space_constraint(x, pltpu.VMEM) for x in arrays]


def norm_kernel(tiles_ref, gain_ref, out_ref, rows, hidden, in_sems, out_sems):
    core = lax.axis_index("sub")
    half, length = rows.shape[:2]
    first = core * half
    copies = [
        pltpu.make_async_copy(tiles_ref.at[first + i], rows.at[i], in_sems.at[i])
        for i in range(half)
    ]
    stores = [
        pltpu.make_async_copy(
            hidden.at[i], out_ref.at[pl.ds(i * length, length)], out_sems.at[i]
        )
        for i in range(half)
    ]
    for copy in copies:
        copy.start()
    gain = gain_ref[...].reshape(1, -1)
    for i in range(half):
        copies[i].wait()

        def some_rows(j, carry):
            here = pl.ds(pl.multiple_of(j * NORM_ROWS, NORM_ROWS), NORM_ROWS)
            hidden[i, here, :] = normed(rows[i, here, :].astype(jnp.float32), gain)
            return carry

        lax.fori_loop(0, length // NORM_ROWS, some_rows, 0, unroll=4)
        stores[i].start()
    for store in stores:
        store.wait()


def norm_tiles(tiles, gain):
    slot_count, length, width = tiles.shape
    half = slot_count // 2
    hbm = pl.BlockSpec(memory_space=pltpu.HBM)
    return pl.pallas_call(
        norm_kernel,
        in_specs=[hbm, pl.BlockSpec(memory_space=pltpu.VMEM)],
        out_specs=hbm,
        out_shape=pltpu.HBM((half * length, width), jnp.bfloat16),
        scratch_shapes=[
            pltpu.VMEM((half, length, width), jnp.bfloat16),
            pltpu.VMEM((half, length, width), jnp.bfloat16),
            pltpu.SemaphoreType.DMA((half,)),
            pltpu.SemaphoreType.DMA((half,)),
        ],
        compiler_params=pltpu.CompilerParams(vmem_limit_bytes=NORM_VMEM),
        cost_estimate=pl.CostEstimate(flops=0, bytes_accessed=0, transcendentals=0),
    )(*in_hbm(tiles), gain)


def after(value, *others):
    return lax.optimization_barrier((value, *others))[0]


class Layout:
    def __init__(self, n_dev, ny, depth):
        self.ny, self.nz, self.depth = ny, n_dev // ny, depth
        self.pair = ny * depth
        self.relative = self.pair % LANES == 0
        self.early_steps = self.nz - 1
        self.early = self.early_steps * self.pair if self.relative else 0
        cut = max(ROW_TILE, depth // 2 // ROW_TILE * ROW_TILE)
        self.parts = [slice(0, cut), slice(cut, depth)]
        self.width = n_dev * depth

    def place(self):
        me = lax.axis_index("dev")
        my_z = me // self.ny
        return my_z, me - my_z * self.ny

    def source(self, step):
        my_z, _ = self.place()
        z = my_z - step
        return jnp.where(z < 0, z + self.nz, z)

    def block_copies(self, blocks, weights, sems):
        _, my_y = self.place()
        copies = []
        n_parts = len(self.parts)
        for k, block in enumerate(blocks):
            step, flip, part = k // n_parts // self.ny, k // n_parts % self.ny, k % n_parts
            y = 1 - my_y if flip else my_y
            at = step if self.relative else self.source(step)
            here = self.parts[part]
            start = pl.multiple_of(at * self.pair + y * self.depth + here.start, ROW_TILE)
            place = weights.at[pl.ds(start, here.stop - here.start)]
            copies.append(pltpu.make_async_copy(block, place, sems.at[k]))
        return copies

    def row_copies(self, tiles_ref, rows, sems, steps):
        if not self.relative:
            return [pltpu.make_async_copy(tiles_ref, rows, sems.at[0])]
        copies = []
        for step in steps:
            start = pl.multiple_of(self.source(step) * self.pair, LANES)
            copies.append(
                pltpu.make_async_copy(
                    tiles_ref.at[:, pl.ds(start, self.pair)],
                    rows.at[:, step * self.pair : (step + 1) * self.pair],
                    sems.at[step],
                )
            )
        return copies


def gated_means(both, out_ref, at, length):
    cols = both.shape[1] // 2
    for tile in range(both.shape[0] // length):
        total = jnp.zeros((8, cols), jnp.float32)
        for first in range(tile * length, (tile + 1) * length, UNIT_ROWS):
            gate = both[first : first + UNIT_ROWS, :cols]
            up_part = both[first : first + UNIT_ROWS, cols:]
            silu = gate * (0.5 * jnp.tanh(0.5 * gate) + 0.5)
            gated = (silu * up_part).astype(jnp.bfloat16).astype(jnp.float32)
            total = total + jnp.sum(gated.reshape(UNIT_ROWS // 8, 8, cols), axis=0)
        out_ref[at + tile : at + tile + 1, :] = jnp.sum(total, axis=0, keepdims=True) * (
            1.0 / length
        )


def product(rows, weights, first, last):
    return jnp.dot(
        rows[:, first:last], weights[first:last, :], preferred_element_type=jnp.float32
    )


def early_kernel(layout, *refs):
    steps = range(layout.early_steps)
    n_blocks = len(steps) * layout.ny * len(layout.parts)
    blocks, tile_refs = refs[:n_blocks], refs[n_blocks : n_blocks + 2]
    out_ref, weights, rows, sums, weight_sems, row_sems, out_sems = refs[n_blocks + 2 :]
    loads = layout.block_copies(blocks, weights, weight_sems)
    row_loads = [
        layout.row_copies(ref, rows.at[i], row_sems.at[i], steps)
        for i, ref in enumerate(tile_refs)
    ]
    for copy in row_loads[0] + loads + row_loads[1]:
        copy.start()
    for copy in loads:
        copy.wait()
    stores = []
    for i in range(2):
        for copy in row_loads[i]:
            copy.wait()
        sums[i] = product(rows.at[i], weights, 0, layout.early)
        stores.append(pltpu.make_async_copy(sums.at[i], out_ref.at[i], out_sems.at[i]))
        stores[i].start()
    for store in stores:
        store.wait()


def early_mlp(layout, blocks, tiles):
    n_rows = tiles[0].shape[0]
    cols = blocks[0].shape[1]
    hbm = pl.BlockSpec(memory_space=pltpu.HBM)
    return pl.pallas_call(
        functools.partial(early_kernel, layout),
        in_specs=[hbm] * (len(blocks) + 2),
        out_specs=hbm,
        out_shape=pltpu.HBM((2, n_rows, cols), jnp.float32),
        scratch_shapes=[
            pltpu.VMEM((layout.early, cols), jnp.bfloat16),
            pltpu.VMEM((2, n_rows, layout.early), jnp.bfloat16),
            pltpu.VMEM((2, n_rows, cols), jnp.float32),
            pltpu.SemaphoreType.DMA((len(blocks),)),
            pltpu.SemaphoreType.DMA((2, layout.nz)),
            pltpu.SemaphoreType.DMA((2,)),
        ],
        compiler_params=pltpu.CompilerParams(vmem_limit_bytes=MLP_VMEM),
        cost_estimate=pl.CostEstimate(
            flops=4 * n_rows * layout.early * cols,
            bytes_accessed=2 * layout.early * (cols + 2 * n_rows) + 8 * n_rows * cols,
            transcendentals=0,
        ),
    )(*in_hbm(*blocks, *tiles))


def middle_kernel(layout, length, *refs):
    n_blocks = layout.nz * layout.ny * len(layout.parts)
    n_sums = 1 if layout.relative else 0
    blocks, tile_refs = refs[:n_blocks], refs[n_blocks : n_blocks + 3]
    sum_refs = refs[n_blocks + 3 : n_blocks + 3 + n_sums]
    out_ref, weights, rows, sums, even, odd, weight_sems, row_sems, sum_sems = refs[
        n_blocks + 3 + n_sums :
    ]
    early = layout.early
    loads = layout.block_copies(blocks, weights, weight_sems)
    late_blocks = early // layout.depth * len(layout.parts)
    steps = [range(early // layout.pair, layout.nz)] * 2 + [range(layout.nz)]
    row_loads = [
        layout.row_copies(ref, rows.at[i], row_sems.at[i], steps[i])
        for i, ref in enumerate(tile_refs)
    ]
    sum_loads = [
        pltpu.make_async_copy(ref.at[i], sums.at[i], sum_sems.at[i])
        for ref in sum_refs
        for i in range(2)
    ]
    for copy in loads[late_blocks:] + row_loads[0] + sum_loads[:1]:
        copy.start()
    for copy in row_loads[1] + sum_loads[1:] + row_loads[2] + loads[:late_blocks]:
        copy.start()
    waits = [
        loads[late_blocks:] + row_loads[0] + sum_loads[:1],
        row_loads[1] + sum_loads[1:],
        row_loads[2] + loads[:late_blocks],
    ]
    pending = None
    for i in range(3):
        for copy in waits[i]:
            copy.wait()
        both = (even, odd)[i % 2]
        if i < 2 and n_sums:
            both[...] = product(rows.at[i], weights, early, layout.width) + sums[i]
        else:
            both[...] = product(rows.at[i], weights, 0, layout.width)
        if pending is not None:
            gated_means(*pending, length)
        pending = (both, out_ref, 2 * i)
    gated_means(*pending, length)


def middle_mlp(layout, blocks, tiles, sums, length):
    n_rows, width = tiles[0].shape
    cols = blocks[0].shape[1]
    hbm = pl.BlockSpec(memory_space=pltpu.HBM)
    return pl.pallas_call(
        functools.partial(middle_kernel, layout, length),
        in_specs=[hbm] * (len(blocks) + 3 + len(sums)),
        out_specs=pl.BlockSpec(memory_space=pltpu.VMEM),
        out_shape=jax.ShapeDtypeStruct((3 * n_rows // length, cols // 2), jnp.float32),
        scratch_shapes=[
            pltpu.VMEM((width, cols), jnp.bfloat16),
            pltpu.VMEM((3, n_rows, width), jnp.bfloat16),
            pltpu.VMEM((2, n_rows, cols), jnp.float32),
            pltpu.VMEM((n_rows, cols), jnp.float32),
            pltpu.VMEM((n_rows, cols), jnp.float32),
            pltpu.SemaphoreType.DMA((len(blocks),)),
            pltpu.SemaphoreType.DMA((3, layout.nz)),
            pltpu.SemaphoreType.DMA((2,)),
        ],
        compiler_params=pltpu.CompilerParams(vmem_limit_bytes=MLP_VMEM),
        cost_estimate=pl.CostEstimate(
            flops=4 * n_rows * width * cols,
            bytes_accessed=2 * (3 * n_rows * width + width * cols) + 8 * n_rows * cols,
            transcendentals=0,
        ),
    )(*in_hbm(*blocks[:-2]), *blocks[-2:], *in_hbm(*tiles, *sums))


def last_kernel(layout, length, n_grp, n_sub, means_ref, *refs):
    n_blocks = layout.nz * layout.ny * len(layout.parts)
    blocks, tiles_ref = refs[:n_blocks], refs[n_blocks]
    out_ref, weights, rows, both, means, weight_sems, row_sems = refs[n_blocks + 1 :]
    loads = layout.block_copies(blocks, weights, weight_sems)
    row_loads = layout.row_copies(tiles_ref, rows, row_sems, range(layout.nz))
    for copy in row_loads + loads:
        copy.start()
    for copy in row_loads + loads:
        copy.wait()
    n_rows = rows.shape[0]
    for i in range(0, n_rows, length):
        here = slice(i, i + length)
        both[here, :] = product(rows.at[here], weights, 0, layout.width)
    gated_means(both, means, 0, length)

    group, core = lax.axis_index("grp"), lax.axis_index("sub")
    low = core == 0
    half = n_rows // length

    def packed(mine, others):
        rows = jnp.concatenate(
            [jnp.where(low, mine, others), jnp.where(low, others, mine)], axis=0
        )
        return jnp.concatenate(
            [rows[:, k : k + LANES] for k in range(0, rows.shape[1], LANES)], axis=0
        )

    before = means_ref[...]
    own = packed(before[:half], before[half : 2 * half])
    pair = packed(before[2 * half :], means[...])
    for g in range(n_grp):
        chosen = jnp.where(group == g, own, pair).astype(jnp.bfloat16)
        for s in range(n_sub):
            out_ref[g * n_sub + s] = chosen


def last_mlp(layout, means, blocks, tiles, length, n_grp, n_sub):
    n_rows, width = tiles.shape
    cols = blocks[0].shape[1]
    half = n_rows // length
    hbm = pl.BlockSpec(memory_space=pltpu.HBM)
    vmem = pl.BlockSpec(memory_space=pltpu.VMEM)
    return pl.pallas_call(
        functools.partial(last_kernel, layout, length, n_grp, n_sub),
        in_specs=[vmem] + [hbm] * (len(blocks) + 1),
        out_specs=vmem,
        out_shape=jax.ShapeDtypeStruct(
            (n_grp * n_sub, half * cols // LANES, LANES), jnp.bfloat16
        ),
        scratch_shapes=[
            pltpu.VMEM((width, cols), jnp.bfloat16),
            pltpu.VMEM((n_rows, width), jnp.bfloat16),
            pltpu.VMEM((n_rows, cols), jnp.float32),
            pltpu.VMEM((half, cols // 2), jnp.float32),
            pltpu.SemaphoreType.DMA((len(blocks),)),
            pltpu.SemaphoreType.DMA((layout.nz,)),
        ],
        compiler_params=pltpu.CompilerParams(vmem_limit_bytes=MLP_VMEM),
        cost_estimate=pl.CostEstimate(
            flops=2 * n_rows * width * cols,
            bytes_accessed=2 * (n_rows * width + width * cols),
            transcendentals=0,
        ),
    )(means, *in_hbm(*blocks[:-2]), *blocks[-2:], tiles)


def small_mod(value, rate):
    return jnp.where(
        rate == 1,
        0,
        jnp.where(rate == 2, value & 1, jnp.where(rate == 3, lax.rem(value, 3), value & 3)),
    )


def multiplicity_kernel(n_dev, slot_count, heads, counts_ref, slide_ref, rates_ref, out_ref):
    me, core = lax.axis_index("dev"), lax.axis_index("sub")
    shape = out_ref.shape
    row = lax.broadcasted_iota(jnp.int32, shape, 0)
    col = lax.broadcasted_iota(jnp.int32, shape, 1)
    head = row // QROWS + core * (heads // 2)
    head = jnp.where(head >= heads, head - heads, head)
    query = row % QROWS
    device, slot = col // slot_count, col % slot_count
    rate = jnp.full(shape, 1, jnp.int32)
    for h in range(heads):
        rate = jnp.where(head == h, rates_ref[h], rate)
    my_slide = slide_ref[me]
    first = me
    count = jnp.zeros(shape, jnp.int32)
    slide = jnp.zeros(shape, jnp.int32)
    for k in reversed(range(n_dev)):
        first = jnp.where(slide_ref[k] == my_slide, k, first)
        count = jnp.where(device == k, counts_ref[k], count)
        slide = jnp.where(device == k, slide_ref[k], slide)
    offset = small_mod(head, rate)
    query_position = (me - first) * slot_count + query
    key_position = (device - first) * slot_count + slot
    valid = slot < count
    near = jnp.where((device == me) & valid, 1.0, 0.0)
    far = jnp.where(
        (slide == my_slide)
        & valid
        & (small_mod(query_position, rate) == offset)
        & (small_mod(key_position, rate) == offset),
        1.0,
        0.0,
    )
    out_ref[...] = near + far


def embed_kernel(
    n_sub, counts_ref, parts_ref, gain_ref, near_ref, far_ref, embed_ref, mixed_ref, sent_ref
):
    slot_count, half = embed_ref.shape
    n_blocks = half // 2 // LANES
    group, core = lax.axis_index("grp"), lax.axis_index("sub")
    count = counts_ref[lax.axis_index("dev")]
    base = group // 2 * 2
    halves = []
    for s in range(n_sub):
        pieces = []
        for x in range(2):
            part = parts_ref[(base + x) * n_sub + s].astype(jnp.float32)
            pieces += [part[k * slot_count : (k + 1) * slot_count] for k in range(n_blocks)]
        rows = jnp.concatenate(pieces, axis=1)
        slot = lax.broadcasted_iota(jnp.int32, rows.shape, 0)
        halves.append(jnp.where(slot < count, rows, 0.0))
    low = core == 0
    near = jnp.where(low, halves[0], halves[1]).astype(jnp.bfloat16)
    far = jnp.where(low, halves[1], halves[0]).astype(jnp.bfloat16)
    embed_ref[...] = near
    mixed = jnp.dot(near, near_ref[...], preferred_element_type=jnp.float32) + jnp.dot(
        far, far_ref[...], preferred_element_type=jnp.float32
    )
    mixed_ref[...] = jnp.concatenate([mixed, mixed], axis=0)
    hidden = normed(mixed, gain_ref[...].reshape(1, -1)).astype(jnp.float32)
    width = sent_ref.shape[2]
    pieces = [hidden[:, k : k + width] for k in range(0, hidden.shape[1], width)]
    pieces += [jnp.zeros_like(pieces[0])] * (sent_ref.shape[1] // slot_count - len(pieces))
    sent = jnp.concatenate(pieces, axis=0).astype(jnp.bfloat16)
    for k in range(sent_ref.shape[0]):
        sent_ref[k] = sent


def project(rows, near_ref, far_ref):
    return jnp.concatenate(
        [
            jnp.dot(rows, near_ref[...], preferred_element_type=jnp.float32),
            jnp.dot(rows, far_ref[...], preferred_element_type=jnp.float32),
        ],
        axis=1,
    )


def heads_of(shape):
    return (
        lax.broadcasted_iota(jnp.int32, shape, 0) // QROWS
        == lax.broadcasted_iota(jnp.int32, shape, 1) // HD
    )


def query_kernel(heads, mixed_ref, gain_ref, *refs):
    n_in = (len(refs) - 1) // 2
    weights, (out_ref, *kept), (wq, sems) = refs[:n_in], refs[n_in:-2], refs[-2:]
    copies = [
        pltpu.make_async_copy(weight, place, sems.at[k])
        for k, (weight, place) in enumerate(zip(weights, [wq.at[0], wq.at[1], *kept]))
    ]
    for copy in copies:
        copy.start()
    hidden = normed(mixed_ref[...], gain_ref[...].reshape(1, -1))
    for copy in copies[:2]:
        copy.wait()
    query = project(hidden, wq.at[0], wq.at[1])
    spread = jnp.concatenate([query] * heads, axis=0)
    out_ref[...] = jnp.where(heads_of(spread.shape), spread, 0.0).astype(jnp.bfloat16)
    for copy in copies[2:]:
        copy.wait()


def slide_kernel(
    heads,
    counts_ref,
    sent_ref,
    mixed_ref,
    query_ref,
    wk_ref,
    wk_far_ref,
    wv_ref,
    wv_far_ref,
    wo_ref,
    wo_far_ref,
    many_ref,
    out_ref,
    rows,
):
    slot_count, half = out_ref.shape
    core = lax.axis_index("sub")
    count = counts_ref[lax.axis_index("dev")]
    width = sent_ref.shape[2]
    for k in range(sent_ref.shape[0]):
        sent = sent_ref[k].astype(jnp.float32)
        rows[k * slot_count : (k + 1) * slot_count, :] = jnp.concatenate(
            [
                sent[j * slot_count : (j + 1) * slot_count]
                for j in range(rows.shape[1] // width)
            ],
            axis=1,
        )
    hidden = rows[...].astype(jnp.bfloat16)
    keys = project(hidden, wk_ref, wk_far_ref).astype(jnp.bfloat16)
    scores = lax.dot_general(
        query_ref[...], keys, (((1,), (1,)), ((), ())), preferred_element_type=jnp.float32
    ) * (1.0 / math.sqrt(HD))
    values = project(hidden, wv_ref, wv_far_ref).astype(jnp.bfloat16)
    many = many_ref[...]
    masked = jnp.where(many > 0.0, scores, FLOOR)
    weights = many * jnp.exp(masked - jnp.max(masked, axis=1, keepdims=True))
    weights = weights / jnp.sum(weights, axis=1, keepdims=True)
    context = jnp.dot(weights.astype(jnp.bfloat16), values, preferred_element_type=jnp.float32)
    context = jnp.where(heads_of(context.shape), context, 0.0)
    context = context.reshape(heads, QROWS, context.shape[1])
    context = jnp.sum(context, axis=0).astype(jnp.bfloat16)
    columns = pl.ds(pl.multiple_of(core * half, LANES), half)
    attended = jnp.dot(
        context[:, :half], wo_ref[:, columns], preferred_element_type=jnp.float32
    ) + jnp.dot(context[:, half:], wo_far_ref[...], preferred_element_type=jnp.float32)
    total = mixed_ref[:, columns] + attended
    slot = lax.broadcasted_iota(jnp.int32, total.shape, 0)
    total = jnp.where(slot < count, total, 0.0)
    out_ref[...] = total[:slot_count].astype(jnp.bfloat16)


def on_device(
    tiles,
    counts,
    slide_of,
    rates,
    tile_gain,
    gate_weight,
    up_weight,
    embed_proj,
    slide_gain,
    slide_wq,
    slide_wk,
    slide_wv,
    slide_wo,
):
    slot_count, length, width = tiles.shape
    hidden_cols = gate_weight.shape[1]
    n_grp, n_dev, n_sub = (lax.axis_size(a) for a in ("grp", "dev", "sub"))
    ny = 2
    nz = n_dev // ny
    heads = slide_wq.shape[1] * n_sub // HD
    group, core = lax.axis_index("grp"), lax.axis_index("sub")

    to_pair = [(g, g ^ 1) for g in range(n_grp)]
    to_sibling = [(s, s ^ 1) for s in range(n_sub)]
    along_z = [(d, (d + ny) % n_dev) for d in range(n_dev)]
    along_y = [(d, d ^ 1) for d in range(n_dev)]

    half_cols = hidden_cols // 2
    layout = Layout(n_dev, ny, gate_weight.shape[0])
    held = [
        jnp.concatenate(
            [
                lax.dynamic_slice_in_dim(w[part], (group % 2) * half_cols, half_cols, 1)
                for w in (gate_weight, up_weight)
            ],
            axis=1,
        )
        for part in layout.parts
    ]
    first = norm_tiles(tiles, tile_gain)
    second = lax.ppermute(first, "sub", to_sibling)
    pair_first = lax.ppermute(first, "grp", to_pair)

    proj_far = lax.ppermute(embed_proj, "sub", to_sibling)
    wq_far = lax.ppermute(slide_wq, "sub", to_sibling)
    wk_far = lax.ppermute(slide_wk, "sub", to_sibling)
    wv_far = lax.ppermute(slide_wv, "sub", to_sibling)
    out_cols = slide_wo.shape[1] // n_sub
    wo_far = lax.ppermute(
        lax.dynamic_slice_in_dim(slide_wo, (1 - core) * out_cols, out_cols, 1), "sub", to_sibling
    )
    smem = pl.BlockSpec(memory_space=pltpu.SMEM)
    vmem = pl.BlockSpec(memory_space=pltpu.VMEM)
    many = pl.pallas_call(
        functools.partial(multiplicity_kernel, n_dev, slot_count, heads),
        in_specs=[smem] * 3,
        out_specs=vmem,
        out_shape=jax.ShapeDtypeStruct((heads * QROWS, n_dev * slot_count), jnp.float32),
        compiler_params=pltpu.CompilerParams(vmem_limit_bytes=SMALL_VMEM),
    )(counts, slide_of, rates)

    held[1] = after(held[1], first, proj_far, wq_far)
    steps = []
    last = None
    for step in range(nz):
        sent = []
        for part in range(len(held)):
            if step:
                arrived = lax.ppermute(held[part], "dev", along_z)
                others = [steps[-1][len(held) + part]]
                if (step, part) == (1, 1):
                    others += [second, many]
                if last is not None:
                    others.append(last)
                held[part] = last = after(arrived, *others)
            sent.append(lax.ppermute(held[part], "dev", along_y))
        steps.append([*held, *sent])
    blocks = [block for step in steps for block in step]
    sums = []
    if layout.relative:
        early_blocks = blocks[: layout.early_steps * len(steps[0])]
        sums = [early_mlp(layout, early_blocks, [after(first, last), second])]
    pair_first = after(pair_first, *steps[-1][-2:], *sums)
    pair_second = lax.ppermute(pair_first, "sub", to_sibling)

    means = middle_mlp(layout, blocks, [first, second, pair_first], sums, length)
    means = after(means, wk_far, wv_far, wo_far)
    parts = last_mlp(layout, means, blocks, pair_second, length, n_grp, n_sub)
    parts = lax.all_to_all(parts, ("grp", "sub"), split_axis=0, concat_axis=0, tiled=True)

    out_width = embed_proj.shape[1]
    sent_rows = 16
    sent_cols = 2 * LANES
    small = pltpu.CompilerParams(vmem_limit_bytes=SMALL_VMEM)
    tile_embed, mixed, sent = pl.pallas_call(
        functools.partial(embed_kernel, n_sub),
        in_specs=[smem] + [vmem] * 4,
        out_specs=(vmem, vmem, vmem),
        out_shape=(
            jax.ShapeDtypeStruct((slot_count, hidden_cols), jnp.bfloat16),
            pltpu.VMEM((QROWS, out_width), jnp.float32),
            pltpu.VMEM((n_dev, sent_rows, sent_cols), jnp.bfloat16),
        ),
        compiler_params=small,
    )(counts, *in_vmem(parts), slide_gain, embed_proj, proj_far)
    sent = lax.all_to_all(sent, "dev", split_axis=0, concat_axis=0, tiled=True)
    hbm = pl.BlockSpec(memory_space=pltpu.HBM)
    weights = [slide_wk, wk_far, slide_wv, wv_far, slide_wo, wo_far, many]
    query, *weights = pl.pallas_call(
        functools.partial(query_kernel, heads),
        in_specs=[vmem] * 2 + [hbm] * (2 + len(weights)),
        out_specs=[vmem] * (1 + len(weights)),
        out_shape=[
            pltpu.VMEM((heads * QROWS, out_width), jnp.bfloat16),
            *[pltpu.VMEM(x.shape, x.dtype) for x in weights],
        ],
        scratch_shapes=[
            pltpu.VMEM((2, *slide_wq.shape), jnp.bfloat16),
            pltpu.SemaphoreType.DMA((2 + len(weights),)),
        ],
        compiler_params=small,
    )(*in_vmem(mixed), slide_gain, *in_hbm(slide_wq, wq_far, *weights))
    slide_out = pl.pallas_call(
        functools.partial(slide_kernel, heads),
        in_specs=[smem] + [vmem] * 10,
        out_specs=vmem,
        out_shape=jax.ShapeDtypeStruct((slot_count, out_cols), jnp.bfloat16),
        scratch_shapes=[pltpu.VMEM((n_dev * slot_count, out_width), jnp.float32)],
        compiler_params=small,
    )(counts, *in_vmem(sent, mixed, query, *weights))
    return (tile_embed, slide_out)


def solution(mesh):
    placed = (
        P(("grp", "dev"), None, None),
        P("grp"),
        P("grp"),
        P(),
        P(),
        P("dev", "sub"),
        P("dev", "sub"),
        P("sub", None),
        P(),
        P(None, "sub"),
        P(None, "sub"),
        P(None, "sub"),
        P("sub", None),
    )
    return jax.shard_map(
        on_device,
        mesh=mesh,
        in_specs=placed,
        out_specs=(P(("grp", "dev"), "sub"), P(("grp", "dev"), "sub")),
        check_vma=False,
    )
```

```python
import functools
import math

import jax
import jax.numpy as jnp
from jax import lax
from jax.experimental import pallas as pl
from jax.experimental.pallas import tpu as pltpu
from jax.sharding import PartitionSpec as P

HD = 64
EPSILON = 1e-06
FLOOR = -1e30
QROWS = 8
NORM_ROWS = 16
NORM_PIECE = 128
LANES = 128
UNIT_ROWS = 16
ROW_TILE = 16
MXU = 256
MLP_VMEM = 24 * 1024 * 1024
NORM_VMEM = 8 * 1024 * 1024
SMALL_VMEM = 4 * 1024 * 1024


def normed(rows_in, gains):
    average = jnp.mean(rows_in, axis=-1, keepdims=True)
    centred = rows_in - average
    variance = jnp.mean(centred * centred, axis=-1, keepdims=True)
    return (centred * lax.rsqrt(variance + EPSILON) * gains).astype(jnp.bfloat16)


def in_hbm(*arrays):
    return [pltpu.with_memory_space_constraint(x, pltpu.HBM) for x in arrays]


def in_vmem(*arrays):
    return [pltpu.with_memory_space_constraint(x, pltpu.VMEM) for x in arrays]


def start_kernel(parts, tiles_ref, gain_ref, gate_ref, up_ref, *refs):
    out_ref, *block_refs = refs[: 1 + len(parts)]
    rows, hidden, gain, in_sems, out_sems, block_sems, gain_sem = refs[1 + len(parts) :]
    core = lax.axis_index("sub")
    half, length = tiles_ref.shape[0] // 2, tiles_ref.shape[1]
    half_cols = gate_ref.shape[1] // 2
    n_pieces = rows.shape[0] // NORM_PIECE
    gain_copy = pltpu.make_async_copy(gain_ref, gain, gain_sem)
    gain_copy.start()
    copies, stores = [], []
    for i in range(n_pieces):
        here = pl.ds(i * NORM_PIECE, NORM_PIECE)
        tile, first = divmod(i * NORM_PIECE, length)
        source = tiles_ref.at[core * half + tile, pl.ds(first, NORM_PIECE)]
        copies.append(pltpu.make_async_copy(source, rows.at[here], in_sems.at[i]))
        stores.append(pltpu.make_async_copy(hidden.at[here], out_ref.at[here], out_sems.at[i]))
        copies[-1].start()
    packs = []
    columns = pl.ds(pl.multiple_of(lax.rem(lax.axis_index("grp"), 2) * half_cols, LANES), half_cols)
    for k, (part, block_ref) in enumerate(zip(parts, block_refs)):
        for i, ref in enumerate((gate_ref, up_ref)):
            packs.append(
                pltpu.make_async_copy(
                    ref.at[part, columns],
                    block_ref.at[:, i * half_cols : (i + 1) * half_cols],
                    block_sems.at[k, i],
                )
            )
            packs[-1].start()
    gain_copy.wait()
    gains = gain[...].reshape(1, -1)
    for i in range(n_pieces):
        copies[i].wait()

        def some_rows(j, carry):
            start = pl.multiple_of(i * NORM_PIECE + j * NORM_ROWS, NORM_ROWS)
            here = pl.ds(start, NORM_ROWS)
            hidden[here, :] = normed(rows[here, :].astype(jnp.float32), gains)
            return carry

        lax.fori_loop(0, NORM_PIECE // NORM_ROWS, some_rows, 0, unroll=True)
        stores[i].start()
    for copy in packs + stores:
        copy.wait()


def start_work(tiles, gain, gate_weight, up_weight, parts):
    slot_count, length, width = tiles.shape
    n_rows = slot_count // 2 * length
    hbm = pl.BlockSpec(memory_space=pltpu.HBM)
    cols = gate_weight.shape[1]
    return pl.pallas_call(
        functools.partial(start_kernel, parts),
        in_specs=[hbm] * 4,
        out_specs=[hbm] * (1 + len(parts)),
        out_shape=[
            pltpu.HBM((n_rows, width), jnp.bfloat16),
            *[pltpu.HBM((part.stop - part.start, cols), jnp.bfloat16) for part in parts],
        ],
        scratch_shapes=[
            pltpu.VMEM((n_rows, width), jnp.bfloat16),
            pltpu.VMEM((n_rows, width), jnp.bfloat16),
            pltpu.VMEM((width,), jnp.float32),
            pltpu.SemaphoreType.DMA((n_rows // NORM_PIECE,)),
            pltpu.SemaphoreType.DMA((n_rows // NORM_PIECE,)),
            pltpu.SemaphoreType.DMA((len(parts), 2)),
            pltpu.SemaphoreType.DMA(()),
        ],
        compiler_params=pltpu.CompilerParams(vmem_limit_bytes=NORM_VMEM),
        cost_estimate=pl.CostEstimate(flops=0, bytes_accessed=0, transcendentals=0),
    )(*in_hbm(tiles, gain, gate_weight, up_weight))


def after(value, *others):
    return lax.optimization_barrier((value, *others))[0]


class Layout:
    def __init__(self, n_dev, ny, depth):
        self.ny, self.nz, self.depth = ny, n_dev // ny, depth
        self.pair = ny * depth
        self.relative = self.pair % LANES == 0
        self.early_steps = self.nz - 1
        self.early = self.early_steps * self.pair // MXU * MXU if self.relative else 0
        cut = max(ROW_TILE, depth // 2 // ROW_TILE * ROW_TILE)
        self.parts = [slice(0, cut), slice(cut, depth)]
        self.width = n_dev * depth

    def place(self):
        me = lax.axis_index("dev")
        my_z = me // self.ny
        return my_z, me - my_z * self.ny

    def source(self, step):
        my_z, _ = self.place()
        z = my_z - step
        return jnp.where(z < 0, z + self.nz, z)

    def block_copies(self, blocks, weights, sems, end=None):
        _, my_y = self.place()
        copies = []
        n_parts = len(self.parts)
        first = 0 if end is None else end - len(blocks) // n_parts // self.ny
        for k, block in enumerate(blocks):
            step, flip, part = first + k // n_parts // self.ny, k // n_parts % self.ny, k % n_parts
            y = 1 - my_y if flip else my_y
            at = step if self.relative else self.source(step)
            here = self.parts[part]
            start = pl.multiple_of(at * self.pair + y * self.depth + here.start, ROW_TILE)
            place = weights.at[pl.ds(start, here.stop - here.start)]
            copies.append(pltpu.make_async_copy(block, place, sems.at[k]))
        return copies

    def row_copies(self, tiles_ref, rows, sems, steps):
        if not self.relative:
            return [pltpu.make_async_copy(tiles_ref, rows, sems.at[0])]
        copies = []
        for step in steps:
            start = pl.multiple_of(self.source(step) * self.pair, LANES)
            copies.append(
                pltpu.make_async_copy(
                    tiles_ref.at[:, pl.ds(start, self.pair)],
                    rows.at[:, step * self.pair : (step + 1) * self.pair],
                    sems.at[step],
                )
            )
        return copies


def gated_means(both, out_ref, at, length):
    cols = both.shape[1] // 2
    for tile in range(both.shape[0] // length):
        total = jnp.zeros((8, cols), jnp.float32)
        for first in range(tile * length, (tile + 1) * length, UNIT_ROWS):
            gate = both[first : first + UNIT_ROWS, :cols]
            up_part = both[first : first + UNIT_ROWS, cols:]
            silu = gate * (0.5 * jnp.tanh(0.5 * gate) + 0.5)
            gated = (silu * up_part).astype(jnp.bfloat16).astype(jnp.float32)
            total = total + jnp.sum(gated.reshape(UNIT_ROWS // 8, 8, cols), axis=0)
        out_ref[at + tile : at + tile + 1, :] = jnp.sum(total, axis=0, keepdims=True) * (
            1.0 / length
        )


def product(rows, weights, first, last):
    return jnp.dot(
        rows[:, first:last], weights[first:last, :], preferred_element_type=jnp.float32
    )


def early_kernel(layout, *refs):
    steps = range(layout.early_steps)
    n_blocks = len(steps) * layout.ny * len(layout.parts)
    blocks, tile_refs = refs[:n_blocks], refs[n_blocks : n_blocks + 2]
    out_ref, weights, rows, weight_sems, row_sems = refs[n_blocks + 2 :]
    loads = layout.block_copies(blocks, weights, weight_sems)
    row_loads = [
        layout.row_copies(ref, rows.at[i], row_sems.at[i], steps)
        for i, ref in enumerate(tile_refs)
    ]
    for copy in row_loads[0] + loads + row_loads[1]:
        copy.start()
    for copy in loads:
        copy.wait()
    for i in range(2):
        for copy in row_loads[i]:
            copy.wait()
        out_ref[i] = product(rows.at[i], weights, 0, layout.early)


def early_mlp(layout, blocks, tiles):
    n_rows = tiles[0].shape[0]
    cols = blocks[0].shape[1]
    hbm = pl.BlockSpec(memory_space=pltpu.HBM)
    vmem = pl.BlockSpec(memory_space=pltpu.VMEM)
    return pl.pallas_call(
        functools.partial(early_kernel, layout),
        in_specs=[hbm] * (len(blocks) + 2),
        out_specs=(vmem, vmem),
        out_shape=(
            pltpu.VMEM((2, n_rows, cols), jnp.float32),
            pltpu.VMEM((layout.width, cols), jnp.bfloat16),
        ),
        scratch_shapes=[
            pltpu.VMEM((2, n_rows, layout.early_steps * layout.pair), jnp.bfloat16),
            pltpu.SemaphoreType.DMA((len(blocks),)),
            pltpu.SemaphoreType.DMA((2, layout.nz)),
        ],
        compiler_params=pltpu.CompilerParams(vmem_limit_bytes=MLP_VMEM),
        cost_estimate=pl.CostEstimate(
            flops=4 * n_rows * layout.early * cols,
            bytes_accessed=2 * layout.early * (cols + 2 * n_rows) + 8 * n_rows * cols,
            transcendentals=0,
        ),
    )(*in_hbm(*blocks, *tiles))


def middle_kernel(layout, length, n_blocks, *refs):
    blocks, tile_refs = refs[:n_blocks], refs[n_blocks : n_blocks + 3]
    early_refs = refs[n_blocks + 3 : -7]
    out_ref, weights, rows, even, odd, weight_sems, row_sems = refs[-7:]
    early = layout.early
    loads = layout.block_copies(blocks, weights, weight_sems, layout.nz)
    steps = [range(early // layout.pair, layout.nz)] * 2 + [range(layout.nz)]
    row_loads = [
        layout.row_copies(ref, rows.at[i], row_sems.at[i], steps[i])
        for i, ref in enumerate(tile_refs)
    ]
    waits = [row_loads[0] + loads, row_loads[1], row_loads[2]]
    for copies in waits:
        for copy in copies:
            copy.start()
    pending = None
    for i in range(3):
        for copy in waits[i]:
            copy.wait()
        both = (even, odd)[i % 2]
        if i < 2 and early:
            both[...] = product(rows.at[i], weights, early, layout.width) + early_refs[0][i]
        else:
            both[...] = product(rows.at[i], weights, 0, layout.width)
        if pending is not None:
            gated_means(*pending, length)
        pending = (both, out_ref, 2 * i)
    gated_means(*pending, length)


def middle_mlp(layout, blocks, tiles, early, length):
    n_rows, width = tiles[0].shape
    cols = blocks[0].shape[1]
    hbm = pl.BlockSpec(memory_space=pltpu.HBM)
    vmem = pl.BlockSpec(memory_space=pltpu.VMEM)
    return pl.pallas_call(
        functools.partial(middle_kernel, layout, length, len(blocks)),
        in_specs=[hbm] * (len(blocks) + 3) + [vmem] * len(early),
        out_specs=(vmem, vmem),
        out_shape=(
            pltpu.VMEM((3 * n_rows // length, cols // 2), jnp.float32),
            pltpu.VMEM((width, cols), jnp.bfloat16),
        ),
        input_output_aliases={len(blocks) + 4: 1} if early else {},
        scratch_shapes=[
            pltpu.VMEM((3, n_rows, width), jnp.bfloat16),
            pltpu.VMEM((n_rows, cols), jnp.float32),
            pltpu.VMEM((n_rows, cols), jnp.float32),
            pltpu.SemaphoreType.DMA((len(blocks),)),
            pltpu.SemaphoreType.DMA((3, layout.nz)),
        ],
        compiler_params=pltpu.CompilerParams(vmem_limit_bytes=MLP_VMEM),
        cost_estimate=pl.CostEstimate(
            flops=4 * n_rows * width * cols,
            bytes_accessed=2 * (3 * n_rows * width + width * cols),
            transcendentals=0,
        ),
    )(*blocks, *in_hbm(*tiles), *in_vmem(*early))


def last_kernel(
    layout, length, n_grp, n_sub, means_ref, weights, tiles_ref, out_ref, rows, both, means, row_sems
):
    row_loads = layout.row_copies(tiles_ref, rows, row_sems, range(layout.nz))
    for copy in row_loads:
        copy.start()
    for copy in row_loads:
        copy.wait()
    n_rows = rows.shape[0]
    half = n_rows // length
    for i in range(half):
        here = slice(i * length, (i + 1) * length)
        both[i][...] = product(rows.at[here], weights, 0, layout.width)
        if i:
            gated_means(both[i - 1], means, i - 1, length)
    gated_means(both[half - 1], means, half - 1, length)

    group, core = lax.axis_index("grp"), lax.axis_index("sub")
    low = core == 0

    def packed(mine, others):
        rows = jnp.concatenate(
            [jnp.where(low, mine, others), jnp.where(low, others, mine)], axis=0
        )
        return jnp.concatenate(
            [rows[:, k : k + LANES] for k in range(0, rows.shape[1], LANES)], axis=0
        )

    before = means_ref[...]
    own = packed(before[:half], before[half : 2 * half])
    pair = packed(before[2 * half :], means[...])
    for g in range(n_grp):
        chosen = jnp.where(group == g, own, pair).astype(jnp.bfloat16)
        for s in range(n_sub):
            out_ref[g * n_sub + s] = chosen


def last_mlp(layout, means, weights, tiles, length, n_grp, n_sub):
    n_rows, width = tiles.shape
    cols = weights.shape[1]
    half = n_rows // length
    any_spec = pl.BlockSpec(memory_space=pl.ANY)
    vmem = pl.BlockSpec(memory_space=pltpu.VMEM)
    return pl.pallas_call(
        functools.partial(last_kernel, layout, length, n_grp, n_sub),
        in_specs=[vmem, vmem, any_spec],
        out_specs=vmem,
        out_shape=jax.ShapeDtypeStruct(
            (n_grp * n_sub, half * cols // LANES, LANES), jnp.bfloat16
        ),
        scratch_shapes=[
            pltpu.VMEM((n_rows, width), jnp.bfloat16),
            [pltpu.VMEM((length, cols), jnp.float32) for _ in range(half)],
            pltpu.VMEM((half, cols // 2), jnp.float32),
            pltpu.SemaphoreType.DMA((layout.nz,)),
        ],
        compiler_params=pltpu.CompilerParams(vmem_limit_bytes=MLP_VMEM),
        cost_estimate=pl.CostEstimate(
            flops=2 * n_rows * width * cols,
            bytes_accessed=2 * (n_rows * width + width * cols),
            transcendentals=0,
        ),
    )(*in_vmem(means, weights), tiles)


def small_mod(value, rate):
    return jnp.where(
        rate == 1,
        0,
        jnp.where(rate == 2, value & 1, jnp.where(rate == 3, lax.rem(value, 3), value & 3)),
    )


def multiplicity_kernel(n_dev, slot_count, heads, counts_ref, slide_ref, rates_ref, out_ref):
    me, core = lax.axis_index("dev"), lax.axis_index("sub")
    shape = out_ref.shape
    row = lax.broadcasted_iota(jnp.int32, shape, 0)
    col = lax.broadcasted_iota(jnp.int32, shape, 1)
    head = row // QROWS + core * (heads // 2)
    head = jnp.where(head >= heads, head - heads, head)
    query = row % QROWS
    device, slot = col // slot_count, col % slot_count
    rate = jnp.full(shape, 1, jnp.int32)
    for h in range(heads):
        rate = jnp.where(head == h, rates_ref[h], rate)
    my_slide = slide_ref[me]
    first = me
    count = jnp.zeros(shape, jnp.int32)
    slide = jnp.zeros(shape, jnp.int32)
    for k in reversed(range(n_dev)):
        first = jnp.where(slide_ref[k] == my_slide, k, first)
        count = jnp.where(device == k, counts_ref[k], count)
        slide = jnp.where(device == k, slide_ref[k], slide)
    offset = small_mod(head, rate)
    query_position = (me - first) * slot_count + query
    key_position = (device - first) * slot_count + slot
    valid = slot < count
    near = jnp.where((device == me) & valid, 1.0, 0.0)
    far = jnp.where(
        (slide == my_slide)
        & valid
        & (small_mod(query_position, rate) == offset)
        & (small_mod(key_position, rate) == offset),
        1.0,
        0.0,
    )
    out_ref[...] = near + far


def embed_kernel(
    n_sub, counts_ref, parts_ref, gain_ref, near_ref, far_ref, embed_ref, mixed_ref, sent_ref
):
    slot_count, half = embed_ref.shape
    n_blocks = half // 2 // LANES
    group, core = lax.axis_index("grp"), lax.axis_index("sub")
    count = counts_ref[lax.axis_index("dev")]
    base = group // 2 * 2
    halves = []
    for s in range(n_sub):
        pieces = []
        for x in range(2):
            part = parts_ref[(base + x) * n_sub + s].astype(jnp.float32)
            pieces += [part[k * slot_count : (k + 1) * slot_count] for k in range(n_blocks)]
        rows = jnp.concatenate(pieces, axis=1)
        slot = lax.broadcasted_iota(jnp.int32, rows.shape, 0)
        halves.append(jnp.where(slot < count, rows, 0.0))
    low = core == 0
    near = jnp.where(low, halves[0], halves[1]).astype(jnp.bfloat16)
    far = jnp.where(low, halves[1], halves[0]).astype(jnp.bfloat16)
    embed_ref[...] = near
    mixed = jnp.dot(near, near_ref[...], preferred_element_type=jnp.float32) + jnp.dot(
        far, far_ref[...], preferred_element_type=jnp.float32
    )
    mixed_ref[...] = jnp.concatenate([mixed, mixed], axis=0)
    hidden = normed(mixed, gain_ref[...].reshape(1, -1)).astype(jnp.float32)
    width = sent_ref.shape[2]
    pieces = [hidden[:, k : k + width] for k in range(0, hidden.shape[1], width)]
    pieces += [jnp.zeros_like(pieces[0])] * (sent_ref.shape[1] // slot_count - len(pieces))
    sent = jnp.concatenate(pieces, axis=0).astype(jnp.bfloat16)
    for k in range(sent_ref.shape[0]):
        sent_ref[k] = sent


def project(rows, near_ref, far_ref):
    return jnp.concatenate(
        [
            jnp.dot(rows, near_ref[...], preferred_element_type=jnp.float32),
            jnp.dot(rows, far_ref[...], preferred_element_type=jnp.float32),
        ],
        axis=1,
    )


def heads_of(shape):
    return (
        lax.broadcasted_iota(jnp.int32, shape, 0) // QROWS
        == lax.broadcasted_iota(jnp.int32, shape, 1) // HD
    )


def query_kernel(heads, mixed_ref, gain_ref, *refs):
    n_in = (len(refs) - 1) // 2
    weights, (out_ref, *kept), (wq, sems) = refs[:n_in], refs[n_in:-2], refs[-2:]
    copies = [
        pltpu.make_async_copy(weight, place, sems.at[k])
        for k, (weight, place) in enumerate(zip(weights, [wq.at[0], wq.at[1], *kept]))
    ]
    for copy in copies:
        copy.start()
    hidden = normed(mixed_ref[...], gain_ref[...].reshape(1, -1))
    for copy in copies[:2]:
        copy.wait()
    query = project(hidden, wq.at[0], wq.at[1])
    spread = jnp.concatenate([query] * heads, axis=0)
    out_ref[...] = jnp.where(heads_of(spread.shape), spread, 0.0).astype(jnp.bfloat16)
    for copy in copies[2:]:
        copy.wait()


def slide_kernel(
    heads,
    counts_ref,
    sent_ref,
    mixed_ref,
    query_ref,
    wk_ref,
    wk_far_ref,
    wv_ref,
    wv_far_ref,
    wo_ref,
    wo_far_ref,
    many_ref,
    out_ref,
    rows,
):
    slot_count, half = out_ref.shape
    core = lax.axis_index("sub")
    count = counts_ref[lax.axis_index("dev")]
    width = sent_ref.shape[2]
    for k in range(sent_ref.shape[0]):
        sent = sent_ref[k].astype(jnp.float32)
        rows[k * slot_count : (k + 1) * slot_count, :] = jnp.concatenate(
            [
                sent[j * slot_count : (j + 1) * slot_count]
                for j in range(rows.shape[1] // width)
            ],
            axis=1,
        )
    hidden = rows[...].astype(jnp.bfloat16)
    keys = project(hidden, wk_ref, wk_far_ref).astype(jnp.bfloat16)
    scores = lax.dot_general(
        query_ref[...], keys, (((1,), (1,)), ((), ())), preferred_element_type=jnp.float32
    ) * (1.0 / math.sqrt(HD))
    values = project(hidden, wv_ref, wv_far_ref).astype(jnp.bfloat16)
    many = many_ref[...]
    masked = jnp.where(many > 0.0, scores, FLOOR)
    weights = many * jnp.exp(masked - jnp.max(masked, axis=1, keepdims=True))
    weights = weights / jnp.sum(weights, axis=1, keepdims=True)
    context = jnp.dot(weights.astype(jnp.bfloat16), values, preferred_element_type=jnp.float32)
    context = jnp.where(heads_of(context.shape), context, 0.0)
    context = context.reshape(heads, QROWS, context.shape[1])
    context = jnp.sum(context, axis=0).astype(jnp.bfloat16)
    columns = pl.ds(pl.multiple_of(core * half, LANES), half)
    attended = jnp.dot(
        context[:, :half], wo_ref[:, columns], preferred_element_type=jnp.float32
    ) + jnp.dot(context[:, half:], wo_far_ref[...], preferred_element_type=jnp.float32)
    total = mixed_ref[:, columns] + attended
    slot = lax.broadcasted_iota(jnp.int32, total.shape, 0)
    total = jnp.where(slot < count, total, 0.0)
    out_ref[...] = total[:slot_count].astype(jnp.bfloat16)


def on_device(
    tiles,
    counts,
    slide_of,
    rates,
    tile_gain,
    gate_weight,
    up_weight,
    embed_proj,
    slide_gain,
    slide_wq,
    slide_wk,
    slide_wv,
    slide_wo,
):
    slot_count, length, width = tiles.shape
    hidden_cols = gate_weight.shape[1]
    n_grp, n_dev, n_sub = (lax.axis_size(a) for a in ("grp", "dev", "sub"))
    ny = 2
    nz = n_dev // ny
    heads = slide_wq.shape[1] * n_sub // HD
    core = lax.axis_index("sub")

    to_pair = [(g, g ^ 1) for g in range(n_grp)]
    to_sibling = [(s, s ^ 1) for s in range(n_sub)]
    along_z = [(d, (d + ny) % n_dev) for d in range(n_dev)]
    along_y = [(d, d ^ 1) for d in range(n_dev)]

    layout = Layout(n_dev, ny, gate_weight.shape[0])
    first, *held = start_work(tiles, tile_gain, gate_weight, up_weight, layout.parts)
    second = lax.ppermute(first, "sub", to_sibling)
    pair_first = lax.ppermute(first, "grp", to_pair)

    proj_far = lax.ppermute(embed_proj, "sub", to_sibling)
    wq_far = lax.ppermute(slide_wq, "sub", to_sibling)
    wk_far = lax.ppermute(slide_wk, "sub", to_sibling)
    wv_far = lax.ppermute(slide_wv, "sub", to_sibling)
    out_cols = slide_wo.shape[1] // n_sub
    wo_part = lax.dynamic_slice_in_dim(slide_wo, (1 - core) * out_cols, out_cols, 1)
    wo_far = lax.ppermute(wo_part, "sub", to_sibling)
    smem = pl.BlockSpec(memory_space=pltpu.SMEM)
    vmem = pl.BlockSpec(memory_space=pltpu.VMEM)
    many = pl.pallas_call(
        functools.partial(multiplicity_kernel, n_dev, slot_count, heads),
        in_specs=[smem] * 3,
        out_specs=vmem,
        out_shape=jax.ShapeDtypeStruct((heads * QROWS, n_dev * slot_count), jnp.float32),
        compiler_params=pltpu.CompilerParams(vmem_limit_bytes=SMALL_VMEM),
    )(counts, slide_of, rates)

    held[1] = after(held[1], proj_far, wq_far)
    steps = []
    last = None
    for step in range(nz):
        sent = []
        for part in range(len(held)):
            if step:
                arrived = lax.ppermute(held[part], "dev", along_z)
                others = [steps[-1][len(held) + part]]
                if (step, part) == (1, 1):
                    others += [second]
                if (step, part) == (nz - 1, 0):
                    others += [many, wo_part]
                if last is not None:
                    others.append(last)
                held[part] = last = after(arrived, *others)
            sent.append(lax.ppermute(held[part], "dev", along_y))
        steps.append([*held, *sent])
    blocks = [block for step in steps for block in step]
    early = []
    if layout.relative:
        n_early = layout.early_steps * len(steps[0])
        early = early_mlp(layout, blocks[:n_early], [after(first, last), second])
        blocks = blocks[n_early:]
    pair_first = after(pair_first, *steps[-1][-2:], *early)
    pair_second = lax.ppermute(pair_first, "sub", to_sibling)
    means, weights = middle_mlp(layout, blocks, [first, second, pair_first], early, length)
    parts = last_mlp(layout, means, weights, pair_second, length, n_grp, n_sub)
    parts = lax.all_to_all(parts, ("grp", "sub"), split_axis=0, concat_axis=0, tiled=True)

    out_width = embed_proj.shape[1]
    sent_rows = 16
    sent_cols = 2 * LANES
    small = pltpu.CompilerParams(vmem_limit_bytes=SMALL_VMEM)
    tile_embed, mixed, sent = pl.pallas_call(
        functools.partial(embed_kernel, n_sub),
        in_specs=[smem] + [vmem] * 4,
        out_specs=(vmem, vmem, vmem),
        out_shape=(
            jax.ShapeDtypeStruct((slot_count, hidden_cols), jnp.bfloat16),
            pltpu.VMEM((QROWS, out_width), jnp.float32),
            pltpu.VMEM((n_dev, sent_rows, sent_cols), jnp.bfloat16),
        ),
        compiler_params=small,
    )(counts, *in_vmem(parts), slide_gain, embed_proj, proj_far)
    sent = lax.all_to_all(sent, "dev", split_axis=0, concat_axis=0, tiled=True)
    hbm = pl.BlockSpec(memory_space=pltpu.HBM)
    weights = [slide_wk, wk_far, slide_wv, wv_far, slide_wo, wo_far, many]
    query, *weights = pl.pallas_call(
        functools.partial(query_kernel, heads),
        in_specs=[vmem] * 2 + [hbm] * (2 + len(weights)),
        out_specs=[vmem] * (1 + len(weights)),
        out_shape=[
            pltpu.VMEM((heads * QROWS, out_width), jnp.bfloat16),
            *[pltpu.VMEM(x.shape, x.dtype) for x in weights],
        ],
        scratch_shapes=[
            pltpu.VMEM((2, *slide_wq.shape), jnp.bfloat16),
            pltpu.SemaphoreType.DMA((2 + len(weights),)),
        ],
        compiler_params=small,
    )(*in_vmem(mixed), slide_gain, *in_hbm(slide_wq, wq_far, *weights))
    slide_out = pl.pallas_call(
        functools.partial(slide_kernel, heads),
        in_specs=[smem] + [vmem] * 10,
        out_specs=vmem,
        out_shape=jax.ShapeDtypeStruct((slot_count, out_cols), jnp.bfloat16),
        scratch_shapes=[pltpu.VMEM((n_dev * slot_count, out_width), jnp.float32)],
        compiler_params=small,
    )(counts, *in_vmem(sent, mixed, query, *weights))
    return (tile_embed, slide_out)


def solution(mesh):
    placed = (
        P(("grp", "dev"), None, None),
        P("grp"),
        P("grp"),
        P(),
        P(),
        P("dev", "sub"),
        P("dev", "sub"),
        P("sub", None),
        P(),
        P(None, "sub"),
        P(None, "sub"),
        P(None, "sub"),
        P("sub", None),
    )
    return jax.shard_map(
        on_device,
        mesh=mesh,
        in_specs=placed,
        out_specs=(P(("grp", "dev"), "sub"), P(("grp", "dev"), "sub")),
        check_vma=False,
    )
```

```python
import functools
import math

import jax
import jax.numpy as jnp
from jax import lax
from jax.experimental import pallas as pl
from jax.experimental.pallas import tpu as pltpu
from jax.sharding import PartitionSpec as P

HD = 64
EPSILON = 1e-06
FLOOR = -1e30
QROWS = 8
NORM_ROWS = 16
LANES = 128
UNIT_ROWS = 16
ROW_TILE = 16
MXU = 256
MLP_VMEM = 24 * 1024 * 1024
NORM_VMEM = 8 * 1024 * 1024
SMALL_VMEM = 4 * 1024 * 1024


def normed(rows_in, gains):
    average = jnp.mean(rows_in, axis=-1, keepdims=True)
    centred = rows_in - average
    variance = jnp.mean(centred * centred, axis=-1, keepdims=True)
    return (centred * lax.rsqrt(variance + EPSILON) * gains).astype(jnp.bfloat16)


def in_hbm(*arrays):
    return [pltpu.with_memory_space_constraint(x, pltpu.HBM) for x in arrays]


def in_vmem(*arrays):
    return [pltpu.with_memory_space_constraint(x, pltpu.VMEM) for x in arrays]


def start_kernel(parts, *refs):
    tiles_ref, gain_ref, gate_ref, up_ref, *slide_refs = refs[:8]
    out_ref, pack_ref, *block_refs = refs[8 : 10 + len(parts)]
    rows, hidden, gain, in_sems, out_sems, block_sems, slide_sems, gain_sem = refs[10 + len(parts) :]
    core = lax.axis_index("sub")
    half, length = rows.shape[:2]
    half_cols = gate_ref.shape[1] // 2
    gain_copy = pltpu.make_async_copy(gain_ref, gain, gain_sem)
    copies = [
        pltpu.make_async_copy(tiles_ref.at[core * half + i], rows.at[i], in_sems.at[i])
        for i in range(half)
    ]
    stores = [
        pltpu.make_async_copy(
            hidden.at[i], out_ref.at[pl.ds(i * length, length)], out_sems.at[i]
        )
        for i in range(half)
    ]
    packs = []
    columns = pl.ds(pl.multiple_of(lax.rem(lax.axis_index("grp"), 2) * half_cols, LANES), half_cols)
    for k, (part, block_ref) in enumerate(zip(parts, block_refs)):
        for i, ref in enumerate((gate_ref, up_ref)):
            place = block_ref.at[:, i * half_cols : (i + 1) * half_cols]
            packs.append(
                pltpu.make_async_copy(ref.at[part, columns], place, block_sems.at[k, i])
            )
    cols = pack_ref.shape[1]
    others = pl.ds(pl.multiple_of((1 - core) * cols, LANES), cols)
    at = 0
    for k, ref in enumerate(slide_refs):
        place = pack_ref.at[at : at + ref.shape[0]]
        source = ref if ref.shape[1] == cols else ref.at[:, others]
        packs.append(pltpu.make_async_copy(source, place, slide_sems.at[k]))
        at += ref.shape[0]
    for copy in [gain_copy] + copies + packs:
        copy.start()
    gain_copy.wait()
    gains = gain[...].reshape(1, -1)
    for i in range(half):
        copies[i].wait()

        def some_rows(j, carry):
            here = pl.ds(pl.multiple_of(j * NORM_ROWS, NORM_ROWS), NORM_ROWS)
            hidden[i, here, :] = normed(rows[i, here, :].astype(jnp.float32), gains)
            return carry

        lax.fori_loop(0, length // NORM_ROWS, some_rows, 0, unroll=4)
        stores[i].start()
    for copy in packs + stores:
        copy.wait()


def start_work(tiles, gain, gate_weight, up_weight, slide_weights, parts):
    slot_count, length, width = tiles.shape
    half = slot_count // 2
    hbm = pl.BlockSpec(memory_space=pltpu.HBM)
    vmem = pl.BlockSpec(memory_space=pltpu.VMEM)
    cols = gate_weight.shape[1]
    pack = (sum(w.shape[0] for w in slide_weights), slide_weights[0].shape[1])
    return pl.pallas_call(
        functools.partial(start_kernel, parts),
        in_specs=[hbm] * (4 + len(slide_weights)),
        out_specs=[hbm] + [vmem] * (1 + len(parts)),
        out_shape=[
            pltpu.HBM((half * length, width), jnp.bfloat16),
            pltpu.VMEM(pack, jnp.bfloat16),
            *[pltpu.VMEM((part.stop - part.start, cols), jnp.bfloat16) for part in parts],
        ],
        scratch_shapes=[
            pltpu.VMEM((half, length, width), jnp.bfloat16),
            pltpu.VMEM((half, length, width), jnp.bfloat16),
            pltpu.VMEM((width,), jnp.float32),
            pltpu.SemaphoreType.DMA((half,)),
            pltpu.SemaphoreType.DMA((half,)),
            pltpu.SemaphoreType.DMA((len(parts), 2)),
            pltpu.SemaphoreType.DMA((len(slide_weights),)),
            pltpu.SemaphoreType.DMA(()),
        ],
        compiler_params=pltpu.CompilerParams(vmem_limit_bytes=NORM_VMEM),
        cost_estimate=pl.CostEstimate(flops=0, bytes_accessed=0, transcendentals=0),
    )(*in_hbm(tiles, gain, gate_weight, up_weight, *slide_weights))


def after(value, *others):
    return lax.optimization_barrier((value, *others))[0]


class Layout:
    def __init__(self, n_dev, ny, depth):
        self.ny, self.nz, self.depth = ny, n_dev // ny, depth
        self.pair = ny * depth
        self.relative = self.pair % LANES == 0
        self.early_steps = self.nz - 1
        self.early = self.early_steps * self.pair // MXU * MXU if self.relative else 0
        cut = max(ROW_TILE, depth // 2 // ROW_TILE * ROW_TILE)
        self.parts = [slice(0, cut), slice(cut, depth)]
        self.width = n_dev * depth

    def place(self):
        me = lax.axis_index("dev")
        my_z = me // self.ny
        return my_z, me - my_z * self.ny

    def source(self, step):
        my_z, _ = self.place()
        z = my_z - step
        return jnp.where(z < 0, z + self.nz, z)

    def block_copies(self, blocks, weights, sems, end=None):
        _, my_y = self.place()
        copies = []
        n_parts = len(self.parts)
        first = 0 if end is None else end - len(blocks) // n_parts // self.ny
        for k, block in enumerate(blocks):
            step, flip, part = first + k // n_parts // self.ny, k // n_parts % self.ny, k % n_parts
            y = 1 - my_y if flip else my_y
            at = step if self.relative else self.source(step)
            here = self.parts[part]
            start = pl.multiple_of(at * self.pair + y * self.depth + here.start, ROW_TILE)
            place = weights.at[pl.ds(start, here.stop - here.start)]
            copies.append(pltpu.make_async_copy(block, place, sems.at[k]))
        return copies

    def row_copies(self, tiles_ref, rows, sems, steps):
        if not self.relative:
            return [pltpu.make_async_copy(tiles_ref, rows, sems.at[0])]
        copies = []
        for step in steps:
            start = pl.multiple_of(self.source(step) * self.pair, LANES)
            copies.append(
                pltpu.make_async_copy(
                    tiles_ref.at[:, pl.ds(start, self.pair)],
                    rows.at[:, step * self.pair : (step + 1) * self.pair],
                    sems.at[step],
                )
            )
        return copies


def gated_means(both, out_ref, at, length):
    cols = both.shape[1] // 2
    for tile in range(both.shape[0] // length):
        total = jnp.zeros((8, cols), jnp.float32)
        for first in range(tile * length, (tile + 1) * length, UNIT_ROWS):
            gate = both[first : first + UNIT_ROWS, :cols]
            up_part = both[first : first + UNIT_ROWS, cols:]
            silu = gate * (0.5 * jnp.tanh(0.5 * gate) + 0.5)
            gated = (silu * up_part).astype(jnp.bfloat16).astype(jnp.float32)
            total = total + jnp.sum(gated.reshape(UNIT_ROWS // 8, 8, cols), axis=0)
        out_ref[at + tile : at + tile + 1, :] = jnp.sum(total, axis=0, keepdims=True) * (
            1.0 / length
        )


def product(out, rows, weights, first, last, more=None):
    for at in range(0, rows.shape[0], MXU):
        here = slice(at, at + MXU)
        both = jnp.dot(
            rows[here, first:last], weights[first:last, :], preferred_element_type=jnp.float32
        )
        out[here, :] = both if more is None else both + more[here, :]


def early_kernel(layout, *refs):
    steps = range(layout.early_steps)
    n_blocks = len(steps) * layout.ny * len(layout.parts)
    blocks, tile_refs = refs[:n_blocks], refs[n_blocks : n_blocks + 2]
    out_ref, weights, rows, weight_sems, row_sems = refs[n_blocks + 2 :]
    loads = layout.block_copies(blocks, weights, weight_sems)
    row_loads = [
        layout.row_copies(ref, rows.at[i], row_sems.at[i], steps)
        for i, ref in enumerate(tile_refs)
    ]
    for copy in row_loads[0] + loads + row_loads[1]:
        copy.start()
    for copy in loads:
        copy.wait()
    for i in range(2):
        for copy in row_loads[i]:
            copy.wait()
        product(out_ref.at[i], rows.at[i], weights, 0, layout.early)


def early_mlp(layout, blocks, tiles):
    n_rows = tiles[0].shape[0]
    cols = blocks[0].shape[1]
    hbm = pl.BlockSpec(memory_space=pltpu.HBM)
    vmem = pl.BlockSpec(memory_space=pltpu.VMEM)
    return pl.pallas_call(
        functools.partial(early_kernel, layout),
        in_specs=[hbm] * (len(blocks) + 2),
        out_specs=(vmem, vmem),
        out_shape=(
            pltpu.VMEM((2, n_rows, cols), jnp.float32),
            pltpu.VMEM((layout.width, cols), jnp.bfloat16),
        ),
        scratch_shapes=[
            pltpu.VMEM((2, n_rows, layout.early_steps * layout.pair), jnp.bfloat16),
            pltpu.SemaphoreType.DMA((len(blocks),)),
            pltpu.SemaphoreType.DMA((2, layout.nz)),
        ],
        compiler_params=pltpu.CompilerParams(vmem_limit_bytes=MLP_VMEM),
        cost_estimate=pl.CostEstimate(
            flops=4 * n_rows * layout.early * cols,
            bytes_accessed=2 * layout.early * (cols + 2 * n_rows) + 8 * n_rows * cols,
            transcendentals=0,
        ),
    )(*in_hbm(*blocks, *tiles))


def middle_kernel(layout, length, n_blocks, *refs):
    blocks, tile_refs = refs[:n_blocks], refs[n_blocks : n_blocks + 3]
    early_refs = refs[n_blocks + 3 : -7]
    out_ref, weights, rows, even, odd, weight_sems, row_sems = refs[-7:]
    early = layout.early
    loads = layout.block_copies(blocks, weights, weight_sems, layout.nz)
    steps = [range(early // layout.pair, layout.nz)] * 2 + [range(layout.nz)]
    row_loads = [
        layout.row_copies(ref, rows.at[i], row_sems.at[i], steps[i])
        for i, ref in enumerate(tile_refs)
    ]
    waits = [row_loads[0] + loads, row_loads[1], row_loads[2]]
    for copies in waits:
        for copy in copies:
            copy.start()
    pending = None
    for i in range(3):
        for copy in waits[i]:
            copy.wait()
        for j in range(rows.shape[1] // length):
            here = slice(j * length, (j + 1) * length)
            tile = rows.shape[1] // length * i + j
            both = (even, odd)[tile % 2]
            if i < 2 and early:
                more = early_refs[0].at[i, here]
                product(both, rows.at[i, here], weights, early, layout.width, more)
            else:
                product(both, rows.at[i, here], weights, 0, layout.width)
            if pending is not None:
                gated_means(*pending, length)
            pending = (both, out_ref, tile)
    gated_means(*pending, length)


def middle_mlp(layout, blocks, tiles, early, length):
    n_rows, width = tiles[0].shape
    cols = blocks[0].shape[1]
    hbm = pl.BlockSpec(memory_space=pltpu.HBM)
    vmem = pl.BlockSpec(memory_space=pltpu.VMEM)
    return pl.pallas_call(
        functools.partial(middle_kernel, layout, length, len(blocks)),
        in_specs=[hbm] * (len(blocks) + 3) + [vmem] * len(early),
        out_specs=(vmem, vmem),
        out_shape=(
            pltpu.VMEM((3 * n_rows // length, cols // 2), jnp.float32),
            pltpu.VMEM((width, cols), jnp.bfloat16),
        ),
        input_output_aliases={len(blocks) + 4: 1} if early else {},
        scratch_shapes=[
            pltpu.VMEM((3, n_rows, width), jnp.bfloat16),
            pltpu.VMEM((length, cols), jnp.float32),
            pltpu.VMEM((length, cols), jnp.float32),
            pltpu.SemaphoreType.DMA((len(blocks),)),
            pltpu.SemaphoreType.DMA((3, layout.nz)),
        ],
        compiler_params=pltpu.CompilerParams(vmem_limit_bytes=MLP_VMEM),
        cost_estimate=pl.CostEstimate(
            flops=4 * n_rows * width * cols,
            bytes_accessed=2 * (3 * n_rows * width + width * cols),
            transcendentals=0,
        ),
    )(*blocks, *in_hbm(*tiles), *in_vmem(*early))


def last_kernel(
    layout, length, n_grp, n_sub, means_ref, weights, tiles_ref, out_ref, rows, both, means, row_sems
):
    row_loads = layout.row_copies(tiles_ref, rows, row_sems, range(layout.nz))
    for copy in row_loads:
        copy.start()
    for copy in row_loads:
        copy.wait()
    n_rows = rows.shape[0]
    half = n_rows // length
    for i in range(half):
        here = slice(i * length, (i + 1) * length)
        product(both[i], rows.at[here], weights, 0, layout.width)
        if i:
            gated_means(both[i - 1], means, i - 1, length)
    gated_means(both[half - 1], means, half - 1, length)

    group, core = lax.axis_index("grp"), lax.axis_index("sub")
    low = core == 0

    def packed(mine, others):
        rows = jnp.concatenate(
            [jnp.where(low, mine, others), jnp.where(low, others, mine)], axis=0
        )
        return jnp.concatenate(
            [rows[:, k : k + LANES] for k in range(0, rows.shape[1], LANES)], axis=0
        )

    before = means_ref[...]
    own = packed(before[:half], before[half : 2 * half])
    pair = packed(before[2 * half :], means[...])
    for g in range(n_grp):
        chosen = jnp.where(group == g, own, pair).astype(jnp.bfloat16)
        for s in range(n_sub):
            out_ref[g * n_sub + s] = chosen


def last_mlp(layout, means, weights, tiles, length, n_grp, n_sub):
    n_rows, width = tiles.shape
    cols = weights.shape[1]
    half = n_rows // length
    any_spec = pl.BlockSpec(memory_space=pl.ANY)
    vmem = pl.BlockSpec(memory_space=pltpu.VMEM)
    return pl.pallas_call(
        functools.partial(last_kernel, layout, length, n_grp, n_sub),
        in_specs=[vmem, vmem, any_spec],
        out_specs=vmem,
        out_shape=jax.ShapeDtypeStruct(
            (n_grp * n_sub, half * cols // LANES, LANES), jnp.bfloat16
        ),
        scratch_shapes=[
            pltpu.VMEM((n_rows, width), jnp.bfloat16),
            [pltpu.VMEM((length, cols), jnp.float32) for _ in range(half)],
            pltpu.VMEM((half, cols // 2), jnp.float32),
            pltpu.SemaphoreType.DMA((layout.nz,)),
        ],
        compiler_params=pltpu.CompilerParams(vmem_limit_bytes=MLP_VMEM),
        cost_estimate=pl.CostEstimate(
            flops=2 * n_rows * width * cols,
            bytes_accessed=2 * (n_rows * width + width * cols),
            transcendentals=0,
        ),
    )(*in_vmem(means, weights), tiles)


def small_mod(value, rate):
    return jnp.where(
        rate == 1,
        0,
        jnp.where(rate == 2, value & 1, jnp.where(rate == 3, lax.rem(value, 3), value & 3)),
    )


def multiplicity_kernel(n_dev, slot_count, heads, counts_ref, slide_ref, rates_ref, out_ref):
    me, core = lax.axis_index("dev"), lax.axis_index("sub")
    shape = out_ref.shape
    row = lax.broadcasted_iota(jnp.int32, shape, 0)
    col = lax.broadcasted_iota(jnp.int32, shape, 1)
    head = row // QROWS + core * (heads // 2)
    head = jnp.where(head >= heads, head - heads, head)
    query = row % QROWS
    device, slot = col // slot_count, col % slot_count
    rate = jnp.full(shape, 1, jnp.int32)
    for h in range(heads):
        rate = jnp.where(head == h, rates_ref[h], rate)
    my_slide = slide_ref[me]
    first = me
    count = jnp.zeros(shape, jnp.int32)
    slide = jnp.zeros(shape, jnp.int32)
    for k in reversed(range(n_dev)):
        first = jnp.where(slide_ref[k] == my_slide, k, first)
        count = jnp.where(device == k, counts_ref[k], count)
        slide = jnp.where(device == k, slide_ref[k], slide)
    offset = small_mod(head, rate)
    query_position = (me - first) * slot_count + query
    key_position = (device - first) * slot_count + slot
    valid = slot < count
    near = jnp.where((device == me) & valid, 1.0, 0.0)
    far = jnp.where(
        (slide == my_slide)
        & valid
        & (small_mod(query_position, rate) == offset)
        & (small_mod(key_position, rate) == offset),
        1.0,
        0.0,
    )
    out_ref[...] = near + far


def embed_kernel(
    n_sub, counts_ref, parts_ref, gain_ref, near_ref, far_ref, embed_ref, mixed_ref, sent_ref
):
    slot_count, half = embed_ref.shape
    n_blocks = half // 2 // LANES
    group, core = lax.axis_index("grp"), lax.axis_index("sub")
    count = counts_ref[lax.axis_index("dev")]
    base = group // 2 * 2
    halves = []
    for s in range(n_sub):
        pieces = []
        for x in range(2):
            part = parts_ref[(base + x) * n_sub + s].astype(jnp.float32)
            pieces += [part[k * slot_count : (k + 1) * slot_count] for k in range(n_blocks)]
        rows = jnp.concatenate(pieces, axis=1)
        slot = lax.broadcasted_iota(jnp.int32, rows.shape, 0)
        halves.append(jnp.where(slot < count, rows, 0.0))
    low = core == 0
    near = jnp.where(low, halves[0], halves[1]).astype(jnp.bfloat16)
    far = jnp.where(low, halves[1], halves[0]).astype(jnp.bfloat16)
    embed_ref[...] = near
    mixed = jnp.dot(near, near_ref[...], preferred_element_type=jnp.float32) + jnp.dot(
        far, far_ref[...], preferred_element_type=jnp.float32
    )
    mixed_ref[...] = jnp.concatenate([mixed, mixed], axis=0)
    hidden = normed(mixed, gain_ref[...].reshape(1, -1)).astype(jnp.float32)
    width = sent_ref.shape[2]
    pieces = [hidden[:, k : k + width] for k in range(0, hidden.shape[1], width)]
    pieces += [jnp.zeros_like(pieces[0])] * (sent_ref.shape[1] // slot_count - len(pieces))
    sent = jnp.concatenate(pieces, axis=0).astype(jnp.bfloat16)
    for k in range(sent_ref.shape[0]):
        sent_ref[k] = sent


def project(rows, near_ref, far_ref):
    return jnp.concatenate(
        [
            jnp.dot(rows, near_ref[...], preferred_element_type=jnp.float32),
            jnp.dot(rows, far_ref[...], preferred_element_type=jnp.float32),
        ],
        axis=1,
    )


def heads_of(shape):
    return (
        lax.broadcasted_iota(jnp.int32, shape, 0) // QROWS
        == lax.broadcasted_iota(jnp.int32, shape, 1) // HD
    )


def query_kernel(heads, mixed_ref, gain_ref, far_ref, *refs):
    near_refs, (many_ref, out_ref, many, *kept), (wq, sems) = refs[:4], refs[4:-2], refs[-2:]
    places = [wq.at[0], wq.at[1], *kept]
    copies = []
    at = 0
    for k, near in enumerate(near_refs):
        far = far_ref.at[at : at + near.shape[0]]
        at += near.shape[0]
        for i, source in enumerate((near, far)):
            copies.append(pltpu.make_async_copy(source, places[2 * k + i], sems.at[2 * k + i]))
    copies.append(pltpu.make_async_copy(many_ref, many, sems.at[len(copies)]))
    for copy in copies:
        copy.start()
    hidden = normed(mixed_ref[...], gain_ref[...].reshape(1, -1))
    for copy in copies[:2]:
        copy.wait()
    query = project(hidden, wq.at[0], wq.at[1])
    spread = jnp.concatenate([query] * heads, axis=0)
    out_ref[...] = jnp.where(heads_of(spread.shape), spread, 0.0).astype(jnp.bfloat16)
    for copy in copies[2:]:
        copy.wait()


def slide_kernel(
    heads,
    counts_ref,
    sent_ref,
    mixed_ref,
    query_ref,
    wk_ref,
    wk_far_ref,
    wv_ref,
    wv_far_ref,
    wo_ref,
    wo_far_ref,
    many_ref,
    out_ref,
    rows,
):
    slot_count, half = out_ref.shape
    core = lax.axis_index("sub")
    count = counts_ref[lax.axis_index("dev")]
    width = sent_ref.shape[2]
    for k in range(sent_ref.shape[0]):
        sent = sent_ref[k].astype(jnp.float32)
        rows[k * slot_count : (k + 1) * slot_count, :] = jnp.concatenate(
            [
                sent[j * slot_count : (j + 1) * slot_count]
                for j in range(rows.shape[1] // width)
            ],
            axis=1,
        )
    hidden = rows[...].astype(jnp.bfloat16)
    keys = project(hidden, wk_ref, wk_far_ref).astype(jnp.bfloat16)
    scores = lax.dot_general(
        query_ref[...], keys, (((1,), (1,)), ((), ())), preferred_element_type=jnp.float32
    ) * (1.0 / math.sqrt(HD))
    values = project(hidden, wv_ref, wv_far_ref).astype(jnp.bfloat16)
    many = many_ref[...]
    masked = jnp.where(many > 0.0, scores, FLOOR)
    weights = many * jnp.exp(masked - jnp.max(masked, axis=1, keepdims=True))
    weights = weights / jnp.sum(weights, axis=1, keepdims=True)
    context = jnp.dot(weights.astype(jnp.bfloat16), values, preferred_element_type=jnp.float32)
    context = jnp.where(heads_of(context.shape), context, 0.0)
    context = context.reshape(heads, QROWS, context.shape[1])
    context = jnp.sum(context, axis=0).astype(jnp.bfloat16)
    columns = pl.ds(pl.multiple_of(core * half, LANES), half)
    attended = jnp.dot(
        context[:, :half], wo_ref[:, columns], preferred_element_type=jnp.float32
    ) + jnp.dot(context[:, half:], wo_far_ref[...], preferred_element_type=jnp.float32)
    total = mixed_ref[:, columns] + attended
    slot = lax.broadcasted_iota(jnp.int32, total.shape, 0)
    total = jnp.where(slot < count, total, 0.0)
    out_ref[...] = total[:slot_count].astype(jnp.bfloat16)


def on_device(
    tiles,
    counts,
    slide_of,
    rates,
    tile_gain,
    gate_weight,
    up_weight,
    embed_proj,
    slide_gain,
    slide_wq,
    slide_wk,
    slide_wv,
    slide_wo,
):
    slot_count, length, width = tiles.shape
    hidden_cols = gate_weight.shape[1]
    n_grp, n_dev, n_sub = (lax.axis_size(a) for a in ("grp", "dev", "sub"))
    ny = 2
    nz = n_dev // ny
    heads = slide_wq.shape[1] * n_sub // HD
    core = lax.axis_index("sub")

    to_pair = [(g, g ^ 1) for g in range(n_grp)]
    to_sibling = [(s, s ^ 1) for s in range(n_sub)]
    along_z = [(d, (d + ny) % n_dev) for d in range(n_dev)]
    along_y = [(d, d ^ 1) for d in range(n_dev)]

    layout = Layout(n_dev, ny, gate_weight.shape[0])
    slide_weights = [slide_wq, slide_wk, slide_wv, slide_wo]
    first, pack, *held = start_work(
        tiles, tile_gain, gate_weight, up_weight, slide_weights, layout.parts
    )
    second = lax.ppermute(first, "sub", to_sibling)
    pair_first = lax.ppermute(first, "grp", to_pair)
    proj_far = lax.ppermute(embed_proj, "sub", to_sibling)
    pack_far = lax.ppermute(pack, "sub", to_sibling)
    out_cols = slide_wo.shape[1] // n_sub
    smem = pl.BlockSpec(memory_space=pltpu.SMEM)
    vmem = pl.BlockSpec(memory_space=pltpu.VMEM)
    many = pl.pallas_call(
        functools.partial(multiplicity_kernel, n_dev, slot_count, heads),
        in_specs=[smem] * 3,
        out_specs=vmem,
        out_shape=jax.ShapeDtypeStruct((heads * QROWS, n_dev * slot_count), jnp.float32),
        compiler_params=pltpu.CompilerParams(vmem_limit_bytes=SMALL_VMEM),
    )(counts, slide_of, rates)

    held[1] = after(held[1], proj_far, second)
    steps = []
    last = None
    for step in range(nz):
        sent = []
        for part in range(len(held)):
            if step:
                arrived = lax.ppermute(held[part], "dev", along_z)
                others = [steps[-1][len(held) + part]]
                if (step, part) == (nz - 1, 0):
                    others += [many]
                if last is not None:
                    others.append(last)
                held[part] = last = after(arrived, *others)
            sent.append(lax.ppermute(held[part], "dev", along_y))
        steps.append([*held, *sent])
    blocks = [block for step in steps for block in step]
    early = []
    if layout.relative:
        n_early = layout.early_steps * len(steps[0])
        early = early_mlp(layout, blocks[:n_early], [after(first, last), second])
        blocks = blocks[n_early:]
    pair_first = after(pair_first, *steps[-1][-2:], *early)
    pair_second = lax.ppermute(pair_first, "sub", to_sibling)
    means, weights = middle_mlp(layout, blocks, [first, second, pair_first], early, length)
    parts = last_mlp(layout, means, weights, pair_second, length, n_grp, n_sub)
    parts = lax.all_to_all(parts, ("grp", "sub"), split_axis=0, concat_axis=0, tiled=True)

    out_width = embed_proj.shape[1]
    sent_rows = 16
    sent_cols = 2 * LANES
    small = pltpu.CompilerParams(vmem_limit_bytes=SMALL_VMEM)
    tile_embed, mixed, sent = pl.pallas_call(
        functools.partial(embed_kernel, n_sub),
        in_specs=[smem] + [vmem] * 4,
        out_specs=(vmem, vmem, vmem),
        out_shape=(
            jax.ShapeDtypeStruct((slot_count, hidden_cols), jnp.bfloat16),
            pltpu.VMEM((QROWS, out_width), jnp.float32),
            pltpu.VMEM((n_dev, sent_rows, sent_cols), jnp.bfloat16),
        ),
        compiler_params=small,
    )(counts, *in_vmem(parts), slide_gain, embed_proj, proj_far)
    sent = lax.all_to_all(sent, "dev", split_axis=0, concat_axis=0, tiled=True)
    hbm = pl.BlockSpec(memory_space=pltpu.HBM)
    far_shape = (slide_wo.shape[0], out_cols)
    kept = [slide_wk.shape] * 4 + [slide_wo.shape, far_shape]
    query, many, *weights = pl.pallas_call(
        functools.partial(query_kernel, heads),
        in_specs=[vmem] * 2 + [hbm] * 6,
        out_specs=[vmem] * (2 + len(kept)),
        out_shape=[
            pltpu.VMEM((heads * QROWS, out_width), jnp.bfloat16),
            pltpu.VMEM(many.shape, many.dtype),
            *[pltpu.VMEM(shape, jnp.bfloat16) for shape in kept],
        ],
        scratch_shapes=[
            pltpu.VMEM((2, *slide_wq.shape), jnp.bfloat16),
            pltpu.SemaphoreType.DMA((3 + len(kept),)),
        ],
        compiler_params=small,
    )(*in_vmem(mixed), slide_gain, *in_hbm(pack_far, *slide_weights, many))
    slide_out = pl.pallas_call(
        functools.partial(slide_kernel, heads),
        in_specs=[smem] + [vmem] * 10,
        out_specs=vmem,
        out_shape=jax.ShapeDtypeStruct((slot_count, out_cols), jnp.bfloat16),
        scratch_shapes=[pltpu.VMEM((n_dev * slot_count, out_width), jnp.float32)],
        compiler_params=small,
    )(counts, *in_vmem(sent, mixed, query, *weights, many))
    return (tile_embed, slide_out)


def solution(mesh):
    placed = (
        P(("grp", "dev"), None, None),
        P("grp"),
        P("grp"),
        P(),
        P(),
        P("dev", "sub"),
        P("dev", "sub"),
        P("sub", None),
        P(),
        P(None, "sub"),
        P(None, "sub"),
        P(None, "sub"),
        P("sub", None),
    )
    return jax.shard_map(
        on_device,
        mesh=mesh,
        in_specs=placed,
        out_specs=(P(("grp", "dev"), "sub"), P(("grp", "dev"), "sub")),
        check_vma=False,
    )
```

```python
import functools
import math

import jax
import jax.numpy as jnp
from jax import lax
from jax.experimental import pallas as pl
from jax.experimental.pallas import tpu as pltpu
from jax.sharding import PartitionSpec as P

HD = 64
EPSILON = 1e-06
FLOOR = -1e30
QROWS = 8
NORM_ROWS = 16
NORM_PIECE = 128
NORM_UNROLL = 8
LANES = 128
UNIT_ROWS = 16
ROW_TILE = 16
MXU = 256
MLP_VMEM = 24 * 1024 * 1024
NORM_VMEM = 8 * 1024 * 1024
SMALL_VMEM = 4 * 1024 * 1024


def normed(rows_in, gains):
    average = jnp.mean(rows_in, axis=-1, keepdims=True)
    centred = rows_in - average
    variance = jnp.mean(centred * centred, axis=-1, keepdims=True)
    return (centred * lax.rsqrt(variance + EPSILON) * gains).astype(jnp.bfloat16)


def in_hbm(*arrays):
    return [pltpu.with_memory_space_constraint(x, pltpu.HBM) for x in arrays]


def in_vmem(*arrays):
    return [pltpu.with_memory_space_constraint(x, pltpu.VMEM) for x in arrays]


def start_kernel(parts, *refs):
    tiles_ref, gain_ref, gate_ref, up_ref, *slide_refs = refs[:8]
    out_ref, pack_ref, *block_refs = refs[8 : 10 + len(parts)]
    (
        rows,
        hidden,
        gain,
        average,
        scale,
        in_sems,
        out_sems,
        block_sems,
        slide_sems,
        gain_sem,
    ) = refs[10 + len(parts) :]
    core = lax.axis_index("sub")
    pieces, piece = rows.shape[:2]
    half, length = tiles_ref.shape[0] // 2, tiles_ref.shape[1]
    half_cols = gate_ref.shape[1] // 2
    gain_copy = pltpu.make_async_copy(gain_ref, gain, gain_sem)
    copies = [
        pltpu.make_async_copy(
            tiles_ref.at[core * half + i * piece // length, pl.ds(i * piece % length, piece)],
            rows.at[i],
            in_sems.at[i],
        )
        for i in range(pieces)
    ]
    stores = [
        pltpu.make_async_copy(hidden.at[i], out_ref.at[pl.ds(i * piece, piece)], out_sems.at[i])
        for i in range(pieces)
    ]
    packs = []
    columns = pl.ds(pl.multiple_of(lax.rem(lax.axis_index("grp"), 2) * half_cols, LANES), half_cols)
    for k, (part, block_ref) in enumerate(zip(parts, block_refs)):
        for i, ref in enumerate((gate_ref, up_ref)):
            place = block_ref.at[:, i * half_cols : (i + 1) * half_cols]
            packs.append(
                pltpu.make_async_copy(ref.at[part, columns], place, block_sems.at[k, i])
            )
    cols = pack_ref.shape[1]
    others = pl.ds(pl.multiple_of((1 - core) * cols, LANES), cols)
    at = 0
    for k, ref in enumerate(slide_refs):
        place = pack_ref.at[at : at + ref.shape[0]]
        source = ref if ref.shape[1] == cols else ref.at[:, others]
        packs.append(pltpu.make_async_copy(source, place, slide_sems.at[k]))
        at += ref.shape[0]
    for copy in [gain_copy] + copies + packs:
        copy.start()
    gain_copy.wait()
    gains = gain[...].reshape(1, -1)
    width = gains.shape[1]

    def grouped(function):
        def some_rows(j, carry):
            function(pl.ds(pl.multiple_of(j * NORM_ROWS, NORM_ROWS), NORM_ROWS))
            return carry

        lax.fori_loop(0, rows.shape[1] // NORM_ROWS, some_rows, 0, unroll=NORM_UNROLL)

    def lane_sum(values):
        total = values[:, :LANES]
        for k in range(LANES, width, LANES):
            total = total + values[:, k : k + LANES]
        return jnp.sum(total, axis=1, keepdims=True)

    for i in range(rows.shape[0]):
        copies[i].wait()

        def sum_rows(here):
            total = lane_sum(rows[i, here, :].astype(jnp.float32))
            average[here, :] = jnp.broadcast_to(total * (1.0 / width), (NORM_ROWS, LANES))

        def scale_rows(here):
            centred = rows[i, here, :].astype(jnp.float32) - average[here, :1]
            variance = lane_sum(centred * centred) * (1.0 / width)
            scale[here, :] = jnp.broadcast_to(
                lax.rsqrt(variance + EPSILON), (NORM_ROWS, LANES)
            )

        def norm_rows(here):
            centred = rows[i, here, :].astype(jnp.float32) - average[here, :1]
            hidden[i, here, :] = (centred * scale[here, :1] * gains).astype(jnp.bfloat16)

        grouped(sum_rows)
        grouped(scale_rows)
        grouped(norm_rows)
        stores[i].start()
    for copy in packs + stores:
        copy.wait()


def start_work(tiles, gain, gate_weight, up_weight, slide_weights, parts):
    slot_count, length, width = tiles.shape
    half = slot_count // 2
    pieces = half * length // NORM_PIECE
    hbm = pl.BlockSpec(memory_space=pltpu.HBM)
    vmem = pl.BlockSpec(memory_space=pltpu.VMEM)
    cols = gate_weight.shape[1]
    pack = (sum(w.shape[0] for w in slide_weights), slide_weights[0].shape[1])
    return pl.pallas_call(
        functools.partial(start_kernel, parts),
        in_specs=[hbm] * (4 + len(slide_weights)),
        out_specs=[hbm] + [vmem] * (1 + len(parts)),
        out_shape=[
            pltpu.HBM((half * length, width), jnp.bfloat16),
            pltpu.VMEM(pack, jnp.bfloat16),
            *[pltpu.VMEM((part.stop - part.start, cols), jnp.bfloat16) for part in parts],
        ],
        scratch_shapes=[
            pltpu.VMEM((pieces, NORM_PIECE, width), jnp.bfloat16),
            pltpu.VMEM((pieces, NORM_PIECE, width), jnp.bfloat16),
            pltpu.VMEM((width,), jnp.float32),
            pltpu.VMEM((NORM_PIECE, LANES), jnp.float32),
            pltpu.VMEM((NORM_PIECE, LANES), jnp.float32),
            pltpu.SemaphoreType.DMA((pieces,)),
            pltpu.SemaphoreType.DMA((pieces,)),
            pltpu.SemaphoreType.DMA((len(parts), 2)),
            pltpu.SemaphoreType.DMA((len(slide_weights),)),
            pltpu.SemaphoreType.DMA(()),
        ],
        compiler_params=pltpu.CompilerParams(vmem_limit_bytes=NORM_VMEM),
        cost_estimate=pl.CostEstimate(flops=0, bytes_accessed=0, transcendentals=0),
    )(*in_hbm(tiles, gain, gate_weight, up_weight, *slide_weights))


def after(value, *others):
    return lax.optimization_barrier((value, *others))[0]


class Layout:
    def __init__(self, n_dev, ny, depth):
        self.ny, self.nz, self.depth = ny, n_dev // ny, depth
        self.pair = ny * depth
        self.relative = self.pair % LANES == 0
        self.early_steps = self.nz - 1
        self.early = self.early_steps * self.pair // MXU * MXU if self.relative else 0
        cut = max(ROW_TILE, depth // 2 // ROW_TILE * ROW_TILE)
        self.parts = [slice(0, cut), slice(cut, depth)]
        self.width = n_dev * depth

    def place(self):
        me = lax.axis_index("dev")
        my_z = me // self.ny
        return my_z, me - my_z * self.ny

    def source(self, step):
        my_z, _ = self.place()
        z = my_z - step
        return jnp.where(z < 0, z + self.nz, z)

    def block_copies(self, blocks, weights, sems, end=None):
        _, my_y = self.place()
        copies = []
        n_parts = len(self.parts)
        first = 0 if end is None else end - len(blocks) // n_parts // self.ny
        for k, block in enumerate(blocks):
            step, flip, part = first + k // n_parts // self.ny, k // n_parts % self.ny, k % n_parts
            y = 1 - my_y if flip else my_y
            at = step if self.relative else self.source(step)
            here = self.parts[part]
            start = pl.multiple_of(at * self.pair + y * self.depth + here.start, ROW_TILE)
            place = weights.at[pl.ds(start, here.stop - here.start)]
            copies.append(pltpu.make_async_copy(block, place, sems.at[k]))
        return copies

    def row_copies(self, tiles_ref, rows, sems, steps):
        if not self.relative:
            return [pltpu.make_async_copy(tiles_ref, rows, sems.at[0])]
        copies = []
        for step in steps:
            start = pl.multiple_of(self.source(step) * self.pair, LANES)
            copies.append(
                pltpu.make_async_copy(
                    tiles_ref.at[:, pl.ds(start, self.pair)],
                    rows.at[:, step * self.pair : (step + 1) * self.pair],
                    sems.at[step],
                )
            )
        return copies


def gated_means(both, out_ref, at, length):
    cols = both.shape[1] // 2
    for tile in range(both.shape[0] // length):
        total = jnp.zeros((8, cols), jnp.float32)
        for first in range(tile * length, (tile + 1) * length, UNIT_ROWS):
            gate = both[first : first + UNIT_ROWS, :cols]
            up_part = both[first : first + UNIT_ROWS, cols:]
            silu = gate * (0.5 * jnp.tanh(0.5 * gate) + 0.5)
            gated = (silu * up_part).astype(jnp.bfloat16).astype(jnp.float32)
            total = total + jnp.sum(gated.reshape(UNIT_ROWS // 8, 8, cols), axis=0)
        out_ref[at + tile : at + tile + 1, :] = jnp.sum(total, axis=0, keepdims=True) * (
            1.0 / length
        )


def product(out, rows, weights, first, last, more=None):
    for at in range(0, rows.shape[0], MXU):
        here = slice(at, at + MXU)
        both = jnp.dot(
            rows[here, first:last], weights[first:last, :], preferred_element_type=jnp.float32
        )
        out[here, :] = both if more is None else both + more[here, :]


def early_kernel(layout, *refs):
    steps = range(layout.early_steps)
    n_blocks = len(steps) * layout.ny * len(layout.parts)
    blocks, tile_refs = refs[:n_blocks], refs[n_blocks : n_blocks + 2]
    out_ref, weights, rows, weight_sems, row_sems = refs[n_blocks + 2 :]
    loads = layout.block_copies(blocks, weights, weight_sems)
    row_loads = [
        layout.row_copies(ref, rows.at[i], row_sems.at[i], steps)
        for i, ref in enumerate(tile_refs)
    ]
    late_loads = [
        copy
        for i, ref in enumerate(tile_refs)
        for copy in layout.row_copies(
            ref, rows.at[i], row_sems.at[i], range(layout.early_steps, layout.nz)
        )
    ]
    for copy in row_loads[0] + loads + row_loads[1] + late_loads:
        copy.start()
    for copy in loads:
        copy.wait()
    for i in range(2):
        for copy in row_loads[i]:
            copy.wait()
        product(out_ref.at[i], rows.at[i], weights, 0, layout.early)
    for copy in late_loads:
        copy.wait()


def early_mlp(layout, blocks, tiles):
    n_rows = tiles[0].shape[0]
    cols = blocks[0].shape[1]
    hbm = pl.BlockSpec(memory_space=pltpu.HBM)
    vmem = pl.BlockSpec(memory_space=pltpu.VMEM)
    return pl.pallas_call(
        functools.partial(early_kernel, layout),
        in_specs=[hbm] * (len(blocks) + 2),
        out_specs=(vmem, vmem, vmem),
        out_shape=(
            pltpu.VMEM((2, n_rows, cols), jnp.float32),
            pltpu.VMEM((layout.width, cols), jnp.bfloat16),
            pltpu.VMEM((2, n_rows, layout.width), jnp.bfloat16),
        ),
        scratch_shapes=[
            pltpu.SemaphoreType.DMA((len(blocks),)),
            pltpu.SemaphoreType.DMA((2, layout.nz)),
        ],
        compiler_params=pltpu.CompilerParams(vmem_limit_bytes=MLP_VMEM),
        cost_estimate=pl.CostEstimate(
            flops=4 * n_rows * layout.early * cols,
            bytes_accessed=2 * layout.early * (cols + 2 * n_rows) + 8 * n_rows * cols,
            transcendentals=0,
        ),
    )(*in_hbm(*blocks, *tiles))


def middle_kernel(layout, length, n_blocks, n_tiles, *refs):
    blocks, tile_refs = refs[:n_blocks], refs[n_blocks : n_blocks + n_tiles]
    early_refs = refs[n_blocks + n_tiles : -7]
    out_ref, weights, rows, even, odd, weight_sems, row_sems = refs[-7:]
    early = layout.early
    loads = layout.block_copies(blocks, weights, weight_sems, layout.nz)
    row_loads = [
        layout.row_copies(ref, rows.at[i], row_sems.at[i], range(layout.nz))
        for i, ref in enumerate(tile_refs)
    ]
    for copy in [copy for copies in [loads, *row_loads] for copy in copies]:
        copy.start()
    for copy in loads:
        copy.wait()
    units = [(early_refs[2].at[i], early_refs[0].at[i], []) for i in range(2)] if early else []
    units += [(rows.at[i], None, row_loads[i]) for i in range(n_tiles)]
    pending = None
    for i, (unit, more, waits) in enumerate(units):
        for copy in waits:
            copy.wait()
        for j in range(unit.shape[0] // length):
            here = slice(j * length, (j + 1) * length)
            tile = unit.shape[0] // length * i + j
            both = (even, odd)[tile % 2]
            if more is None:
                product(both, unit.at[here], weights, 0, layout.width)
            else:
                product(both, unit.at[here], weights, early, layout.width, more.at[here])
            if pending is not None:
                gated_means(*pending, length)
            pending = (both, out_ref, tile)
    gated_means(*pending, length)


def middle_mlp(layout, blocks, tiles, early, length):
    n_rows, width = tiles[0].shape
    cols = blocks[0].shape[1]
    tiles = tiles[2:] if early else tiles
    hbm = pl.BlockSpec(memory_space=pltpu.HBM)
    vmem = pl.BlockSpec(memory_space=pltpu.VMEM)
    return pl.pallas_call(
        functools.partial(middle_kernel, layout, length, len(blocks), len(tiles)),
        in_specs=[hbm] * (len(blocks) + len(tiles)) + [vmem] * len(early),
        out_specs=(vmem, vmem),
        out_shape=(
            pltpu.VMEM((3 * n_rows // length, cols // 2), jnp.float32),
            pltpu.VMEM((width, cols), jnp.bfloat16),
        ),
        input_output_aliases={len(blocks) + len(tiles) + 1: 1} if early else {},
        scratch_shapes=[
            pltpu.VMEM((len(tiles), n_rows, width), jnp.bfloat16),
            pltpu.VMEM((length, cols), jnp.float32),
            pltpu.VMEM((length, cols), jnp.float32),
            pltpu.SemaphoreType.DMA((len(blocks),)),
            pltpu.SemaphoreType.DMA((len(tiles), layout.nz)),
        ],
        compiler_params=pltpu.CompilerParams(vmem_limit_bytes=MLP_VMEM),
        cost_estimate=pl.CostEstimate(
            flops=4 * n_rows * width * cols,
            bytes_accessed=2 * (3 * n_rows * width + width * cols),
            transcendentals=0,
        ),
    )(*blocks, *in_hbm(*tiles), *in_vmem(*early))


def last_kernel(
    layout, length, n_grp, n_sub, means_ref, weights, tiles_ref, out_ref, rows, both, means, row_sems
):
    row_loads = layout.row_copies(tiles_ref, rows, row_sems, range(layout.nz))
    for copy in row_loads:
        copy.start()
    for copy in row_loads:
        copy.wait()
    n_rows = rows.shape[0]
    half = n_rows // length
    for i in range(half):
        here = slice(i * length, (i + 1) * length)
        product(both[i], rows.at[here], weights, 0, layout.width)
        if i:
            gated_means(both[i - 1], means, i - 1, length)
    gated_means(both[half - 1], means, half - 1, length)

    group, core = lax.axis_index("grp"), lax.axis_index("sub")
    low = core == 0

    def packed(mine, others):
        rows = jnp.concatenate(
            [jnp.where(low, mine, others), jnp.where(low, others, mine)], axis=0
        )
        return jnp.concatenate(
            [rows[:, k : k + LANES] for k in range(0, rows.shape[1], LANES)], axis=0
        )

    before = means_ref[...]
    own = packed(before[:half], before[half : 2 * half])
    pair = packed(before[2 * half :], means[...])
    for g in range(n_grp):
        chosen = jnp.where(group == g, own, pair).astype(jnp.bfloat16)
        for s in range(n_sub):
            out_ref[g * n_sub + s] = chosen


def last_mlp(layout, means, weights, tiles, length, n_grp, n_sub):
    n_rows, width = tiles.shape
    cols = weights.shape[1]
    half = n_rows // length
    any_spec = pl.BlockSpec(memory_space=pl.ANY)
    vmem = pl.BlockSpec(memory_space=pltpu.VMEM)
    return pl.pallas_call(
        functools.partial(last_kernel, layout, length, n_grp, n_sub),
        in_specs=[vmem, vmem, any_spec],
        out_specs=vmem,
        out_shape=jax.ShapeDtypeStruct(
            (n_grp * n_sub, half * cols // LANES, LANES), jnp.bfloat16
        ),
        scratch_shapes=[
            pltpu.VMEM((n_rows, width), jnp.bfloat16),
            [pltpu.VMEM((length, cols), jnp.float32) for _ in range(half)],
            pltpu.VMEM((half, cols // 2), jnp.float32),
            pltpu.SemaphoreType.DMA((layout.nz,)),
        ],
        compiler_params=pltpu.CompilerParams(vmem_limit_bytes=MLP_VMEM),
        cost_estimate=pl.CostEstimate(
            flops=2 * n_rows * width * cols,
            bytes_accessed=2 * (n_rows * width + width * cols),
            transcendentals=0,
        ),
    )(*in_vmem(means, weights), tiles)


def small_mod(value, rate):
    return jnp.where(
        rate == 1,
        0,
        jnp.where(rate == 2, value & 1, jnp.where(rate == 3, lax.rem(value, 3), value & 3)),
    )


def multiplicity_kernel(n_dev, slot_count, heads, counts_ref, slide_ref, rates_ref, out_ref):
    me, core = lax.axis_index("dev"), lax.axis_index("sub")
    shape = out_ref.shape
    row = lax.broadcasted_iota(jnp.int32, shape, 0)
    col = lax.broadcasted_iota(jnp.int32, shape, 1)
    head = row // QROWS + core * (heads // 2)
    head = jnp.where(head >= heads, head - heads, head)
    query = row % QROWS
    device, slot = col // slot_count, col % slot_count
    rate = jnp.full(shape, 1, jnp.int32)
    for h in range(heads):
        rate = jnp.where(head == h, rates_ref[h], rate)
    my_slide = slide_ref[me]
    first = me
    count = jnp.zeros(shape, jnp.int32)
    slide = jnp.zeros(shape, jnp.int32)
    for k in reversed(range(n_dev)):
        first = jnp.where(slide_ref[k] == my_slide, k, first)
        count = jnp.where(device == k, counts_ref[k], count)
        slide = jnp.where(device == k, slide_ref[k], slide)
    offset = small_mod(head, rate)
    query_position = (me - first) * slot_count + query
    key_position = (device - first) * slot_count + slot
    valid = slot < count
    near = jnp.where((device == me) & valid, 1.0, 0.0)
    far = jnp.where(
        (slide == my_slide)
        & valid
        & (small_mod(query_position, rate) == offset)
        & (small_mod(key_position, rate) == offset),
        1.0,
        0.0,
    )
    out_ref[...] = near + far


def embed_kernel(
    n_sub, counts_ref, parts_ref, gain_ref, near_ref, far_ref, embed_ref, mixed_ref, sent_ref
):
    slot_count, half = embed_ref.shape
    n_blocks = half // 2 // LANES
    group, core = lax.axis_index("grp"), lax.axis_index("sub")
    count = counts_ref[lax.axis_index("dev")]
    base = group // 2 * 2
    halves = []
    for s in range(n_sub):
        pieces = []
        for x in range(2):
            part = parts_ref[(base + x) * n_sub + s].astype(jnp.float32)
            pieces += [part[k * slot_count : (k + 1) * slot_count] for k in range(n_blocks)]
        rows = jnp.concatenate(pieces, axis=1)
        slot = lax.broadcasted_iota(jnp.int32, rows.shape, 0)
        halves.append(jnp.where(slot < count, rows, 0.0))
    low = core == 0
    near = jnp.where(low, halves[0], halves[1]).astype(jnp.bfloat16)
    far = jnp.where(low, halves[1], halves[0]).astype(jnp.bfloat16)
    embed_ref[...] = near
    mixed = jnp.dot(near, near_ref[...], preferred_element_type=jnp.float32) + jnp.dot(
        far, far_ref[...], preferred_element_type=jnp.float32
    )
    mixed_ref[...] = jnp.concatenate([mixed, mixed], axis=0)
    hidden = normed(mixed, gain_ref[...].reshape(1, -1)).astype(jnp.float32)
    width = sent_ref.shape[2]
    pieces = [hidden[:, k : k + width] for k in range(0, hidden.shape[1], width)]
    pieces += [jnp.zeros_like(pieces[0])] * (sent_ref.shape[1] // slot_count - len(pieces))
    sent = jnp.concatenate(pieces, axis=0).astype(jnp.bfloat16)
    for k in range(sent_ref.shape[0]):
        sent_ref[k] = sent


def project(rows, near_ref, far_ref):
    return jnp.concatenate(
        [
            jnp.dot(rows, near_ref[...], preferred_element_type=jnp.float32),
            jnp.dot(rows, far_ref[...], preferred_element_type=jnp.float32),
        ],
        axis=1,
    )


def heads_of(shape):
    return (
        lax.broadcasted_iota(jnp.int32, shape, 0) // QROWS
        == lax.broadcasted_iota(jnp.int32, shape, 1) // HD
    )


def query_kernel(heads, mixed_ref, gain_ref, far_ref, *refs):
    near_refs, (many_ref, out_ref, many, *kept), (wq, sems) = refs[:4], refs[4:-2], refs[-2:]
    places = [wq.at[0], wq.at[1], *kept]
    copies = []
    at = 0
    for k, near in enumerate(near_refs):
        far = far_ref.at[at : at + near.shape[0]]
        at += near.shape[0]
        for i, source in enumerate((near, far)):
            copies.append(pltpu.make_async_copy(source, places[2 * k + i], sems.at[2 * k + i]))
    copies.append(pltpu.make_async_copy(many_ref, many, sems.at[len(copies)]))
    for copy in copies:
        copy.start()
    hidden = normed(mixed_ref[...], gain_ref[...].reshape(1, -1))
    for copy in copies[:2]:
        copy.wait()
    query = project(hidden, wq.at[0], wq.at[1])
    spread = jnp.concatenate([query] * heads, axis=0)
    out_ref[...] = jnp.where(heads_of(spread.shape), spread, 0.0).astype(jnp.bfloat16)
    for copy in copies[2:]:
        copy.wait()


def slide_kernel(
    heads,
    counts_ref,
    sent_ref,
    mixed_ref,
    query_ref,
    wk_ref,
    wk_far_ref,
    wv_ref,
    wv_far_ref,
    wo_ref,
    wo_far_ref,
    many_ref,
    out_ref,
    rows,
):
    slot_count, half = out_ref.shape
    core = lax.axis_index("sub")
    count = counts_ref[lax.axis_index("dev")]
    width = sent_ref.shape[2]
    for k in range(sent_ref.shape[0]):
        sent = sent_ref[k].astype(jnp.float32)
        rows[k * slot_count : (k + 1) * slot_count, :] = jnp.concatenate(
            [
                sent[j * slot_count : (j + 1) * slot_count]
                for j in range(rows.shape[1] // width)
            ],
            axis=1,
        )
    hidden = rows[...].astype(jnp.bfloat16)
    keys = project(hidden, wk_ref, wk_far_ref).astype(jnp.bfloat16)
    scores = lax.dot_general(
        query_ref[...], keys, (((1,), (1,)), ((), ())), preferred_element_type=jnp.float32
    ) * (1.0 / math.sqrt(HD))
    values = project(hidden, wv_ref, wv_far_ref).astype(jnp.bfloat16)
    many = many_ref[...]
    masked = jnp.where(many > 0.0, scores, FLOOR)
    weights = many * jnp.exp(masked - jnp.max(masked, axis=1, keepdims=True))
    weights = weights / jnp.sum(weights, axis=1, keepdims=True)
    context = jnp.dot(weights.astype(jnp.bfloat16), values, preferred_element_type=jnp.float32)
    context = jnp.where(heads_of(context.shape), context, 0.0)
    context = context.reshape(heads, QROWS, context.shape[1])
    context = jnp.sum(context, axis=0).astype(jnp.bfloat16)
    columns = pl.ds(pl.multiple_of(core * half, LANES), half)
    attended = jnp.dot(
        context[:, :half], wo_ref[:, columns], preferred_element_type=jnp.float32
    ) + jnp.dot(context[:, half:], wo_far_ref[...], preferred_element_type=jnp.float32)
    total = mixed_ref[:, columns] + attended
    slot = lax.broadcasted_iota(jnp.int32, total.shape, 0)
    total = jnp.where(slot < count, total, 0.0)
    out_ref[...] = total[:slot_count].astype(jnp.bfloat16)


def on_device(
    tiles,
    counts,
    slide_of,
    rates,
    tile_gain,
    gate_weight,
    up_weight,
    embed_proj,
    slide_gain,
    slide_wq,
    slide_wk,
    slide_wv,
    slide_wo,
):
    slot_count, length, width = tiles.shape
    hidden_cols = gate_weight.shape[1]
    n_grp, n_dev, n_sub = (lax.axis_size(a) for a in ("grp", "dev", "sub"))
    ny = 2
    nz = n_dev // ny
    heads = slide_wq.shape[1] * n_sub // HD
    core = lax.axis_index("sub")

    to_pair = [(g, g ^ 1) for g in range(n_grp)]
    to_sibling = [(s, s ^ 1) for s in range(n_sub)]
    along_z = [(d, (d + ny) % n_dev) for d in range(n_dev)]
    along_y = [(d, d ^ 1) for d in range(n_dev)]

    layout = Layout(n_dev, ny, gate_weight.shape[0])
    slide_weights = [slide_wq, slide_wk, slide_wv, slide_wo]
    first, pack, *held = start_work(
        tiles, tile_gain, gate_weight, up_weight, slide_weights, layout.parts
    )
    second = lax.ppermute(first, "sub", to_sibling)
    pair_first = lax.ppermute(first, "grp", to_pair)
    proj_far = lax.ppermute(embed_proj, "sub", to_sibling)
    pack_far = lax.ppermute(pack, "sub", to_sibling)
    out_cols = slide_wo.shape[1] // n_sub
    smem = pl.BlockSpec(memory_space=pltpu.SMEM)
    vmem = pl.BlockSpec(memory_space=pltpu.VMEM)
    many = pl.pallas_call(
        functools.partial(multiplicity_kernel, n_dev, slot_count, heads),
        in_specs=[smem] * 3,
        out_specs=vmem,
        out_shape=jax.ShapeDtypeStruct((heads * QROWS, n_dev * slot_count), jnp.float32),
        compiler_params=pltpu.CompilerParams(vmem_limit_bytes=SMALL_VMEM),
    )(counts, slide_of, rates)

    held[1] = after(held[1], proj_far, second)
    steps = []
    last = None
    for step in range(nz):
        sent = []
        for part in range(len(held)):
            if step:
                arrived = lax.ppermute(held[part], "dev", along_z)
                others = [steps[-1][len(held) + part]]
                if (step, part) == (nz - 1, 0):
                    others += [many]
                if last is not None:
                    others.append(last)
                held[part] = last = after(arrived, *others)
            sent.append(lax.ppermute(held[part], "dev", along_y))
        steps.append([*held, *sent])
    blocks = [block for step in steps for block in step]
    early = []
    if layout.relative:
        n_early = layout.early_steps * len(steps[0])
        early = early_mlp(layout, blocks[:n_early], [after(first, last), second])
        blocks = blocks[n_early:]
    pair_first = after(pair_first, *steps[-1][-2:], *early)
    pair_second = lax.ppermute(pair_first, "sub", to_sibling)
    means, weights = middle_mlp(layout, blocks, [first, second, pair_first], early, length)
    parts = last_mlp(layout, means, weights, pair_second, length, n_grp, n_sub)
    parts = lax.all_to_all(parts, ("grp", "sub"), split_axis=0, concat_axis=0, tiled=True)

    out_width = embed_proj.shape[1]
    sent_rows = 16
    sent_cols = 2 * LANES
    small = pltpu.CompilerParams(vmem_limit_bytes=SMALL_VMEM)
    tile_embed, mixed, sent = pl.pallas_call(
        functools.partial(embed_kernel, n_sub),
        in_specs=[smem] + [vmem] * 4,
        out_specs=(vmem, vmem, vmem),
        out_shape=(
            jax.ShapeDtypeStruct((slot_count, hidden_cols), jnp.bfloat16),
            pltpu.VMEM((QROWS, out_width), jnp.float32),
            pltpu.VMEM((n_dev, sent_rows, sent_cols), jnp.bfloat16),
        ),
        compiler_params=small,
    )(counts, *in_vmem(parts), slide_gain, embed_proj, proj_far)
    sent = lax.all_to_all(sent, "dev", split_axis=0, concat_axis=0, tiled=True)
    hbm = pl.BlockSpec(memory_space=pltpu.HBM)
    far_shape = (slide_wo.shape[0], out_cols)
    kept = [slide_wk.shape] * 4 + [slide_wo.shape, far_shape]
    query, many, *weights = pl.pallas_call(
        functools.partial(query_kernel, heads),
        in_specs=[vmem] * 2 + [hbm] * 6,
        out_specs=[vmem] * (2 + len(kept)),
        out_shape=[
            pltpu.VMEM((heads * QROWS, out_width), jnp.bfloat16),
            pltpu.VMEM(many.shape, many.dtype),
            *[pltpu.VMEM(shape, jnp.bfloat16) for shape in kept],
        ],
        scratch_shapes=[
            pltpu.VMEM((2, *slide_wq.shape), jnp.bfloat16),
            pltpu.SemaphoreType.DMA((3 + len(kept),)),
        ],
        compiler_params=small,
    )(*in_vmem(mixed), slide_gain, *in_hbm(pack_far, *slide_weights, many))
    slide_out = pl.pallas_call(
        functools.partial(slide_kernel, heads),
        in_specs=[smem] + [vmem] * 10,
        out_specs=vmem,
        out_shape=jax.ShapeDtypeStruct((slot_count, out_cols), jnp.bfloat16),
        scratch_shapes=[pltpu.VMEM((n_dev * slot_count, out_width), jnp.float32)],
        compiler_params=small,
    )(counts, *in_vmem(sent, mixed, query, *weights, many))
    return (tile_embed, slide_out)


def solution(mesh):
    placed = (
        P(("grp", "dev"), None, None),
        P("grp"),
        P("grp"),
        P(),
        P(),
        P("dev", "sub"),
        P("dev", "sub"),
        P("sub", None),
        P(),
        P(None, "sub"),
        P(None, "sub"),
        P(None, "sub"),
        P("sub", None),
    )
    return jax.shard_map(
        on_device,
        mesh=mesh,
        in_specs=placed,
        out_specs=(P(("grp", "dev"), "sub"), P(("grp", "dev"), "sub")),
        check_vma=False,
    )
```

```python
import functools
import math

import jax
import jax.numpy as jnp
from jax import lax
from jax.experimental import pallas as pl
from jax.experimental.pallas import tpu as pltpu
from jax.sharding import PartitionSpec as P

HD = 64
EPSILON = 1e-06
FLOOR = -1e30
QROWS = 8
NORM_ROWS = 16
NORM_PIECE = 128
NORM_UNROLL = 8
LANES = 128
UNIT_ROWS = 16
ROW_TILE = 16
MXU = 256
MLP_VMEM = 24 * 1024 * 1024
NORM_VMEM = 12 * 1024 * 1024
SMALL_VMEM = 4 * 1024 * 1024


def normed(rows_in, gains):
    average = jnp.mean(rows_in, axis=-1, keepdims=True)
    centred = rows_in - average
    variance = jnp.mean(centred * centred, axis=-1, keepdims=True)
    return (centred * lax.rsqrt(variance + EPSILON) * gains).astype(jnp.bfloat16)


def in_hbm(*arrays):
    return [pltpu.with_memory_space_constraint(x, pltpu.HBM) for x in arrays]


def in_vmem(*arrays):
    return [pltpu.with_memory_space_constraint(x, pltpu.VMEM) for x in arrays]


def start_kernel(parts, *refs):
    tiles_ref, gain_ref, gate_ref, up_ref, *slide_refs = refs[:8]
    out_ref, pack_ref, *block_refs = refs[8 : 10 + len(parts)]
    (
        rows,
        hidden,
        gain,
        average,
        scale,
        whole,
        whole_slide,
        in_sems,
        out_sems,
        block_sems,
        slide_sems,
        gain_sem,
    ) = refs[10 + len(parts) :]
    core = lax.axis_index("sub")
    pieces, piece = rows.shape[:2]
    half, length = tiles_ref.shape[0] // 2, tiles_ref.shape[1]
    half_cols = gate_ref.shape[1] // 2
    gain_copy = pltpu.make_async_copy(gain_ref, gain, gain_sem)
    copies = [
        pltpu.make_async_copy(
            tiles_ref.at[core * half + i * piece // length, pl.ds(i * piece % length, piece)],
            rows.at[i],
            in_sems.at[i],
        )
        for i in range(pieces)
    ]
    stores = [
        pltpu.make_async_copy(hidden.at[i], out_ref.at[pl.ds(i * piece, piece)], out_sems.at[i])
        for i in range(pieces)
    ]
    packs = [
        pltpu.make_async_copy(ref, whole.at[i], block_sems.at[i])
        for i, ref in enumerate((gate_ref, up_ref))
    ]
    selects = []
    columns = pl.ds(pl.multiple_of(lax.rem(lax.axis_index("grp"), 2) * half_cols, LANES), half_cols)
    for k, (part, block_ref) in enumerate(zip(parts, block_refs)):
        for i, ref in enumerate((gate_ref, up_ref)):
            selects.append((block_ref, i * half_cols, whole.at[i, part, columns]))
    cols = pack_ref.shape[1]
    others = pl.ds(pl.multiple_of((1 - core) * cols, LANES), cols)
    at = 0
    for k, ref in enumerate(slide_refs):
        place = pack_ref.at[at : at + ref.shape[0]]
        if ref.shape[1] == cols:
            packs.append(pltpu.make_async_copy(ref, place, slide_sems.at[k]))
        else:
            packs.append(pltpu.make_async_copy(ref, whole_slide, slide_sems.at[k]))
            selects.append((place, 0, whole_slide.at[:, others]))
        at += ref.shape[0]
    for copy in [gain_copy] + copies + packs:
        copy.start()
    gain_copy.wait()
    gains = gain[...].reshape(1, -1)
    width = gains.shape[1]

    def grouped(function):
        def some_rows(j, carry):
            function(pl.ds(pl.multiple_of(j * NORM_ROWS, NORM_ROWS), NORM_ROWS))
            return carry

        lax.fori_loop(0, rows.shape[1] // NORM_ROWS, some_rows, 0, unroll=NORM_UNROLL)

    def lane_sum(values):
        total = values[:, :LANES]
        for k in range(LANES, width, LANES):
            total = total + values[:, k : k + LANES]
        return jnp.sum(total, axis=1, keepdims=True)

    for i in range(rows.shape[0]):
        copies[i].wait()

        def sum_rows(here):
            total = lane_sum(rows[i, here, :].astype(jnp.float32))
            average[here, :] = jnp.broadcast_to(total * (1.0 / width), (NORM_ROWS, LANES))

        def scale_rows(here):
            centred = rows[i, here, :].astype(jnp.float32) - average[here, :1]
            variance = lane_sum(centred * centred) * (1.0 / width)
            scale[here, :] = jnp.broadcast_to(
                lax.rsqrt(variance + EPSILON), (NORM_ROWS, LANES)
            )

        def norm_rows(here):
            centred = rows[i, here, :].astype(jnp.float32) - average[here, :1]
            hidden[i, here, :] = (centred * scale[here, :1] * gains).astype(jnp.bfloat16)

        grouped(sum_rows)
        grouped(scale_rows)
        grouped(norm_rows)
        stores[i].start()
    for copy in packs:
        copy.wait()
    for place, at, source in selects:
        place[:, at : at + source.shape[1]] = source[...]
    for copy in stores:
        copy.wait()


def start_work(tiles, gain, gate_weight, up_weight, slide_weights, parts):
    slot_count, length, width = tiles.shape
    half = slot_count // 2
    pieces = half * length // NORM_PIECE
    hbm = pl.BlockSpec(memory_space=pltpu.HBM)
    vmem = pl.BlockSpec(memory_space=pltpu.VMEM)
    cols = gate_weight.shape[1]
    pack = (sum(w.shape[0] for w in slide_weights), slide_weights[0].shape[1])
    return pl.pallas_call(
        functools.partial(start_kernel, parts),
        in_specs=[hbm] * (4 + len(slide_weights)),
        out_specs=[hbm] + [vmem] * (1 + len(parts)),
        out_shape=[
            pltpu.HBM((half * length, width), jnp.bfloat16),
            pltpu.VMEM(pack, jnp.bfloat16),
            *[pltpu.VMEM((part.stop - part.start, cols), jnp.bfloat16) for part in parts],
        ],
        scratch_shapes=[
            pltpu.VMEM((pieces, NORM_PIECE, width), jnp.bfloat16),
            pltpu.VMEM((pieces, NORM_PIECE, width), jnp.bfloat16),
            pltpu.VMEM((width,), jnp.float32),
            pltpu.VMEM((NORM_PIECE, LANES), jnp.float32),
            pltpu.VMEM((NORM_PIECE, LANES), jnp.float32),
            pltpu.VMEM((2, *gate_weight.shape), jnp.bfloat16),
            pltpu.VMEM(slide_weights[-1].shape, jnp.bfloat16),
            pltpu.SemaphoreType.DMA((pieces,)),
            pltpu.SemaphoreType.DMA((pieces,)),
            pltpu.SemaphoreType.DMA((2,)),
            pltpu.SemaphoreType.DMA((len(slide_weights),)),
            pltpu.SemaphoreType.DMA(()),
        ],
        compiler_params=pltpu.CompilerParams(vmem_limit_bytes=NORM_VMEM),
        cost_estimate=pl.CostEstimate(flops=0, bytes_accessed=0, transcendentals=0),
    )(*in_hbm(tiles, gain, gate_weight, up_weight, *slide_weights))


def after(value, *others):
    return lax.optimization_barrier((value, *others))[0]


class Layout:
    def __init__(self, n_dev, ny, depth):
        self.ny, self.nz, self.depth = ny, n_dev // ny, depth
        self.pair = ny * depth
        self.relative = self.pair % LANES == 0
        self.early_steps = self.nz - 1
        self.early = self.early_steps * self.pair // MXU * MXU if self.relative else 0
        cut = max(ROW_TILE, depth // 2 // ROW_TILE * ROW_TILE)
        self.parts = [slice(0, cut), slice(cut, depth)]
        self.width = n_dev * depth

    def place(self):
        me = lax.axis_index("dev")
        my_z = me // self.ny
        return my_z, me - my_z * self.ny

    def source(self, step):
        my_z, _ = self.place()
        z = my_z - step
        return jnp.where(z < 0, z + self.nz, z)

    def block_copies(self, blocks, weights, sems, end=None):
        _, my_y = self.place()
        copies = []
        n_parts = len(self.parts)
        first = 0 if end is None else end - len(blocks) // n_parts // self.ny
        for k, block in enumerate(blocks):
            step, flip, part = first + k // n_parts // self.ny, k // n_parts % self.ny, k % n_parts
            y = 1 - my_y if flip else my_y
            at = step if self.relative else self.source(step)
            here = self.parts[part]
            start = pl.multiple_of(at * self.pair + y * self.depth + here.start, ROW_TILE)
            place = weights.at[pl.ds(start, here.stop - here.start)]
            copies.append(pltpu.make_async_copy(block, place, sems.at[k]))
        return copies

    def row_copies(self, tiles_ref, rows, sems, steps):
        if not self.relative:
            return [pltpu.make_async_copy(tiles_ref, rows, sems.at[0])]
        copies = []
        for step in steps:
            start = pl.multiple_of(self.source(step) * self.pair, LANES)
            copies.append(
                pltpu.make_async_copy(
                    tiles_ref.at[:, pl.ds(start, self.pair)],
                    rows.at[:, step * self.pair : (step + 1) * self.pair],
                    sems.at[step],
                )
            )
        return copies


def gated_means(both, out_ref, at, length):
    cols = both.shape[1] // 2
    for tile in range(both.shape[0] // length):
        total = jnp.zeros((8, cols), jnp.float32)
        for first in range(tile * length, (tile + 1) * length, UNIT_ROWS):
            gate = both[first : first + UNIT_ROWS, :cols]
            up_part = both[first : first + UNIT_ROWS, cols:]
            silu = gate * (0.5 * jnp.tanh(0.5 * gate) + 0.5)
            gated = (silu * up_part).astype(jnp.bfloat16).astype(jnp.float32)
            total = total + jnp.sum(gated.reshape(UNIT_ROWS // 8, 8, cols), axis=0)
        out_ref[at + tile : at + tile + 1, :] = jnp.sum(total, axis=0, keepdims=True) * (
            1.0 / length
        )


def product(out, rows, weights, first, last, more=None):
    for at in range(0, rows.shape[0], MXU):
        here = slice(at, at + MXU)
        both = jnp.dot(
            rows[here, first:last], weights[first:last, :], preferred_element_type=jnp.float32
        )
        out[here, :] = both if more is None else both + more[here, :]


def early_kernel(layout, *refs):
    steps = range(layout.early_steps)
    n_blocks = len(steps) * layout.ny * len(layout.parts)
    blocks, tile_refs = refs[:n_blocks], refs[n_blocks : n_blocks + 2]
    out_ref, weights, rows, weight_sems, row_sems = refs[n_blocks + 2 :]
    loads = layout.block_copies(blocks, weights, weight_sems)
    row_loads = [
        layout.row_copies(ref, rows.at[i], row_sems.at[i], steps)
        for i, ref in enumerate(tile_refs)
    ]
    late_loads = [
        copy
        for i, ref in enumerate(tile_refs)
        for copy in layout.row_copies(
            ref, rows.at[i], row_sems.at[i], range(layout.early_steps, layout.nz)
        )
    ]
    for copy in row_loads[0] + loads + row_loads[1] + late_loads:
        copy.start()
    for copy in loads:
        copy.wait()
    for i in range(2):
        for copy in row_loads[i]:
            copy.wait()
        product(out_ref.at[i], rows.at[i], weights, 0, layout.early)
    for copy in late_loads:
        copy.wait()


def early_mlp(layout, blocks, tiles):
    n_rows = tiles[0].shape[0]
    cols = blocks[0].shape[1]
    hbm = pl.BlockSpec(memory_space=pltpu.HBM)
    vmem = pl.BlockSpec(memory_space=pltpu.VMEM)
    return pl.pallas_call(
        functools.partial(early_kernel, layout),
        in_specs=[hbm] * (len(blocks) + 2),
        out_specs=(vmem, vmem, vmem),
        out_shape=(
            pltpu.VMEM((2, n_rows, cols), jnp.float32),
            pltpu.VMEM((layout.width, cols), jnp.bfloat16),
            pltpu.VMEM((2, n_rows, layout.width), jnp.bfloat16),
        ),
        scratch_shapes=[
            pltpu.SemaphoreType.DMA((len(blocks),)),
            pltpu.SemaphoreType.DMA((2, layout.nz)),
        ],
        compiler_params=pltpu.CompilerParams(vmem_limit_bytes=MLP_VMEM),
        cost_estimate=pl.CostEstimate(
            flops=4 * n_rows * layout.early * cols,
            bytes_accessed=2 * layout.early * (cols + 2 * n_rows) + 8 * n_rows * cols,
            transcendentals=0,
        ),
    )(*in_hbm(*blocks, *tiles))


def packed(mine, others):
    low = lax.axis_index("sub") == 0
    rows = jnp.concatenate([jnp.where(low, mine, others), jnp.where(low, others, mine)], axis=0)
    return jnp.concatenate(
        [rows[:, k : k + LANES] for k in range(0, rows.shape[1], LANES)], axis=0
    ).astype(jnp.bfloat16)


def middle_kernel(layout, length, n_blocks, n_tiles, *refs):
    blocks, tile_refs = refs[:n_blocks], refs[n_blocks : n_blocks + n_tiles]
    early_refs = refs[n_blocks + n_tiles : -9]
    pair_ref, weights, own_ref, rows, even, odd, means, weight_sems, row_sems = refs[-9:]
    early = layout.early
    loads = layout.block_copies(blocks, weights, weight_sems, layout.nz)
    row_loads = [
        layout.row_copies(ref, rows.at[i], row_sems.at[i], range(layout.nz))
        for i, ref in enumerate(tile_refs)
    ]
    for copy in [copy for copies in [loads, *row_loads] for copy in copies]:
        copy.start()
    for copy in loads:
        copy.wait()
    units = [(early_refs[2].at[i], early_refs[0].at[i], []) for i in range(2)] if early else []
    units += [(rows.at[i], None, row_loads[i]) for i in range(n_tiles)]
    pending = None
    for i, (unit, more, waits) in enumerate(units):
        for copy in waits:
            copy.wait()
        for j in range(unit.shape[0] // length):
            here = slice(j * length, (j + 1) * length)
            tile = unit.shape[0] // length * i + j
            both = (even, odd)[tile % 2]
            if more is None:
                product(both, unit.at[here], weights, 0, layout.width)
            else:
                product(both, unit.at[here], weights, early, layout.width, more.at[here])
            if pending is not None:
                gated_means(*pending, length)
            pending = (both, means, tile)
    gated_means(*pending, length)
    half = means.shape[0] // 3
    own_ref[...] = packed(means[:half, :], means[half : 2 * half, :])
    pair_ref[...] = means[2 * half :, :]


def middle_mlp(layout, blocks, tiles, early, length):
    n_rows, width = tiles[0].shape
    cols = blocks[0].shape[1]
    half = n_rows // length
    tiles = tiles[2:] if early else tiles
    vmem = pl.BlockSpec(memory_space=pltpu.VMEM)
    return pl.pallas_call(
        functools.partial(middle_kernel, layout, length, len(blocks), len(tiles)),
        in_specs=[pl.BlockSpec(memory_space=pl.ANY)] * (len(blocks) + len(tiles))
        + [vmem] * len(early),
        out_specs=(vmem, vmem, vmem),
        out_shape=(
            pltpu.VMEM((half, cols // 2), jnp.float32),
            pltpu.VMEM((width, cols), jnp.bfloat16),
            jax.ShapeDtypeStruct((half * cols // LANES, LANES), jnp.bfloat16),
        ),
        input_output_aliases={len(blocks) + len(tiles) + 1: 1} if early else {},
        scratch_shapes=[
            pltpu.VMEM((len(tiles), n_rows, width), jnp.bfloat16),
            pltpu.VMEM((length, cols), jnp.float32),
            pltpu.VMEM((length, cols), jnp.float32),
            pltpu.VMEM((3 * half, cols // 2), jnp.float32),
            pltpu.SemaphoreType.DMA((len(blocks),)),
            pltpu.SemaphoreType.DMA((len(tiles), layout.nz)),
        ],
        compiler_params=pltpu.CompilerParams(vmem_limit_bytes=MLP_VMEM),
        cost_estimate=pl.CostEstimate(
            flops=4 * n_rows * width * cols,
            bytes_accessed=2 * (3 * n_rows * width + width * cols),
            transcendentals=0,
        ),
    )(*blocks, *(tiles if early else in_hbm(*tiles)), *in_vmem(*early))


def last_kernel(layout, length, means_ref, weights, tiles_ref, out_ref, rows, both, means, row_sems):
    row_loads = layout.row_copies(tiles_ref, rows, row_sems, range(layout.nz))
    for copy in row_loads:
        copy.start()
    for copy in row_loads:
        copy.wait()
    half = rows.shape[0] // length
    for i in range(half):
        here = slice(i * length, (i + 1) * length)
        product(both[i], rows.at[here], weights, 0, layout.width)
        if i:
            gated_means(both[i - 1], means, i - 1, length)
    gated_means(both[half - 1], means, half - 1, length)
    out_ref[...] = packed(means_ref[...], means[...])


def last_mlp(layout, means, weights, tiles, length):
    n_rows, width = tiles.shape
    cols = weights.shape[1]
    half = n_rows // length
    any_spec = pl.BlockSpec(memory_space=pl.ANY)
    vmem = pl.BlockSpec(memory_space=pltpu.VMEM)
    return pl.pallas_call(
        functools.partial(last_kernel, layout, length),
        in_specs=[vmem, vmem, any_spec],
        out_specs=vmem,
        out_shape=jax.ShapeDtypeStruct((half * cols // LANES, LANES), jnp.bfloat16),
        scratch_shapes=[
            pltpu.VMEM((n_rows, width), jnp.bfloat16),
            [pltpu.VMEM((length, cols), jnp.float32) for _ in range(half)],
            pltpu.VMEM((half, cols // 2), jnp.float32),
            pltpu.SemaphoreType.DMA((layout.nz,)),
        ],
        compiler_params=pltpu.CompilerParams(vmem_limit_bytes=MLP_VMEM),
        cost_estimate=pl.CostEstimate(
            flops=2 * n_rows * width * cols,
            bytes_accessed=2 * (n_rows * width + width * cols),
            transcendentals=0,
        ),
    )(*in_vmem(means, weights), tiles)


def small_mod(value, rate):
    return jnp.where(
        rate == 1,
        0,
        jnp.where(rate == 2, value & 1, jnp.where(rate == 3, lax.rem(value, 3), value & 3)),
    )


def multiplicity_kernel(n_dev, slot_count, heads, counts_ref, slide_ref, rates_ref, out_ref):
    me, core = lax.axis_index("dev"), lax.axis_index("sub")
    shape = out_ref.shape
    row = lax.broadcasted_iota(jnp.int32, shape, 0)
    col = lax.broadcasted_iota(jnp.int32, shape, 1)
    head = row // QROWS + core * (heads // 2)
    head = jnp.where(head >= heads, head - heads, head)
    query = row % QROWS
    device, slot = col // slot_count, col % slot_count
    rate = jnp.full(shape, 1, jnp.int32)
    for h in range(heads):
        rate = jnp.where(head == h, rates_ref[h], rate)
    my_slide = slide_ref[me]
    first = me
    count = jnp.zeros(shape, jnp.int32)
    slide = jnp.zeros(shape, jnp.int32)
    for k in reversed(range(n_dev)):
        first = jnp.where(slide_ref[k] == my_slide, k, first)
        count = jnp.where(device == k, counts_ref[k], count)
        slide = jnp.where(device == k, slide_ref[k], slide)
    offset = small_mod(head, rate)
    query_position = (me - first) * slot_count + query
    key_position = (device - first) * slot_count + slot
    valid = slot < count
    near = jnp.where((device == me) & valid, 1.0, 0.0)
    far = jnp.where(
        (slide == my_slide)
        & valid
        & (small_mod(query_position, rate) == offset)
        & (small_mod(key_position, rate) == offset),
        1.0,
        0.0,
    )
    out_ref[...] = near + far


def embed_kernel(
    counts_ref,
    own_ref,
    own_far_ref,
    pair_ref,
    pair_far_ref,
    gain_ref,
    near_ref,
    far_ref,
    embed_ref,
    mixed_ref,
    sent_ref,
):
    slot_count, half = embed_ref.shape
    n_blocks = half // 2 // LANES
    low = lax.rem(lax.axis_index("grp"), 2) == 0
    count = counts_ref[lax.axis_index("dev")]

    def features(mine_ref, theirs_ref):
        sides = []
        for ref in (mine_ref, theirs_ref):
            part = ref[...].astype(jnp.float32)
            pieces = [part[k * slot_count : (k + 1) * slot_count] for k in range(n_blocks)]
            sides.append(jnp.concatenate(pieces, axis=1))
        mine, theirs = sides
        rows = jnp.concatenate(
            [jnp.where(low, mine, theirs), jnp.where(low, theirs, mine)], axis=1
        )
        slot = lax.broadcasted_iota(jnp.int32, rows.shape, 0)
        return jnp.where(slot < count, rows, 0.0).astype(jnp.bfloat16)

    near = features(own_ref, pair_ref)
    far = features(own_far_ref, pair_far_ref)
    embed_ref[...] = near
    mixed = jnp.dot(near, near_ref[...], preferred_element_type=jnp.float32) + jnp.dot(
        far, far_ref[...], preferred_element_type=jnp.float32
    )
    mixed_ref[...] = jnp.concatenate([mixed, mixed], axis=0)
    hidden = normed(mixed, gain_ref[...].reshape(1, -1)).astype(jnp.float32)
    width = sent_ref.shape[2]
    pieces = [hidden[:, k : k + width] for k in range(0, hidden.shape[1], width)]
    pieces += [jnp.zeros_like(pieces[0])] * (sent_ref.shape[1] // slot_count - len(pieces))
    sent = jnp.concatenate(pieces, axis=0).astype(jnp.bfloat16)
    for k in range(sent_ref.shape[0]):
        sent_ref[k] = sent


def project(rows, near_ref, far_ref):
    return jnp.concatenate(
        [
            jnp.dot(rows, near_ref[...], preferred_element_type=jnp.float32),
            jnp.dot(rows, far_ref[...], preferred_element_type=jnp.float32),
        ],
        axis=1,
    )


def heads_of(shape):
    return (
        lax.broadcasted_iota(jnp.int32, shape, 0) // QROWS
        == lax.broadcasted_iota(jnp.int32, shape, 1) // HD
    )


def query_kernel(heads, mixed_ref, gain_ref, far_ref, *refs):
    near_refs, (many_ref, out_ref, many, *kept), (wq, sems) = refs[:4], refs[4:-2], refs[-2:]
    places = [wq.at[0], wq.at[1], *kept]
    copies = []
    at = 0
    for k, near in enumerate(near_refs):
        far = far_ref.at[at : at + near.shape[0]]
        at += near.shape[0]
        for i, source in enumerate((near, far)):
            copies.append(pltpu.make_async_copy(source, places[2 * k + i], sems.at[2 * k + i]))
    copies.append(pltpu.make_async_copy(many_ref, many, sems.at[len(copies)]))
    for copy in copies:
        copy.start()
    hidden = normed(mixed_ref[...], gain_ref[...].reshape(1, -1))
    for copy in copies[:2]:
        copy.wait()
    query = project(hidden, wq.at[0], wq.at[1])
    spread = jnp.concatenate([query] * heads, axis=0)
    out_ref[...] = jnp.where(heads_of(spread.shape), spread, 0.0).astype(jnp.bfloat16)
    for copy in copies[2:]:
        copy.wait()


def slide_kernel(
    heads,
    counts_ref,
    sent_ref,
    mixed_ref,
    query_ref,
    wk_ref,
    wk_far_ref,
    wv_ref,
    wv_far_ref,
    wo_ref,
    wo_far_ref,
    many_ref,
    out_ref,
    rows,
):
    slot_count, half = out_ref.shape
    core = lax.axis_index("sub")
    count = counts_ref[lax.axis_index("dev")]
    width = sent_ref.shape[2]
    for k in range(sent_ref.shape[0]):
        sent = sent_ref[k].astype(jnp.float32)
        rows[k * slot_count : (k + 1) * slot_count, :] = jnp.concatenate(
            [
                sent[j * slot_count : (j + 1) * slot_count]
                for j in range(rows.shape[1] // width)
            ],
            axis=1,
        )
    hidden = rows[...].astype(jnp.bfloat16)
    keys = project(hidden, wk_ref, wk_far_ref).astype(jnp.bfloat16)
    scores = lax.dot_general(
        query_ref[...], keys, (((1,), (1,)), ((), ())), preferred_element_type=jnp.float32
    ) * (1.0 / math.sqrt(HD))
    values = project(hidden, wv_ref, wv_far_ref).astype(jnp.bfloat16)
    many = many_ref[...]
    masked = jnp.where(many > 0.0, scores, FLOOR)
    weights = many * jnp.exp(masked - jnp.max(masked, axis=1, keepdims=True))
    weights = weights / jnp.sum(weights, axis=1, keepdims=True)
    context = jnp.dot(weights.astype(jnp.bfloat16), values, preferred_element_type=jnp.float32)
    context = jnp.where(heads_of(context.shape), context, 0.0)
    context = context.reshape(heads, QROWS, context.shape[1])
    context = jnp.sum(context, axis=0).astype(jnp.bfloat16)
    columns = pl.ds(pl.multiple_of(core * half, LANES), half)
    attended = jnp.dot(
        context[:, :half], wo_ref[:, columns], preferred_element_type=jnp.float32
    ) + jnp.dot(context[:, half:], wo_far_ref[...], preferred_element_type=jnp.float32)
    total = mixed_ref[:, columns] + attended
    slot = lax.broadcasted_iota(jnp.int32, total.shape, 0)
    total = jnp.where(slot < count, total, 0.0)
    out_ref[...] = total[:slot_count].astype(jnp.bfloat16)


def on_device(
    tiles,
    counts,
    slide_of,
    rates,
    tile_gain,
    gate_weight,
    up_weight,
    embed_proj,
    slide_gain,
    slide_wq,
    slide_wk,
    slide_wv,
    slide_wo,
):
    slot_count, length, width = tiles.shape
    hidden_cols = gate_weight.shape[1]
    n_grp, n_dev, n_sub = (lax.axis_size(a) for a in ("grp", "dev", "sub"))
    ny = 2
    nz = n_dev // ny
    heads = slide_wq.shape[1] * n_sub // HD
    core = lax.axis_index("sub")

    to_pair = [(g, g ^ 1) for g in range(n_grp)]
    to_sibling = [(s, s ^ 1) for s in range(n_sub)]
    along_z = [(d, (d + ny) % n_dev) for d in range(n_dev)]
    along_y = [(d, d ^ 1) for d in range(n_dev)]

    layout = Layout(n_dev, ny, gate_weight.shape[0])
    slide_weights = [slide_wq, slide_wk, slide_wv, slide_wo]
    first, pack, *held = start_work(
        tiles, tile_gain, gate_weight, up_weight, slide_weights, layout.parts
    )
    second = lax.ppermute(first, "sub", to_sibling)
    pair_first = lax.ppermute(first, "grp", to_pair)
    proj_far = lax.ppermute(embed_proj, "sub", to_sibling)
    pack_far = lax.ppermute(pack, "sub", to_sibling)
    out_cols = slide_wo.shape[1] // n_sub
    smem = pl.BlockSpec(memory_space=pltpu.SMEM)
    vmem = pl.BlockSpec(memory_space=pltpu.VMEM)
    many = pl.pallas_call(
        functools.partial(multiplicity_kernel, n_dev, slot_count, heads),
        in_specs=[smem] * 3,
        out_specs=vmem,
        out_shape=jax.ShapeDtypeStruct((heads * QROWS, n_dev * slot_count), jnp.float32),
        compiler_params=pltpu.CompilerParams(vmem_limit_bytes=SMALL_VMEM),
    )(counts, slide_of, rates)

    held[1] = after(held[1], proj_far, second)
    steps = []
    last = None
    for step in range(nz):
        sent = []
        for part in range(len(held)):
            if step:
                arrived = lax.ppermute(held[part], "dev", along_z)
                others = [steps[-1][len(held) + part]]
                if (step, part) == (nz - 1, 0):
                    others += [many]
                if last is not None:
                    others.append(last)
                held[part] = last = after(arrived, *others)
            sent.append(lax.ppermute(held[part], "dev", along_y))
        steps.append([*held, *sent])
    blocks = [block for step in steps for block in step]
    early = []
    if layout.relative:
        n_early = layout.early_steps * len(steps[0])
        early = early_mlp(layout, blocks[:n_early], [after(first, last), second])
        blocks = blocks[n_early:]
    pair_first = after(pair_first, *steps[-1][-2:], *early)
    pair_second = lax.ppermute(pair_first, "sub", to_sibling)
    means, weights, own = middle_mlp(
        layout, blocks, [first, second, pair_first], early, length
    )
    own_far = lax.ppermute(own, "sub", to_sibling)
    pair = last_mlp(layout, means, weights, pair_second, length)
    across = [
        (g * n_sub + s, (g ^ 1) * n_sub + (s ^ 1)) for g in range(n_grp) for s in range(n_sub)
    ]
    pair_far = lax.ppermute(pair, ("grp", "sub"), across)
    pair = lax.ppermute(pair, "grp", to_pair)

    out_width = embed_proj.shape[1]
    sent_rows = 16
    sent_cols = 2 * LANES
    small = pltpu.CompilerParams(vmem_limit_bytes=SMALL_VMEM)
    tile_embed, mixed, sent = pl.pallas_call(
        embed_kernel,
        in_specs=[smem] + [vmem] * 7,
        out_specs=(vmem, vmem, vmem),
        out_shape=(
            jax.ShapeDtypeStruct((slot_count, hidden_cols), jnp.bfloat16),
            pltpu.VMEM((QROWS, out_width), jnp.float32),
            pltpu.VMEM((n_dev, sent_rows, sent_cols), jnp.bfloat16),
        ),
        compiler_params=small,
    )(counts, *in_vmem(own, own_far, pair, pair_far), slide_gain, embed_proj, proj_far)
    sent = lax.all_to_all(sent, "dev", split_axis=0, concat_axis=0, tiled=True)
    hbm = pl.BlockSpec(memory_space=pltpu.HBM)
    far_shape = (slide_wo.shape[0], out_cols)
    kept = [slide_wk.shape] * 4 + [slide_wo.shape, far_shape]
    query, many, *weights = pl.pallas_call(
        functools.partial(query_kernel, heads),
        in_specs=[vmem] * 2 + [hbm] * 6,
        out_specs=[vmem] * (2 + len(kept)),
        out_shape=[
            pltpu.VMEM((heads * QROWS, out_width), jnp.bfloat16),
            pltpu.VMEM(many.shape, many.dtype),
            *[pltpu.VMEM(shape, jnp.bfloat16) for shape in kept],
        ],
        scratch_shapes=[
            pltpu.VMEM((2, *slide_wq.shape), jnp.bfloat16),
            pltpu.SemaphoreType.DMA((3 + len(kept),)),
        ],
        compiler_params=small,
    )(*in_vmem(mixed), slide_gain, *in_hbm(pack_far, *slide_weights, many))
    slide_out = pl.pallas_call(
        functools.partial(slide_kernel, heads),
        in_specs=[smem] + [vmem] * 10,
        out_specs=vmem,
        out_shape=jax.ShapeDtypeStruct((slot_count, out_cols), jnp.bfloat16),
        scratch_shapes=[pltpu.VMEM((n_dev * slot_count, out_width), jnp.float32)],
        compiler_params=small,
    )(counts, *in_vmem(sent, mixed, query, *weights, many))
    return (tile_embed, slide_out)


def solution(mesh):
    placed = (
        P(("grp", "dev"), None, None),
        P("grp"),
        P("grp"),
        P(),
        P(),
        P("dev", "sub"),
        P("dev", "sub"),
        P("sub", None),
        P(),
        P(None, "sub"),
        P(None, "sub"),
        P(None, "sub"),
        P("sub", None),
    )
    return jax.shard_map(
        on_device,
        mesh=mesh,
        in_specs=placed,
        out_specs=(P(("grp", "dev"), "sub"), P(("grp", "dev"), "sub")),
        check_vma=False,
    )
```

```python
import functools
import math

import jax
import jax.numpy as jnp
from jax import lax
from jax.experimental import pallas as pl
from jax.experimental.pallas import tpu as pltpu
from jax.sharding import PartitionSpec as P

HD = 64
EPSILON = 1e-06
FLOOR = -1e30
QROWS = 8
NORM_ROWS = 16
NORM_PIECE = 128
NORM_UNROLL = 8
LANES = 128
UNIT_ROWS = 16
ROW_TILE = 16
MXU = 256
MLP_VMEM = 24 * 1024 * 1024
NORM_VMEM = 12 * 1024 * 1024
SMALL_VMEM = 4 * 1024 * 1024


def normed(rows_in, gains):
    average = jnp.mean(rows_in, axis=-1, keepdims=True)
    centred = rows_in - average
    variance = jnp.mean(centred * centred, axis=-1, keepdims=True)
    return (centred * lax.rsqrt(variance + EPSILON) * gains).astype(jnp.bfloat16)


def in_hbm(*arrays):
    return [pltpu.with_memory_space_constraint(x, pltpu.HBM) for x in arrays]


def in_vmem(*arrays):
    return [pltpu.with_memory_space_constraint(x, pltpu.VMEM) for x in arrays]


def start_kernel(parts, *refs):
    tiles_ref, gain_ref, gate_ref, up_ref, *slide_refs = refs[:8]
    out_ref, pack_ref, *block_refs = refs[8 : 10 + len(parts)]
    (
        rows,
        hidden,
        gain,
        average,
        scale,
        whole,
        whole_slide,
        in_sems,
        out_sems,
        block_sems,
        slide_sems,
        gain_sem,
    ) = refs[10 + len(parts) :]
    core = lax.axis_index("sub")
    pieces, piece = rows.shape[:2]
    half, length = tiles_ref.shape[0] // 2, tiles_ref.shape[1]
    half_cols = gate_ref.shape[1] // 2
    gain_copy = pltpu.make_async_copy(gain_ref, gain, gain_sem)
    copies = [
        pltpu.make_async_copy(
            tiles_ref.at[core * half + i * piece // length, pl.ds(i * piece % length, piece)],
            rows.at[i],
            in_sems.at[i],
        )
        for i in range(pieces)
    ]
    stores = [
        pltpu.make_async_copy(hidden.at[i], out_ref.at[pl.ds(i * piece, piece)], out_sems.at[i])
        for i in range(pieces)
    ]
    packs = [
        pltpu.make_async_copy(ref, whole.at[i], block_sems.at[i])
        for i, ref in enumerate((gate_ref, up_ref))
    ]
    selects = []
    columns = pl.ds(pl.multiple_of(lax.rem(lax.axis_index("grp"), 2) * half_cols, LANES), half_cols)
    for k, (part, block_ref) in enumerate(zip(parts, block_refs)):
        for i, ref in enumerate((gate_ref, up_ref)):
            selects.append((block_ref, i * half_cols, whole.at[i, part, columns]))
    cols = pack_ref.shape[1]
    others = pl.ds(pl.multiple_of((1 - core) * cols, LANES), cols)
    at = 0
    for k, ref in enumerate(slide_refs):
        place = pack_ref.at[at : at + ref.shape[0]]
        if ref.shape[1] == cols:
            packs.append(pltpu.make_async_copy(ref, place, slide_sems.at[k]))
        else:
            packs.append(pltpu.make_async_copy(ref, whole_slide, slide_sems.at[k]))
            selects.append((place, 0, whole_slide.at[:, others]))
        at += ref.shape[0]
    for copy in [gain_copy] + copies + packs:
        copy.start()
    gain_copy.wait()
    gains = gain[...].reshape(1, -1)
    width = gains.shape[1]

    def grouped(function):
        def some_rows(j, carry):
            function(pl.ds(pl.multiple_of(j * NORM_ROWS, NORM_ROWS), NORM_ROWS))
            return carry

        lax.fori_loop(0, rows.shape[1] // NORM_ROWS, some_rows, 0, unroll=NORM_UNROLL)

    def lane_sum(values):
        total = values[:, :LANES]
        for k in range(LANES, width, LANES):
            total = total + values[:, k : k + LANES]
        return jnp.sum(total, axis=1, keepdims=True)

    for i in range(rows.shape[0]):
        copies[i].wait()

        def sum_rows(here):
            total = lane_sum(rows[i, here, :].astype(jnp.float32))
            average[here, :] = jnp.broadcast_to(total * (1.0 / width), (NORM_ROWS, LANES))

        def scale_rows(here):
            centred = rows[i, here, :].astype(jnp.float32) - average[here, :1]
            variance = lane_sum(centred * centred) * (1.0 / width)
            scale[here, :] = jnp.broadcast_to(
                lax.rsqrt(variance + EPSILON), (NORM_ROWS, LANES)
            )

        def norm_rows(here):
            centred = rows[i, here, :].astype(jnp.float32) - average[here, :1]
            hidden[i, here, :] = (centred * scale[here, :1] * gains).astype(jnp.bfloat16)

        grouped(sum_rows)
        grouped(scale_rows)
        grouped(norm_rows)
        stores[i].start()
    for copy in packs:
        copy.wait()
    for place, at, source in selects:
        place[:, at : at + source.shape[1]] = source[...]
    for copy in stores:
        copy.wait()


def start_work(tiles, gain, gate_weight, up_weight, slide_weights, parts):
    slot_count, length, width = tiles.shape
    half = slot_count // 2
    pieces = half * length // NORM_PIECE
    hbm = pl.BlockSpec(memory_space=pltpu.HBM)
    vmem = pl.BlockSpec(memory_space=pltpu.VMEM)
    cols = gate_weight.shape[1]
    pack = (sum(w.shape[0] for w in slide_weights), slide_weights[0].shape[1])
    return pl.pallas_call(
        functools.partial(start_kernel, parts),
        in_specs=[hbm] * (4 + len(slide_weights)),
        out_specs=[hbm] + [vmem] * (1 + len(parts)),
        out_shape=[
            pltpu.HBM((half * length, width), jnp.bfloat16),
            pltpu.VMEM(pack, jnp.bfloat16),
            *[pltpu.VMEM((part.stop - part.start, cols), jnp.bfloat16) for part in parts],
        ],
        scratch_shapes=[
            pltpu.VMEM((pieces, NORM_PIECE, width), jnp.bfloat16),
            pltpu.VMEM((pieces, NORM_PIECE, width), jnp.bfloat16),
            pltpu.VMEM((width,), jnp.float32),
            pltpu.VMEM((NORM_PIECE, LANES), jnp.float32),
            pltpu.VMEM((NORM_PIECE, LANES), jnp.float32),
            pltpu.VMEM((2, *gate_weight.shape), jnp.bfloat16),
            pltpu.VMEM(slide_weights[-1].shape, jnp.bfloat16),
            pltpu.SemaphoreType.DMA((pieces,)),
            pltpu.SemaphoreType.DMA((pieces,)),
            pltpu.SemaphoreType.DMA((2,)),
            pltpu.SemaphoreType.DMA((len(slide_weights),)),
            pltpu.SemaphoreType.DMA(()),
        ],
        compiler_params=pltpu.CompilerParams(vmem_limit_bytes=NORM_VMEM),
        cost_estimate=pl.CostEstimate(flops=0, bytes_accessed=0, transcendentals=0),
    )(*in_hbm(tiles, gain, gate_weight, up_weight, *slide_weights))


def after(value, *others):
    return lax.optimization_barrier((value, *others))[0]


class Layout:
    def __init__(self, n_dev, ny, depth):
        self.ny, self.nz, self.depth = ny, n_dev // ny, depth
        self.pair = ny * depth
        self.relative = self.pair % LANES == 0
        self.early_steps = self.nz - 1
        self.early = self.early_steps * self.pair // MXU * MXU if self.relative else 0
        cut = max(ROW_TILE, depth // 2 // ROW_TILE * ROW_TILE)
        self.parts = [slice(0, cut), slice(cut, depth)]
        self.width = n_dev * depth

    def place(self):
        me = lax.axis_index("dev")
        my_z = me // self.ny
        return my_z, me - my_z * self.ny

    def ring(self):
        return [*range(0, self.nz, 2), *range(self.nz - 1, 0, -2)]

    def source(self, step):
        my_z, _ = self.place()
        spot = jnp.where(my_z % 2 == 0, my_z // 2, self.nz - (my_z + 1) // 2)
        spot = spot - step
        spot = jnp.where(spot < 0, spot + self.nz, spot)
        return jnp.where(spot < self.nz // 2, 2 * spot, 2 * (self.nz - spot) - 1)

    def block_copies(self, blocks, weights, sems, end=None):
        _, my_y = self.place()
        copies = []
        n_parts = len(self.parts)
        first = 0 if end is None else end - len(blocks) // n_parts // self.ny
        for k, block in enumerate(blocks):
            step, flip, part = first + k // n_parts // self.ny, k // n_parts % self.ny, k % n_parts
            y = 1 - my_y if flip else my_y
            at = step if self.relative else self.source(step)
            here = self.parts[part]
            start = pl.multiple_of(at * self.pair + y * self.depth + here.start, ROW_TILE)
            place = weights.at[pl.ds(start, here.stop - here.start)]
            copies.append(pltpu.make_async_copy(block, place, sems.at[k]))
        return copies

    def row_copies(self, tiles_ref, rows, sems, steps):
        if not self.relative:
            return [pltpu.make_async_copy(tiles_ref, rows, sems.at[0])]
        copies = []
        for step in steps:
            start = pl.multiple_of(self.source(step) * self.pair, LANES)
            copies.append(
                pltpu.make_async_copy(
                    tiles_ref.at[:, pl.ds(start, self.pair)],
                    rows.at[:, step * self.pair : (step + 1) * self.pair],
                    sems.at[step],
                )
            )
        return copies


def gated_means(both, out_ref, at, length):
    cols = both.shape[1] // 2
    for tile in range(both.shape[0] // length):
        total = jnp.zeros((8, cols), jnp.float32)
        for first in range(tile * length, (tile + 1) * length, UNIT_ROWS):
            gate = both[first : first + UNIT_ROWS, :cols]
            up_part = both[first : first + UNIT_ROWS, cols:]
            silu = gate * (0.5 * jnp.tanh(0.5 * gate) + 0.5)
            gated = (silu * up_part).astype(jnp.bfloat16).astype(jnp.float32)
            total = total + jnp.sum(gated.reshape(UNIT_ROWS // 8, 8, cols), axis=0)
        out_ref[at + tile : at + tile + 1, :] = jnp.sum(total, axis=0, keepdims=True) * (
            1.0 / length
        )


def product(out, rows, weights, first, last, more=None):
    for at in range(0, rows.shape[0], MXU):
        here = slice(at, at + MXU)
        both = jnp.dot(
            rows[here, first:last], weights[first:last, :], preferred_element_type=jnp.float32
        )
        out[here, :] = both if more is None else both + more[here, :]


def early_kernel(layout, *refs):
    steps = range(layout.early_steps)
    n_blocks = len(steps) * layout.ny * len(layout.parts)
    blocks, tile_refs = refs[:n_blocks], refs[n_blocks : n_blocks + 2]
    out_ref, weights, rows, weight_sems, row_sems = refs[n_blocks + 2 :]
    loads = layout.block_copies(blocks, weights, weight_sems)
    row_loads = [
        layout.row_copies(ref, rows.at[i], row_sems.at[i], steps)
        for i, ref in enumerate(tile_refs)
    ]
    late_loads = [
        copy
        for i, ref in enumerate(tile_refs)
        for copy in layout.row_copies(
            ref, rows.at[i], row_sems.at[i], range(layout.early_steps, layout.nz)
        )
    ]
    for copy in row_loads[0] + loads + row_loads[1] + late_loads:
        copy.start()
    for copy in loads:
        copy.wait()
    for i in range(2):
        for copy in row_loads[i]:
            copy.wait()
        product(out_ref.at[i], rows.at[i], weights, 0, layout.early)
    for copy in late_loads:
        copy.wait()


def early_mlp(layout, blocks, tiles):
    n_rows = tiles[0].shape[0]
    cols = blocks[0].shape[1]
    hbm = pl.BlockSpec(memory_space=pltpu.HBM)
    vmem = pl.BlockSpec(memory_space=pltpu.VMEM)
    return pl.pallas_call(
        functools.partial(early_kernel, layout),
        in_specs=[hbm] * (len(blocks) + 2),
        out_specs=(vmem, vmem, vmem),
        out_shape=(
            pltpu.VMEM((2, n_rows, cols), jnp.float32),
            pltpu.VMEM((layout.width, cols), jnp.bfloat16),
            pltpu.VMEM((2, n_rows, layout.width), jnp.bfloat16),
        ),
        scratch_shapes=[
            pltpu.SemaphoreType.DMA((len(blocks),)),
            pltpu.SemaphoreType.DMA((2, layout.nz)),
        ],
        compiler_params=pltpu.CompilerParams(vmem_limit_bytes=MLP_VMEM),
        cost_estimate=pl.CostEstimate(
            flops=4 * n_rows * layout.early * cols,
            bytes_accessed=2 * layout.early * (cols + 2 * n_rows) + 8 * n_rows * cols,
            transcendentals=0,
        ),
    )(*in_hbm(*blocks, *tiles))


def packed(mine, others):
    low = lax.axis_index("sub") == 0
    rows = jnp.concatenate([jnp.where(low, mine, others), jnp.where(low, others, mine)], axis=0)
    return jnp.concatenate(
        [rows[:, k : k + LANES] for k in range(0, rows.shape[1], LANES)], axis=0
    ).astype(jnp.bfloat16)


def middle_kernel(layout, length, n_blocks, n_tiles, *refs):
    blocks, tile_refs = refs[:n_blocks], refs[n_blocks : n_blocks + n_tiles]
    early_refs = refs[n_blocks + n_tiles : -9]
    pair_ref, weights, own_ref, rows, even, odd, means, weight_sems, row_sems = refs[-9:]
    early = layout.early
    loads = layout.block_copies(blocks, weights, weight_sems, layout.nz)
    row_loads = [
        layout.row_copies(ref, rows.at[i], row_sems.at[i], range(layout.nz))
        for i, ref in enumerate(tile_refs)
    ]
    for copy in [copy for copies in [loads, *row_loads] for copy in copies]:
        copy.start()
    for copy in loads:
        copy.wait()
    units = [(early_refs[2].at[i], early_refs[0].at[i], []) for i in range(2)] if early else []
    units += [(rows.at[i], None, row_loads[i]) for i in range(n_tiles)]
    pending = None
    for i, (unit, more, waits) in enumerate(units):
        for copy in waits:
            copy.wait()
        for j in range(unit.shape[0] // length):
            here = slice(j * length, (j + 1) * length)
            tile = unit.shape[0] // length * i + j
            both = (even, odd)[tile % 2]
            if more is None:
                product(both, unit.at[here], weights, 0, layout.width)
            else:
                product(both, unit.at[here], weights, early, layout.width, more.at[here])
            if pending is not None:
                gated_means(*pending, length)
            pending = (both, means, tile)
    gated_means(*pending, length)
    half = means.shape[0] // 3
    own_ref[...] = packed(means[:half, :], means[half : 2 * half, :])
    pair_ref[...] = means[2 * half :, :]


def middle_mlp(layout, blocks, tiles, early, length):
    n_rows, width = tiles[0].shape
    cols = blocks[0].shape[1]
    half = n_rows // length
    tiles = tiles[2:] if early else tiles
    vmem = pl.BlockSpec(memory_space=pltpu.VMEM)
    return pl.pallas_call(
        functools.partial(middle_kernel, layout, length, len(blocks), len(tiles)),
        in_specs=[pl.BlockSpec(memory_space=pl.ANY)] * (len(blocks) + len(tiles))
        + [vmem] * len(early),
        out_specs=(vmem, vmem, vmem),
        out_shape=(
            pltpu.VMEM((half, cols // 2), jnp.float32),
            pltpu.VMEM((width, cols), jnp.bfloat16),
            jax.ShapeDtypeStruct((half * cols // LANES, LANES), jnp.bfloat16),
        ),
        input_output_aliases={len(blocks) + len(tiles) + 1: 1} if early else {},
        scratch_shapes=[
            pltpu.VMEM((len(tiles), n_rows, width), jnp.bfloat16),
            pltpu.VMEM((length, cols), jnp.float32),
            pltpu.VMEM((length, cols), jnp.float32),
            pltpu.VMEM((3 * half, cols // 2), jnp.float32),
            pltpu.SemaphoreType.DMA((len(blocks),)),
            pltpu.SemaphoreType.DMA((len(tiles), layout.nz)),
        ],
        compiler_params=pltpu.CompilerParams(vmem_limit_bytes=MLP_VMEM),
        cost_estimate=pl.CostEstimate(
            flops=4 * n_rows * width * cols,
            bytes_accessed=2 * (3 * n_rows * width + width * cols),
            transcendentals=0,
        ),
    )(*blocks, *(tiles if early else in_hbm(*tiles)), *in_vmem(*early))


def last_kernel(layout, length, means_ref, weights, tiles_ref, out_ref, rows, both, means, row_sems):
    row_loads = layout.row_copies(tiles_ref, rows, row_sems, range(layout.nz))
    for copy in row_loads:
        copy.start()
    for copy in row_loads:
        copy.wait()
    half = rows.shape[0] // length
    for i in range(half):
        here = slice(i * length, (i + 1) * length)
        product(both[i], rows.at[here], weights, 0, layout.width)
        if i:
            gated_means(both[i - 1], means, i - 1, length)
    gated_means(both[half - 1], means, half - 1, length)
    out_ref[...] = packed(means_ref[...], means[...])


def last_mlp(layout, means, weights, tiles, length):
    n_rows, width = tiles.shape
    cols = weights.shape[1]
    half = n_rows // length
    any_spec = pl.BlockSpec(memory_space=pl.ANY)
    vmem = pl.BlockSpec(memory_space=pltpu.VMEM)
    return pl.pallas_call(
        functools.partial(last_kernel, layout, length),
        in_specs=[vmem, vmem, any_spec],
        out_specs=vmem,
        out_shape=jax.ShapeDtypeStruct((half * cols // LANES, LANES), jnp.bfloat16),
        scratch_shapes=[
            pltpu.VMEM((n_rows, width), jnp.bfloat16),
            [pltpu.VMEM((length, cols), jnp.float32) for _ in range(half)],
            pltpu.VMEM((half, cols // 2), jnp.float32),
            pltpu.SemaphoreType.DMA((layout.nz,)),
        ],
        compiler_params=pltpu.CompilerParams(vmem_limit_bytes=MLP_VMEM),
        cost_estimate=pl.CostEstimate(
            flops=2 * n_rows * width * cols,
            bytes_accessed=2 * (n_rows * width + width * cols),
            transcendentals=0,
        ),
    )(*in_vmem(means, weights), tiles)


def small_mod(value, rate):
    return jnp.where(
        rate == 1,
        0,
        jnp.where(rate == 2, value & 1, jnp.where(rate == 3, lax.rem(value, 3), value & 3)),
    )


def multiplicity_kernel(n_dev, slot_count, heads, counts_ref, slide_ref, rates_ref, out_ref):
    me, core = lax.axis_index("dev"), lax.axis_index("sub")
    shape = out_ref.shape
    row = lax.broadcasted_iota(jnp.int32, shape, 0)
    col = lax.broadcasted_iota(jnp.int32, shape, 1)
    head = row // QROWS + core * (heads // 2)
    head = jnp.where(head >= heads, head - heads, head)
    query = row % QROWS
    device, slot = col // slot_count, col % slot_count
    rate = jnp.full(shape, 1, jnp.int32)
    for h in range(heads):
        rate = jnp.where(head == h, rates_ref[h], rate)
    my_slide = slide_ref[me]
    first = me
    count = jnp.zeros(shape, jnp.int32)
    slide = jnp.zeros(shape, jnp.int32)
    for k in reversed(range(n_dev)):
        first = jnp.where(slide_ref[k] == my_slide, k, first)
        count = jnp.where(device == k, counts_ref[k], count)
        slide = jnp.where(device == k, slide_ref[k], slide)
    offset = small_mod(head, rate)
    query_position = (me - first) * slot_count + query
    key_position = (device - first) * slot_count + slot
    valid = slot < count
    near = jnp.where((device == me) & valid, 1.0, 0.0)
    far = jnp.where(
        (slide == my_slide)
        & valid
        & (small_mod(query_position, rate) == offset)
        & (small_mod(key_position, rate) == offset),
        1.0,
        0.0,
    )
    out_ref[...] = near + far


def embed_kernel(
    counts_ref,
    own_ref,
    own_far_ref,
    pair_ref,
    pair_far_ref,
    gain_ref,
    near_ref,
    far_ref,
    embed_ref,
    mixed_ref,
    sent_ref,
):
    slot_count, half = embed_ref.shape
    n_blocks = half // 2 // LANES
    low = lax.rem(lax.axis_index("grp"), 2) == 0
    count = counts_ref[lax.axis_index("dev")]

    def features(mine_ref, theirs_ref):
        sides = []
        for ref in (mine_ref, theirs_ref):
            part = ref[...].astype(jnp.float32)
            pieces = [part[k * slot_count : (k + 1) * slot_count] for k in range(n_blocks)]
            sides.append(jnp.concatenate(pieces, axis=1))
        mine, theirs = sides
        rows = jnp.concatenate(
            [jnp.where(low, mine, theirs), jnp.where(low, theirs, mine)], axis=1
        )
        slot = lax.broadcasted_iota(jnp.int32, rows.shape, 0)
        return jnp.where(slot < count, rows, 0.0).astype(jnp.bfloat16)

    near = features(own_ref, pair_ref)
    far = features(own_far_ref, pair_far_ref)
    embed_ref[...] = near
    mixed = jnp.dot(near, near_ref[...], preferred_element_type=jnp.float32) + jnp.dot(
        far, far_ref[...], preferred_element_type=jnp.float32
    )
    mixed_ref[...] = jnp.concatenate([mixed, mixed], axis=0)
    hidden = normed(mixed, gain_ref[...].reshape(1, -1)).astype(jnp.float32)
    width = sent_ref.shape[2]
    pieces = [hidden[:, k : k + width] for k in range(0, hidden.shape[1], width)]
    pieces += [jnp.zeros_like(pieces[0])] * (sent_ref.shape[1] // slot_count - len(pieces))
    sent = jnp.concatenate(pieces, axis=0).astype(jnp.bfloat16)
    for k in range(sent_ref.shape[0]):
        sent_ref[k] = sent


def project(rows, near_ref, far_ref):
    return jnp.concatenate(
        [
            jnp.dot(rows, near_ref[...], preferred_element_type=jnp.float32),
            jnp.dot(rows, far_ref[...], preferred_element_type=jnp.float32),
        ],
        axis=1,
    )


def heads_of(shape):
    return (
        lax.broadcasted_iota(jnp.int32, shape, 0) // QROWS
        == lax.broadcasted_iota(jnp.int32, shape, 1) // HD
    )


def query_kernel(heads, mixed_ref, gain_ref, far_ref, *refs):
    near_refs, (many_ref, out_ref, many, *kept), (wq, sems) = refs[:4], refs[4:-2], refs[-2:]
    places = [wq.at[0], wq.at[1], *kept]
    copies = []
    at = 0
    for k, near in enumerate(near_refs):
        far = far_ref.at[at : at + near.shape[0]]
        at += near.shape[0]
        for i, source in enumerate((near, far)):
            copies.append(pltpu.make_async_copy(source, places[2 * k + i], sems.at[2 * k + i]))
    copies.append(pltpu.make_async_copy(many_ref, many, sems.at[len(copies)]))
    for copy in copies:
        copy.start()
    hidden = normed(mixed_ref[...], gain_ref[...].reshape(1, -1))
    for copy in copies[:2]:
        copy.wait()
    query = project(hidden, wq.at[0], wq.at[1])
    spread = jnp.concatenate([query] * heads, axis=0)
    out_ref[...] = jnp.where(heads_of(spread.shape), spread, 0.0).astype(jnp.bfloat16)
    for copy in copies[2:]:
        copy.wait()


def slide_kernel(
    heads,
    counts_ref,
    sent_ref,
    mixed_ref,
    query_ref,
    wk_ref,
    wk_far_ref,
    wv_ref,
    wv_far_ref,
    wo_ref,
    wo_far_ref,
    many_ref,
    out_ref,
    rows,
):
    slot_count, half = out_ref.shape
    core = lax.axis_index("sub")
    count = counts_ref[lax.axis_index("dev")]
    width = sent_ref.shape[2]
    for k in range(sent_ref.shape[0]):
        sent = sent_ref[k].astype(jnp.float32)
        rows[k * slot_count : (k + 1) * slot_count, :] = jnp.concatenate(
            [
                sent[j * slot_count : (j + 1) * slot_count]
                for j in range(rows.shape[1] // width)
            ],
            axis=1,
        )
    hidden = rows[...].astype(jnp.bfloat16)
    keys = project(hidden, wk_ref, wk_far_ref).astype(jnp.bfloat16)
    scores = lax.dot_general(
        query_ref[...], keys, (((1,), (1,)), ((), ())), preferred_element_type=jnp.float32
    ) * (1.0 / math.sqrt(HD))
    values = project(hidden, wv_ref, wv_far_ref).astype(jnp.bfloat16)
    many = many_ref[...]
    masked = jnp.where(many > 0.0, scores, FLOOR)
    weights = many * jnp.exp(masked - jnp.max(masked, axis=1, keepdims=True))
    weights = weights / jnp.sum(weights, axis=1, keepdims=True)
    context = jnp.dot(weights.astype(jnp.bfloat16), values, preferred_element_type=jnp.float32)
    context = jnp.where(heads_of(context.shape), context, 0.0)
    context = context.reshape(heads, QROWS, context.shape[1])
    context = jnp.sum(context, axis=0).astype(jnp.bfloat16)
    columns = pl.ds(pl.multiple_of(core * half, LANES), half)
    attended = jnp.dot(
        context[:, :half], wo_ref[:, columns], preferred_element_type=jnp.float32
    ) + jnp.dot(context[:, half:], wo_far_ref[...], preferred_element_type=jnp.float32)
    total = mixed_ref[:, columns] + attended
    slot = lax.broadcasted_iota(jnp.int32, total.shape, 0)
    total = jnp.where(slot < count, total, 0.0)
    out_ref[...] = total[:slot_count].astype(jnp.bfloat16)


def on_device(
    tiles,
    counts,
    slide_of,
    rates,
    tile_gain,
    gate_weight,
    up_weight,
    embed_proj,
    slide_gain,
    slide_wq,
    slide_wk,
    slide_wv,
    slide_wo,
):
    slot_count, length, width = tiles.shape
    hidden_cols = gate_weight.shape[1]
    n_grp, n_dev, n_sub = (lax.axis_size(a) for a in ("grp", "dev", "sub"))
    ny = 2
    nz = n_dev // ny
    heads = slide_wq.shape[1] * n_sub // HD
    core = lax.axis_index("sub")

    to_pair = [(g, g ^ 1) for g in range(n_grp)]
    to_sibling = [(s, s ^ 1) for s in range(n_sub)]
    along_y = [(d, d ^ 1) for d in range(n_dev)]

    layout = Layout(n_dev, ny, gate_weight.shape[0])
    ring = layout.ring()
    along_z = [
        (z * ny + y, ring[(i + 1) % nz] * ny + y) for i, z in enumerate(ring) for y in range(ny)
    ]
    slide_weights = [slide_wq, slide_wk, slide_wv, slide_wo]
    first, pack, *held = start_work(
        tiles, tile_gain, gate_weight, up_weight, slide_weights, layout.parts
    )
    second = lax.ppermute(first, "sub", to_sibling)
    pair_first = lax.ppermute(first, "grp", to_pair)
    proj_far = lax.ppermute(embed_proj, "sub", to_sibling)
    pack_far = lax.ppermute(pack, "sub", to_sibling)
    out_cols = slide_wo.shape[1] // n_sub
    smem = pl.BlockSpec(memory_space=pltpu.SMEM)
    vmem = pl.BlockSpec(memory_space=pltpu.VMEM)
    many = pl.pallas_call(
        functools.partial(multiplicity_kernel, n_dev, slot_count, heads),
        in_specs=[smem] * 3,
        out_specs=vmem,
        out_shape=jax.ShapeDtypeStruct((heads * QROWS, n_dev * slot_count), jnp.float32),
        compiler_params=pltpu.CompilerParams(vmem_limit_bytes=SMALL_VMEM),
    )(counts, slide_of, rates)

    held[1] = after(held[1], proj_far, second)
    steps = []
    last = None
    for step in range(nz):
        sent = []
        for part in range(len(held)):
            if step:
                arrived = lax.ppermute(held[part], "dev", along_z)
                others = [steps[-1][len(held) + part]]
                if (step, part) == (nz - 1, 0):
                    others += [many]
                if last is not None:
                    others.append(last)
                held[part] = last = after(arrived, *others)
            sent.append(lax.ppermute(held[part], "dev", along_y))
        steps.append([*held, *sent])
    blocks = [block for step in steps for block in step]
    early = []
    if layout.relative:
        n_early = layout.early_steps * len(steps[0])
        early = early_mlp(layout, blocks[:n_early], [after(first, last), second])
        blocks = blocks[n_early:]
    pair_first = after(pair_first, *steps[-1][-2:], *early)
    pair_second = lax.ppermute(pair_first, "sub", to_sibling)
    means, weights, own = middle_mlp(
        layout, blocks, [first, second, pair_first], early, length
    )
    own_far = lax.ppermute(own, "sub", to_sibling)
    pair = last_mlp(layout, means, weights, pair_second, length)
    across = [
        (g * n_sub + s, (g ^ 1) * n_sub + (s ^ 1)) for g in range(n_grp) for s in range(n_sub)
    ]
    pair_far = lax.ppermute(pair, ("grp", "sub"), across)
    pair = lax.ppermute(pair, "grp", to_pair)

    out_width = embed_proj.shape[1]
    sent_rows = 16
    sent_cols = 2 * LANES
    small = pltpu.CompilerParams(vmem_limit_bytes=SMALL_VMEM)
    tile_embed, mixed, sent = pl.pallas_call(
        embed_kernel,
        in_specs=[smem] + [vmem] * 7,
        out_specs=(vmem, vmem, vmem),
        out_shape=(
            jax.ShapeDtypeStruct((slot_count, hidden_cols), jnp.bfloat16),
            pltpu.VMEM((QROWS, out_width), jnp.float32),
            pltpu.VMEM((n_dev, sent_rows, sent_cols), jnp.bfloat16),
        ),
        compiler_params=small,
    )(counts, *in_vmem(own, own_far, pair, pair_far), slide_gain, embed_proj, proj_far)
    sent = lax.all_to_all(sent, "dev", split_axis=0, concat_axis=0, tiled=True)
    hbm = pl.BlockSpec(memory_space=pltpu.HBM)
    far_shape = (slide_wo.shape[0], out_cols)
    kept = [slide_wk.shape] * 4 + [slide_wo.shape, far_shape]
    query, many, *weights = pl.pallas_call(
        functools.partial(query_kernel, heads),
        in_specs=[vmem] * 2 + [hbm] * 6,
        out_specs=[vmem] * (2 + len(kept)),
        out_shape=[
            pltpu.VMEM((heads * QROWS, out_width), jnp.bfloat16),
            pltpu.VMEM(many.shape, many.dtype),
            *[pltpu.VMEM(shape, jnp.bfloat16) for shape in kept],
        ],
        scratch_shapes=[
            pltpu.VMEM((2, *slide_wq.shape), jnp.bfloat16),
            pltpu.SemaphoreType.DMA((3 + len(kept),)),
        ],
        compiler_params=small,
    )(*in_vmem(mixed), slide_gain, *in_hbm(pack_far, *slide_weights, many))
    slide_out = pl.pallas_call(
        functools.partial(slide_kernel, heads),
        in_specs=[smem] + [vmem] * 10,
        out_specs=vmem,
        out_shape=jax.ShapeDtypeStruct((slot_count, out_cols), jnp.bfloat16),
        scratch_shapes=[pltpu.VMEM((n_dev * slot_count, out_width), jnp.float32)],
        compiler_params=small,
    )(counts, *in_vmem(sent, mixed, query, *weights, many))
    return (tile_embed, slide_out)


def solution(mesh):
    placed = (
        P(("grp", "dev"), None, None),
        P("grp"),
        P("grp"),
        P(),
        P(),
        P("dev", "sub"),
        P("dev", "sub"),
        P("sub", None),
        P(),
        P(None, "sub"),
        P(None, "sub"),
        P(None, "sub"),
        P("sub", None),
    )
    return jax.shard_map(
        on_device,
        mesh=mesh,
        in_specs=placed,
        out_specs=(P(("grp", "dev"), "sub"), P(("grp", "dev"), "sub")),
        check_vma=False,
    )
```

```python
import functools
import math

import jax
import jax.numpy as jnp
from jax import lax
from jax.experimental import pallas as pl
from jax.experimental.pallas import tpu as pltpu
from jax.sharding import PartitionSpec as P

HD = 64
EPSILON = 1e-06
FLOOR = -1e30
QROWS = 8
NORM_ROWS = 16
NORM_PIECE = 128
NORM_UNROLL = 8
LANES = 128
UNIT_ROWS = 16
ROW_TILE = 16
MXU = 256
MLP_VMEM = 24 * 1024 * 1024
NORM_VMEM = 12 * 1024 * 1024
SMALL_VMEM = 4 * 1024 * 1024


def normed(rows_in, gains):
    average = jnp.mean(rows_in, axis=-1, keepdims=True)
    centred = rows_in - average
    variance = jnp.mean(centred * centred, axis=-1, keepdims=True)
    return (centred * lax.rsqrt(variance + EPSILON) * gains).astype(jnp.bfloat16)


def in_hbm(*arrays):
    return [pltpu.with_memory_space_constraint(x, pltpu.HBM) for x in arrays]


def in_vmem(*arrays):
    return [pltpu.with_memory_space_constraint(x, pltpu.VMEM) for x in arrays]


def start_kernel(parts, *refs):
    tiles_ref, gain_ref, gate_ref, up_ref, *slide_refs = refs[:8]
    out_ref, pack_ref, *block_refs = refs[8 : 10 + len(parts)]
    (
        rows,
        gain,
        average,
        scale,
        whole,
        whole_slide,
        in_sems,
        block_sems,
        slide_sems,
        gain_sem,
    ) = refs[10 + len(parts) :]
    core = lax.axis_index("sub")
    pieces, piece = rows.shape[:2]
    half, length = tiles_ref.shape[0] // 2, tiles_ref.shape[1]
    half_cols = gate_ref.shape[1] // 2
    gain_copy = pltpu.make_async_copy(gain_ref, gain, gain_sem)
    copies = [
        pltpu.make_async_copy(
            tiles_ref.at[core * half + i * piece // length, pl.ds(i * piece % length, piece)],
            rows.at[i],
            in_sems.at[i],
        )
        for i in range(pieces)
    ]
    packs = [
        pltpu.make_async_copy(ref, whole.at[i], block_sems.at[i])
        for i, ref in enumerate((gate_ref, up_ref))
    ]
    selects = []
    columns = pl.ds(pl.multiple_of(lax.rem(lax.axis_index("grp"), 2) * half_cols, LANES), half_cols)
    for k, (part, block_ref) in enumerate(zip(parts, block_refs)):
        for i, ref in enumerate((gate_ref, up_ref)):
            selects.append((block_ref, i * half_cols, whole.at[i, part, columns]))
    cols = pack_ref.shape[1]
    others = pl.ds(pl.multiple_of((1 - core) * cols, LANES), cols)
    at = 0
    for k, ref in enumerate(slide_refs):
        place = pack_ref.at[at : at + ref.shape[0]]
        if ref.shape[1] == cols:
            packs.append(pltpu.make_async_copy(ref, place, slide_sems.at[k]))
        else:
            packs.append(pltpu.make_async_copy(ref, whole_slide, slide_sems.at[k]))
            selects.append((place, 0, whole_slide.at[:, others]))
        at += ref.shape[0]
    for copy in [gain_copy] + copies + packs:
        copy.start()
    gain_copy.wait()
    gains = gain[...].reshape(1, -1)
    width = gains.shape[1]

    def grouped(function):
        def some_rows(j, carry):
            function(pl.ds(pl.multiple_of(j * NORM_ROWS, NORM_ROWS), NORM_ROWS))
            return carry

        lax.fori_loop(0, rows.shape[1] // NORM_ROWS, some_rows, 0, unroll=NORM_UNROLL)

    def lane_sum(values):
        total = values[:, :LANES]
        for k in range(LANES, width, LANES):
            total = total + values[:, k : k + LANES]
        return jnp.sum(total, axis=1, keepdims=True)

    for i in range(rows.shape[0]):
        copies[i].wait()

        def sum_rows(here):
            total = lane_sum(rows[i, here, :].astype(jnp.float32))
            average[here, :] = jnp.broadcast_to(total * (1.0 / width), (NORM_ROWS, LANES))

        def scale_rows(here):
            centred = rows[i, here, :].astype(jnp.float32) - average[here, :1]
            variance = lane_sum(centred * centred) * (1.0 / width)
            scale[here, :] = jnp.broadcast_to(
                lax.rsqrt(variance + EPSILON), (NORM_ROWS, LANES)
            )

        def norm_rows(here):
            centred = rows[i, here, :].astype(jnp.float32) - average[here, :1]
            place = pl.ds(pl.multiple_of(here.start + i * piece, NORM_ROWS), NORM_ROWS)
            out_ref[place, :] = (centred * scale[here, :1] * gains).astype(jnp.bfloat16)

        grouped(sum_rows)
        grouped(scale_rows)
        grouped(norm_rows)
    for copy in packs:
        copy.wait()
    for place, at, source in selects:
        place[:, at : at + source.shape[1]] = source[...]


def start_work(tiles, gain, gate_weight, up_weight, slide_weights, parts):
    slot_count, length, width = tiles.shape
    half = slot_count // 2
    pieces = half * length // NORM_PIECE
    hbm = pl.BlockSpec(memory_space=pltpu.HBM)
    vmem = pl.BlockSpec(memory_space=pltpu.VMEM)
    cols = gate_weight.shape[1]
    pack = (sum(w.shape[0] for w in slide_weights), slide_weights[0].shape[1])
    return pl.pallas_call(
        functools.partial(start_kernel, parts),
        in_specs=[hbm] * (4 + len(slide_weights)),
        out_specs=[vmem] * (2 + len(parts)),
        out_shape=[
            pltpu.VMEM((half * length, width), jnp.bfloat16),
            pltpu.VMEM(pack, jnp.bfloat16),
            *[pltpu.VMEM((part.stop - part.start, cols), jnp.bfloat16) for part in parts],
        ],
        scratch_shapes=[
            pltpu.VMEM((pieces, NORM_PIECE, width), jnp.bfloat16),
            pltpu.VMEM((width,), jnp.float32),
            pltpu.VMEM((NORM_PIECE, LANES), jnp.float32),
            pltpu.VMEM((NORM_PIECE, LANES), jnp.float32),
            pltpu.VMEM((2, *gate_weight.shape), jnp.bfloat16),
            pltpu.VMEM(slide_weights[-1].shape, jnp.bfloat16),
            pltpu.SemaphoreType.DMA((pieces,)),
            pltpu.SemaphoreType.DMA((2,)),
            pltpu.SemaphoreType.DMA((len(slide_weights),)),
            pltpu.SemaphoreType.DMA(()),
        ],
        compiler_params=pltpu.CompilerParams(vmem_limit_bytes=NORM_VMEM),
        cost_estimate=pl.CostEstimate(flops=0, bytes_accessed=0, transcendentals=0),
    )(*in_hbm(tiles, gain, gate_weight, up_weight, *slide_weights))


def after(value, *others):
    return lax.optimization_barrier((value, *others))[0]


class Layout:
    def __init__(self, n_dev, ny, depth):
        self.ny, self.nz, self.depth = ny, n_dev // ny, depth
        self.pair = ny * depth
        self.relative = self.pair % LANES == 0
        self.early_steps = self.nz - 1
        self.early = self.early_steps * self.pair // MXU * MXU if self.relative else 0
        cut = max(ROW_TILE, depth // 2 // ROW_TILE * ROW_TILE)
        self.parts = [slice(0, cut), slice(cut, depth)]
        self.width = n_dev * depth

    def place(self):
        me = lax.axis_index("dev")
        my_z = me // self.ny
        return my_z, me - my_z * self.ny

    def ring(self):
        return [*range(0, self.nz, 2), *range(self.nz - 1, 0, -2)]

    def source(self, step):
        my_z, _ = self.place()
        spot = jnp.where(my_z % 2 == 0, my_z // 2, self.nz - (my_z + 1) // 2)
        spot = spot - step
        spot = jnp.where(spot < 0, spot + self.nz, spot)
        return jnp.where(spot < self.nz // 2, 2 * spot, 2 * (self.nz - spot) - 1)

    def block_copies(self, blocks, weights, sems, end=None):
        _, my_y = self.place()
        copies = []
        n_parts = len(self.parts)
        first = 0 if end is None else end - len(blocks) // n_parts // self.ny
        for k, block in enumerate(blocks):
            step, flip, part = first + k // n_parts // self.ny, k // n_parts % self.ny, k % n_parts
            y = 1 - my_y if flip else my_y
            at = step if self.relative else self.source(step)
            here = self.parts[part]
            start = pl.multiple_of(at * self.pair + y * self.depth + here.start, ROW_TILE)
            place = weights.at[pl.ds(start, here.stop - here.start)]
            copies.append(pltpu.make_async_copy(block, place, sems.at[k]))
        return copies

    def row_copies(self, tiles_ref, rows, sems, steps):
        if not self.relative:
            return [pltpu.make_async_copy(tiles_ref, rows, sems.at[0])]
        copies = []
        for step in steps:
            start = pl.multiple_of(self.source(step) * self.pair, LANES)
            copies.append(
                pltpu.make_async_copy(
                    tiles_ref.at[:, pl.ds(start, self.pair)],
                    rows.at[:, step * self.pair : (step + 1) * self.pair],
                    sems.at[step],
                )
            )
        return copies


def gated_means(both, out_ref, at, length):
    cols = both.shape[1] // 2
    for tile in range(both.shape[0] // length):
        total = jnp.zeros((8, cols), jnp.float32)
        for first in range(tile * length, (tile + 1) * length, UNIT_ROWS):
            half_gate = 0.5 * both[first : first + UNIT_ROWS, :cols]
            up_part = both[first : first + UNIT_ROWS, cols:]
            gated = (half_gate * jnp.tanh(half_gate) + half_gate) * up_part
            total = total + jnp.sum(gated.reshape(UNIT_ROWS // 8, 8, cols), axis=0)
        out_ref[at + tile : at + tile + 1, :] = jnp.sum(total, axis=0, keepdims=True) * (
            1.0 / length
        )


def product(out, rows, weights, first, last, more=None):
    for at in range(0, rows.shape[0], MXU):
        here = slice(at, at + MXU)
        both = jnp.dot(
            rows[here, first:last], weights[first:last, :], preferred_element_type=jnp.float32
        )
        out[here, :] = both if more is None else both + more[here, :]


def early_kernel(layout, *refs):
    steps = range(layout.early_steps)
    n_blocks = len(steps) * layout.ny * len(layout.parts)
    blocks, tile_refs = refs[:n_blocks], refs[n_blocks : n_blocks + 2]
    out_ref, weights, rows, weight_sems, row_sems = refs[n_blocks + 2 :]
    loads = layout.block_copies(blocks, weights, weight_sems)
    row_loads = [
        layout.row_copies(ref, rows.at[i], row_sems.at[i], steps)
        for i, ref in enumerate(tile_refs)
    ]
    late_loads = [
        copy
        for i, ref in enumerate(tile_refs)
        for copy in layout.row_copies(
            ref, rows.at[i], row_sems.at[i], range(layout.early_steps, layout.nz)
        )
    ]
    for copy in row_loads[0] + loads + row_loads[1] + late_loads:
        copy.start()
    for copy in loads:
        copy.wait()
    for i in range(2):
        for copy in row_loads[i]:
            copy.wait()
        product(out_ref.at[i], rows.at[i], weights, 0, layout.early)
    for copy in late_loads:
        copy.wait()


def early_mlp(layout, blocks, tiles):
    n_rows = tiles[0].shape[0]
    cols = blocks[0].shape[1]
    hbm = pl.BlockSpec(memory_space=pltpu.HBM)
    vmem = pl.BlockSpec(memory_space=pltpu.VMEM)
    return pl.pallas_call(
        functools.partial(early_kernel, layout),
        in_specs=[hbm] * len(blocks) + [pl.BlockSpec(memory_space=pl.ANY)] * 2,
        out_specs=(vmem, vmem, vmem),
        out_shape=(
            pltpu.VMEM((2, n_rows, cols), jnp.float32),
            pltpu.VMEM((layout.width, cols), jnp.bfloat16),
            pltpu.VMEM((2, n_rows, layout.width), jnp.bfloat16),
        ),
        scratch_shapes=[
            pltpu.SemaphoreType.DMA((len(blocks),)),
            pltpu.SemaphoreType.DMA((2, layout.nz)),
        ],
        compiler_params=pltpu.CompilerParams(vmem_limit_bytes=MLP_VMEM),
        cost_estimate=pl.CostEstimate(
            flops=4 * n_rows * layout.early * cols,
            bytes_accessed=2 * layout.early * (cols + 2 * n_rows) + 8 * n_rows * cols,
            transcendentals=0,
        ),
    )(*in_hbm(*blocks), *tiles)


def packed(mine, others):
    low = lax.axis_index("sub") == 0
    rows = jnp.concatenate([jnp.where(low, mine, others), jnp.where(low, others, mine)], axis=0)
    return jnp.concatenate(
        [rows[:, k : k + LANES] for k in range(0, rows.shape[1], LANES)], axis=0
    ).astype(jnp.bfloat16)


def middle_kernel(layout, length, n_blocks, n_tiles, *refs):
    blocks, tile_refs = refs[:n_blocks], refs[n_blocks : n_blocks + n_tiles]
    early_refs = refs[n_blocks + n_tiles : -9]
    pair_ref, weights, own_ref, rows, even, odd, means, weight_sems, row_sems = refs[-9:]
    early = layout.early
    loads = layout.block_copies(blocks, weights, weight_sems, layout.nz)
    row_loads = [
        layout.row_copies(ref, rows.at[i], row_sems.at[i], range(layout.nz))
        for i, ref in enumerate(tile_refs)
    ]
    for copy in [copy for copies in [loads, *row_loads] for copy in copies]:
        copy.start()
    for copy in loads:
        copy.wait()
    units = [(early_refs[2].at[i], early_refs[0].at[i], []) for i in range(2)] if early else []
    units += [(rows.at[i], None, row_loads[i]) for i in range(n_tiles)]
    pending = None
    for i, (unit, more, waits) in enumerate(units):
        for copy in waits:
            copy.wait()
        for j in range(unit.shape[0] // length):
            here = slice(j * length, (j + 1) * length)
            tile = unit.shape[0] // length * i + j
            both = (even, odd)[tile % 2]
            if more is None:
                product(both, unit.at[here], weights, 0, layout.width)
            else:
                product(both, unit.at[here], weights, early, layout.width, more.at[here])
            if pending is not None:
                gated_means(*pending, length)
            pending = (both, means, tile)
    gated_means(*pending, length)
    half = means.shape[0] // 3
    own_ref[...] = packed(means[:half, :], means[half : 2 * half, :])
    pair_ref[...] = means[2 * half :, :]


def middle_mlp(layout, blocks, tiles, early, length):
    n_rows, width = tiles[0].shape
    cols = blocks[0].shape[1]
    half = n_rows // length
    tiles = tiles[2:] if early else tiles
    vmem = pl.BlockSpec(memory_space=pltpu.VMEM)
    return pl.pallas_call(
        functools.partial(middle_kernel, layout, length, len(blocks), len(tiles)),
        in_specs=[pl.BlockSpec(memory_space=pl.ANY)] * (len(blocks) + len(tiles))
        + [vmem] * len(early),
        out_specs=(vmem, vmem, vmem),
        out_shape=(
            pltpu.VMEM((half, cols // 2), jnp.float32),
            pltpu.VMEM((width, cols), jnp.bfloat16),
            jax.ShapeDtypeStruct((half * cols // LANES, LANES), jnp.bfloat16),
        ),
        input_output_aliases={len(blocks) + len(tiles) + 1: 1} if early else {},
        scratch_shapes=[
            pltpu.VMEM((len(tiles), n_rows, width), jnp.bfloat16),
            pltpu.VMEM((length, cols), jnp.float32),
            pltpu.VMEM((length, cols), jnp.float32),
            pltpu.VMEM((3 * half, cols // 2), jnp.float32),
            pltpu.SemaphoreType.DMA((len(blocks),)),
            pltpu.SemaphoreType.DMA((len(tiles), layout.nz)),
        ],
        compiler_params=pltpu.CompilerParams(vmem_limit_bytes=MLP_VMEM),
        cost_estimate=pl.CostEstimate(
            flops=4 * n_rows * width * cols,
            bytes_accessed=2 * (3 * n_rows * width + width * cols),
            transcendentals=0,
        ),
    )(*blocks, *(tiles if early else in_hbm(*tiles)), *in_vmem(*early))


def last_kernel(layout, length, means_ref, weights, tiles_ref, out_ref, rows, both, means, row_sems):
    row_loads = layout.row_copies(tiles_ref, rows, row_sems, range(layout.nz))
    for copy in row_loads:
        copy.start()
    for copy in row_loads:
        copy.wait()
    half = rows.shape[0] // length
    for i in range(half):
        here = slice(i * length, (i + 1) * length)
        product(both[i], rows.at[here], weights, 0, layout.width)
        if i:
            gated_means(both[i - 1], means, i - 1, length)
    gated_means(both[half - 1], means, half - 1, length)
    out_ref[...] = packed(means_ref[...], means[...])


def last_mlp(layout, means, weights, tiles, length):
    n_rows, width = tiles.shape
    cols = weights.shape[1]
    half = n_rows // length
    any_spec = pl.BlockSpec(memory_space=pl.ANY)
    vmem = pl.BlockSpec(memory_space=pltpu.VMEM)
    return pl.pallas_call(
        functools.partial(last_kernel, layout, length),
        in_specs=[vmem, vmem, any_spec],
        out_specs=vmem,
        out_shape=jax.ShapeDtypeStruct((half * cols // LANES, LANES), jnp.bfloat16),
        scratch_shapes=[
            pltpu.VMEM((n_rows, width), jnp.bfloat16),
            [pltpu.VMEM((length, cols), jnp.float32) for _ in range(half)],
            pltpu.VMEM((half, cols // 2), jnp.float32),
            pltpu.SemaphoreType.DMA((layout.nz,)),
        ],
        compiler_params=pltpu.CompilerParams(vmem_limit_bytes=MLP_VMEM),
        cost_estimate=pl.CostEstimate(
            flops=2 * n_rows * width * cols,
            bytes_accessed=2 * (n_rows * width + width * cols),
            transcendentals=0,
        ),
    )(*in_vmem(means, weights), tiles)


def small_mod(value, rate):
    return jnp.where(
        rate == 1,
        0,
        jnp.where(rate == 2, value & 1, jnp.where(rate == 3, lax.rem(value, 3), value & 3)),
    )


def multiplicity_kernel(n_dev, slot_count, heads, counts_ref, slide_ref, rates_ref, out_ref):
    me, core = lax.axis_index("dev"), lax.axis_index("sub")
    shape = out_ref.shape
    row = lax.broadcasted_iota(jnp.int32, shape, 0)
    col = lax.broadcasted_iota(jnp.int32, shape, 1)
    head = row // QROWS + core * (heads // 2)
    head = jnp.where(head >= heads, head - heads, head)
    query = row % QROWS
    device, slot = col // slot_count, col % slot_count
    rate = jnp.full(shape, 1, jnp.int32)
    for h in range(heads):
        rate = jnp.where(head == h, rates_ref[h], rate)
    my_slide = slide_ref[me]
    first = me
    count = jnp.zeros(shape, jnp.int32)
    slide = jnp.zeros(shape, jnp.int32)
    for k in reversed(range(n_dev)):
        first = jnp.where(slide_ref[k] == my_slide, k, first)
        count = jnp.where(device == k, counts_ref[k], count)
        slide = jnp.where(device == k, slide_ref[k], slide)
    offset = small_mod(head, rate)
    query_position = (me - first) * slot_count + query
    key_position = (device - first) * slot_count + slot
    valid = slot < count
    near = jnp.where((device == me) & valid, 1.0, 0.0)
    far = jnp.where(
        (slide == my_slide)
        & valid
        & (small_mod(query_position, rate) == offset)
        & (small_mod(key_position, rate) == offset),
        1.0,
        0.0,
    )
    out_ref[...] = near + far


def embed_kernel(
    counts_ref,
    own_ref,
    own_far_ref,
    pair_ref,
    pair_far_ref,
    gain_ref,
    near_ref,
    far_ref,
    embed_ref,
    mixed_ref,
    sent_ref,
):
    slot_count, half = embed_ref.shape
    n_blocks = half // 2 // LANES
    low = lax.rem(lax.axis_index("grp"), 2) == 0
    count = counts_ref[lax.axis_index("dev")]

    def features(mine_ref, theirs_ref):
        sides = []
        for ref in (mine_ref, theirs_ref):
            part = ref[...].astype(jnp.float32)
            pieces = [part[k * slot_count : (k + 1) * slot_count] for k in range(n_blocks)]
            sides.append(jnp.concatenate(pieces, axis=1))
        mine, theirs = sides
        rows = jnp.concatenate(
            [jnp.where(low, mine, theirs), jnp.where(low, theirs, mine)], axis=1
        )
        slot = lax.broadcasted_iota(jnp.int32, rows.shape, 0)
        return jnp.where(slot < count, rows, 0.0).astype(jnp.bfloat16)

    near = features(own_ref, pair_ref)
    far = features(own_far_ref, pair_far_ref)
    embed_ref[...] = near
    mixed = jnp.dot(near, near_ref[...], preferred_element_type=jnp.float32) + jnp.dot(
        far, far_ref[...], preferred_element_type=jnp.float32
    )
    mixed_ref[...] = jnp.concatenate([mixed, mixed], axis=0)
    hidden = normed(mixed, gain_ref[...].reshape(1, -1)).astype(jnp.float32)
    width = sent_ref.shape[2]
    pieces = [hidden[:, k : k + width] for k in range(0, hidden.shape[1], width)]
    pieces += [jnp.zeros_like(pieces[0])] * (sent_ref.shape[1] // slot_count - len(pieces))
    sent = jnp.concatenate(pieces, axis=0).astype(jnp.bfloat16)
    for k in range(sent_ref.shape[0]):
        sent_ref[k] = sent


def project(rows, near_ref, far_ref):
    return jnp.concatenate(
        [
            jnp.dot(rows, near_ref[...], preferred_element_type=jnp.float32),
            jnp.dot(rows, far_ref[...], preferred_element_type=jnp.float32),
        ],
        axis=1,
    )


def heads_of(shape):
    return (
        lax.broadcasted_iota(jnp.int32, shape, 0) // QROWS
        == lax.broadcasted_iota(jnp.int32, shape, 1) // HD
    )


def query_kernel(heads, mixed_ref, gain_ref, far_ref, *refs):
    near_refs, (many_ref, out_ref, many, *kept), (wq, sems) = refs[:4], refs[4:-2], refs[-2:]
    places = [wq.at[0], wq.at[1], *kept]
    copies = []
    at = 0
    for k, near in enumerate(near_refs):
        far = far_ref.at[at : at + near.shape[0]]
        at += near.shape[0]
        for i, source in enumerate((near, far)):
            copies.append(pltpu.make_async_copy(source, places[2 * k + i], sems.at[2 * k + i]))
    copies.append(pltpu.make_async_copy(many_ref, many, sems.at[len(copies)]))
    for copy in copies:
        copy.start()
    hidden = normed(mixed_ref[...], gain_ref[...].reshape(1, -1))
    for copy in copies[:2]:
        copy.wait()
    query = project(hidden, wq.at[0], wq.at[1])
    spread = jnp.concatenate([query] * heads, axis=0)
    out_ref[...] = jnp.where(heads_of(spread.shape), spread, 0.0).astype(jnp.bfloat16)
    for copy in copies[2:]:
        copy.wait()


def slide_kernel(
    heads,
    counts_ref,
    sent_ref,
    mixed_ref,
    query_ref,
    wk_ref,
    wk_far_ref,
    wv_ref,
    wv_far_ref,
    wo_ref,
    wo_far_ref,
    many_ref,
    out_ref,
    rows,
):
    slot_count, half = out_ref.shape
    core = lax.axis_index("sub")
    count = counts_ref[lax.axis_index("dev")]
    width = sent_ref.shape[2]
    for k in range(sent_ref.shape[0]):
        sent = sent_ref[k].astype(jnp.float32)
        rows[k * slot_count : (k + 1) * slot_count, :] = jnp.concatenate(
            [
                sent[j * slot_count : (j + 1) * slot_count]
                for j in range(rows.shape[1] // width)
            ],
            axis=1,
        )
    hidden = rows[...].astype(jnp.bfloat16)
    keys = project(hidden, wk_ref, wk_far_ref).astype(jnp.bfloat16)
    scores = lax.dot_general(
        query_ref[...], keys, (((1,), (1,)), ((), ())), preferred_element_type=jnp.float32
    ) * (1.0 / math.sqrt(HD))
    values = project(hidden, wv_ref, wv_far_ref).astype(jnp.bfloat16)
    many = many_ref[...]
    masked = jnp.where(many > 0.0, scores, FLOOR)
    weights = many * jnp.exp(masked - jnp.max(masked, axis=1, keepdims=True))
    weights = weights / jnp.sum(weights, axis=1, keepdims=True)
    context = jnp.dot(weights.astype(jnp.bfloat16), values, preferred_element_type=jnp.float32)
    context = jnp.where(heads_of(context.shape), context, 0.0)
    context = context.reshape(heads, QROWS, context.shape[1])
    context = jnp.sum(context, axis=0).astype(jnp.bfloat16)
    columns = pl.ds(pl.multiple_of(core * half, LANES), half)
    attended = jnp.dot(
        context[:, :half], wo_ref[:, columns], preferred_element_type=jnp.float32
    ) + jnp.dot(context[:, half:], wo_far_ref[...], preferred_element_type=jnp.float32)
    total = mixed_ref[:, columns] + attended
    slot = lax.broadcasted_iota(jnp.int32, total.shape, 0)
    total = jnp.where(slot < count, total, 0.0)
    out_ref[...] = total[:slot_count].astype(jnp.bfloat16)


def on_device(
    tiles,
    counts,
    slide_of,
    rates,
    tile_gain,
    gate_weight,
    up_weight,
    embed_proj,
    slide_gain,
    slide_wq,
    slide_wk,
    slide_wv,
    slide_wo,
):
    slot_count, length, width = tiles.shape
    hidden_cols = gate_weight.shape[1]
    n_grp, n_dev, n_sub = (lax.axis_size(a) for a in ("grp", "dev", "sub"))
    ny = 2
    nz = n_dev // ny
    heads = slide_wq.shape[1] * n_sub // HD
    core = lax.axis_index("sub")

    to_pair = [(g, g ^ 1) for g in range(n_grp)]
    to_sibling = [(s, s ^ 1) for s in range(n_sub)]
    along_y = [(d, d ^ 1) for d in range(n_dev)]

    layout = Layout(n_dev, ny, gate_weight.shape[0])
    ring = layout.ring()
    along_z = [
        (z * ny + y, ring[(i + 1) % nz] * ny + y) for i, z in enumerate(ring) for y in range(ny)
    ]
    slide_weights = [slide_wq, slide_wk, slide_wv, slide_wo]
    first, pack, *held = start_work(
        tiles, tile_gain, gate_weight, up_weight, slide_weights, layout.parts
    )
    second = lax.ppermute(first, "sub", to_sibling)
    pair_first = lax.ppermute(first, "grp", to_pair)
    proj_far = lax.ppermute(embed_proj, "sub", to_sibling)
    pack_far = lax.ppermute(pack, "sub", to_sibling)
    out_cols = slide_wo.shape[1] // n_sub
    smem = pl.BlockSpec(memory_space=pltpu.SMEM)
    vmem = pl.BlockSpec(memory_space=pltpu.VMEM)
    many = pl.pallas_call(
        functools.partial(multiplicity_kernel, n_dev, slot_count, heads),
        in_specs=[smem] * 3,
        out_specs=vmem,
        out_shape=jax.ShapeDtypeStruct((heads * QROWS, n_dev * slot_count), jnp.float32),
        compiler_params=pltpu.CompilerParams(vmem_limit_bytes=SMALL_VMEM),
    )(counts, slide_of, rates)

    held[1] = after(held[1], proj_far, second)
    steps = []
    last = None
    for step in range(nz):
        sent = []
        for part in range(len(held)):
            if step:
                arrived = lax.ppermute(held[part], "dev", along_z)
                others = [steps[-1][len(held) + part]]
                if (step, part) == (nz - 1, 0):
                    others += [many]
                if last is not None:
                    others.append(last)
                held[part] = last = after(arrived, *others)
            sent.append(lax.ppermute(held[part], "dev", along_y))
        steps.append([*held, *sent])
    blocks = [block for step in steps for block in step]
    early = []
    if layout.relative:
        n_early = layout.early_steps * len(steps[0])
        early = early_mlp(layout, blocks[:n_early], [after(first, last), second])
        blocks = blocks[n_early:]
    pair_first = after(pair_first, *steps[-1][-2:], *early)
    pair_second = lax.ppermute(pair_first, "sub", to_sibling)
    means, weights, own = middle_mlp(
        layout, blocks, [first, second, pair_first], early, length
    )
    own_far = lax.ppermute(own, "sub", to_sibling)
    pair = last_mlp(layout, means, weights, pair_second, length)
    across = [
        (g * n_sub + s, (g ^ 1) * n_sub + (s ^ 1)) for g in range(n_grp) for s in range(n_sub)
    ]
    pair_far = lax.ppermute(pair, ("grp", "sub"), across)
    pair = lax.ppermute(pair, "grp", to_pair)

    out_width = embed_proj.shape[1]
    sent_rows = 16
    sent_cols = 2 * LANES
    small = pltpu.CompilerParams(vmem_limit_bytes=SMALL_VMEM)
    tile_embed, mixed, sent = pl.pallas_call(
        embed_kernel,
        in_specs=[smem] + [vmem] * 7,
        out_specs=(vmem, vmem, vmem),
        out_shape=(
            jax.ShapeDtypeStruct((slot_count, hidden_cols), jnp.bfloat16),
            pltpu.VMEM((QROWS, out_width), jnp.float32),
            pltpu.VMEM((n_dev, sent_rows, sent_cols), jnp.bfloat16),
        ),
        compiler_params=small,
    )(counts, *in_vmem(own, own_far, pair, pair_far), slide_gain, embed_proj, proj_far)
    sent = lax.all_to_all(sent, "dev", split_axis=0, concat_axis=0, tiled=True)
    hbm = pl.BlockSpec(memory_space=pltpu.HBM)
    far_shape = (slide_wo.shape[0], out_cols)
    kept = [slide_wk.shape] * 4 + [slide_wo.shape, far_shape]
    query, many, *weights = pl.pallas_call(
        functools.partial(query_kernel, heads),
        in_specs=[vmem] * 2 + [hbm] * 6,
        out_specs=[vmem] * (2 + len(kept)),
        out_shape=[
            pltpu.VMEM((heads * QROWS, out_width), jnp.bfloat16),
            pltpu.VMEM(many.shape, many.dtype),
            *[pltpu.VMEM(shape, jnp.bfloat16) for shape in kept],
        ],
        scratch_shapes=[
            pltpu.VMEM((2, *slide_wq.shape), jnp.bfloat16),
            pltpu.SemaphoreType.DMA((3 + len(kept),)),
        ],
        compiler_params=small,
    )(*in_vmem(mixed), slide_gain, *in_hbm(pack_far, *slide_weights, many))
    slide_out = pl.pallas_call(
        functools.partial(slide_kernel, heads),
        in_specs=[smem] + [vmem] * 10,
        out_specs=vmem,
        out_shape=jax.ShapeDtypeStruct((slot_count, out_cols), jnp.bfloat16),
        scratch_shapes=[pltpu.VMEM((n_dev * slot_count, out_width), jnp.float32)],
        compiler_params=small,
    )(counts, *in_vmem(sent, mixed, query, *weights, many))
    return (tile_embed, slide_out)


def solution(mesh):
    placed = (
        P(("grp", "dev"), None, None),
        P("grp"),
        P("grp"),
        P(),
        P(),
        P("dev", "sub"),
        P("dev", "sub"),
        P("sub", None),
        P(),
        P(None, "sub"),
        P(None, "sub"),
        P(None, "sub"),
        P("sub", None),
    )
    return jax.shard_map(
        on_device,
        mesh=mesh,
        in_specs=placed,
        out_specs=(P(("grp", "dev"), "sub"), P(("grp", "dev"), "sub")),
        check_vma=False,
    )
```

```python
import functools
import math

import jax
import jax.numpy as jnp
from jax import lax
from jax.experimental import pallas as pl
from jax.experimental.pallas import tpu as pltpu
from jax.sharding import PartitionSpec as P

HD = 64
EPSILON = 1e-06
FLOOR = -1e30
QROWS = 8
NORM_ROWS = 16
NORM_PIECE = 128
NORM_UNROLL = 8
LANES = 128
UNIT_ROWS = 16
ROW_TILE = 16
MXU = 256
MLP_VMEM = 24 * 1024 * 1024
NORM_VMEM = 12 * 1024 * 1024
SMALL_VMEM = 4 * 1024 * 1024


def normed(rows_in, gains):
    average = jnp.mean(rows_in, axis=-1, keepdims=True)
    centred = rows_in - average
    variance = jnp.mean(centred * centred, axis=-1, keepdims=True)
    return (centred * lax.rsqrt(variance + EPSILON) * gains).astype(jnp.bfloat16)


def in_hbm(*arrays):
    return [pltpu.with_memory_space_constraint(x, pltpu.HBM) for x in arrays]


def in_vmem(*arrays):
    return [pltpu.with_memory_space_constraint(x, pltpu.VMEM) for x in arrays]


def start_kernel(parts, *refs):
    tiles_ref, gain_ref, gate_ref, up_ref, *slide_refs = refs[:8]
    out_ref, pack_ref, *block_refs = refs[8 : 10 + len(parts)]
    (
        rows,
        gain,
        average,
        scale,
        whole,
        whole_slide,
        in_sems,
        block_sems,
        slide_sems,
        gain_sem,
    ) = refs[10 + len(parts) :]
    core = lax.axis_index("sub")
    pieces, piece = rows.shape[:2]
    half, length = tiles_ref.shape[0] // 2, tiles_ref.shape[1]
    half_cols = gate_ref.shape[1] // 2
    gain_copy = pltpu.make_async_copy(gain_ref, gain, gain_sem)
    copies = [
        pltpu.make_async_copy(
            tiles_ref.at[core * half + i * piece // length, pl.ds(i * piece % length, piece)],
            rows.at[i],
            in_sems.at[i],
        )
        for i in range(pieces)
    ]
    packs = [
        pltpu.make_async_copy(ref, whole.at[i], block_sems.at[i])
        for i, ref in enumerate((gate_ref, up_ref))
    ]
    selects = []
    columns = pl.ds(pl.multiple_of(lax.rem(lax.axis_index("grp"), 2) * half_cols, LANES), half_cols)
    for k, (part, block_ref) in enumerate(zip(parts, block_refs)):
        for i, ref in enumerate((gate_ref, up_ref)):
            selects.append((block_ref, i * half_cols, whole.at[i, part, columns]))
    cols = pack_ref.shape[1]
    others = pl.ds(pl.multiple_of((1 - core) * cols, LANES), cols)
    at = 0
    for k, ref in enumerate(slide_refs):
        place = pack_ref.at[at : at + ref.shape[0]]
        if ref.shape[1] == cols:
            packs.append(pltpu.make_async_copy(ref, place, slide_sems.at[k]))
        else:
            packs.append(pltpu.make_async_copy(ref, whole_slide, slide_sems.at[k]))
            selects.append((place, 0, whole_slide.at[:, others]))
        at += ref.shape[0]
    for copy in [gain_copy] + copies + packs:
        copy.start()
    gain_copy.wait()
    gains = gain[...].reshape(1, -1)
    width = gains.shape[1]

    def grouped(function):
        def some_rows(j, carry):
            function(pl.ds(pl.multiple_of(j * NORM_ROWS, NORM_ROWS), NORM_ROWS))
            return carry

        lax.fori_loop(0, rows.shape[1] // NORM_ROWS, some_rows, 0, unroll=NORM_UNROLL)

    def lane_sum(values):
        total = values[:, :LANES]
        for k in range(LANES, width, LANES):
            total = total + values[:, k : k + LANES]
        return jnp.sum(total, axis=1, keepdims=True)

    for i in range(rows.shape[0]):
        copies[i].wait()

        def sum_rows(here):
            total = lane_sum(rows[i, here, :].astype(jnp.float32))
            average[here, :] = jnp.broadcast_to(total * (1.0 / width), (NORM_ROWS, LANES))

        def scale_rows(here):
            centred = rows[i, here, :].astype(jnp.float32) - average[here, :1]
            variance = lane_sum(centred * centred) * (1.0 / width)
            scale[here, :] = jnp.broadcast_to(
                lax.rsqrt(variance + EPSILON), (NORM_ROWS, LANES)
            )

        def norm_rows(here):
            centred = rows[i, here, :].astype(jnp.float32) - average[here, :1]
            place = pl.ds(pl.multiple_of(here.start + i * piece, NORM_ROWS), NORM_ROWS)
            out_ref[place, :] = (centred * scale[here, :1] * gains).astype(jnp.bfloat16)

        grouped(sum_rows)
        grouped(scale_rows)
        grouped(norm_rows)
    for copy in packs:
        copy.wait()
    for place, at, source in selects:
        place[:, at : at + source.shape[1]] = source[...]


def start_work(tiles, gain, gate_weight, up_weight, slide_weights, parts):
    slot_count, length, width = tiles.shape
    half = slot_count // 2
    pieces = half * length // NORM_PIECE
    hbm = pl.BlockSpec(memory_space=pltpu.HBM)
    vmem = pl.BlockSpec(memory_space=pltpu.VMEM)
    cols = gate_weight.shape[1]
    pack = (sum(w.shape[0] for w in slide_weights), slide_weights[0].shape[1])
    return pl.pallas_call(
        functools.partial(start_kernel, parts),
        in_specs=[hbm] * (4 + len(slide_weights)),
        out_specs=[vmem] * (2 + len(parts)),
        out_shape=[
            pltpu.VMEM((half * length, width), jnp.bfloat16),
            pltpu.VMEM(pack, jnp.bfloat16),
            *[pltpu.VMEM((part.stop - part.start, cols), jnp.bfloat16) for part in parts],
        ],
        scratch_shapes=[
            pltpu.VMEM((pieces, NORM_PIECE, width), jnp.bfloat16),
            pltpu.VMEM((width,), jnp.float32),
            pltpu.VMEM((NORM_PIECE, LANES), jnp.float32),
            pltpu.VMEM((NORM_PIECE, LANES), jnp.float32),
            pltpu.VMEM((2, *gate_weight.shape), jnp.bfloat16),
            pltpu.VMEM(slide_weights[-1].shape, jnp.bfloat16),
            pltpu.SemaphoreType.DMA((pieces,)),
            pltpu.SemaphoreType.DMA((2,)),
            pltpu.SemaphoreType.DMA((len(slide_weights),)),
            pltpu.SemaphoreType.DMA(()),
        ],
        compiler_params=pltpu.CompilerParams(vmem_limit_bytes=NORM_VMEM),
        cost_estimate=pl.CostEstimate(flops=0, bytes_accessed=0, transcendentals=0),
    )(*in_hbm(tiles, gain, gate_weight, up_weight, *slide_weights))


def after(value, *others):
    return lax.optimization_barrier((value, *others))[0]


class Layout:
    def __init__(self, n_dev, ny, depth):
        self.ny, self.nz, self.depth = ny, n_dev // ny, depth
        self.pair = ny * depth
        self.relative = self.pair % LANES == 0
        self.early_steps = self.nz - 1
        self.early = self.early_steps * self.pair // MXU * MXU if self.relative else 0
        cut = max(ROW_TILE, depth // 2 // ROW_TILE * ROW_TILE)
        self.parts = [slice(0, cut), slice(cut, depth)]
        self.width = n_dev * depth

    def place(self):
        me = lax.axis_index("dev")
        my_z = me // self.ny
        return my_z, me - my_z * self.ny

    def ring(self):
        return [*range(0, self.nz, 2), *range(self.nz - 1, 0, -2)]

    def source(self, step):
        my_z, _ = self.place()
        spot = jnp.where(my_z % 2 == 0, my_z // 2, self.nz - (my_z + 1) // 2)
        spot = spot - step
        spot = jnp.where(spot < 0, spot + self.nz, spot)
        return jnp.where(spot < self.nz // 2, 2 * spot, 2 * (self.nz - spot) - 1)

    def block_copies(self, blocks, weights, sems, end=None):
        _, my_y = self.place()
        copies = []
        n_parts = len(self.parts)
        first = 0 if end is None else end - len(blocks) // n_parts // self.ny
        for k, block in enumerate(blocks):
            step, flip, part = first + k // n_parts // self.ny, k // n_parts % self.ny, k % n_parts
            y = 1 - my_y if flip else my_y
            at = step if self.relative else self.source(step)
            here = self.parts[part]
            start = pl.multiple_of(at * self.pair + y * self.depth + here.start, ROW_TILE)
            place = weights.at[pl.ds(start, here.stop - here.start)]
            copies.append(pltpu.make_async_copy(block, place, sems.at[k]))
        return copies

    def row_copies(self, tiles_ref, rows, sems, steps):
        if not self.relative:
            return [pltpu.make_async_copy(tiles_ref, rows, sems.at[0])]
        copies = []
        for step in steps:
            start = pl.multiple_of(self.source(step) * self.pair, LANES)
            copies.append(
                pltpu.make_async_copy(
                    tiles_ref.at[:, pl.ds(start, self.pair)],
                    rows.at[:, step * self.pair : (step + 1) * self.pair],
                    sems.at[step],
                )
            )
        return copies


def gated_means(both, out_ref, at, length):
    cols = both.shape[1] // 2
    for tile in range(both.shape[0] // length):
        total = jnp.zeros((8, cols), jnp.float32)
        for first in range(tile * length, (tile + 1) * length, UNIT_ROWS):
            half_gate = 0.5 * both[first : first + UNIT_ROWS, :cols]
            up_part = both[first : first + UNIT_ROWS, cols:]
            gated = (half_gate * jnp.tanh(half_gate) + half_gate) * up_part
            total = total + jnp.sum(gated.reshape(UNIT_ROWS // 8, 8, cols), axis=0)
        out_ref[at + tile : at + tile + 1, :] = jnp.sum(total, axis=0, keepdims=True) * (
            1.0 / length
        )


def product(out, rows, weights, first, last, more=None):
    for at in range(0, rows.shape[0], MXU):
        here = slice(at, at + MXU)
        both = jnp.dot(
            rows[here, first:last], weights[first:last, :], preferred_element_type=jnp.float32
        )
        out[here, :] = both if more is None else both + more[here, :]


def early_kernel(layout, *refs):
    steps = range(layout.early_steps)
    n_blocks = len(steps) * layout.ny * len(layout.parts)
    blocks, tile_refs = refs[:n_blocks], refs[n_blocks : n_blocks + 2]
    out_ref, weights, rows, weight_sems, row_sems = refs[n_blocks + 2 :]
    loads = layout.block_copies(blocks, weights, weight_sems)
    row_loads = [
        layout.row_copies(ref, rows.at[i], row_sems.at[i], steps)
        for i, ref in enumerate(tile_refs)
    ]
    late_loads = [
        copy
        for i, ref in enumerate(tile_refs)
        for copy in layout.row_copies(
            ref, rows.at[i], row_sems.at[i], range(layout.early_steps, layout.nz)
        )
    ]
    for copy in row_loads[0] + loads + row_loads[1] + late_loads:
        copy.start()
    for copy in loads:
        copy.wait()
    for i in range(2):
        for copy in row_loads[i]:
            copy.wait()
        product(out_ref.at[i], rows.at[i], weights, 0, layout.early)
    for copy in late_loads:
        copy.wait()


def early_mlp(layout, blocks, tiles):
    n_rows = tiles[0].shape[0]
    cols = blocks[0].shape[1]
    hbm = pl.BlockSpec(memory_space=pltpu.HBM)
    vmem = pl.BlockSpec(memory_space=pltpu.VMEM)
    return pl.pallas_call(
        functools.partial(early_kernel, layout),
        in_specs=[hbm] * len(blocks) + [pl.BlockSpec(memory_space=pl.ANY)] * 2,
        out_specs=(vmem, vmem, vmem),
        out_shape=(
            pltpu.VMEM((2, n_rows, cols), jnp.float32),
            pltpu.VMEM((layout.width, cols), jnp.bfloat16),
            pltpu.VMEM((2, n_rows, layout.width), jnp.bfloat16),
        ),
        scratch_shapes=[
            pltpu.SemaphoreType.DMA((len(blocks),)),
            pltpu.SemaphoreType.DMA((2, layout.nz)),
        ],
        compiler_params=pltpu.CompilerParams(vmem_limit_bytes=MLP_VMEM),
        cost_estimate=pl.CostEstimate(
            flops=4 * n_rows * layout.early * cols,
            bytes_accessed=2 * layout.early * (cols + 2 * n_rows) + 8 * n_rows * cols,
            transcendentals=0,
        ),
    )(*in_hbm(*blocks), *tiles)


def packed(mine, others):
    low = lax.axis_index("sub") == 0
    rows = jnp.concatenate([jnp.where(low, mine, others), jnp.where(low, others, mine)], axis=0)
    return jnp.concatenate(
        [rows[:, k : k + LANES] for k in range(0, rows.shape[1], LANES)], axis=0
    ).astype(jnp.bfloat16)


def middle_kernel(layout, length, n_blocks, n_tiles, *refs):
    blocks, tile_refs = refs[:n_blocks], refs[n_blocks : n_blocks + n_tiles]
    early_refs = refs[n_blocks + n_tiles : -9]
    pair_ref, weights, own_ref, rows, even, odd, means, weight_sems, row_sems = refs[-9:]
    early = layout.early
    loads = layout.block_copies(blocks, weights, weight_sems, layout.nz)
    row_loads = [
        layout.row_copies(ref, rows.at[i], row_sems.at[i], range(layout.nz))
        for i, ref in enumerate(tile_refs)
    ]
    for copy in [copy for copies in [loads, *row_loads] for copy in copies]:
        copy.start()
    for copy in loads:
        copy.wait()
    units = [(early_refs[2].at[i], early_refs[0].at[i], []) for i in range(2)] if early else []
    units += [(rows.at[i], None, row_loads[i]) for i in range(n_tiles)]
    pending = None
    for i, (unit, more, waits) in enumerate(units):
        for copy in waits:
            copy.wait()
        for j in range(unit.shape[0] // length):
            here = slice(j * length, (j + 1) * length)
            tile = unit.shape[0] // length * i + j
            both = (even, odd)[tile % 2]
            if more is None:
                product(both, unit.at[here], weights, 0, layout.width)
            else:
                product(both, unit.at[here], weights, early, layout.width, more.at[here])
            if pending is not None:
                gated_means(*pending, length)
            pending = (both, means, tile)
    gated_means(*pending, length)
    half = means.shape[0] // 3
    own_ref[...] = packed(means[:half, :], means[half : 2 * half, :])
    pair_ref[...] = means[2 * half :, :]


def middle_mlp(layout, blocks, tiles, early, length):
    n_rows, width = tiles[0].shape
    cols = blocks[0].shape[1]
    half = n_rows // length
    tiles = tiles[2:] if early else tiles
    vmem = pl.BlockSpec(memory_space=pltpu.VMEM)
    return pl.pallas_call(
        functools.partial(middle_kernel, layout, length, len(blocks), len(tiles)),
        in_specs=[pl.BlockSpec(memory_space=pl.ANY)] * (len(blocks) + len(tiles))
        + [vmem] * len(early),
        out_specs=(vmem, vmem, vmem),
        out_shape=(
            pltpu.VMEM((half, cols // 2), jnp.float32),
            pltpu.VMEM((width, cols), jnp.bfloat16),
            jax.ShapeDtypeStruct((half * cols // LANES, LANES), jnp.bfloat16),
        ),
        input_output_aliases={len(blocks) + len(tiles) + 1: 1} if early else {},
        scratch_shapes=[
            pltpu.VMEM((len(tiles), n_rows, width), jnp.bfloat16),
            pltpu.VMEM((length, cols), jnp.float32),
            pltpu.VMEM((length, cols), jnp.float32),
            pltpu.VMEM((3 * half, cols // 2), jnp.float32),
            pltpu.SemaphoreType.DMA((len(blocks),)),
            pltpu.SemaphoreType.DMA((len(tiles), layout.nz)),
        ],
        compiler_params=pltpu.CompilerParams(vmem_limit_bytes=MLP_VMEM),
        cost_estimate=pl.CostEstimate(
            flops=4 * n_rows * width * cols,
            bytes_accessed=2 * (3 * n_rows * width + width * cols),
            transcendentals=0,
        ),
    )(*blocks, *(tiles if early else in_hbm(*tiles)), *in_vmem(*early))


def last_kernel(layout, length, means_ref, weights, tiles_ref, out_ref, rows, both, means, row_sems):
    row_loads = layout.row_copies(tiles_ref, rows, row_sems, range(layout.nz))
    for copy in row_loads:
        copy.start()
    for copy in row_loads:
        copy.wait()
    half = rows.shape[0] // length
    for i in range(half):
        here = slice(i * length, (i + 1) * length)
        product(both[i], rows.at[here], weights, 0, layout.width)
        if i:
            gated_means(both[i - 1], means, i - 1, length)
    gated_means(both[half - 1], means, half - 1, length)
    out_ref[...] = packed(means_ref[...], means[...])


def last_mlp(layout, means, weights, tiles, length):
    n_rows, width = tiles.shape
    cols = weights.shape[1]
    half = n_rows // length
    any_spec = pl.BlockSpec(memory_space=pl.ANY)
    vmem = pl.BlockSpec(memory_space=pltpu.VMEM)
    return pl.pallas_call(
        functools.partial(last_kernel, layout, length),
        in_specs=[vmem, vmem, any_spec],
        out_specs=vmem,
        out_shape=jax.ShapeDtypeStruct((half * cols // LANES, LANES), jnp.bfloat16),
        scratch_shapes=[
            pltpu.VMEM((n_rows, width), jnp.bfloat16),
            [pltpu.VMEM((length, cols), jnp.float32) for _ in range(half)],
            pltpu.VMEM((half, cols // 2), jnp.float32),
            pltpu.SemaphoreType.DMA((layout.nz,)),
        ],
        compiler_params=pltpu.CompilerParams(vmem_limit_bytes=MLP_VMEM),
        cost_estimate=pl.CostEstimate(
            flops=2 * n_rows * width * cols,
            bytes_accessed=2 * (n_rows * width + width * cols),
            transcendentals=0,
        ),
    )(*in_vmem(means, weights), tiles)


def small_mod(value, rate):
    return jnp.where(
        rate == 1,
        0,
        jnp.where(rate == 2, value & 1, jnp.where(rate == 3, lax.rem(value, 3), value & 3)),
    )


def multiplicity_kernel(n_dev, slot_count, heads, counts_ref, slide_ref, rates_ref, out_ref):
    me, core = lax.axis_index("dev"), lax.axis_index("sub")
    shape = out_ref.shape
    row = lax.broadcasted_iota(jnp.int32, shape, 0)
    col = lax.broadcasted_iota(jnp.int32, shape, 1)
    head = row // QROWS + core * (heads // 2)
    head = jnp.where(head >= heads, head - heads, head)
    query = row % QROWS
    device, slot = col // slot_count, col % slot_count
    rate = jnp.full(shape, 1, jnp.int32)
    for h in range(heads):
        rate = jnp.where(head == h, rates_ref[h], rate)
    my_slide = slide_ref[me]
    first = me
    count = jnp.zeros(shape, jnp.int32)
    slide = jnp.zeros(shape, jnp.int32)
    for k in reversed(range(n_dev)):
        first = jnp.where(slide_ref[k] == my_slide, k, first)
        count = jnp.where(device == k, counts_ref[k], count)
        slide = jnp.where(device == k, slide_ref[k], slide)
    offset = small_mod(head, rate)
    query_position = (me - first) * slot_count + query
    key_position = (device - first) * slot_count + slot
    valid = slot < count
    near = jnp.where((device == me) & valid, 1.0, 0.0)
    far = jnp.where(
        (slide == my_slide)
        & valid
        & (small_mod(query_position, rate) == offset)
        & (small_mod(key_position, rate) == offset),
        1.0,
        0.0,
    )
    out_ref[...] = near + far


def embed_kernel(
    counts_ref,
    own_ref,
    own_far_ref,
    pair_ref,
    pair_far_ref,
    gain_ref,
    near_ref,
    far_ref,
    embed_ref,
    mixed_ref,
    sent_ref,
):
    slot_count, half = embed_ref.shape
    n_blocks = half // 2 // LANES
    low = lax.rem(lax.axis_index("grp"), 2) == 0
    count = counts_ref[lax.axis_index("dev")]

    def features(mine_ref, theirs_ref):
        sides = []
        for ref in (mine_ref, theirs_ref):
            part = ref[...].astype(jnp.float32)
            pieces = [part[k * slot_count : (k + 1) * slot_count] for k in range(n_blocks)]
            sides.append(jnp.concatenate(pieces, axis=1))
        mine, theirs = sides
        rows = jnp.concatenate(
            [jnp.where(low, mine, theirs), jnp.where(low, theirs, mine)], axis=1
        )
        slot = lax.broadcasted_iota(jnp.int32, rows.shape, 0)
        return jnp.where(slot < count, rows, 0.0).astype(jnp.bfloat16)

    near = features(own_ref, pair_ref)
    far = features(own_far_ref, pair_far_ref)
    embed_ref[...] = near
    mixed = jnp.dot(near, near_ref[...], preferred_element_type=jnp.float32) + jnp.dot(
        far, far_ref[...], preferred_element_type=jnp.float32
    )
    mixed_ref[...] = jnp.concatenate([mixed, mixed], axis=0)
    hidden = normed(mixed, gain_ref[...].reshape(1, -1)).astype(jnp.float32)
    width = sent_ref.shape[2]
    pieces = [hidden[:, k : k + width] for k in range(0, hidden.shape[1], width)]
    pieces += [jnp.zeros_like(pieces[0])] * (sent_ref.shape[1] // slot_count - len(pieces))
    sent = jnp.concatenate(pieces, axis=0).astype(jnp.bfloat16)
    for k in range(sent_ref.shape[0]):
        sent_ref[k] = sent


def project(rows, near_ref, far_ref):
    return jnp.concatenate(
        [
            jnp.dot(rows, near_ref[...], preferred_element_type=jnp.float32),
            jnp.dot(rows, far_ref[...], preferred_element_type=jnp.float32),
        ],
        axis=1,
    )


def heads_of(shape):
    return (
        lax.broadcasted_iota(jnp.int32, shape, 0) // QROWS
        == lax.broadcasted_iota(jnp.int32, shape, 1) // HD
    )


def query_kernel(heads, mixed_ref, gain_ref, far_ref, *refs):
    near_refs, (many_ref, out_ref, many, *kept), (wq, sems) = refs[:4], refs[4:-2], refs[-2:]
    places = [wq.at[0], wq.at[1], *kept]
    copies = []
    at = 0
    for k, near in enumerate(near_refs):
        far = far_ref.at[at : at + near.shape[0]]
        at += near.shape[0]
        for i, source in enumerate((near, far)):
            copies.append(pltpu.make_async_copy(source, places[2 * k + i], sems.at[2 * k + i]))
    copies.append(pltpu.make_async_copy(many_ref, many, sems.at[len(copies)]))
    for copy in copies:
        copy.start()
    hidden = normed(mixed_ref[...], gain_ref[...].reshape(1, -1))
    for copy in copies[:2]:
        copy.wait()
    query = project(hidden, wq.at[0], wq.at[1])
    spread = jnp.concatenate([query] * heads, axis=0)
    out_ref[...] = jnp.where(heads_of(spread.shape), spread, 0.0).astype(jnp.bfloat16)
    for copy in copies[2:]:
        copy.wait()


def slide_kernel(
    heads,
    counts_ref,
    sent_ref,
    mixed_ref,
    query_ref,
    wk_ref,
    wk_far_ref,
    wv_ref,
    wv_far_ref,
    wo_ref,
    wo_far_ref,
    many_ref,
    out_ref,
    rows,
):
    slot_count, half = out_ref.shape
    core = lax.axis_index("sub")
    count = counts_ref[lax.axis_index("dev")]
    width = sent_ref.shape[2]
    for k in range(sent_ref.shape[0]):
        sent = sent_ref[k].astype(jnp.float32)
        rows[k * slot_count : (k + 1) * slot_count, :] = jnp.concatenate(
            [
                sent[j * slot_count : (j + 1) * slot_count]
                for j in range(rows.shape[1] // width)
            ],
            axis=1,
        )
    hidden = rows[...].astype(jnp.bfloat16)
    keys = project(hidden, wk_ref, wk_far_ref).astype(jnp.bfloat16)
    scores = lax.dot_general(
        query_ref[...], keys, (((1,), (1,)), ((), ())), preferred_element_type=jnp.float32
    ) * (1.0 / math.sqrt(HD))
    values = project(hidden, wv_ref, wv_far_ref).astype(jnp.bfloat16)
    many = many_ref[...]
    masked = jnp.where(many > 0.0, scores, FLOOR)
    weights = many * jnp.exp(masked - jnp.max(masked, axis=1, keepdims=True))
    weights = weights / jnp.sum(weights, axis=1, keepdims=True)
    context = jnp.dot(weights.astype(jnp.bfloat16), values, preferred_element_type=jnp.float32)
    context = jnp.where(heads_of(context.shape), context, 0.0)
    context = context.reshape(heads, QROWS, context.shape[1])
    context = jnp.sum(context, axis=0).astype(jnp.bfloat16)
    columns = pl.ds(pl.multiple_of(core * half, LANES), half)
    attended = jnp.dot(
        context[:, :half], wo_ref[:, columns], preferred_element_type=jnp.float32
    ) + jnp.dot(context[:, half:], wo_far_ref[...], preferred_element_type=jnp.float32)
    total = mixed_ref[:, columns] + attended
    slot = lax.broadcasted_iota(jnp.int32, total.shape, 0)
    total = jnp.where(slot < count, total, 0.0)
    out_ref[...] = total[:slot_count].astype(jnp.bfloat16)


def on_device(
    tiles,
    counts,
    slide_of,
    rates,
    tile_gain,
    gate_weight,
    up_weight,
    embed_proj,
    slide_gain,
    slide_wq,
    slide_wk,
    slide_wv,
    slide_wo,
):
    slot_count, length, width = tiles.shape
    hidden_cols = gate_weight.shape[1]
    n_grp, n_dev, n_sub = (lax.axis_size(a) for a in ("grp", "dev", "sub"))
    ny = 2
    nz = n_dev // ny
    heads = slide_wq.shape[1] * n_sub // HD
    core = lax.axis_index("sub")

    to_pair = [(g, g ^ 1) for g in range(n_grp)]
    to_sibling = [(s, s ^ 1) for s in range(n_sub)]
    along_y = [(d, d ^ 1) for d in range(n_dev)]

    layout = Layout(n_dev, ny, gate_weight.shape[0])
    ring = layout.ring()
    along_z = [
        (z * ny + y, ring[(i + 1) % nz] * ny + y) for i, z in enumerate(ring) for y in range(ny)
    ]
    slide_weights = [slide_wq, slide_wk, slide_wv, slide_wo]
    first, pack, *held = start_work(
        tiles, tile_gain, gate_weight, up_weight, slide_weights, layout.parts
    )
    second = lax.ppermute(first, "sub", to_sibling)
    pair_first = lax.ppermute(first, "grp", to_pair)
    proj_far = lax.ppermute(embed_proj, "sub", to_sibling)
    pack_far = lax.ppermute(pack, "sub", to_sibling)
    out_cols = slide_wo.shape[1] // n_sub
    smem = pl.BlockSpec(memory_space=pltpu.SMEM)
    vmem = pl.BlockSpec(memory_space=pltpu.VMEM)
    many = pl.pallas_call(
        functools.partial(multiplicity_kernel, n_dev, slot_count, heads),
        in_specs=[smem] * 3,
        out_specs=vmem,
        out_shape=jax.ShapeDtypeStruct((heads * QROWS, n_dev * slot_count), jnp.float32),
        compiler_params=pltpu.CompilerParams(vmem_limit_bytes=SMALL_VMEM),
    )(counts, slide_of, rates)

    held[1] = after(held[1], proj_far, second)
    steps = []
    last = None
    for step in range(nz):
        sent = []
        for part in range(len(held)):
            over = None
            if step:
                arrived = lax.ppermute(held[part], "dev", along_z)
                others = [] if last is None else [last]
                over = steps[-1][len(held) + part]
                if (step, part) != (nz - 1, 1):
                    others.append(over)
                if (step, part) == (nz - 1, 0):
                    others += [many]
                held[part] = last = after(arrived, *others)
            if (step, part) == (nz - 1, 0):
                sent.append(lax.ppermute(after(over, last), "dev", along_z))
            else:
                sent.append(lax.ppermute(held[part], "dev", along_y))
        steps.append([*held, *sent])
    blocks = [block for step in steps for block in step]
    early = []
    if layout.relative:
        n_early = layout.early_steps * len(steps[0])
        early = early_mlp(layout, blocks[:n_early], [after(first, last), second])
        blocks = blocks[n_early:]
    pair_first = after(pair_first, *steps[-1][-2:], *early)
    pair_second = lax.ppermute(pair_first, "sub", to_sibling)
    means, weights, own = middle_mlp(
        layout, blocks, [first, second, pair_first], early, length
    )
    own_far = lax.ppermute(own, "sub", to_sibling)
    pair = last_mlp(layout, means, weights, pair_second, length)
    across = [
        (g * n_sub + s, (g ^ 1) * n_sub + (s ^ 1)) for g in range(n_grp) for s in range(n_sub)
    ]
    pair_far = lax.ppermute(pair, ("grp", "sub"), across)
    pair = lax.ppermute(pair, "grp", to_pair)

    out_width = embed_proj.shape[1]
    sent_rows = 16
    sent_cols = 2 * LANES
    small = pltpu.CompilerParams(vmem_limit_bytes=SMALL_VMEM)
    tile_embed, mixed, sent = pl.pallas_call(
        embed_kernel,
        in_specs=[smem] + [vmem] * 7,
        out_specs=(vmem, vmem, vmem),
        out_shape=(
            jax.ShapeDtypeStruct((slot_count, hidden_cols), jnp.bfloat16),
            pltpu.VMEM((QROWS, out_width), jnp.float32),
            pltpu.VMEM((n_dev, sent_rows, sent_cols), jnp.bfloat16),
        ),
        compiler_params=small,
    )(counts, *in_vmem(own, own_far, pair, pair_far), slide_gain, embed_proj, proj_far)
    sent = lax.all_to_all(sent, "dev", split_axis=0, concat_axis=0, tiled=True)
    hbm = pl.BlockSpec(memory_space=pltpu.HBM)
    far_shape = (slide_wo.shape[0], out_cols)
    kept = [slide_wk.shape] * 4 + [slide_wo.shape, far_shape]
    query, many, *weights = pl.pallas_call(
        functools.partial(query_kernel, heads),
        in_specs=[vmem] * 2 + [hbm] * 6,
        out_specs=[vmem] * (2 + len(kept)),
        out_shape=[
            pltpu.VMEM((heads * QROWS, out_width), jnp.bfloat16),
            pltpu.VMEM(many.shape, many.dtype),
            *[pltpu.VMEM(shape, jnp.bfloat16) for shape in kept],
        ],
        scratch_shapes=[
            pltpu.VMEM((2, *slide_wq.shape), jnp.bfloat16),
            pltpu.SemaphoreType.DMA((3 + len(kept),)),
        ],
        compiler_params=small,
    )(*in_vmem(mixed), slide_gain, *in_hbm(pack_far, *slide_weights, many))
    slide_out = pl.pallas_call(
        functools.partial(slide_kernel, heads),
        in_specs=[smem] + [vmem] * 10,
        out_specs=vmem,
        out_shape=jax.ShapeDtypeStruct((slot_count, out_cols), jnp.bfloat16),
        scratch_shapes=[pltpu.VMEM((n_dev * slot_count, out_width), jnp.float32)],
        compiler_params=small,
    )(counts, *in_vmem(sent, mixed, query, *weights, many))
    return (tile_embed, slide_out)


def solution(mesh):
    placed = (
        P(("grp", "dev"), None, None),
        P("grp"),
        P("grp"),
        P(),
        P(),
        P("dev", "sub"),
        P("dev", "sub"),
        P("sub", None),
        P(),
        P(None, "sub"),
        P(None, "sub"),
        P(None, "sub"),
        P("sub", None),
    )
    return jax.shard_map(
        on_device,
        mesh=mesh,
        in_specs=placed,
        out_specs=(P(("grp", "dev"), "sub"), P(("grp", "dev"), "sub")),
        check_vma=False,
    )
```

```python
import functools
import math

import jax
import jax.numpy as jnp
from jax import lax
from jax.experimental import pallas as pl
from jax.experimental.pallas import tpu as pltpu
from jax.sharding import PartitionSpec as P

HD = 64
EPSILON = 1e-06
FLOOR = -1e30
QROWS = 8
NORM_ROWS = 32
NORM_PIECE = 128
NORM_UNROLL = 4
LANES = 128
UNIT_ROWS = 16
ROW_TILE = 16
MXU = 256
MLP_VMEM = 24 * 1024 * 1024
NORM_VMEM = 12 * 1024 * 1024
SMALL_VMEM = 4 * 1024 * 1024


def normed(rows_in, gains):
    average = jnp.mean(rows_in, axis=-1, keepdims=True)
    centred = rows_in - average
    variance = jnp.mean(centred * centred, axis=-1, keepdims=True)
    return (centred * lax.rsqrt(variance + EPSILON) * gains).astype(jnp.bfloat16)


def in_hbm(*arrays):
    return [pltpu.with_memory_space_constraint(x, pltpu.HBM) for x in arrays]


def in_vmem(*arrays):
    return [pltpu.with_memory_space_constraint(x, pltpu.VMEM) for x in arrays]


def start_kernel(parts, *refs):
    tiles_ref, gain_ref, gate_ref, up_ref, *slide_refs = refs[:8]
    out_ref, pack_ref, *block_refs = refs[8 : 10 + len(parts)]
    (
        rows,
        gain,
        average,
        scale,
        whole,
        whole_slide,
        in_sems,
        block_sems,
        slide_sems,
        gain_sem,
    ) = refs[10 + len(parts) :]
    core = lax.axis_index("sub")
    pieces, piece = rows.shape[:2]
    half, length = tiles_ref.shape[0] // 2, tiles_ref.shape[1]
    half_cols = gate_ref.shape[1] // 2
    gain_copy = pltpu.make_async_copy(gain_ref, gain, gain_sem)
    copies = [
        pltpu.make_async_copy(
            tiles_ref.at[core * half + i * piece // length, pl.ds(i * piece % length, piece)],
            rows.at[i],
            in_sems.at[i],
        )
        for i in range(pieces)
    ]
    packs = [
        pltpu.make_async_copy(ref, whole.at[i], block_sems.at[i])
        for i, ref in enumerate((gate_ref, up_ref))
    ]
    selects = []
    columns = pl.ds(pl.multiple_of(lax.rem(lax.axis_index("grp"), 2) * half_cols, LANES), half_cols)
    for k, (part, block_ref) in enumerate(zip(parts, block_refs)):
        for i, ref in enumerate((gate_ref, up_ref)):
            selects.append((block_ref, i * half_cols, whole.at[i, part, columns]))
    cols = pack_ref.shape[1]
    others = pl.ds(pl.multiple_of((1 - core) * cols, LANES), cols)
    at = 0
    for k, ref in enumerate(slide_refs):
        place = pack_ref.at[at : at + ref.shape[0]]
        if ref.shape[1] == cols:
            packs.append(pltpu.make_async_copy(ref, place, slide_sems.at[k]))
        else:
            packs.append(pltpu.make_async_copy(ref, whole_slide, slide_sems.at[k]))
            selects.append((place, 0, whole_slide.at[:, others]))
        at += ref.shape[0]
    for copy in [gain_copy] + copies + packs:
        copy.start()
    gain_copy.wait()
    gains = gain[...].reshape(1, -1)
    width = gains.shape[1]

    def grouped(function):
        def some_rows(j, carry):
            function(pl.ds(pl.multiple_of(j * NORM_ROWS, NORM_ROWS), NORM_ROWS))
            return carry

        lax.fori_loop(0, rows.shape[1] // NORM_ROWS, some_rows, 0, unroll=NORM_UNROLL)

    def lane_sum(values):
        total = values[:, :LANES]
        for k in range(LANES, width, LANES):
            total = total + values[:, k : k + LANES]
        return jnp.sum(total, axis=1, keepdims=True)

    for i in range(rows.shape[0]):
        copies[i].wait()

        def sum_rows(here):
            total = lane_sum(rows[i, here, :].astype(jnp.float32))
            average[here, :] = jnp.broadcast_to(total * (1.0 / width), (NORM_ROWS, LANES))

        def scale_rows(here):
            centred = rows[i, here, :].astype(jnp.float32) - average[here, :1]
            variance = lane_sum(centred * centred) * (1.0 / width)
            scale[here, :] = jnp.broadcast_to(
                lax.rsqrt(variance + EPSILON), (NORM_ROWS, LANES)
            )

        def norm_rows(here):
            centred = rows[i, here, :].astype(jnp.float32) - average[here, :1]
            place = pl.ds(pl.multiple_of(here.start + i * piece, NORM_ROWS), NORM_ROWS)
            out_ref[place, :] = (centred * scale[here, :1] * gains).astype(jnp.bfloat16)

        grouped(sum_rows)
        grouped(scale_rows)
        grouped(norm_rows)
    for copy in packs:
        copy.wait()
    for place, at, source in selects:
        place[:, at : at + source.shape[1]] = source[...]


def start_work(tiles, gain, gate_weight, up_weight, slide_weights, parts):
    slot_count, length, width = tiles.shape
    half = slot_count // 2
    pieces = half * length // NORM_PIECE
    hbm = pl.BlockSpec(memory_space=pltpu.HBM)
    vmem = pl.BlockSpec(memory_space=pltpu.VMEM)
    cols = gate_weight.shape[1]
    pack = (sum(w.shape[0] for w in slide_weights), slide_weights[0].shape[1])
    return pl.pallas_call(
        functools.partial(start_kernel, parts),
        in_specs=[hbm] * (4 + len(slide_weights)),
        out_specs=[vmem] * (2 + len(parts)),
        out_shape=[
            pltpu.VMEM((half * length, width), jnp.bfloat16),
            pltpu.VMEM(pack, jnp.bfloat16),
            *[pltpu.VMEM((part.stop - part.start, cols), jnp.bfloat16) for part in parts],
        ],
        scratch_shapes=[
            pltpu.VMEM((pieces, NORM_PIECE, width), jnp.bfloat16),
            pltpu.VMEM((width,), jnp.float32),
            pltpu.VMEM((NORM_PIECE, LANES), jnp.float32),
            pltpu.VMEM((NORM_PIECE, LANES), jnp.float32),
            pltpu.VMEM((2, *gate_weight.shape), jnp.bfloat16),
            pltpu.VMEM(slide_weights[-1].shape, jnp.bfloat16),
            pltpu.SemaphoreType.DMA((pieces,)),
            pltpu.SemaphoreType.DMA((2,)),
            pltpu.SemaphoreType.DMA((len(slide_weights),)),
            pltpu.SemaphoreType.DMA(()),
        ],
        compiler_params=pltpu.CompilerParams(vmem_limit_bytes=NORM_VMEM),
        cost_estimate=pl.CostEstimate(flops=0, bytes_accessed=0, transcendentals=0),
    )(*in_hbm(tiles, gain, gate_weight, up_weight, *slide_weights))


def after(value, *others):
    return lax.optimization_barrier((value, *others))[0]


class Layout:
    def __init__(self, n_dev, ny, depth):
        self.ny, self.nz, self.depth = ny, n_dev // ny, depth
        self.pair = ny * depth
        self.relative = self.pair % LANES == 0
        self.early_steps = self.nz - 1
        self.early = self.early_steps * self.pair // MXU * MXU if self.relative else 0
        cut = max(ROW_TILE, depth // 2 // ROW_TILE * ROW_TILE)
        self.parts = [slice(0, cut), slice(cut, depth)]
        self.width = n_dev * depth

    def place(self):
        me = lax.axis_index("dev")
        my_z = me // self.ny
        return my_z, me - my_z * self.ny

    def ring(self):
        return [*range(0, self.nz, 2), *range(self.nz - 1, 0, -2)]

    def source(self, step):
        my_z, _ = self.place()
        spot = jnp.where(my_z % 2 == 0, my_z // 2, self.nz - (my_z + 1) // 2)
        spot = spot - step
        spot = jnp.where(spot < 0, spot + self.nz, spot)
        return jnp.where(spot < self.nz // 2, 2 * spot, 2 * (self.nz - spot) - 1)

    def block_copies(self, blocks, weights, sems, end=None):
        _, my_y = self.place()
        copies = []
        n_parts = len(self.parts)
        first = 0 if end is None else end - len(blocks) // n_parts // self.ny
        for k, block in enumerate(blocks):
            step, flip, part = first + k // n_parts // self.ny, k // n_parts % self.ny, k % n_parts
            y = 1 - my_y if flip else my_y
            at = step if self.relative else self.source(step)
            here = self.parts[part]
            start = pl.multiple_of(at * self.pair + y * self.depth + here.start, ROW_TILE)
            place = weights.at[pl.ds(start, here.stop - here.start)]
            copies.append(pltpu.make_async_copy(block, place, sems.at[k]))
        return copies

    def row_copies(self, tiles_ref, rows, sems, steps):
        if not self.relative:
            return [pltpu.make_async_copy(tiles_ref, rows, sems.at[0])]
        copies = []
        for step in steps:
            start = pl.multiple_of(self.source(step) * self.pair, LANES)
            copies.append(
                pltpu.make_async_copy(
                    tiles_ref.at[:, pl.ds(start, self.pair)],
                    rows.at[:, step * self.pair : (step + 1) * self.pair],
                    sems.at[step],
                )
            )
        return copies


def gated_means(both, out_ref, at, length):
    cols = both.shape[1] // 2
    for tile in range(both.shape[0] // length):
        total = jnp.zeros((8, cols), jnp.float32)
        for first in range(tile * length, (tile + 1) * length, UNIT_ROWS):
            half_gate = 0.5 * both[first : first + UNIT_ROWS, :cols]
            up_part = both[first : first + UNIT_ROWS, cols:]
            gated = (half_gate * jnp.tanh(half_gate) + half_gate) * up_part
            total = total + jnp.sum(gated.reshape(UNIT_ROWS // 8, 8, cols), axis=0)
        out_ref[at + tile : at + tile + 1, :] = jnp.sum(total, axis=0, keepdims=True) * (
            1.0 / length
        )


def product(out, rows, weights, first, last, more=None):
    for at in range(0, rows.shape[0], MXU):
        here = slice(at, at + MXU)
        both = jnp.dot(
            rows[here, first:last], weights[first:last, :], preferred_element_type=jnp.float32
        )
        out[here, :] = both if more is None else both + more[here, :]


def early_kernel(layout, *refs):
    steps = range(layout.early_steps)
    n_blocks = len(steps) * layout.ny * len(layout.parts)
    blocks, tile_refs = refs[:n_blocks], refs[n_blocks : n_blocks + 2]
    out_ref, weights, rows, weight_sems, row_sems = refs[n_blocks + 2 :]
    loads = layout.block_copies(blocks, weights, weight_sems)
    row_loads = [
        layout.row_copies(ref, rows.at[i], row_sems.at[i], steps)
        for i, ref in enumerate(tile_refs)
    ]
    late_loads = [
        copy
        for i, ref in enumerate(tile_refs)
        for copy in layout.row_copies(
            ref, rows.at[i], row_sems.at[i], range(layout.early_steps, layout.nz)
        )
    ]
    for copy in row_loads[0] + loads + row_loads[1] + late_loads:
        copy.start()
    for copy in loads:
        copy.wait()
    for i in range(2):
        for copy in row_loads[i]:
            copy.wait()
        product(out_ref.at[i], rows.at[i], weights, 0, layout.early)
    for copy in late_loads:
        copy.wait()


def early_mlp(layout, blocks, tiles):
    n_rows = tiles[0].shape[0]
    cols = blocks[0].shape[1]
    hbm = pl.BlockSpec(memory_space=pltpu.HBM)
    vmem = pl.BlockSpec(memory_space=pltpu.VMEM)
    return pl.pallas_call(
        functools.partial(early_kernel, layout),
        in_specs=[hbm] * (len(blocks) - 4) + [pl.BlockSpec(memory_space=pl.ANY)] * 6,
        out_specs=(vmem, vmem, vmem),
        out_shape=(
            pltpu.VMEM((2, n_rows, cols), jnp.float32),
            pltpu.VMEM((layout.width, cols), jnp.bfloat16),
            pltpu.VMEM((2, n_rows, layout.width), jnp.bfloat16),
        ),
        scratch_shapes=[
            pltpu.SemaphoreType.DMA((len(blocks),)),
            pltpu.SemaphoreType.DMA((2, layout.nz)),
        ],
        compiler_params=pltpu.CompilerParams(vmem_limit_bytes=MLP_VMEM),
        cost_estimate=pl.CostEstimate(
            flops=4 * n_rows * layout.early * cols,
            bytes_accessed=2 * layout.early * (cols + 2 * n_rows) + 8 * n_rows * cols,
            transcendentals=0,
        ),
    )(*in_hbm(*blocks[:-4]), *blocks[-4:], *tiles)


def packed(mine, others):
    low = lax.axis_index("sub") == 0
    rows = jnp.concatenate([jnp.where(low, mine, others), jnp.where(low, others, mine)], axis=0)
    return jnp.concatenate(
        [rows[:, k : k + LANES] for k in range(0, rows.shape[1], LANES)], axis=0
    ).astype(jnp.bfloat16)


def middle_kernel(layout, length, n_blocks, n_tiles, *refs):
    blocks, tile_refs = refs[:n_blocks], refs[n_blocks : n_blocks + n_tiles]
    early_refs = refs[n_blocks + n_tiles : -9]
    pair_ref, weights, own_ref, rows, even, odd, means, weight_sems, row_sems = refs[-9:]
    early = layout.early
    loads = layout.block_copies(blocks, weights, weight_sems, layout.nz)
    row_loads = [
        layout.row_copies(ref, rows.at[i], row_sems.at[i], range(layout.nz))
        for i, ref in enumerate(tile_refs)
    ]
    for copy in [copy for copies in [loads, *row_loads] for copy in copies]:
        copy.start()
    for copy in loads:
        copy.wait()
    units = [(early_refs[2].at[i], early_refs[0].at[i], []) for i in range(2)] if early else []
    units += [(rows.at[i], None, row_loads[i]) for i in range(n_tiles)]
    pending = None
    for i, (unit, more, waits) in enumerate(units):
        for copy in waits:
            copy.wait()
        for j in range(unit.shape[0] // length):
            here = slice(j * length, (j + 1) * length)
            tile = unit.shape[0] // length * i + j
            both = (even, odd)[tile % 2]
            if more is None:
                product(both, unit.at[here], weights, 0, layout.width)
            else:
                product(both, unit.at[here], weights, early, layout.width, more.at[here])
            if pending is not None:
                gated_means(*pending, length)
            pending = (both, means, tile)
    gated_means(*pending, length)
    half = means.shape[0] // 3
    own_ref[...] = packed(means[:half, :], means[half : 2 * half, :])
    pair_ref[...] = means[2 * half :, :]


def middle_mlp(layout, blocks, tiles, early, length):
    n_rows, width = tiles[0].shape
    cols = blocks[0].shape[1]
    half = n_rows // length
    tiles = tiles[2:] if early else tiles
    vmem = pl.BlockSpec(memory_space=pltpu.VMEM)
    return pl.pallas_call(
        functools.partial(middle_kernel, layout, length, len(blocks), len(tiles)),
        in_specs=[pl.BlockSpec(memory_space=pl.ANY)] * (len(blocks) + len(tiles))
        + [vmem] * len(early),
        out_specs=(vmem, vmem, vmem),
        out_shape=(
            pltpu.VMEM((half, cols // 2), jnp.float32),
            pltpu.VMEM((width, cols), jnp.bfloat16),
            jax.ShapeDtypeStruct((half * cols // LANES, LANES), jnp.bfloat16),
        ),
        input_output_aliases={len(blocks) + len(tiles) + 1: 1} if early else {},
        scratch_shapes=[
            pltpu.VMEM((len(tiles), n_rows, width), jnp.bfloat16),
            pltpu.VMEM((length, cols), jnp.float32),
            pltpu.VMEM((length, cols), jnp.float32),
            pltpu.VMEM((3 * half, cols // 2), jnp.float32),
            pltpu.SemaphoreType.DMA((len(blocks),)),
            pltpu.SemaphoreType.DMA((len(tiles), layout.nz)),
        ],
        compiler_params=pltpu.CompilerParams(vmem_limit_bytes=MLP_VMEM),
        cost_estimate=pl.CostEstimate(
            flops=4 * n_rows * width * cols,
            bytes_accessed=2 * (3 * n_rows * width + width * cols),
            transcendentals=0,
        ),
    )(*blocks, *(tiles if early else in_hbm(*tiles)), *in_vmem(*early))


def last_kernel(layout, length, means_ref, weights, tiles_ref, out_ref, rows, both, means, row_sems):
    row_loads = layout.row_copies(tiles_ref, rows, row_sems, range(layout.nz))
    for copy in row_loads:
        copy.start()
    for copy in row_loads:
        copy.wait()
    half = rows.shape[0] // length
    for i in range(half):
        here = slice(i * length, (i + 1) * length)
        product(both[i], rows.at[here], weights, 0, layout.width)
        if i:
            gated_means(both[i - 1], means, i - 1, length)
    gated_means(both[half - 1], means, half - 1, length)
    out_ref[...] = packed(means_ref[...], means[...])


def last_mlp(layout, means, weights, tiles, length):
    n_rows, width = tiles.shape
    cols = weights.shape[1]
    half = n_rows // length
    any_spec = pl.BlockSpec(memory_space=pl.ANY)
    vmem = pl.BlockSpec(memory_space=pltpu.VMEM)
    return pl.pallas_call(
        functools.partial(last_kernel, layout, length),
        in_specs=[vmem, vmem, any_spec],
        out_specs=vmem,
        out_shape=jax.ShapeDtypeStruct((half * cols // LANES, LANES), jnp.bfloat16),
        scratch_shapes=[
            pltpu.VMEM((n_rows, width), jnp.bfloat16),
            [pltpu.VMEM((length, cols), jnp.float32) for _ in range(half)],
            pltpu.VMEM((half, cols // 2), jnp.float32),
            pltpu.SemaphoreType.DMA((layout.nz,)),
        ],
        compiler_params=pltpu.CompilerParams(vmem_limit_bytes=MLP_VMEM),
        cost_estimate=pl.CostEstimate(
            flops=2 * n_rows * width * cols,
            bytes_accessed=2 * (n_rows * width + width * cols),
            transcendentals=0,
        ),
    )(*in_vmem(means, weights), tiles)


def small_mod(value, rate):
    return jnp.where(
        rate == 1,
        0,
        jnp.where(rate == 2, value & 1, jnp.where(rate == 3, lax.rem(value, 3), value & 3)),
    )


def multiplicity_kernel(n_dev, slot_count, heads, counts_ref, slide_ref, rates_ref, out_ref):
    me, core = lax.axis_index("dev"), lax.axis_index("sub")
    shape = out_ref.shape
    row = lax.broadcasted_iota(jnp.int32, shape, 0)
    col = lax.broadcasted_iota(jnp.int32, shape, 1)
    head = row // QROWS + core * (heads // 2)
    head = jnp.where(head >= heads, head - heads, head)
    query = row % QROWS
    device, slot = col // slot_count, col % slot_count
    rate = jnp.full(shape, 1, jnp.int32)
    for h in range(heads):
        rate = jnp.where(head == h, rates_ref[h], rate)
    my_slide = slide_ref[me]
    first = me
    count = jnp.zeros(shape, jnp.int32)
    slide = jnp.zeros(shape, jnp.int32)
    for k in reversed(range(n_dev)):
        first = jnp.where(slide_ref[k] == my_slide, k, first)
        count = jnp.where(device == k, counts_ref[k], count)
        slide = jnp.where(device == k, slide_ref[k], slide)
    offset = small_mod(head, rate)
    query_position = (me - first) * slot_count + query
    key_position = (device - first) * slot_count + slot
    valid = slot < count
    near = jnp.where((device == me) & valid, 1.0, 0.0)
    far = jnp.where(
        (slide == my_slide)
        & valid
        & (small_mod(query_position, rate) == offset)
        & (small_mod(key_position, rate) == offset),
        1.0,
        0.0,
    )
    out_ref[...] = near + far


def embed_kernel(
    counts_ref,
    own_ref,
    own_far_ref,
    pair_ref,
    pair_far_ref,
    gain_ref,
    near_ref,
    far_ref,
    embed_ref,
    mixed_ref,
    sent_ref,
):
    slot_count, half = embed_ref.shape
    n_blocks = half // 2 // LANES
    low = lax.rem(lax.axis_index("grp"), 2) == 0
    count = counts_ref[lax.axis_index("dev")]

    def features(mine_ref, theirs_ref):
        sides = []
        for ref in (mine_ref, theirs_ref):
            part = ref[...].astype(jnp.float32)
            pieces = [part[k * slot_count : (k + 1) * slot_count] for k in range(n_blocks)]
            sides.append(jnp.concatenate(pieces, axis=1))
        mine, theirs = sides
        rows = jnp.concatenate(
            [jnp.where(low, mine, theirs), jnp.where(low, theirs, mine)], axis=1
        )
        slot = lax.broadcasted_iota(jnp.int32, rows.shape, 0)
        return jnp.where(slot < count, rows, 0.0).astype(jnp.bfloat16)

    near = features(own_ref, pair_ref)
    far = features(own_far_ref, pair_far_ref)
    embed_ref[...] = near
    mixed = jnp.dot(near, near_ref[...], preferred_element_type=jnp.float32) + jnp.dot(
        far, far_ref[...], preferred_element_type=jnp.float32
    )
    mixed_ref[...] = jnp.concatenate([mixed, mixed], axis=0)
    hidden = normed(mixed, gain_ref[...].reshape(1, -1)).astype(jnp.float32)
    width = sent_ref.shape[2]
    pieces = [hidden[:, k : k + width] for k in range(0, hidden.shape[1], width)]
    pieces += [jnp.zeros_like(pieces[0])] * (sent_ref.shape[1] // slot_count - len(pieces))
    sent = jnp.concatenate(pieces, axis=0).astype(jnp.bfloat16)
    for k in range(sent_ref.shape[0]):
        sent_ref[k] = sent


def project(rows, near_ref, far_ref):
    return jnp.concatenate(
        [
            jnp.dot(rows, near_ref[...], preferred_element_type=jnp.float32),
            jnp.dot(rows, far_ref[...], preferred_element_type=jnp.float32),
        ],
        axis=1,
    )


def heads_of(shape):
    return (
        lax.broadcasted_iota(jnp.int32, shape, 0) // QROWS
        == lax.broadcasted_iota(jnp.int32, shape, 1) // HD
    )


def query_kernel(heads, mixed_ref, gain_ref, far_ref, *refs):
    near_refs, (many_ref, out_ref, many, *kept), (wq, sems) = refs[:4], refs[4:-2], refs[-2:]
    places = [wq.at[0], wq.at[1], *kept]
    copies = []
    at = 0
    for k, near in enumerate(near_refs):
        far = far_ref.at[at : at + near.shape[0]]
        at += near.shape[0]
        for i, source in enumerate((near, far)):
            copies.append(pltpu.make_async_copy(source, places[2 * k + i], sems.at[2 * k + i]))
    copies.append(pltpu.make_async_copy(many_ref, many, sems.at[len(copies)]))
    for copy in copies:
        copy.start()
    hidden = normed(mixed_ref[...], gain_ref[...].reshape(1, -1))
    for copy in copies[:2]:
        copy.wait()
    query = project(hidden, wq.at[0], wq.at[1])
    spread = jnp.concatenate([query] * heads, axis=0)
    out_ref[...] = jnp.where(heads_of(spread.shape), spread, 0.0).astype(jnp.bfloat16)
    for copy in copies[2:]:
        copy.wait()


def slide_kernel(
    heads,
    counts_ref,
    sent_ref,
    mixed_ref,
    query_ref,
    wk_ref,
    wk_far_ref,
    wv_ref,
    wv_far_ref,
    wo_ref,
    wo_far_ref,
    many_ref,
    out_ref,
    rows,
):
    slot_count, half = out_ref.shape
    core = lax.axis_index("sub")
    count = counts_ref[lax.axis_index("dev")]
    width = sent_ref.shape[2]
    for k in range(sent_ref.shape[0]):
        sent = sent_ref[k].astype(jnp.float32)
        rows[k * slot_count : (k + 1) * slot_count, :] = jnp.concatenate(
            [
                sent[j * slot_count : (j + 1) * slot_count]
                for j in range(rows.shape[1] // width)
            ],
            axis=1,
        )
    hidden = rows[...].astype(jnp.bfloat16)
    keys = project(hidden, wk_ref, wk_far_ref).astype(jnp.bfloat16)
    scores = lax.dot_general(
        query_ref[...], keys, (((1,), (1,)), ((), ())), preferred_element_type=jnp.float32
    ) * (1.0 / math.sqrt(HD))
    values = project(hidden, wv_ref, wv_far_ref).astype(jnp.bfloat16)
    many = many_ref[...]
    masked = jnp.where(many > 0.0, scores, FLOOR)
    weights = many * jnp.exp(masked - jnp.max(masked, axis=1, keepdims=True))
    weights = weights / jnp.sum(weights, axis=1, keepdims=True)
    context = jnp.dot(weights.astype(jnp.bfloat16), values, preferred_element_type=jnp.float32)
    context = jnp.where(heads_of(context.shape), context, 0.0)
    context = context.reshape(heads, QROWS, context.shape[1])
    context = jnp.sum(context, axis=0).astype(jnp.bfloat16)
    columns = pl.ds(pl.multiple_of(core * half, LANES), half)
    attended = jnp.dot(
        context[:, :half], wo_ref[:, columns], preferred_element_type=jnp.float32
    ) + jnp.dot(context[:, half:], wo_far_ref[...], preferred_element_type=jnp.float32)
    total = mixed_ref[:, columns] + attended
    slot = lax.broadcasted_iota(jnp.int32, total.shape, 0)
    total = jnp.where(slot < count, total, 0.0)
    out_ref[...] = total[:slot_count].astype(jnp.bfloat16)


def on_device(
    tiles,
    counts,
    slide_of,
    rates,
    tile_gain,
    gate_weight,
    up_weight,
    embed_proj,
    slide_gain,
    slide_wq,
    slide_wk,
    slide_wv,
    slide_wo,
):
    slot_count, length, width = tiles.shape
    hidden_cols = gate_weight.shape[1]
    n_grp, n_dev, n_sub = (lax.axis_size(a) for a in ("grp", "dev", "sub"))
    ny = 2
    nz = n_dev // ny
    heads = slide_wq.shape[1] * n_sub // HD
    core = lax.axis_index("sub")

    to_pair = [(g, g ^ 1) for g in range(n_grp)]
    to_sibling = [(s, s ^ 1) for s in range(n_sub)]
    along_y = [(d, d ^ 1) for d in range(n_dev)]

    layout = Layout(n_dev, ny, gate_weight.shape[0])
    ring = layout.ring()
    along_z = [
        (z * ny + y, ring[(i + 1) % nz] * ny + y) for i, z in enumerate(ring) for y in range(ny)
    ]
    slide_weights = [slide_wq, slide_wk, slide_wv, slide_wo]
    first, pack, *held = start_work(
        tiles, tile_gain, gate_weight, up_weight, slide_weights, layout.parts
    )
    second = lax.ppermute(first, "sub", to_sibling)
    pair_first = lax.ppermute(first, "grp", to_pair)
    proj_far = lax.ppermute(embed_proj, "sub", to_sibling)
    pack_far = lax.ppermute(pack, "sub", to_sibling)
    out_cols = slide_wo.shape[1] // n_sub
    smem = pl.BlockSpec(memory_space=pltpu.SMEM)
    vmem = pl.BlockSpec(memory_space=pltpu.VMEM)
    many = pl.pallas_call(
        functools.partial(multiplicity_kernel, n_dev, slot_count, heads),
        in_specs=[smem] * 3,
        out_specs=vmem,
        out_shape=jax.ShapeDtypeStruct((heads * QROWS, n_dev * slot_count), jnp.float32),
        compiler_params=pltpu.CompilerParams(vmem_limit_bytes=SMALL_VMEM),
    )(counts, slide_of, rates)

    held[1] = after(held[1], proj_far, second)
    steps = []
    last = None
    for step in range(nz):
        sent = []
        for part in range(len(held)):
            over = None
            if step:
                arrived = lax.ppermute(held[part], "dev", along_z)
                others = [] if last is None else [last]
                over = steps[-1][len(held) + part]
                if (step, part) != (nz - 1, 1):
                    others.append(over)
                if (step, part) == (nz - 1, 0):
                    others += [many]
                held[part] = last = after(arrived, *others)
            if (step, part) == (nz - 1, 0):
                sent.append(lax.ppermute(after(over, last), "dev", along_z))
            else:
                sent.append(lax.ppermute(held[part], "dev", along_y))
        steps.append([*held, *sent])
    blocks = [block for step in steps for block in step]
    early = []
    if layout.relative:
        n_early = layout.early_steps * len(steps[0])
        early = early_mlp(layout, blocks[:n_early], [after(first, last), second])
        blocks = blocks[n_early:]
    pair_first = after(pair_first, *steps[-1][-2:], *early)
    pair_second = lax.ppermute(pair_first, "sub", to_sibling)
    means, weights, own = middle_mlp(
        layout, blocks, [first, second, pair_first], early, length
    )
    own_far = lax.ppermute(own, "sub", to_sibling)
    pair = last_mlp(layout, means, weights, pair_second, length)
    across = [
        (g * n_sub + s, (g ^ 1) * n_sub + (s ^ 1)) for g in range(n_grp) for s in range(n_sub)
    ]
    pair_far = lax.ppermute(pair, ("grp", "sub"), across)
    pair = lax.ppermute(pair, "grp", to_pair)

    out_width = embed_proj.shape[1]
    sent_rows = 16
    sent_cols = 2 * LANES
    small = pltpu.CompilerParams(vmem_limit_bytes=SMALL_VMEM)
    tile_embed, mixed, sent = pl.pallas_call(
        embed_kernel,
        in_specs=[smem] + [vmem] * 7,
        out_specs=(vmem, vmem, vmem),
        out_shape=(
            jax.ShapeDtypeStruct((slot_count, hidden_cols), jnp.bfloat16),
            pltpu.VMEM((QROWS, out_width), jnp.float32),
            pltpu.VMEM((n_dev, sent_rows, sent_cols), jnp.bfloat16),
        ),
        compiler_params=small,
    )(counts, *in_vmem(own, own_far, pair, pair_far), slide_gain, embed_proj, proj_far)
    sent = lax.all_to_all(sent, "dev", split_axis=0, concat_axis=0, tiled=True)
    hbm = pl.BlockSpec(memory_space=pltpu.HBM)
    far_shape = (slide_wo.shape[0], out_cols)
    kept = [slide_wk.shape] * 4 + [slide_wo.shape, far_shape]
    query, many, *weights = pl.pallas_call(
        functools.partial(query_kernel, heads),
        in_specs=[vmem] * 2 + [hbm] * 6,
        out_specs=[vmem] * (2 + len(kept)),
        out_shape=[
            pltpu.VMEM((heads * QROWS, out_width), jnp.bfloat16),
            pltpu.VMEM(many.shape, many.dtype),
            *[pltpu.VMEM(shape, jnp.bfloat16) for shape in kept],
        ],
        scratch_shapes=[
            pltpu.VMEM((2, *slide_wq.shape), jnp.bfloat16),
            pltpu.SemaphoreType.DMA((3 + len(kept),)),
        ],
        compiler_params=small,
    )(*in_vmem(mixed), slide_gain, *in_hbm(pack_far, *slide_weights, many))
    slide_out = pl.pallas_call(
        functools.partial(slide_kernel, heads),
        in_specs=[smem] + [vmem] * 10,
        out_specs=vmem,
        out_shape=jax.ShapeDtypeStruct((slot_count, out_cols), jnp.bfloat16),
        scratch_shapes=[pltpu.VMEM((n_dev * slot_count, out_width), jnp.float32)],
        compiler_params=small,
    )(counts, *in_vmem(sent, mixed, query, *weights, many))
    return (tile_embed, slide_out)


def solution(mesh):
    placed = (
        P(("grp", "dev"), None, None),
        P("grp"),
        P("grp"),
        P(),
        P(),
        P("dev", "sub"),
        P("dev", "sub"),
        P("sub", None),
        P(),
        P(None, "sub"),
        P(None, "sub"),
        P(None, "sub"),
        P("sub", None),
    )
    return jax.shard_map(
        on_device,
        mesh=mesh,
        in_specs=placed,
        out_specs=(P(("grp", "dev"), "sub"), P(("grp", "dev"), "sub")),
        check_vma=False,
    )
```

```python
import functools
import math

import jax
import jax.numpy as jnp
from jax import lax
from jax.experimental import pallas as pl
from jax.experimental.pallas import tpu as pltpu
from jax.sharding import PartitionSpec as P

HD = 64
EPSILON = 1e-06
FLOOR = -1e30
QROWS = 8
NORM_ROWS = 32
NORM_PIECE = 128
NORM_UNROLL = 4
LANES = 128
UNIT_ROWS = 16
ROW_TILE = 16
MXU = 256
MLP_VMEM = 24 * 1024 * 1024
NORM_VMEM = 12 * 1024 * 1024
SMALL_VMEM = 4 * 1024 * 1024


def normed(rows_in, gains):
    average = jnp.mean(rows_in, axis=-1, keepdims=True)
    centred = rows_in - average
    variance = jnp.mean(centred * centred, axis=-1, keepdims=True)
    return (centred * lax.rsqrt(variance + EPSILON) * gains).astype(jnp.bfloat16)


def in_hbm(*arrays):
    return [pltpu.with_memory_space_constraint(x, pltpu.HBM) for x in arrays]


def in_vmem(*arrays):
    return [pltpu.with_memory_space_constraint(x, pltpu.VMEM) for x in arrays]


def start_kernel(parts, *refs):
    tiles_ref, gain_ref, gate_ref, up_ref, *slide_refs = refs[:8]
    out_ref, pack_ref, whole_ref, *block_refs = refs[8 : 11 + len(parts)]
    (
        rows,
        gain,
        average,
        scale,
        whole,
        whole_slide,
        in_sems,
        block_sems,
        slide_sems,
        gain_sem,
    ) = refs[11 + len(parts) :]
    core = lax.axis_index("sub")
    pieces, piece = rows.shape[:2]
    half, length = tiles_ref.shape[0] // 2, tiles_ref.shape[1]
    half_cols = gate_ref.shape[1] // 2
    gain_copy = pltpu.make_async_copy(gain_ref, gain, gain_sem)
    copies = [
        pltpu.make_async_copy(
            tiles_ref.at[core * half + i * piece // length, pl.ds(i * piece % length, piece)],
            rows.at[i],
            in_sems.at[i],
        )
        for i in range(pieces)
    ]
    packs = [
        pltpu.make_async_copy(ref, whole.at[i], block_sems.at[i])
        for i, ref in enumerate((gate_ref, up_ref))
    ]
    selects = []
    columns = pl.ds(pl.multiple_of(lax.rem(lax.axis_index("grp"), 2) * half_cols, LANES), half_cols)
    for k, (part, block_ref) in enumerate(zip(parts, block_refs)):
        for i, ref in enumerate((gate_ref, up_ref)):
            selects.append((block_ref, i * half_cols, whole.at[i, part, columns]))
    for i in range(2):
        selects.append((whole_ref, i * half_cols, whole.at[i, :, columns]))
    cols = pack_ref.shape[1]
    others = pl.ds(pl.multiple_of((1 - core) * cols, LANES), cols)
    at = 0
    for k, ref in enumerate(slide_refs):
        place = pack_ref.at[at : at + ref.shape[0]]
        if ref.shape[1] == cols:
            packs.append(pltpu.make_async_copy(ref, place, slide_sems.at[k]))
        else:
            packs.append(pltpu.make_async_copy(ref, whole_slide, slide_sems.at[k]))
            selects.append((place, 0, whole_slide.at[:, others]))
        at += ref.shape[0]
    for copy in [gain_copy] + copies + packs:
        copy.start()
    gain_copy.wait()
    gains = gain[...].reshape(1, -1)
    width = gains.shape[1]

    def grouped(function):
        def some_rows(j, carry):
            function(pl.ds(pl.multiple_of(j * NORM_ROWS, NORM_ROWS), NORM_ROWS))
            return carry

        lax.fori_loop(0, rows.shape[1] // NORM_ROWS, some_rows, 0, unroll=NORM_UNROLL)

    def lane_sum(values):
        total = values[:, :LANES]
        for k in range(LANES, width, LANES):
            total = total + values[:, k : k + LANES]
        return jnp.sum(total, axis=1, keepdims=True)

    for i in range(rows.shape[0]):
        copies[i].wait()

        def sum_rows(here):
            total = lane_sum(rows[i, here, :].astype(jnp.float32))
            average[here, :] = jnp.broadcast_to(total * (1.0 / width), (NORM_ROWS, LANES))

        def scale_rows(here):
            centred = rows[i, here, :].astype(jnp.float32) - average[here, :1]
            variance = lane_sum(centred * centred) * (1.0 / width)
            scale[here, :] = jnp.broadcast_to(
                lax.rsqrt(variance + EPSILON), (NORM_ROWS, LANES)
            )

        def norm_rows(here):
            centred = rows[i, here, :].astype(jnp.float32) - average[here, :1]
            place = pl.ds(pl.multiple_of(here.start + i * piece, NORM_ROWS), NORM_ROWS)
            out_ref[place, :] = (centred * scale[here, :1] * gains).astype(jnp.bfloat16)

        grouped(sum_rows)
        grouped(scale_rows)
        grouped(norm_rows)
    for copy in packs:
        copy.wait()
    for place, at, source in selects:
        place[:, at : at + source.shape[1]] = source[...]


def start_work(tiles, gain, gate_weight, up_weight, slide_weights, parts):
    slot_count, length, width = tiles.shape
    half = slot_count // 2
    pieces = half * length // NORM_PIECE
    hbm = pl.BlockSpec(memory_space=pltpu.HBM)
    vmem = pl.BlockSpec(memory_space=pltpu.VMEM)
    cols = gate_weight.shape[1]
    pack = (sum(w.shape[0] for w in slide_weights), slide_weights[0].shape[1])
    return pl.pallas_call(
        functools.partial(start_kernel, parts),
        in_specs=[hbm] * (4 + len(slide_weights)),
        out_specs=[vmem] * (3 + len(parts)),
        out_shape=[
            pltpu.VMEM((half * length, width), jnp.bfloat16),
            pltpu.VMEM(pack, jnp.bfloat16),
            pltpu.VMEM(gate_weight.shape, jnp.bfloat16),
            *[pltpu.VMEM((part.stop - part.start, cols), jnp.bfloat16) for part in parts],
        ],
        scratch_shapes=[
            pltpu.VMEM((pieces, NORM_PIECE, width), jnp.bfloat16),
            pltpu.VMEM((width,), jnp.float32),
            pltpu.VMEM((NORM_PIECE, LANES), jnp.float32),
            pltpu.VMEM((NORM_PIECE, LANES), jnp.float32),
            pltpu.VMEM((2, *gate_weight.shape), jnp.bfloat16),
            pltpu.VMEM(slide_weights[-1].shape, jnp.bfloat16),
            pltpu.SemaphoreType.DMA((pieces,)),
            pltpu.SemaphoreType.DMA((2,)),
            pltpu.SemaphoreType.DMA((len(slide_weights),)),
            pltpu.SemaphoreType.DMA(()),
        ],
        compiler_params=pltpu.CompilerParams(vmem_limit_bytes=NORM_VMEM),
        cost_estimate=pl.CostEstimate(flops=0, bytes_accessed=0, transcendentals=0),
    )(*in_hbm(tiles, gain, gate_weight, up_weight, *slide_weights))


def after(value, *others):
    return lax.optimization_barrier((value, *others))[0]


class Layout:
    def __init__(self, n_dev, ny, depth):
        self.ny, self.nz, self.depth = ny, n_dev // ny, depth
        self.pair = ny * depth
        self.relative = self.pair % LANES == 0
        self.early_steps = self.nz - 1
        self.early = self.early_steps * self.pair // MXU * MXU if self.relative else 0
        cut = max(ROW_TILE, depth // 2 // ROW_TILE * ROW_TILE)
        self.parts = [slice(0, cut), slice(cut, depth)]
        self.width = n_dev * depth

    def place(self):
        me = lax.axis_index("dev")
        my_z = me // self.ny
        return my_z, me - my_z * self.ny

    def ring(self):
        return [*range(0, self.nz, 2), *range(self.nz - 1, 0, -2)]

    def source(self, step):
        my_z, _ = self.place()
        spot = jnp.where(my_z % 2 == 0, my_z // 2, self.nz - (my_z + 1) // 2)
        spot = spot - step
        spot = jnp.where(spot < 0, spot + self.nz, spot)
        return jnp.where(spot < self.nz // 2, 2 * spot, 2 * (self.nz - spot) - 1)

    def block_copies(self, blocks, weights, sems, end=None):
        _, my_y = self.place()
        copies = []
        n_parts = len(self.parts)
        first = 0 if end is None else end - len(blocks) // n_parts // self.ny
        for k, block in enumerate(blocks):
            step, flip, part = first + k // n_parts // self.ny, k // n_parts % self.ny, k % n_parts
            y = 1 - my_y if flip else my_y
            at = step if self.relative else self.source(step)
            here = self.parts[part]
            start = pl.multiple_of(at * self.pair + y * self.depth + here.start, ROW_TILE)
            place = weights.at[pl.ds(start, here.stop - here.start)]
            copies.append(pltpu.make_async_copy(block, place, sems.at[k]))
        return copies

    def halves(self, blocks):
        n = len(self.parts)
        return [*blocks[:n], *[blocks[n].at[part] for part in self.parts], *blocks[n + 1 :]]

    def row_copies(self, tiles_ref, rows, sems, steps):
        if not self.relative:
            return [pltpu.make_async_copy(tiles_ref, rows, sems.at[0])]
        copies = []
        for step in steps:
            start = pl.multiple_of(self.source(step) * self.pair, LANES)
            copies.append(
                pltpu.make_async_copy(
                    tiles_ref.at[:, pl.ds(start, self.pair)],
                    rows.at[:, step * self.pair : (step + 1) * self.pair],
                    sems.at[step],
                )
            )
        return copies


def gated_means(both, out_ref, at, length):
    cols = both.shape[1] // 2
    for tile in range(both.shape[0] // length):
        total = jnp.zeros((8, cols), jnp.float32)
        for first in range(tile * length, (tile + 1) * length, UNIT_ROWS):
            half_gate = 0.5 * both[first : first + UNIT_ROWS, :cols]
            up_part = both[first : first + UNIT_ROWS, cols:]
            gated = (half_gate * jnp.tanh(half_gate) + half_gate) * up_part
            total = total + jnp.sum(gated.reshape(UNIT_ROWS // 8, 8, cols), axis=0)
        out_ref[at + tile : at + tile + 1, :] = jnp.sum(total, axis=0, keepdims=True) * (
            1.0 / length
        )


def product(out, rows, weights, first, last, more=None):
    for at in range(0, rows.shape[0], MXU):
        here = slice(at, at + MXU)
        both = jnp.dot(
            rows[here, first:last], weights[first:last, :], preferred_element_type=jnp.float32
        )
        out[here, :] = both if more is None else both + more[here, :]


def early_kernel(layout, *refs):
    steps = range(layout.early_steps)
    n_blocks = len(steps) * layout.ny * len(layout.parts) - 1
    blocks, tile_refs = layout.halves(refs[:n_blocks]), refs[n_blocks : n_blocks + 2]
    out_ref, weights, rows, weight_sems, row_sems = refs[n_blocks + 2 :]
    loads = layout.block_copies(blocks, weights, weight_sems)
    row_loads = [
        layout.row_copies(ref, rows.at[i], row_sems.at[i], steps)
        for i, ref in enumerate(tile_refs)
    ]
    late_loads = [
        copy
        for i, ref in enumerate(tile_refs)
        for copy in layout.row_copies(
            ref, rows.at[i], row_sems.at[i], range(layout.early_steps, layout.nz)
        )
    ]
    for copy in row_loads[0] + loads + row_loads[1] + late_loads:
        copy.start()
    for copy in loads:
        copy.wait()
    for i in range(2):
        for copy in row_loads[i]:
            copy.wait()
        product(out_ref.at[i], rows.at[i], weights, 0, layout.early)
    for copy in late_loads:
        copy.wait()


def early_mlp(layout, blocks, tiles):
    n_rows = tiles[0].shape[0]
    cols = blocks[0].shape[1]
    hbm = pl.BlockSpec(memory_space=pltpu.HBM)
    vmem = pl.BlockSpec(memory_space=pltpu.VMEM)
    return pl.pallas_call(
        functools.partial(early_kernel, layout),
        in_specs=[hbm] * (len(blocks) - 4) + [pl.BlockSpec(memory_space=pl.ANY)] * 6,
        out_specs=(vmem, vmem, vmem),
        out_shape=(
            pltpu.VMEM((2, n_rows, cols), jnp.float32),
            pltpu.VMEM((layout.width, cols), jnp.bfloat16),
            pltpu.VMEM((2, n_rows, layout.width), jnp.bfloat16),
        ),
        scratch_shapes=[
            pltpu.SemaphoreType.DMA((len(blocks) + 1,)),
            pltpu.SemaphoreType.DMA((2, layout.nz)),
        ],
        compiler_params=pltpu.CompilerParams(vmem_limit_bytes=MLP_VMEM),
        cost_estimate=pl.CostEstimate(
            flops=4 * n_rows * layout.early * cols,
            bytes_accessed=2 * layout.early * (cols + 2 * n_rows) + 8 * n_rows * cols,
            transcendentals=0,
        ),
    )(*in_hbm(*blocks[:-4]), *blocks[-4:], *tiles)


def packed(mine, others):
    low = lax.axis_index("sub") == 0
    rows = jnp.concatenate([jnp.where(low, mine, others), jnp.where(low, others, mine)], axis=0)
    return jnp.concatenate(
        [rows[:, k : k + LANES] for k in range(0, rows.shape[1], LANES)], axis=0
    ).astype(jnp.bfloat16)


def middle_kernel(layout, length, n_blocks, n_tiles, *refs):
    blocks, tile_refs = refs[:n_blocks], refs[n_blocks : n_blocks + n_tiles]
    early_refs = refs[n_blocks + n_tiles : -9]
    pair_ref, weights, own_ref, rows, even, odd, means, weight_sems, row_sems = refs[-9:]
    early = layout.early
    if not early:
        blocks = layout.halves(blocks)
    loads = layout.block_copies(blocks, weights, weight_sems, layout.nz)
    row_loads = [
        layout.row_copies(ref, rows.at[i], row_sems.at[i], range(layout.nz))
        for i, ref in enumerate(tile_refs)
    ]
    for copy in [copy for copies in [loads, *row_loads] for copy in copies]:
        copy.start()
    for copy in loads:
        copy.wait()
    units = [(early_refs[2].at[i], early_refs[0].at[i], []) for i in range(2)] if early else []
    units += [(rows.at[i], None, row_loads[i]) for i in range(n_tiles)]
    pending = None
    for i, (unit, more, waits) in enumerate(units):
        for copy in waits:
            copy.wait()
        for j in range(unit.shape[0] // length):
            here = slice(j * length, (j + 1) * length)
            tile = unit.shape[0] // length * i + j
            both = (even, odd)[tile % 2]
            if more is None:
                product(both, unit.at[here], weights, 0, layout.width)
            else:
                product(both, unit.at[here], weights, early, layout.width, more.at[here])
            if pending is not None:
                gated_means(*pending, length)
            pending = (both, means, tile)
    gated_means(*pending, length)
    half = means.shape[0] // 3
    own_ref[...] = packed(means[:half, :], means[half : 2 * half, :])
    pair_ref[...] = means[2 * half :, :]


def middle_mlp(layout, blocks, tiles, early, length):
    n_rows, width = tiles[0].shape
    cols = blocks[0].shape[1]
    half = n_rows // length
    tiles = tiles[2:] if early else tiles
    vmem = pl.BlockSpec(memory_space=pltpu.VMEM)
    return pl.pallas_call(
        functools.partial(middle_kernel, layout, length, len(blocks), len(tiles)),
        in_specs=[pl.BlockSpec(memory_space=pl.ANY)] * (len(blocks) + len(tiles))
        + [vmem] * len(early),
        out_specs=(vmem, vmem, vmem),
        out_shape=(
            pltpu.VMEM((half, cols // 2), jnp.float32),
            pltpu.VMEM((width, cols), jnp.bfloat16),
            jax.ShapeDtypeStruct((half * cols // LANES, LANES), jnp.bfloat16),
        ),
        input_output_aliases={len(blocks) + len(tiles) + 1: 1} if early else {},
        scratch_shapes=[
            pltpu.VMEM((len(tiles), n_rows, width), jnp.bfloat16),
            pltpu.VMEM((length, cols), jnp.float32),
            pltpu.VMEM((length, cols), jnp.float32),
            pltpu.VMEM((3 * half, cols // 2), jnp.float32),
            pltpu.SemaphoreType.DMA((len(blocks) + 1,)),
            pltpu.SemaphoreType.DMA((len(tiles), layout.nz)),
        ],
        compiler_params=pltpu.CompilerParams(vmem_limit_bytes=MLP_VMEM),
        cost_estimate=pl.CostEstimate(
            flops=4 * n_rows * width * cols,
            bytes_accessed=2 * (3 * n_rows * width + width * cols),
            transcendentals=0,
        ),
    )(*blocks, *(tiles if early else in_hbm(*tiles)), *in_vmem(*early))


def last_kernel(layout, length, means_ref, weights, tiles_ref, out_ref, rows, both, means, row_sems):
    row_loads = layout.row_copies(tiles_ref, rows, row_sems, range(layout.nz))
    for copy in row_loads:
        copy.start()
    for copy in row_loads:
        copy.wait()
    half = rows.shape[0] // length
    for i in range(half):
        here = slice(i * length, (i + 1) * length)
        product(both[i], rows.at[here], weights, 0, layout.width)
        if i:
            gated_means(both[i - 1], means, i - 1, length)
    gated_means(both[half - 1], means, half - 1, length)
    out_ref[...] = packed(means_ref[...], means[...])


def last_mlp(layout, means, weights, tiles, length):
    n_rows, width = tiles.shape
    cols = weights.shape[1]
    half = n_rows // length
    any_spec = pl.BlockSpec(memory_space=pl.ANY)
    vmem = pl.BlockSpec(memory_space=pltpu.VMEM)
    return pl.pallas_call(
        functools.partial(last_kernel, layout, length),
        in_specs=[vmem, vmem, any_spec],
        out_specs=vmem,
        out_shape=jax.ShapeDtypeStruct((half * cols // LANES, LANES), jnp.bfloat16),
        scratch_shapes=[
            pltpu.VMEM((n_rows, width), jnp.bfloat16),
            [pltpu.VMEM((length, cols), jnp.float32) for _ in range(half)],
            pltpu.VMEM((half, cols // 2), jnp.float32),
            pltpu.SemaphoreType.DMA((layout.nz,)),
        ],
        compiler_params=pltpu.CompilerParams(vmem_limit_bytes=MLP_VMEM),
        cost_estimate=pl.CostEstimate(
            flops=2 * n_rows * width * cols,
            bytes_accessed=2 * (n_rows * width + width * cols),
            transcendentals=0,
        ),
    )(*in_vmem(means, weights), tiles)


def small_mod(value, rate):
    return jnp.where(
        rate == 1,
        0,
        jnp.where(rate == 2, value & 1, jnp.where(rate == 3, lax.rem(value, 3), value & 3)),
    )


def multiplicity_kernel(n_dev, slot_count, heads, counts_ref, slide_ref, rates_ref, out_ref):
    me, core = lax.axis_index("dev"), lax.axis_index("sub")
    shape = out_ref.shape
    row = lax.broadcasted_iota(jnp.int32, shape, 0)
    col = lax.broadcasted_iota(jnp.int32, shape, 1)
    head = row // QROWS + core * (heads // 2)
    head = jnp.where(head >= heads, head - heads, head)
    query = row % QROWS
    device, slot = col // slot_count, col % slot_count
    rate = jnp.full(shape, 1, jnp.int32)
    for h in range(heads):
        rate = jnp.where(head == h, rates_ref[h], rate)
    my_slide = slide_ref[me]
    first = me
    count = jnp.zeros(shape, jnp.int32)
    slide = jnp.zeros(shape, jnp.int32)
    for k in reversed(range(n_dev)):
        first = jnp.where(slide_ref[k] == my_slide, k, first)
        count = jnp.where(device == k, counts_ref[k], count)
        slide = jnp.where(device == k, slide_ref[k], slide)
    offset = small_mod(head, rate)
    query_position = (me - first) * slot_count + query
    key_position = (device - first) * slot_count + slot
    valid = slot < count
    near = jnp.where((device == me) & valid, 1.0, 0.0)
    far = jnp.where(
        (slide == my_slide)
        & valid
        & (small_mod(query_position, rate) == offset)
        & (small_mod(key_position, rate) == offset),
        1.0,
        0.0,
    )
    out_ref[...] = near + far


def embed_kernel(
    counts_ref,
    own_ref,
    own_far_ref,
    pair_ref,
    pair_far_ref,
    gain_ref,
    near_ref,
    far_ref,
    embed_ref,
    mixed_ref,
    sent_ref,
):
    slot_count, half = embed_ref.shape
    n_blocks = half // 2 // LANES
    low = lax.rem(lax.axis_index("grp"), 2) == 0
    count = counts_ref[lax.axis_index("dev")]

    def features(mine_ref, theirs_ref):
        sides = []
        for ref in (mine_ref, theirs_ref):
            part = ref[...].astype(jnp.float32)
            pieces = [part[k * slot_count : (k + 1) * slot_count] for k in range(n_blocks)]
            sides.append(jnp.concatenate(pieces, axis=1))
        mine, theirs = sides
        rows = jnp.concatenate(
            [jnp.where(low, mine, theirs), jnp.where(low, theirs, mine)], axis=1
        )
        slot = lax.broadcasted_iota(jnp.int32, rows.shape, 0)
        return jnp.where(slot < count, rows, 0.0).astype(jnp.bfloat16)

    near = features(own_ref, pair_ref)
    far = features(own_far_ref, pair_far_ref)
    embed_ref[...] = near
    mixed = jnp.dot(near, near_ref[...], preferred_element_type=jnp.float32) + jnp.dot(
        far, far_ref[...], preferred_element_type=jnp.float32
    )
    mixed_ref[...] = jnp.concatenate([mixed, mixed], axis=0)
    hidden = normed(mixed, gain_ref[...].reshape(1, -1)).astype(jnp.float32)
    width = sent_ref.shape[2]
    pieces = [hidden[:, k : k + width] for k in range(0, hidden.shape[1], width)]
    pieces += [jnp.zeros_like(pieces[0])] * (sent_ref.shape[1] // slot_count - len(pieces))
    sent = jnp.concatenate(pieces, axis=0).astype(jnp.bfloat16)
    for k in range(sent_ref.shape[0]):
        sent_ref[k] = sent


def project(rows, near_ref, far_ref):
    return jnp.concatenate(
        [
            jnp.dot(rows, near_ref[...], preferred_element_type=jnp.float32),
            jnp.dot(rows, far_ref[...], preferred_element_type=jnp.float32),
        ],
        axis=1,
    )


def heads_of(shape):
    return (
        lax.broadcasted_iota(jnp.int32, shape, 0) // QROWS
        == lax.broadcasted_iota(jnp.int32, shape, 1) // HD
    )


def query_kernel(heads, mixed_ref, gain_ref, far_ref, *refs):
    near_refs, (many_ref, out_ref, many, *kept), (wq, sems) = refs[:4], refs[4:-2], refs[-2:]
    places = [wq.at[0], wq.at[1], *kept]
    copies = []
    at = 0
    for k, near in enumerate(near_refs):
        far = far_ref.at[at : at + near.shape[0]]
        at += near.shape[0]
        for i, source in enumerate((near, far)):
            copies.append(pltpu.make_async_copy(source, places[2 * k + i], sems.at[2 * k + i]))
    copies.append(pltpu.make_async_copy(many_ref, many, sems.at[len(copies)]))
    for copy in copies:
        copy.start()
    hidden = normed(mixed_ref[...], gain_ref[...].reshape(1, -1))
    for copy in copies[:2]:
        copy.wait()
    query = project(hidden, wq.at[0], wq.at[1])
    spread = jnp.concatenate([query] * heads, axis=0)
    out_ref[...] = jnp.where(heads_of(spread.shape), spread, 0.0).astype(jnp.bfloat16)
    for copy in copies[2:]:
        copy.wait()


def slide_kernel(
    heads,
    counts_ref,
    sent_ref,
    mixed_ref,
    query_ref,
    wk_ref,
    wk_far_ref,
    wv_ref,
    wv_far_ref,
    wo_ref,
    wo_far_ref,
    many_ref,
    out_ref,
    rows,
):
    slot_count, half = out_ref.shape
    core = lax.axis_index("sub")
    count = counts_ref[lax.axis_index("dev")]
    width = sent_ref.shape[2]
    for k in range(sent_ref.shape[0]):
        sent = sent_ref[k].astype(jnp.float32)
        rows[k * slot_count : (k + 1) * slot_count, :] = jnp.concatenate(
            [
                sent[j * slot_count : (j + 1) * slot_count]
                for j in range(rows.shape[1] // width)
            ],
            axis=1,
        )
    hidden = rows[...].astype(jnp.bfloat16)
    keys = project(hidden, wk_ref, wk_far_ref).astype(jnp.bfloat16)
    scores = lax.dot_general(
        query_ref[...], keys, (((1,), (1,)), ((), ())), preferred_element_type=jnp.float32
    ) * (1.0 / math.sqrt(HD))
    values = project(hidden, wv_ref, wv_far_ref).astype(jnp.bfloat16)
    many = many_ref[...]
    masked = jnp.where(many > 0.0, scores, FLOOR)
    weights = many * jnp.exp(masked - jnp.max(masked, axis=1, keepdims=True))
    weights = weights / jnp.sum(weights, axis=1, keepdims=True)
    context = jnp.dot(weights.astype(jnp.bfloat16), values, preferred_element_type=jnp.float32)
    context = jnp.where(heads_of(context.shape), context, 0.0)
    context = context.reshape(heads, QROWS, context.shape[1])
    context = jnp.sum(context, axis=0).astype(jnp.bfloat16)
    columns = pl.ds(pl.multiple_of(core * half, LANES), half)
    attended = jnp.dot(
        context[:, :half], wo_ref[:, columns], preferred_element_type=jnp.float32
    ) + jnp.dot(context[:, half:], wo_far_ref[...], preferred_element_type=jnp.float32)
    total = mixed_ref[:, columns] + attended
    slot = lax.broadcasted_iota(jnp.int32, total.shape, 0)
    total = jnp.where(slot < count, total, 0.0)
    out_ref[...] = total[:slot_count].astype(jnp.bfloat16)


def on_device(
    tiles,
    counts,
    slide_of,
    rates,
    tile_gain,
    gate_weight,
    up_weight,
    embed_proj,
    slide_gain,
    slide_wq,
    slide_wk,
    slide_wv,
    slide_wo,
):
    slot_count, length, width = tiles.shape
    hidden_cols = gate_weight.shape[1]
    n_grp, n_dev, n_sub = (lax.axis_size(a) for a in ("grp", "dev", "sub"))
    ny = 2
    nz = n_dev // ny
    heads = slide_wq.shape[1] * n_sub // HD
    core = lax.axis_index("sub")

    to_pair = [(g, g ^ 1) for g in range(n_grp)]
    to_sibling = [(s, s ^ 1) for s in range(n_sub)]
    along_y = [(d, d ^ 1) for d in range(n_dev)]

    layout = Layout(n_dev, ny, gate_weight.shape[0])
    ring = layout.ring()
    along_z = [
        (z * ny + y, ring[(i + 1) % nz] * ny + y) for i, z in enumerate(ring) for y in range(ny)
    ]
    slide_weights = [slide_wq, slide_wk, slide_wv, slide_wo]
    first, pack, whole, *held = start_work(
        tiles, tile_gain, gate_weight, up_weight, slide_weights, layout.parts
    )
    second = lax.ppermute(first, "sub", to_sibling)
    pair_first = lax.ppermute(first, "grp", to_pair)
    proj_far = lax.ppermute(embed_proj, "sub", to_sibling)
    pack_far = lax.ppermute(pack, "sub", to_sibling)
    out_cols = slide_wo.shape[1] // n_sub
    smem = pl.BlockSpec(memory_space=pltpu.SMEM)
    vmem = pl.BlockSpec(memory_space=pltpu.VMEM)
    many = pl.pallas_call(
        functools.partial(multiplicity_kernel, n_dev, slot_count, heads),
        in_specs=[smem] * 3,
        out_specs=vmem,
        out_shape=jax.ShapeDtypeStruct((heads * QROWS, n_dev * slot_count), jnp.float32),
        compiler_params=pltpu.CompilerParams(vmem_limit_bytes=SMALL_VMEM),
    )(counts, slide_of, rates)

    held[1] = after(held[1], proj_far, second)
    steps = []
    last = None
    for step in range(nz):
        sent = []
        for part in range(len(held)):
            over = None
            if step:
                arrived = lax.ppermute(held[part], "dev", along_z)
                others = [] if last is None else [last]
                over = steps[-1][-1] if step == 1 else steps[-1][len(held) + part]
                if (step, part) not in ((1, 0), (nz - 1, 1)):
                    others.append(over)
                if (step, part) == (nz - 1, 0):
                    others += [many]
                held[part] = last = after(arrived, *others)
            if (step, part) == (nz - 1, 0):
                sent.append(lax.ppermute(after(over, last), "dev", along_z))
            elif step:
                sent.append(lax.ppermute(held[part], "dev", along_y))
        if step == 0:
            sent.append(lax.ppermute(whole, "dev", along_y))
        steps.append([*held, *sent])
    blocks = [block for step in steps for block in step]
    early = []
    if layout.relative:
        n_early = sum(len(step) for step in steps[: layout.early_steps])
        early = early_mlp(layout, blocks[:n_early], [after(first, last), second])
        blocks = blocks[n_early:]
    pair_first = after(pair_first, *steps[-1][-2:], *early)
    pair_second = lax.ppermute(pair_first, "sub", to_sibling)
    means, weights, own = middle_mlp(
        layout, blocks, [first, second, pair_first], early, length
    )
    own_far = lax.ppermute(own, "sub", to_sibling)
    pair = last_mlp(layout, means, weights, pair_second, length)
    across = [
        (g * n_sub + s, (g ^ 1) * n_sub + (s ^ 1)) for g in range(n_grp) for s in range(n_sub)
    ]
    pair_far = lax.ppermute(pair, ("grp", "sub"), across)
    pair = lax.ppermute(pair, "grp", to_pair)

    out_width = embed_proj.shape[1]
    sent_rows = 16
    sent_cols = 2 * LANES
    small = pltpu.CompilerParams(vmem_limit_bytes=SMALL_VMEM)
    tile_embed, mixed, sent = pl.pallas_call(
        embed_kernel,
        in_specs=[smem] + [vmem] * 7,
        out_specs=(vmem, vmem, vmem),
        out_shape=(
            jax.ShapeDtypeStruct((slot_count, hidden_cols), jnp.bfloat16),
            pltpu.VMEM((QROWS, out_width), jnp.float32),
            pltpu.VMEM((n_dev, sent_rows, sent_cols), jnp.bfloat16),
        ),
        compiler_params=small,
    )(counts, *in_vmem(own, own_far, pair, pair_far), slide_gain, embed_proj, proj_far)
    sent = lax.all_to_all(sent, "dev", split_axis=0, concat_axis=0, tiled=True)
    hbm = pl.BlockSpec(memory_space=pltpu.HBM)
    far_shape = (slide_wo.shape[0], out_cols)
    kept = [slide_wk.shape] * 4 + [slide_wo.shape, far_shape]
    query, many, *weights = pl.pallas_call(
        functools.partial(query_kernel, heads),
        in_specs=[vmem] * 2 + [hbm] * 6,
        out_specs=[vmem] * (2 + len(kept)),
        out_shape=[
            pltpu.VMEM((heads * QROWS, out_width), jnp.bfloat16),
            pltpu.VMEM(many.shape, many.dtype),
            *[pltpu.VMEM(shape, jnp.bfloat16) for shape in kept],
        ],
        scratch_shapes=[
            pltpu.VMEM((2, *slide_wq.shape), jnp.bfloat16),
            pltpu.SemaphoreType.DMA((3 + len(kept),)),
        ],
        compiler_params=small,
    )(*in_vmem(mixed), slide_gain, *in_hbm(pack_far, *slide_weights, many))
    slide_out = pl.pallas_call(
        functools.partial(slide_kernel, heads),
        in_specs=[smem] + [vmem] * 10,
        out_specs=vmem,
        out_shape=jax.ShapeDtypeStruct((slot_count, out_cols), jnp.bfloat16),
        scratch_shapes=[pltpu.VMEM((n_dev * slot_count, out_width), jnp.float32)],
        compiler_params=small,
    )(counts, *in_vmem(sent, mixed, query, *weights, many))
    return (tile_embed, slide_out)


def solution(mesh):
    placed = (
        P(("grp", "dev"), None, None),
        P("grp"),
        P("grp"),
        P(),
        P(),
        P("dev", "sub"),
        P("dev", "sub"),
        P("sub", None),
        P(),
        P(None, "sub"),
        P(None, "sub"),
        P(None, "sub"),
        P("sub", None),
    )
    return jax.shard_map(
        on_device,
        mesh=mesh,
        in_specs=placed,
        out_specs=(P(("grp", "dev"), "sub"), P(("grp", "dev"), "sub")),
        check_vma=False,
    )
```
